32 devices in a mesh: dom: 32 (over z, y, x, core).
Axes of the slice: x: 2, y: 2, z: 4, core: 2. Of those that a mesh axis runs over, the one named last changes fastest.
Arguments:
- element_freedom_values: float32 [9, 20, 32768], P(None, None, 'dom'), may hold values from -6 to 6
- scaled_jacobian_matrices: float32 [3, 9, 9, 32768], P(None, None, None, 'dom'), may hold values from -2 to 2
- outward_face_normals: float32 [4, 3, 32768], P(None, None, 'dom'), may hold values from -3 to 3
- largest_wave_speed: float32 [32768], P('dom'), may hold values from 0.5 to 2
- element_cluster_index: int32 [32768], P('dom'), may hold values 0 or 1
- element_new_slot: int32 [32768], P('dom'), may hold values from 0 to 36863, as said below
- neighbours: int32 [4, 32768], P(None, 'dom'), may hold values from 0 to 36607, as said below
- face_rotation_codes: int32 [4, 32768], P(None, 'dom'), may hold values from 0 to 11
- deriv_mats: float32 [3, 20, 20], replicated, may hold values from -1.25 to 1.25
- stiff_mats: float32 [3, 20, 20], replicated, may hold values from -1.25 to 1.25
- face_eval: float32 [12, 20, 16], replicated, may hold values from -1.25 to 1.25
- face_lift: float32 [4, 16, 20], replicated, may hold values from -1.5 to 1.5
Outputs:
- new_state: float32 [9, 20, 36864], P(None, None, 'dom')
The draws below stay inside these ranges and needn't reach their ends.
Inputs may be any that keep to these rules, and one draw needn't show every extreme that they name: `element_new_slot`: one to one into slots partition * 1152 + local slot. Element 896 + j of partition d either stays at its local index or, on partitions that shed work, goes with g = j div 16 to partition (d + max(g * 4, 1)) mod 32, local slot 1024 + g * 16 + j mod 16; a partition sheds all 128 such elements or none; elements below 896 stay. Partitions 0 and 31 receive all 8 groups. `neighbours`: each names an occupied slot whose local index is below 896, on the element's own partition after migration or on one at s partitions' distance, s in -4..4 or s = 16, cyclically; at most one face of an element lies off its partition; from the elements of one partition after migration at most 32 faces name any one other partition, and partition 0 is named by exactly 32 faces from each of the nine partitions at those distances.
All inputs are finite; a program needn't handle non-finite values. No bound on the sum of `element_cluster_index` on one device may be relied on, other than what follows from the above.
Results may differ from the reference program's by a relative error of at most 0.0001.
Values sent between devices are 32-bit elements; how exact they have to be, the bound alone decides.
No kernel may reach another device: no remote copies, remote signals or barrier semaphores. Data moves between devices by JAX's collectives and lax.ppermute only.
A program may use at most 256 MiB of HBM per device.

```python
import math
import jax
import jax.numpy as jnp
from jax import lax

QUANTITY_COUNT = 9
BASIS_COUNT = 20
NQ = 16
NORDER = 4
GROUPS = 8
E_DEV = 1024
CSZ = 16
KEEP = 896
PARTITION_SLOTS = 1152
REQ = 32
NE = 32768
N_DOM = 32


def group_offsets():
    return jnp.maximum(jnp.arange(GROUPS) * (N_DOM // GROUPS), 1)


def shed_flags(key):
    flags = jax.random.randint(jax.random.fold_in(key, 11), (N_DOM,), 0, 2)
    sources = group_offsets()
    flags = flags.at[(0 - sources) % N_DOM].set(1)
    flags = flags.at[(N_DOM - 1 - sources) % N_DOM].set(1)
    return flags


def draw_element_new_slot(key, part):
    flags = shed_flags(key)
    element = jnp.arange(N_DOM * E_DEV)
    device = element // E_DEV
    local = element % E_DEV
    moved = jnp.maximum(local - KEEP, 0)
    member = moved // CSZ
    target = (device + group_offsets()[member]) % N_DOM
    slot = E_DEV + member * CSZ + moved % CSZ
    leaves = (flags[device] == 1) & (local >= KEEP)
    return jnp.where(leaves, target * PARTITION_SLOTS + slot, device * PARTITION_SLOTS + local).astype(jnp.int32)


def new_links(key):
    offsets = jnp.array([1, 2, 3, 4, -1, -2, -3, -4, N_DOM // 2])
    spread = 9
    counts = jax.random.randint(jax.random.fold_in(key, 21), (N_DOM, spread), 1, REQ + 1)
    counts = counts.at[(0 - offsets) % N_DOM, jnp.arange(spread)].set(REQ)
    orders = jax.vmap(lambda sub: jax.random.permutation(sub, KEEP))(jax.random.split(jax.random.fold_in(key, 22), N_DOM))
    roles = jnp.concatenate([orders, jnp.full((N_DOM, PARTITION_SLOTS - KEEP), spread * REQ)], axis=1)
    which = jnp.minimum(roles // REQ, spread - 1)
    within = roles % REQ
    device = jnp.arange(N_DOM)[:, None]
    remote = (roles < spread * REQ) & (within < jnp.take_along_axis(counts, which, axis=1))
    far_device = (device + offsets[which]) % N_DOM
    far_slot = jax.random.randint(jax.random.fold_in(key, 23), (N_DOM, PARTITION_SLOTS), 0, KEEP)
    near_slot = jax.random.randint(jax.random.fold_in(key, 24), (4, N_DOM, PARTITION_SLOTS), 0, KEEP)
    remote_face = jax.random.randint(jax.random.fold_in(key, 25), (N_DOM, PARTITION_SLOTS), 0, 4)
    linked = device[None] * PARTITION_SLOTS + near_slot
    far_link = far_device * PARTITION_SLOTS + far_slot
    use_far = (jnp.arange(4)[:, None, None] == remote_face[None]) & remote[None]
    linked = jnp.where(use_far, far_link[None], linked)
    linked = linked.at[0, 0, PARTITION_SLOTS - 1].set(0)
    linked = linked.at[0, N_DOM - 1, PARTITION_SLOTS - 1].set((N_DOM - 1) * PARTITION_SLOTS + KEEP - 1)
    return linked.reshape(4, N_DOM * PARTITION_SLOTS)


def draw_neighbours(key, part):
    return new_links(key)[:, draw_element_new_slot(key, part)].astype(jnp.int32)


def with_ends(values, key, smallest, high):
    longest = values.shape.index(max(values.shape))
    spots = []
    for shift in (0, 1):
        where = [jax.random.randint(jax.random.fold_in(key, axis), (), 0, length) for axis, length in enumerate(values.shape)]
        where[longest] = (where[longest] + shift) % values.shape[longest]
        spots.append(tuple(where))
    return values.at[spots[0]].set(smallest).at[spots[1]].set(high)


def block_levels(stream_key, extent, cuts, least, largest):
    factor_of = 1.0
    for position, blocks in cuts:
        heights = jax.random.uniform(jax.random.fold_in(jax.random.fold_in(stream_key, 6), position), (blocks,), jnp.float32, least / len(cuts), largest / len(cuts))
        factor_of = factor_of * jnp.repeat(jnp.exp(heights), extent[position] // blocks).reshape((-1,) + (1,) * (len(extent) - 1 - position))
    return factor_of


def normal_values(own_key, dims, deviation, reach, cuts=(), held_as=jnp.bfloat16):
    values = jax.random.normal(own_key, dims, jnp.float32) * deviation
    if len(cuts) > 0:
        values = block_levels(own_key, dims, cuts, -0.22, 0.18) * values
    return jnp.clip(values, min=-reach, max=reach).astype(held_as)


def setup_inputs(seed: int = 0) -> dict:
    arg_keys = jax.random.split(jax.random.key(seed), 13)
    return {
        "element_freedom_values": normal_values(arg_keys[0], (QUANTITY_COUNT, BASIS_COUNT, NE), 1.0, 6.0, ((2, 32),), jnp.float32),
        "scaled_jacobian_matrices": normal_values(arg_keys[1], (3, QUANTITY_COUNT, QUANTITY_COUNT, NE), QUANTITY_COUNT ** -0.5, 2.0, ((3, 32),), jnp.float32),
        "outward_face_normals": normal_values(arg_keys[2], (4, 3, NE), 0.5, 3.0, ((2, 32),), jnp.float32),
        "largest_wave_speed": jnp.clip(jnp.exp(math.log(2.0) - 1.3862944 * jax.random.uniform(arg_keys[3], (NE,), jnp.float32) ** block_levels(arg_keys[3], (NE,), ((0, 32),), -0.2, 0.2)), 0.5, 2.0),
        "element_cluster_index": with_ends((jax.random.randint(arg_keys[4], (NE,), 0, 2) < 1).astype(jnp.int32), jax.random.fold_in(arg_keys[4], 1), 0, 1),
        "element_new_slot": draw_element_new_slot(jax.random.fold_in(arg_keys[12], 71), 0),
        "neighbours": draw_neighbours(jax.random.fold_in(arg_keys[12], 71), 0),
        "face_rotation_codes": with_ends(jax.random.randint(arg_keys[7], (4, NE), 0, 12), jax.random.fold_in(arg_keys[7], 1), 0, 11).astype(jnp.int32),
        "deriv_mats": normal_values(arg_keys[8], (3, BASIS_COUNT, BASIS_COUNT), BASIS_COUNT ** -0.5, 1.25, (), jnp.float32),
        "stiff_mats": normal_values(arg_keys[9], (3, BASIS_COUNT, BASIS_COUNT), BASIS_COUNT ** -0.5, 1.25, (), jnp.float32),
        "face_eval": normal_values(arg_keys[10], (12, BASIS_COUNT, NQ), BASIS_COUNT ** -0.5, 1.25, (), jnp.float32),
        "face_lift": normal_values(arg_keys[11], (4, NQ, BASIS_COUNT), NQ ** -0.5, 1.5, (), jnp.float32),
    }


step_fast = 0.25
precise = lax.Precision.HIGHEST


def coefficients(lower, upper):
    return [(upper ** (degree + 1) - lower ** (degree + 1)) / math.factorial(degree + 1) for degree in range(NORDER)]


def predictor(present_state, element_jacobian_set, deriv_mats):
    series = [present_state]
    for degree in range(NORDER - 1):
        turned = jnp.einsum('qce,dcb->dqbe', series[-1], deriv_mats, precision=precise)
        series.append(-jnp.einsum('dpqe,dqbe->pbe', element_jacobian_set, turned, precision=precise))
    return series


def integrate(series, lower, upper):
    result = jnp.zeros_like(series[0])
    for factor, member in zip(coefficients(lower, upper), series):
        result = result + factor * member
    return result


def update(integral, outside, element_jacobian_set, scaled_normals, element_speeds, face_rotations, stiff_mats, face_eval, face_lift):
    turned = jnp.einsum('qce,dcb->dqbe', integral, stiff_mats, precision=precise)
    change = jnp.einsum('dpqe,dqbe->pbe', element_jacobian_set, turned, precision=precise)
    for which_face in range(4):
        inner = jnp.einsum('pbe,bn->pne', integral, face_eval[3 * which_face], precision=precise)
        picked = jnp.take(face_eval, face_rotations[which_face], axis=0)
        outer = jnp.einsum('pbe,ebn->pne', outside[which_face], picked, precision=precise)
        normal_star = jnp.einsum('de,dpqe->pqe', scaled_normals[which_face], element_jacobian_set, precision=precise)
        flux = 0.5 * jnp.einsum('pqe,qne->pne', normal_star, inner + outer, precision=precise) + 0.5 * element_speeds * (inner - outer)
        change = change - jnp.einsum('pne,nb->pbe', flux, face_lift[which_face], precision=precise)
    return change


def reference(element_freedom_values, scaled_jacobian_matrices, outward_face_normals, largest_wave_speed, element_cluster_index, element_new_slot, neighbours, face_rotation_codes, deriv_mats, stiff_mats, face_eval, face_lift):
    slot_count = PARTITION_SLOTS * N_DOM
    present_state = jnp.zeros((QUANTITY_COUNT, BASIS_COUNT, slot_count), jnp.float32).at[:, :, element_new_slot].set(element_freedom_values)
    element_jacobian_set = jnp.zeros((3, QUANTITY_COUNT, QUANTITY_COUNT, slot_count), jnp.float32).at[:, :, :, element_new_slot].set(scaled_jacobian_matrices)
    scaled_normals = jnp.zeros((4, 3, slot_count), jnp.float32).at[:, :, element_new_slot].set(outward_face_normals)
    element_speeds = jnp.zeros((slot_count,), jnp.float32).at[element_new_slot].set(largest_wave_speed)
    time_clusters = jnp.zeros((slot_count,), jnp.int32).at[element_new_slot].set(element_cluster_index)
    neighbour_links = jnp.zeros((4, slot_count), jnp.int32).at[:, element_new_slot].set(neighbours)
    face_rotations = jnp.zeros((4, slot_count), jnp.int32).at[:, element_new_slot].set(face_rotation_codes)

    def outside(data):
        return [data[:, :, neighbour_links[which_face]] for which_face in range(4)]

    def apply(integral, others):
        return update(integral, others, element_jacobian_set, scaled_normals, element_speeds, face_rotations, stiff_mats, face_eval, face_lift)

    fast = (time_clusters == 0)[None, None, :]
    series = predictor(present_state, element_jacobian_set, deriv_mats)
    first = integrate(series, 0.0, step_fast)
    slow_second = integrate(series, step_fast, 2.0 * step_fast)
    first_out = outside(first)
    midway = jnp.where(fast, present_state + apply(first, first_out), present_state)
    fast_second = integrate(predictor(midway, element_jacobian_set, deriv_mats), 0.0, step_fast)
    second = jnp.where(fast, fast_second, slow_second)
    second_out = outside(second)
    fast_end = midway + apply(second, second_out)
    total = first + second
    total_out = outside(total)
    slow_end = present_state + apply(total, total_out)
    return jnp.where(fast, fast_end, slow_end)
```

```python
import math

import jax
import jax.numpy as jnp
from jax import lax
from jax.experimental import pallas as pl
from jax.experimental.pallas import tpu as pltpu
from jax.sharding import PartitionSpec as P

NV = 9
NB = 20
NBP = 24
NQ = 16
NORDER = 4
GROUPS = 8
CSZ = 16
KEEP = 896
PARTITION_SLOTS = 1152
REQ = 32
PARTNERS = 9
NEAR = 8
LANES = 128
WIDE = 256
ROWS = 216
PACK = 192
MSG = 256
FAR = 384
RECORD = 768
SMALL = 24
MESSAGE1 = REQ + 8

step_fast = 0.25
exact = lax.Precision.HIGHEST
f32 = jnp.float32
bf16 = jnp.bfloat16
i32 = jnp.int32

SPEED, CLUSTER, LINK, ORIENT, OCCUPIED = 12, 13, 14, 18, 22

PARAMS = pltpu.CompilerParams(vmem_limit_bytes=48 << 20)


def coefficients(lower, upper):
    return [
        (upper ** (degree + 1) - lower ** (degree + 1)) / math.factorial(degree + 1)
        for degree in range(NORDER)
    ]


FIRST = coefficients(0.0, step_fast)
SECOND = coefficients(step_fast, 2.0 * step_fast)


def partner_offsets(devices):
    return [1, 2, 3, 4, -1, -2, -3, -4, devices // 2]


def packed_row(quantity, basis):
    group, member = quantity // 3, quantity % 3
    inside = 16 * member + basis if basis < 16 else 48 + 4 * member + (basis - 16)
    return 64 * group + inside


def pack_three(members):
    a, b, c = members
    tail = a[16:24] + pltpu.roll(b[16:24], 4, 0)
    return jnp.concatenate([a[:16], b[:16], c[:16], tail, c[16:24]], axis=0)


def split(values):
    high = values.astype(bf16)
    low = (values - high.astype(f32)).astype(bf16)
    return high, low


def stacked(high, low):
    return jnp.concatenate([high, low, high], axis=0)


def dot(a, b):
    return jnp.dot(a, b, preferred_element_type=f32)


def dot_last(a, b):
    return lax.dot_general(a, b, (((1,), (1,)), ((), ())), preferred_element_type=f32)


def iota(shape, axis):
    return lax.broadcasted_iota(i32, shape, axis)


def one_hot(condition):
    return jnp.where(condition, 1.0, 0.0).astype(bf16)


def weights_kernel(deriv, stiff, evals, lift, evals_flat, w_pred, w_own, w_lift, w_table, square):
    def turned(matrix, rows, columns):
        square[...] = jnp.zeros((LANES, LANES), f32)
        square[:rows, :columns] = matrix
        return square[...].T[:NBP]

    column = iota((LANES, PACK), 1) & 63
    member = jnp.where(column < 48, column >> 4, (column - 48) >> 2)
    basis = jnp.where(column < 48, column & 15, 16 + (column & 3))
    spread = one_hot(iota((LANES, PACK), 0) == jnp.where(member < 3, basis, -1))
    member = member[:NBP]
    part = iota((NBP, PACK), 1)

    def three(matrix):
        high, low = split(turned(matrix, NB, NB))
        row = jnp.where(part < 128, dot(high, spread), dot(low, spread))
        return [jnp.where(member == inner, row, 0.0) for inner in range(3)]

    blocks = []
    for axis in range(3):
        blocks += three(-deriv[axis])
    w_pred[...] = jnp.concatenate(blocks, axis=0).astype(bf16)

    own = [
        jnp.dot(evals[3 * face], lift[face], precision=exact, preferred_element_type=f32) for face in range(4)
    ]
    blocks = []
    for matrix in [stiff[axis] for axis in range(3)] + own + [own[0] + own[1] + own[2] + own[3]]:
        blocks += three(matrix if len(blocks) < 9 else -0.5 * matrix)
    w_own[...] = jnp.concatenate(blocks, axis=0).astype(bf16)

    column = iota((LANES, 144), 1)
    spread = one_hot(iota((LANES, 144), 0) == (column & 15))
    column = column[:NBP]
    block = column >> 4
    member = block - jnp.where(column >= 96, 6, jnp.where(column >= 48, 3, 0))
    for face in range(4):
        high, low = split(turned(lift[face], NQ, NB))
        row = jnp.where(column < 96, dot(high, spread), dot(low, spread))
        rows = [jnp.where(member == inner, -0.5 * row, 0.0) for inner in range(3)]
        w_lift[face] = jnp.concatenate(rows + [-r for r in rows], axis=0).astype(bf16)

    flat = evals_flat[...]
    high = flat.astype(bf16).astype(f32)
    low = flat - high
    source = jnp.concatenate([high, low, jnp.zeros((96, 384), f32)], axis=0)
    w_table[...] = source.T[:320, :32].astype(bf16)


def make_weights(deriv, stiff, evals, lift):
    flat = jnp.pad(evals.reshape(12, NB * NQ), ((0, 4), (0, 384 - NB * NQ)))
    return pl.pallas_call(
        weights_kernel,
        out_shape=(
            jax.ShapeDtypeStruct((ROWS, PACK), bf16),
            jax.ShapeDtypeStruct((576, PACK), bf16),
            jax.ShapeDtypeStruct((4, 144, 144), bf16),
            jax.ShapeDtypeStruct((320, 32), bf16),
        ),
        scratch_shapes=[pltpu.VMEM((LANES, LANES), f32)],
        compiler_params=PARAMS,
        name="weights",
    )(deriv, stiff, evals, lift, flat)


def find_links(devices, tiles, small, aux, asks):
    me = lax.axis_index("dom").astype(f32)
    peer = iota((devices, LANES), 0).astype(f32)
    up_to = one_hot(iota((LANES, LANES), 0) <= iota((LANES, LANES), 1))
    request = (iota((LANES, LANES), 0) & (REQ - 1)).astype(f32)
    carry = jnp.zeros((devices, 1), f32)
    wanted = jnp.zeros((2 * devices, LANES), f32)
    for tile in range(tiles):
        at = slice(tile * LANES, (tile + 1) * LANES)
        occupied = small[OCCUPIED : OCCUPIED + 1, at] > 0.5
        target = jnp.full((1, LANES), -1.0, f32)
        slots = jnp.zeros((1, LANES), f32)
        for face in range(4):
            link = small[LINK + face : LINK + face + 1, at]
            owner = jnp.floor((link + 0.5) * (1.0 / PARTITION_SLOTS))
            slot = link - owner * PARTITION_SLOTS
            near = owner == me
            aux[face : face + 1, at] = jnp.where(near, slot, -1.0).astype(i32)
            away = occupied & jnp.logical_not(near)
            target = jnp.where(away, owner, target)
            slots = jnp.where(away, slot, slots)
        named = jnp.where(peer == target, 1.0, 0.0)
        prefix = dot(named.astype(bf16), up_to) + carry
        carry = carry + jnp.sum(named, axis=1, keepdims=True)
        rank = jnp.sum(named * prefix, axis=0, keepdims=True) - 1.0
        far = target - me
        far = jnp.where(far < 0, far + devices, far)
        partner = jnp.where(far <= 4, far - 1.0, jnp.where(far >= devices - 4, devices + 3.0 - far, 8.0))
        aux[4:5, at] = jnp.where(target >= 0, partner * REQ + rank, -1.0).astype(i32)
        aux[5:8, at] = jnp.zeros((3, LANES), i32)
        high = jnp.floor(slots * (1.0 / 32)) * 32.0
        both = jnp.concatenate([named * high, named * (slots - high)], axis=0).astype(bf16)
        wanted = wanted + dot_last(both, one_hot(request == rank))
    asks[:, 0, :] = wanted[:devices] + wanted[devices:]


def prepare_kernel(devices, tiles, normals, speed, cluster, slot, links, orient, q, jac, small, aux, asks, group, one):
    me = lax.axis_index("dom")
    for face in range(4):
        small[3 * face : 3 * face + 3, :] = normals[face]
    small[SPEED : SPEED + 1, :] = speed[...]
    small[CLUSTER : CLUSTER + 1, :] = cluster[...].astype(f32)
    small[LINK : LINK + 4, :] = links[...].astype(f32)
    small[ORIENT : ORIENT + 4, :] = orient[...].astype(f32)
    where = slot[...]
    stays = (where >= me * PARTITION_SLOTS) & (where < (me + 1) * PARTITION_SLOTS)
    small[OCCUPIED : OCCUPIED + 1, :] = jnp.where(stays, 1.0, 0.0)
    small[OCCUPIED + 1 : SMALL, :] = jnp.zeros((1, tiles * LANES), f32)
    find_links(devices, tiles, small, aux, asks)

    zero4 = jnp.zeros((4, LANES), f32)
    zero7 = jnp.zeros((7, LANES), f32)
    pieces = []
    for p in range(NV):
        pieces += [q[p], zero4]
    for d in range(3):
        for p in range(NV):
            pieces += [jac[d, p], zero7]
    fields = small[:, KEEP:]
    row = iota(fields.shape, 0)
    pieces.append(jnp.where(row == OCCUPIED, 1.0 - fields, fields))
    pieces.append(jnp.zeros((96, LANES), f32))
    whole = jnp.concatenate(pieces, axis=0)
    turned = jnp.concatenate([whole[c : c + LANES].T for c in range(0, RECORD, LANES)], axis=1)
    one[...] = turned[:CSZ]
    position = me // (devices // GROUPS)
    for g in range(GROUPS):
        group[lax.rem(position + g, GROUPS)] = turned[g * CSZ : (g + 1) * CSZ]


def prepare(normals, speed, cluster, slot, links, orient, q, jac, devices):
    count = q.shape[2]

    def body(*refs):
        prepare_kernel(devices, count // LANES, *refs)

    last = KEEP // LANES
    return pl.pallas_call(
        body,
        grid=(1,),
        in_specs=[
            whole_spec(normals),
            whole_spec(speed),
            whole_spec(cluster),
            whole_spec(slot),
            whole_spec(links),
            whole_spec(orient),
            pl.BlockSpec((NV, NB, LANES), lambda i: (0, 0, last)),
            pl.BlockSpec((3, NV, NV, LANES), lambda i: (0, 0, 0, last)),
        ],
        out_specs=[
            pl.BlockSpec((SMALL, count), lambda i: (0, 0)),
            pl.BlockSpec((8, count), lambda i: (0, 0)),
            pl.BlockSpec((devices, 1, LANES), lambda i: (0, 0, 0)),
            pl.BlockSpec((GROUPS, CSZ, RECORD), lambda i: (0, 0, 0)),
            pl.BlockSpec((CSZ, RECORD), lambda i: (0, 0)),
        ],
        out_shape=[
            jax.ShapeDtypeStruct((SMALL, count), f32),
            jax.ShapeDtypeStruct((8, count), i32),
            jax.ShapeDtypeStruct((devices, 1, LANES), f32),
            jax.ShapeDtypeStruct((GROUPS, CSZ, RECORD), f32),
            jax.ShapeDtypeStruct((CSZ, RECORD), f32),
        ],
        compiler_params=PARAMS,
        name="prepare",
    )(normals, speed, cluster, slot, links, orient, q, jac)


def unpack_kernel(devices, group, one, q, jac, small, aux, asks):
    position = lax.axis_index("dom") // (devices // GROUPS)
    rows = [one[...]]
    for g in range(1, GROUPS):
        rows.append(group[lax.rem(position - g + GROUPS, GROUPS)])
    whole = jnp.concatenate(rows, axis=0)
    turned = jnp.concatenate([whole[:, c : c + LANES].T for c in range(0, RECORD, LANES)], axis=0)
    for p in range(NV):
        q[p] = turned[p * NBP : p * NBP + NB]
    for d in range(3):
        for p in range(NV):
            at = ROWS + (d * NV + p) * 16
            jac[d, p] = turned[at : at + NV]
    at = ROWS + 3 * NV * 16
    small[...] = turned[at : at + SMALL]
    find_links(devices, 1, small, aux, asks)


def unpack(group, one, devices):
    def body(*refs):
        unpack_kernel(devices, *refs)

    return pl.pallas_call(
        body,
        out_shape=[
            jax.ShapeDtypeStruct((NV, NB, LANES), f32),
            jax.ShapeDtypeStruct((3, NV, NV, LANES), f32),
            jax.ShapeDtypeStruct((SMALL, LANES), f32),
            jax.ShapeDtypeStruct((8, LANES), i32),
            jax.ShapeDtypeStruct((devices, 1, LANES), f32),
        ],
        compiler_params=PARAMS,
        name="unpack",
    )(group, one)


def seat(offset):
    me = lax.axis_index("dom")
    first = lax.rem(me, NEAR)
    second = lax.rem(me + NEAR // 2, NEAR)
    there = first + offset
    inside = (there >= 0) & (there < NEAR)
    return inside, lax.rem(there + NEAR, NEAR), lax.rem(second + offset + NEAR, NEAR)


def put(offset, far, blocks, first, second, half):
    if far:
        for rows, columns, value in blocks:
            half[rows, columns] = value
        return
    inside, at_first, at_second = seat(offset)

    @pl.when(inside)
    def _():
        for rows, columns, value in blocks:
            first[at_first, rows, columns] = value

    @pl.when(jnp.logical_not(inside))
    def _():
        for rows, columns, value in blocks:
            second[at_second, rows, columns] = value


def take(offset, far, rows, first, second, half):
    if far:
        return half[rows, :]
    inside, at_first, at_second = seat(offset)
    return jnp.where(inside, first[at_first, rows, :], second[at_second, rows, :])


def picked(requests, fields):
    lane = iota((1, LANES), 1)
    tiles = []
    for at in range(0, 12, 4):
        four = [requests[min(at + n, PARTNERS - 1)] for n in range(4)]
        tiles.append(
            jnp.where(lane < 32, four[0], jnp.where(lane < 64, four[1], jnp.where(lane < 96, four[2], four[3])))
        )
    slots = iota((KEEP, FAR), 0).astype(f32)
    return dot(fields, one_hot(slots == jnp.concatenate(tiles, axis=1)))


def message_rows(both):
    value = both[:PACK] + both[PACK:]
    return jnp.concatenate([value, jnp.zeros((MSG - PACK, FAR), f32)], axis=0).T


ALL = slice(0, MSG)


def answer_kernel(devices, asks, moved, field, first, second, half):
    me = lax.axis_index("dom")
    offsets = partner_offsets(devices)
    peers = [lax.rem(me - o + devices, devices) for o in offsets]
    rows = message_rows(picked([asks[p] for p in peers], field[...]))
    for k, offset in enumerate(offsets):
        mine = jnp.broadcast_to(moved[peers[k]], (8, LANES))
        blocks = [
            (slice(0, REQ), ALL, rows[k * REQ : (k + 1) * REQ]),
            (slice(REQ, MESSAGE1), slice(0, LANES), mine),
            (slice(REQ, MESSAGE1), slice(LANES, MSG), jnp.zeros((8, MSG - LANES), f32)),
        ]
        put(-offset, k == PARTNERS - 1, blocks, first, second, half)


def answer_again_kernel(devices, asks, got_first, got_second, got_half, field, later, first, second, half):
    me = lax.axis_index("dom")
    offsets = partner_offsets(devices)
    peers = [lax.rem(me - o + devices, devices) for o in offsets]
    rows = message_rows(picked([asks[p] for p in peers], later[...]))
    moved = []
    for k, offset in enumerate(offsets):
        got = take(-offset, k == PARTNERS - 1, slice(REQ, MESSAGE1), got_first, got_second, got_half)
        moved.append(got[:1, :LANES])
    both = picked(moved, jnp.concatenate([field[...], later[...]], axis=0))
    rows_first = message_rows(both[: 2 * PACK])
    rows_later = message_rows(both[2 * PACK :])
    for k, offset in enumerate(offsets):
        at = slice(k * REQ, (k + 1) * REQ)
        blocks = [
            (slice(0, REQ), ALL, rows[at]),
            (slice(REQ, 2 * REQ), ALL, rows_first[at]),
            (slice(2 * REQ, 3 * REQ), ALL, rows_later[at]),
        ]
        put(-offset, k == PARTNERS - 1, blocks, first, second, half)


def answer(body, rows, devices, arrays, fields):
    def kernel(*refs):
        body(devices, *refs)

    return pl.pallas_call(
        kernel,
        grid=(1,),
        in_specs=[whole_spec(a) for a in arrays]
        + [pl.BlockSpec((2 * PACK, KEEP), lambda i: (0, 0))] * len(fields),
        out_specs=[pl.BlockSpec((NEAR, rows, MSG), lambda i: (0, 0, 0))] * 2
        + [pl.BlockSpec((rows, MSG), lambda i: (0, 0))],
        out_shape=[jax.ShapeDtypeStruct((NEAR, rows, MSG), f32)] * 2 + [jax.ShapeDtypeStruct((rows, MSG), f32)],
        compiler_params=PARAMS,
        name="answer",
    )(*arrays, *fields)


def far_table(devices, part, messages):
    at = slice(part * REQ, (part + 1) * REQ)
    rows = [take(o, k == PARTNERS - 1, at, *messages) for k, o in enumerate(partner_offsets(devices))]
    rows.append(jnp.zeros((FAR - PARTNERS * REQ, MSG), f32))
    turned = jnp.concatenate(rows, axis=0).T[:PACK]
    return jnp.concatenate(split(turned), axis=0)


def lanes(tile):
    return slice(tile * LANES, (tile + 1) * LANES)


def jacobian_apply(jac, tile, parts):
    result = [None] * NV
    for group in range(3):
        for d in range(3):
            for inner in range(3):
                q = 3 * group + inner
                value = parts(d, q)
                for p in range(NV):
                    term = jac[d, p, q : q + 1, lanes(tile)] * value
                    result[p] = term if result[p] is None else result[p] + term
    return result


def packed_split(fields, group):
    packed = [pack_three(tile[3 * group : 3 * group + 3]) for tile in fields]
    return split(jnp.concatenate(packed, axis=1))


def split_fields(fields):
    pairs = [packed_split(fields, group) for group in range(3)]
    return jnp.concatenate([a for a, _ in pairs] + [b for _, b in pairs], axis=0)


def predict(start, jac, w_pred, scales):
    tiles = range(len(start))
    sums = [[[s[0] * x for x in tile] for tile in start] for s in scales]
    now = start
    for degree in range(1, NORDER):
        turned = [dot(w_pred, stacked(*packed_split(now, group))) for group in range(3)]
        now = [
            jacobian_apply(
                jac, t, lambda d, q: turned[q // 3][d * 72 + (q % 3) * NBP : d * 72 + (q % 3) * NBP + NBP, lanes(t)]
            )
            for t in tiles
        ]
        sums = [
            [[a + s[degree] * x for a, x in zip(total[t], now[t])] for t in tiles] for total, s in zip(sums, scales)
        ]
    return sums


def update(own, near, far, small, aux, jac, w_own, w_lift, w_table, gathered):
    count = own.shape[1]
    tiles = range(count // LANES)
    place = aux[4:5, :]
    both = dot(far, one_hot(iota((FAR, count), 0) == place))
    remote = both[:PACK] + both[PACK:]
    slots = iota((KEEP, count), 0)
    codes = iota((16, count), 0).astype(f32)

    def gather(face):
        index = aux[face : face + 1, :]
        both = dot(near, one_hot(slots == index))
        take_far = (index < 0) & (place >= 0)
        gathered[face] = both[:PACK] + both[PACK:] + jnp.where(take_far, remote, 0.0)
        code = one_hot(codes == small[ORIENT + face : ORIENT + face + 1, :])
        return dot(w_table, jnp.concatenate([code, code], axis=0))

    table = gather(0)
    mine = []
    for group in range(3):
        rows = slice(64 * group, 64 * group + 64)
        lower = slice(PACK + 64 * group, PACK + 64 * group + 64)
        mine.append(dot(w_own, stacked(own[rows], own[lower])))

    def of_own(block, q, t):
        at = block * 72 + (q % 3) * NBP
        return mine[q // 3][at : at + NBP, lanes(t)]

    volume = [[[of_own(d, q, t) for q in range(NV)] for d in range(3)] for t in tiles]
    upwind = [[of_own(7, q, t) for q in range(NV)] for t in tiles]
    for face in range(4):
        now = table
        if face < 3:
            table = gather(face + 1)
        outers = []
        for t in tiles:
            outer = [None] * NV
            for b in range(NB):
                values = now[b * NQ : (b + 1) * NQ, lanes(t)]
                for p in range(NV):
                    at = packed_row(p, b)
                    term = gathered[face, at : at + 1, lanes(t)] * values
                    outer[p] = term if outer[p] is None else outer[p] + term
            outers.append(outer)
        for group in range(3):
            joined = [jnp.concatenate(outer[3 * group : 3 * group + 3], axis=0) for outer in outers]
            lifted = dot(w_lift[face], stacked(*split(jnp.concatenate(joined, axis=1))))
            for t in tiles:
                for inner in range(3):
                    q = 3 * group + inner
                    at = inner * NBP
                    mixed = lifted[at : at + NBP, lanes(t)] + of_own(3 + face, q, t)
                    upwind[t][q] = upwind[t][q] + lifted[72 + at : 72 + at + NBP, lanes(t)]
                    for d in range(3):
                        normal = small[3 * face + d : 3 * face + d + 1, lanes(t)]
                        volume[t][d][q] = volume[t][d][q] + normal * mixed
    result = []
    for t in tiles:
        change = jacobian_apply(jac, t, lambda d, q: volume[t][d][q])
        speed = small[SPEED : SPEED + 1, lanes(t)]
        result.append([c + speed * u for c, u in zip(change, upwind[t])])
    return result


def load_state(q, padded):
    padded[:, NB:NBP, :] = jnp.zeros((NV, NBP - NB, padded.shape[2]), f32)
    for p in range(NV):
        padded[p, :NB, :] = q[p]
    return load_field(padded)


def load_field(ref):
    return [[ref[p, :, lanes(t)] for p in range(NV)] for t in range(ref.shape[2] // LANES)]


def store_field(ref, field):
    for t, tile in enumerate(field):
        for p in range(NV):
            ref[p, :, lanes(t)] = tile[p]


def store_result(out, base, change, small):
    for t in range(len(base)):
        occupied = small[OCCUPIED : OCCUPIED + 1, lanes(t)] > 0.5
        for p in range(NV):
            out[p, :, lanes(t)] = jnp.where(occupied, base[t][p] + change[t][p], 0.0)[:NB]


def first_kernel(q, jac, w_pred, packed, slow, padded):
    first, later = predict(load_state(q, padded), jac, w_pred[...], [FIRST, SECOND])
    packed[...] = split_fields(first)
    store_field(slow, later)


def middle_step(start, jac, small, slow, own, near, far, aux, weights, gathered):
    w_pred, w_own, w_lift, w_table = weights
    change = update(own, near, far, small, aux, jac, w_own, w_lift, w_table, gathered)
    base, midway, second = [], [], []
    fast = [small[CLUSTER : CLUSTER + 1, lanes(t)] < 0.5 for t in range(len(start))]
    for t in range(len(start)):
        base.append([a + b for a, b in zip(start[t], change[t])])
        midway.append([jnp.where(fast[t], a, b) for a, b in zip(base[t], start[t])])
    (later,) = predict(midway, jac, w_pred, [FIRST])
    for t in range(len(start)):
        second.append([jnp.where(fast[t], a, b) for a, b in zip(later[t], slow[t])])
    return base, split_fields(second)


def middle_kernel(devices, q, jac, small, slow, own, near, aux, *refs):
    messages = refs[:3]
    w_pred, w_own, w_lift, w_table, base, packed, padded, gathered, far = refs[3:]

    @pl.when(pl.program_id(0) == 0)
    def _():
        far[...] = far_table(devices, 0, messages)

    weights = (w_pred[...], w_own[...], w_lift, w_table[...])
    now, second = middle_step(
        load_state(q, padded), jac, small, load_field(slow), own[...], near[...], far[...], aux, weights, gathered
    )
    store_field(base, now)
    packed[...] = second


def last_kernel(devices, base, jac, small, own, near, aux, *refs):
    messages = refs[:3]
    w_own, w_lift, w_table, out, gathered, far = refs[3:]

    @pl.when(pl.program_id(0) == 0)
    def _():
        far[...] = far_table(devices, 0, messages)

    change = update(
        own[...], near[...], far[...], small, aux, jac, w_own[...], w_lift, w_table[...], gathered
    )
    store_result(out, load_field(base), change, small)


def moved_kernel(devices, q, jac, small, aux, near, later, *refs):
    messages = refs[:3]
    w_pred, w_own, w_lift, w_table, _, out, padded, gathered = refs[3:]
    weights = (w_pred[...], w_own[...], w_lift, w_table[...])
    start = load_state(q, padded)
    first, slow = predict(start, jac, weights[0], [FIRST, SECOND])
    base, second = middle_step(
        start, jac, small, slow, split_fields(first), near[...], far_table(devices, 1, messages), aux, weights, gathered
    )
    change = update(
        second, later[...], far_table(devices, 2, messages), small, aux, jac, *weights[1:], gathered
    )
    store_result(out, base, change, small)


def whole_spec(array):
    rank = array.ndim
    return pl.BlockSpec(array.shape, lambda i: (0,) * rank)


def lane_spec(*lead):
    rank = len(lead)
    return pl.BlockSpec(lead + (WIDE,), lambda i: (0,) * rank + (i,))


def rows_spec(message):
    lead = message.shape[:-2]
    rank = message.ndim
    return pl.BlockSpec(lead + (REQ, MSG), lambda i: (0,) * rank)


Q_SPEC = lane_spec(NV, NB)
J_SPEC = lane_spec(3, NV, NV)
S_SPEC = lane_spec(SMALL)
A_SPEC = lane_spec(8)
F_SPEC = lane_spec(NV, NBP)
X_SPEC = lane_spec(2 * PACK)
N_SPEC = pl.BlockSpec((2 * PACK, KEEP), lambda i: (0, 0))


def scratch_of(width):
    return pltpu.VMEM((NV, NBP, width), f32), pltpu.VMEM((4, PACK, width), f32)


def per_device(
    element_freedom_values,
    scaled_jacobian_matrices,
    outward_face_normals,
    largest_wave_speed,
    element_cluster_index,
    element_new_slot,
    neighbours,
    face_rotation_codes,
    deriv_mats,
    stiff_mats,
    face_eval,
    face_lift,
):
    count = element_freedom_values.shape[2]
    steps = count // WIDE
    devices = lax.axis_size("dom")
    q, jac = element_freedom_values, scaled_jacobian_matrices

    def shift(array, by):
        return lax.ppermute(array, "dom", [(i, (i + by) % devices) for i in range(devices)])

    def swap(array, groups):
        return lax.all_to_all(array, "dom", split_axis=0, concat_axis=0, axis_index_groups=groups, tiled=True)

    def family(begin):
        return [[(b + begin + i) % devices for i in range(NEAR)] for b in range(0, devices, NEAR)]

    def exchange(first, second, half):
        return swap(first, family(0)), swap(second, family(NEAR // 2)), shift(half, devices // 2)

    def on_ring(body):
        def kernel(*refs):
            body(devices, *refs)

        return kernel

    small, aux, asks, group, one = prepare(
        outward_face_normals,
        largest_wave_speed[None],
        element_cluster_index[None],
        element_new_slot[None],
        neighbours,
        face_rotation_codes,
        q,
        jac,
        devices,
    )
    asks = swap(asks, None)
    stride = devices // GROUPS
    group = swap(group, [[r + stride * j for j in range(GROUPS)] for r in range(stride)])
    one = shift(one, 1)
    w_pred, w_own, w_lift, w_table = make_weights(deriv_mats, stiff_mats, face_eval, face_lift)
    weights = [w_pred, w_own, w_lift, w_table]

    padded, gathered = scratch_of(WIDE)
    packed_shape = jax.ShapeDtypeStruct((2 * PACK, count), bf16)
    field_shape = jax.ShapeDtypeStruct((NV, NBP, count), f32)
    far = pltpu.VMEM((2 * PACK, FAR), bf16)
    first, slow = pl.pallas_call(
        first_kernel,
        grid=(steps,),
        in_specs=[Q_SPEC, J_SPEC, whole_spec(w_pred)],
        out_specs=[X_SPEC, F_SPEC],
        out_shape=[packed_shape, field_shape],
        scratch_shapes=[padded],
        compiler_params=PARAMS,
        name="first",
    )(q, jac, w_pred)

    q_moved, jac_moved, small_moved, aux_moved, asks_moved = unpack(group, one, devices)
    messages = exchange(*answer(answer_kernel, MESSAGE1, devices, [asks, asks_moved], [first]))

    base, second = pl.pallas_call(
        on_ring(middle_kernel),
        grid=(steps,),
        in_specs=[Q_SPEC, J_SPEC, S_SPEC, F_SPEC, X_SPEC, N_SPEC, A_SPEC]
        + [rows_spec(m) for m in messages]
        + [whole_spec(w) for w in weights],
        out_specs=[F_SPEC, X_SPEC],
        out_shape=[field_shape, packed_shape],
        scratch_shapes=[padded, gathered, far],
        compiler_params=PARAMS,
        name="middle",
    )(q, jac, small, slow, first, first, aux, *messages, *weights)

    messages = exchange(*answer(answer_again_kernel, 3 * REQ, devices, [asks, *messages], [first, second]))

    new_state = pl.pallas_call(
        on_ring(last_kernel),
        grid=(steps,),
        in_specs=[F_SPEC, J_SPEC, S_SPEC, X_SPEC, N_SPEC, A_SPEC]
        + [rows_spec(m) for m in messages]
        + [whole_spec(w) for w in weights[1:]],
        out_specs=Q_SPEC,
        out_shape=jax.ShapeDtypeStruct((NV, NB, PARTITION_SLOTS), f32),
        scratch_shapes=[gathered, far],
        compiler_params=PARAMS,
        name="last",
    )(base, jac, small, second, second, aux, *messages, *weights[1:])

    return pl.pallas_call(
        on_ring(moved_kernel),
        grid=(1,),
        in_specs=[whole_spec(a) for a in (q_moved, jac_moved, small_moved, aux_moved)]
        + [N_SPEC, N_SPEC]
        + [whole_spec(m) for m in messages]
        + [whole_spec(w) for w in weights]
        + [pl.BlockSpec(memory_space=pl.ANY)],
        out_specs=pl.BlockSpec((NV, NB, LANES), lambda i: (0, 0, count // LANES)),
        out_shape=jax.ShapeDtypeStruct((NV, NB, PARTITION_SLOTS), f32),
        scratch_shapes=scratch_of(LANES),
        input_output_aliases={13: 0},
        compiler_params=PARAMS,
        name="moved",
    )(q_moved, jac_moved, small_moved, aux_moved, first, second, *messages, *weights, new_state)


def solution(mesh):
    placed = (
        P(None, None, "dom"),
        P(None, None, None, "dom"),
        P(None, None, "dom"),
        P("dom"),
        P("dom"),
        P("dom"),
        P(None, "dom"),
        P(None, "dom"),
        P(),
        P(),
        P(),
        P(),
    )
    return jax.shard_map(
        per_device, mesh=mesh, in_specs=placed, out_specs=P(None, None, "dom"), check_vma=False
    )
```

```python
import math

import jax
import jax.numpy as jnp
from jax import lax
from jax.experimental import pallas as pl
from jax.experimental.pallas import tpu as pltpu
from jax.sharding import PartitionSpec as P

NV = 9
NB = 20
NBP = 24
NQ = 16
NORDER = 4
GROUPS = 8
CSZ = 16
KEEP = 896
PARTITION_SLOTS = 1152
REQ = 32
PARTNERS = 9
ASKS = 16
LANES = 128
WIDE = 256
ROWS = 216
PACK = 192
MSG = 256
FAR = 384
RECORD = 768
SMALL = 24
MESSAGE1 = REQ + 8

step_fast = 0.25
exact = lax.Precision.HIGHEST
f32 = jnp.float32
bf16 = jnp.bfloat16
i32 = jnp.int32

SPEED, CLUSTER, LINK, ORIENT, OCCUPIED = 12, 13, 14, 18, 22

PARAMS = pltpu.CompilerParams(vmem_limit_bytes=16 << 20)


def coefficients(lower, upper):
    return [
        (upper ** (degree + 1) - lower ** (degree + 1)) / math.factorial(degree + 1)
        for degree in range(NORDER)
    ]


FIRST = coefficients(0.0, step_fast)
SECOND = coefficients(step_fast, 2.0 * step_fast)


def partner_offsets(devices):
    return [1, 2, 3, 4, -1, -2, -3, -4, devices // 2]


def packed_row(quantity, basis):
    group, member = quantity // 3, quantity % 3
    inside = 16 * member + basis if basis < 16 else 48 + 4 * member + (basis - 16)
    return 64 * group + inside


def pack_three(members):
    a, b, c = members
    tail = a[16:24] + pltpu.roll(b[16:24], 4, 0)
    return jnp.concatenate([a[:16], b[:16], c[:16], tail, c[16:24]], axis=0)


def split(values):
    high = values.astype(bf16)
    low = (values - high.astype(f32)).astype(bf16)
    return high, low


def stacked(high, low):
    return jnp.concatenate([high, low, high], axis=0)


def dot(a, b):
    return jnp.dot(a, b, preferred_element_type=f32)


def dot_last(a, b):
    return lax.dot_general(a, b, (((1,), (1,)), ((), ())), preferred_element_type=f32)


def iota(shape, axis):
    return lax.broadcasted_iota(i32, shape, axis)


def one_hot(condition):
    return jnp.where(condition, 1.0, 0.0).astype(bf16)


def weights_kernel(deriv, stiff, evals, lift, evals_flat, w_pred, w_own, w_lift, w_table, square):
    def turned(matrix, rows, columns):
        square[...] = jnp.zeros((LANES, LANES), f32)
        square[:rows, :columns] = matrix
        return square[...].T[:NBP]

    column = iota((LANES, PACK), 1) & 63
    member = jnp.where(column < 48, column >> 4, (column - 48) >> 2)
    basis = jnp.where(column < 48, column & 15, 16 + (column & 3))
    spread = one_hot(iota((LANES, PACK), 0) == jnp.where(member < 3, basis, -1))
    member = member[:NBP]
    part = iota((NBP, PACK), 1)

    def three(matrix):
        high, low = split(turned(matrix, NB, NB))
        row = jnp.where(part < 128, dot(high, spread), dot(low, spread))
        return [jnp.where(member == inner, row, 0.0) for inner in range(3)]

    blocks = []
    for axis in range(3):
        blocks += three(-deriv[axis])
    w_pred[...] = jnp.concatenate(blocks, axis=0).astype(bf16)

    own = [
        jnp.dot(evals[3 * face], lift[face], precision=exact, preferred_element_type=f32) for face in range(4)
    ]
    blocks = []
    for matrix in [stiff[axis] for axis in range(3)] + own + [own[0] + own[1] + own[2] + own[3]]:
        blocks += three(matrix if len(blocks) < 9 else -0.5 * matrix)
    w_own[...] = jnp.concatenate(blocks, axis=0).astype(bf16)

    column = iota((LANES, 144), 1)
    spread = one_hot(iota((LANES, 144), 0) == (column & 15))
    column = column[:NBP]
    block = column >> 4
    member = block - jnp.where(column >= 96, 6, jnp.where(column >= 48, 3, 0))
    for face in range(4):
        high, low = split(turned(lift[face], NQ, NB))
        row = jnp.where(column < 96, dot(high, spread), dot(low, spread))
        rows = [jnp.where(member == inner, -0.5 * row, 0.0) for inner in range(3)]
        w_lift[face] = jnp.concatenate(rows + [-r for r in rows], axis=0).astype(bf16)

    flat = evals_flat[...]
    high = flat.astype(bf16).astype(f32)
    low = flat - high
    source = jnp.concatenate([high, low, jnp.zeros((96, 384), f32)], axis=0)
    w_table[...] = source.T[:320, :32].astype(bf16)


def make_weights(deriv, stiff, evals, lift):
    flat = jnp.pad(evals.reshape(12, NB * NQ), ((0, 4), (0, 384 - NB * NQ)))
    return pl.pallas_call(
        weights_kernel,
        out_shape=(
            jax.ShapeDtypeStruct((ROWS, PACK), bf16),
            jax.ShapeDtypeStruct((576, PACK), bf16),
            jax.ShapeDtypeStruct((4, 144, 144), bf16),
            jax.ShapeDtypeStruct((320, 32), bf16),
        ),
        scratch_shapes=[pltpu.VMEM((LANES, LANES), f32)],
        compiler_params=PARAMS,
        name="weights",
    )(deriv, stiff, evals, lift, flat)


def find_links(devices, tiles, small, aux, asks):
    me = lax.axis_index("dom").astype(f32)
    row = iota((ASKS, LANES), 0).astype(f32)
    up_to = one_hot(iota((LANES, LANES), 0) <= iota((LANES, LANES), 1))
    request = (iota((LANES, LANES), 0) & (REQ - 1)).astype(f32)
    carry = jnp.zeros((ASKS, 1), f32)
    wanted = jnp.zeros((2 * ASKS, LANES), f32)
    for tile in range(tiles):
        at = slice(tile * LANES, (tile + 1) * LANES)
        occupied = small[OCCUPIED : OCCUPIED + 1, at] > 0.5
        target = jnp.full((1, LANES), -1.0, f32)
        slots = jnp.zeros((1, LANES), f32)
        for face in range(4):
            link = small[LINK + face : LINK + face + 1, at]
            owner = jnp.floor((link + 0.5) * (1.0 / PARTITION_SLOTS))
            slot = link - owner * PARTITION_SLOTS
            near = owner == me
            aux[face : face + 1, at] = jnp.where(near, slot, -1.0).astype(i32)
            away = occupied & jnp.logical_not(near)
            target = jnp.where(away, owner, target)
            slots = jnp.where(away, slot, slots)
        far = target - me
        far = jnp.where(far < 0, far + devices, far)
        partner = jnp.where(far <= 4, far - 1.0, jnp.where(far >= devices - 4, devices + 3.0 - far, 8.0))
        partner = jnp.where(target >= 0, partner, -1.0)
        named = jnp.where(row == partner, 1.0, 0.0)
        prefix = dot(named.astype(bf16), up_to) + carry
        carry = carry + jnp.sum(named, axis=1, keepdims=True)
        rank = jnp.sum(named * prefix, axis=0, keepdims=True) - 1.0
        aux[4:5, at] = jnp.where(target >= 0, partner * REQ + rank, -1.0).astype(i32)
        aux[5:8, at] = jnp.zeros((3, LANES), i32)
        high = jnp.floor(slots * (1.0 / 32)) * 32.0
        both = jnp.concatenate([named * high, named * (slots - high)], axis=0).astype(bf16)
        wanted = wanted + dot_last(both, one_hot(request == rank))
    asks[...] = wanted[:ASKS] + wanted[ASKS:]


def prepare_kernel(devices, tiles, normals, speed, cluster, slot, links, orient, q, jac, small, aux, asks, group, one):
    me = lax.axis_index("dom")
    for face in range(4):
        small[3 * face : 3 * face + 3, :] = normals[face]
    small[SPEED : SPEED + 1, :] = speed[...]
    small[CLUSTER : CLUSTER + 1, :] = cluster[...].astype(f32)
    small[LINK : LINK + 4, :] = links[...].astype(f32)
    small[ORIENT : ORIENT + 4, :] = orient[...].astype(f32)
    where = slot[...]
    stays = (where >= me * PARTITION_SLOTS) & (where < (me + 1) * PARTITION_SLOTS)
    small[OCCUPIED : OCCUPIED + 1, :] = jnp.where(stays, 1.0, 0.0)
    small[OCCUPIED + 1 : SMALL, :] = jnp.zeros((1, tiles * LANES), f32)
    find_links(devices, tiles, small, aux, asks)

    zero4 = jnp.zeros((4, LANES), f32)
    zero7 = jnp.zeros((7, LANES), f32)
    pieces = []
    for p in range(NV):
        pieces += [q[p], zero4]
    for d in range(3):
        for p in range(NV):
            pieces += [jac[d, p], zero7]
    fields = small[:, KEEP:]
    row = iota(fields.shape, 0)
    pieces.append(jnp.where(row == OCCUPIED, 1.0 - fields, fields))
    pieces.append(jnp.zeros((96, LANES), f32))
    whole = jnp.concatenate(pieces, axis=0)
    turned = jnp.concatenate([whole[c : c + LANES].T for c in range(0, RECORD, LANES)], axis=1)
    one[...] = turned[:CSZ]
    position = me // (devices // GROUPS)
    for g in range(GROUPS):
        group[lax.rem(position + g, GROUPS)] = turned[g * CSZ : (g + 1) * CSZ]


def prepare(normals, speed, cluster, slot, links, orient, q, jac, devices):
    count = q.shape[2]

    def body(*refs):
        prepare_kernel(devices, count // LANES, *refs)

    last = KEEP // LANES
    return pl.pallas_call(
        body,
        grid=(1,),
        in_specs=[
            whole_spec(normals),
            whole_spec(speed),
            whole_spec(cluster),
            whole_spec(slot),
            whole_spec(links),
            whole_spec(orient),
            pl.BlockSpec((NV, NB, LANES), lambda i: (0, 0, last)),
            pl.BlockSpec((3, NV, NV, LANES), lambda i: (0, 0, 0, last)),
        ],
        out_specs=[
            pl.BlockSpec((SMALL, count), lambda i: (0, 0)),
            pl.BlockSpec((8, count), lambda i: (0, 0)),
            pl.BlockSpec((ASKS, LANES), lambda i: (0, 0)),
            pl.BlockSpec((GROUPS, CSZ, RECORD), lambda i: (0, 0, 0)),
            pl.BlockSpec((CSZ, RECORD), lambda i: (0, 0)),
        ],
        out_shape=[
            jax.ShapeDtypeStruct((SMALL, count), f32),
            jax.ShapeDtypeStruct((8, count), i32),
            jax.ShapeDtypeStruct((ASKS, LANES), f32),
            jax.ShapeDtypeStruct((GROUPS, CSZ, RECORD), f32),
            jax.ShapeDtypeStruct((CSZ, RECORD), f32),
        ],
        compiler_params=PARAMS,
        name="prepare",
    )(normals, speed, cluster, slot, links, orient, q, jac)


def unpack_kernel(devices, group, one, q, jac, small, aux, asks):
    position = lax.axis_index("dom") // (devices // GROUPS)
    rows = [one[...]]
    for g in range(1, GROUPS):
        rows.append(group[lax.rem(position - g + GROUPS, GROUPS)])
    whole = jnp.concatenate(rows, axis=0)
    turned = jnp.concatenate([whole[:, c : c + LANES].T for c in range(0, RECORD, LANES)], axis=0)
    for p in range(NV):
        q[p] = turned[p * NBP : p * NBP + NB]
    for d in range(3):
        for p in range(NV):
            at = ROWS + (d * NV + p) * 16
            jac[d, p] = turned[at : at + NV]
    at = ROWS + 3 * NV * 16
    small[...] = turned[at : at + SMALL]
    find_links(devices, 1, small, aux, asks)


def unpack(group, one, devices):
    def body(*refs):
        unpack_kernel(devices, *refs)

    return pl.pallas_call(
        body,
        out_shape=[
            jax.ShapeDtypeStruct((NV, NB, LANES), f32),
            jax.ShapeDtypeStruct((3, NV, NV, LANES), f32),
            jax.ShapeDtypeStruct((SMALL, LANES), f32),
            jax.ShapeDtypeStruct((8, LANES), i32),
            jax.ShapeDtypeStruct((ASKS, LANES), f32),
        ],
        compiler_params=PARAMS,
        name="unpack",
    )(group, one)


def picked(requests, fields):
    lane = iota((1, LANES), 1)
    tiles = []
    for at in range(0, 12, 4):
        four = [requests[min(at + n, PARTNERS - 1)] for n in range(4)]
        tiles.append(
            jnp.where(lane < 32, four[0], jnp.where(lane < 64, four[1], jnp.where(lane < 96, four[2], four[3])))
        )
    slots = iota((KEEP, FAR), 0).astype(f32)
    return dot(fields, one_hot(slots == jnp.concatenate(tiles, axis=1)))


def message_rows(both):
    value = both[:PACK] + both[PACK:]
    return jnp.concatenate([value, jnp.zeros((MSG - PACK, FAR), f32)], axis=0).T


def back(k):
    return k if k == PARTNERS - 1 else (k + 4) % 8


def requests_here(devices, asks):
    me = lax.axis_index("dom")
    peers = [lax.rem(me - o + devices, devices) for o in partner_offsets(devices)]
    return [asks[p, k : k + 1, :] for k, p in enumerate(peers)]


def answer_kernel(devices, asks, moved, field, *outs):
    rows = message_rows(picked(requests_here(devices, asks), field[...]))
    for k, out in enumerate(outs):
        out[:REQ] = rows[k * REQ : (k + 1) * REQ]
        out[REQ:, :LANES] = jnp.broadcast_to(moved[back(k) : back(k) + 1, :], (8, LANES))
        out[REQ:, LANES:] = jnp.zeros((8, MSG - LANES), f32)


def answer_again_kernel(devices, asks, *refs):
    got, (field, later), outs = refs[:PARTNERS], refs[PARTNERS : PARTNERS + 2], refs[PARTNERS + 2 :]
    rows = message_rows(picked(requests_here(devices, asks), later[...]))
    moved = [got[back(k)][REQ : REQ + 1, :LANES] for k in range(PARTNERS)]
    both = picked(moved, jnp.concatenate([field[...], later[...]], axis=0))
    rows_first = message_rows(both[: 2 * PACK])
    rows_later = message_rows(both[2 * PACK :])
    for k, out in enumerate(outs):
        at = slice(k * REQ, (k + 1) * REQ)
        out[:REQ] = rows[at]
        out[REQ : 2 * REQ] = rows_first[at]
        out[2 * REQ :] = rows_later[at]


def answer(body, rows, devices, arrays, fields):
    def kernel(*refs):
        body(devices, *refs)

    return pl.pallas_call(
        kernel,
        grid=(1,),
        in_specs=[whole_spec(a) for a in arrays]
        + [pl.BlockSpec((2 * PACK, KEEP), lambda i: (0, 0))] * len(fields),
        out_specs=[pl.BlockSpec((rows, MSG), lambda i: (0, 0))] * PARTNERS,
        out_shape=[jax.ShapeDtypeStruct((rows, MSG), f32)] * PARTNERS,
        compiler_params=PARAMS,
        name="answer",
    )(*arrays, *fields)


def far_table(part, messages):
    rows = [m[part * REQ : (part + 1) * REQ, :] for m in messages]
    rows.append(jnp.zeros((FAR - PARTNERS * REQ, MSG), f32))
    turned = jnp.concatenate(rows, axis=0).T[:PACK]
    return jnp.concatenate(split(turned), axis=0)


def lanes(tile):
    return slice(tile * LANES, (tile + 1) * LANES)


def jacobian_apply(jac, tile, parts):
    result = [None] * NV
    for group in range(3):
        for d in range(3):
            for inner in range(3):
                q = 3 * group + inner
                value = parts(d, q)
                for p in range(NV):
                    term = jac[d, p, q : q + 1, lanes(tile)] * value
                    result[p] = term if result[p] is None else result[p] + term
    return result


def packed_split(fields, group):
    packed = [pack_three(tile[3 * group : 3 * group + 3]) for tile in fields]
    return split(jnp.concatenate(packed, axis=1))


def split_fields(fields):
    pairs = [packed_split(fields, group) for group in range(3)]
    return jnp.concatenate([a for a, _ in pairs] + [b for _, b in pairs], axis=0)


def predict(start, jac, w_pred, scales):
    tiles = range(len(start))
    sums = [[[s[0] * x for x in tile] for tile in start] for s in scales]
    now = start
    for degree in range(1, NORDER):
        turned = [dot(w_pred, stacked(*packed_split(now, group))) for group in range(3)]
        now = [
            jacobian_apply(
                jac, t, lambda d, q: turned[q // 3][d * 72 + (q % 3) * NBP : d * 72 + (q % 3) * NBP + NBP, lanes(t)]
            )
            for t in tiles
        ]
        sums = [
            [[a + s[degree] * x for a, x in zip(total[t], now[t])] for t in tiles] for total, s in zip(sums, scales)
        ]
    return sums


def update(own, near, far, small, aux, jac, w_own, w_lift, w_table, gathered):
    count = own.shape[1]
    tiles = range(count // LANES)
    place = aux[4:5, :]
    both = dot(far, one_hot(iota((FAR, count), 0) == place))
    remote = both[:PACK] + both[PACK:]
    slots = iota((KEEP, count), 0)
    codes = iota((16, count), 0).astype(f32)

    def gather(face):
        index = aux[face : face + 1, :]
        both = dot(near, one_hot(slots == index))
        take_far = (index < 0) & (place >= 0)
        gathered[face] = both[:PACK] + both[PACK:] + jnp.where(take_far, remote, 0.0)
        code = one_hot(codes == small[ORIENT + face : ORIENT + face + 1, :])
        return dot(w_table, jnp.concatenate([code, code], axis=0))

    table = gather(0)
    mine = []
    for group in range(3):
        rows = slice(64 * group, 64 * group + 64)
        lower = slice(PACK + 64 * group, PACK + 64 * group + 64)
        mine.append(dot(w_own, stacked(own[rows], own[lower])))

    def of_own(block, q, t):
        at = block * 72 + (q % 3) * NBP
        return mine[q // 3][at : at + NBP, lanes(t)]

    volume = [[[of_own(d, q, t) for q in range(NV)] for d in range(3)] for t in tiles]
    upwind = [[of_own(7, q, t) for q in range(NV)] for t in tiles]
    for face in range(4):
        now = table
        if face < 3:
            table = gather(face + 1)
        outers = []
        for t in tiles:
            outer = [None] * NV
            for b in range(NB):
                values = now[b * NQ : (b + 1) * NQ, lanes(t)]
                for p in range(NV):
                    at = packed_row(p, b)
                    term = gathered[face, at : at + 1, lanes(t)] * values
                    outer[p] = term if outer[p] is None else outer[p] + term
            outers.append(outer)
        for group in range(3):
            joined = [jnp.concatenate(outer[3 * group : 3 * group + 3], axis=0) for outer in outers]
            lifted = dot(w_lift[face], stacked(*split(jnp.concatenate(joined, axis=1))))
            for t in tiles:
                for inner in range(3):
                    q = 3 * group + inner
                    at = inner * NBP
                    mixed = lifted[at : at + NBP, lanes(t)] + of_own(3 + face, q, t)
                    upwind[t][q] = upwind[t][q] + lifted[72 + at : 72 + at + NBP, lanes(t)]
                    for d in range(3):
                        normal = small[3 * face + d : 3 * face + d + 1, lanes(t)]
                        volume[t][d][q] = volume[t][d][q] + normal * mixed
    result = []
    for t in tiles:
        change = jacobian_apply(jac, t, lambda d, q: volume[t][d][q])
        speed = small[SPEED : SPEED + 1, lanes(t)]
        result.append([c + speed * u for c, u in zip(change, upwind[t])])
    return result


def load_state(q, padded):
    padded[:, NB:NBP, :] = jnp.zeros((NV, NBP - NB, padded.shape[2]), f32)
    for p in range(NV):
        padded[p, :NB, :] = q[p]
    return load_field(padded)


def load_field(ref):
    return [[ref[p, :, lanes(t)] for p in range(NV)] for t in range(ref.shape[2] // LANES)]


def store_field(ref, field):
    for t, tile in enumerate(field):
        for p in range(NV):
            ref[p, :, lanes(t)] = tile[p]


def store_result(out, base, change, small):
    for t in range(len(base)):
        occupied = small[OCCUPIED : OCCUPIED + 1, lanes(t)] > 0.5
        for p in range(NV):
            out[p, :, lanes(t)] = jnp.where(occupied, base[t][p] + change[t][p], 0.0)[:NB]


def first_kernel(q, jac, w_pred, packed, slow, padded):
    first, later = predict(load_state(q, padded), jac, w_pred[...], [FIRST, SECOND])
    packed[...] = split_fields(first)
    store_field(slow, later)


def middle_step(start, jac, small, slow, own, near, far, aux, weights, gathered):
    w_pred, w_own, w_lift, w_table = weights
    change = update(own, near, far, small, aux, jac, w_own, w_lift, w_table, gathered)
    base, midway, second = [], [], []
    fast = [small[CLUSTER : CLUSTER + 1, lanes(t)] < 0.5 for t in range(len(start))]
    for t in range(len(start)):
        base.append([a + b for a, b in zip(start[t], change[t])])
        midway.append([jnp.where(fast[t], a, b) for a, b in zip(base[t], start[t])])
    (later,) = predict(midway, jac, w_pred, [FIRST])
    for t in range(len(start)):
        second.append([jnp.where(fast[t], a, b) for a, b in zip(later[t], slow[t])])
    return base, split_fields(second)


def middle_kernel(q, jac, small, slow, own, near, aux, *refs):
    messages = refs[:PARTNERS]
    w_pred, w_own, w_lift, w_table, base, packed, padded, gathered, far = refs[PARTNERS:]

    @pl.when(pl.program_id(0) == 0)
    def _():
        far[...] = far_table(0, messages)

    weights = (w_pred[...], w_own[...], w_lift, w_table[...])
    now, second = middle_step(
        load_state(q, padded), jac, small, load_field(slow), own[...], near[...], far[...], aux, weights, gathered
    )
    store_field(base, now)
    packed[...] = second


def last_kernel(base, jac, small, own, near, aux, *refs):
    messages = refs[:PARTNERS]
    w_own, w_lift, w_table, out, gathered, far = refs[PARTNERS:]

    @pl.when(pl.program_id(0) == 0)
    def _():
        far[...] = far_table(0, messages)

    change = update(
        own[...], near[...], far[...], small, aux, jac, w_own[...], w_lift, w_table[...], gathered
    )
    store_result(out, load_field(base), change, small)


def moved_kernel(q, jac, small, aux, near, later, *refs):
    messages = refs[:PARTNERS]
    w_pred, w_own, w_lift, w_table, _, out, padded, gathered = refs[PARTNERS:]
    weights = (w_pred[...], w_own[...], w_lift, w_table[...])
    start = load_state(q, padded)
    first, slow = predict(start, jac, weights[0], [FIRST, SECOND])
    base, second = middle_step(
        start, jac, small, slow, split_fields(first), near[...], far_table(1, messages), aux, weights, gathered
    )
    change = update(
        second, later[...], far_table(2, messages), small, aux, jac, *weights[1:], gathered
    )
    store_result(out, base, change, small)


def whole_spec(array):
    rank = array.ndim
    return pl.BlockSpec(array.shape, lambda i: (0,) * rank)


def lane_spec(*lead):
    rank = len(lead)
    return pl.BlockSpec(lead + (WIDE,), lambda i: (0,) * rank + (i,))


def rows_spec(message):
    lead = message.shape[:-2]
    rank = message.ndim
    return pl.BlockSpec(lead + (REQ, MSG), lambda i: (0,) * rank)


Q_SPEC = lane_spec(NV, NB)
J_SPEC = lane_spec(3, NV, NV)
S_SPEC = lane_spec(SMALL)
A_SPEC = lane_spec(8)
F_SPEC = lane_spec(NV, NBP)
X_SPEC = lane_spec(2 * PACK)
N_SPEC = pl.BlockSpec((2 * PACK, KEEP), lambda i: (0, 0))


def scratch_of(width):
    return pltpu.VMEM((NV, NBP, width), f32), pltpu.VMEM((4, PACK, width), f32)


def per_device(
    element_freedom_values,
    scaled_jacobian_matrices,
    outward_face_normals,
    largest_wave_speed,
    element_cluster_index,
    element_new_slot,
    neighbours,
    face_rotation_codes,
    deriv_mats,
    stiff_mats,
    face_eval,
    face_lift,
):
    count = element_freedom_values.shape[2]
    steps = count // WIDE
    devices = lax.axis_size("dom")
    q, jac = element_freedom_values, scaled_jacobian_matrices

    def shift(array, by):
        return lax.ppermute(array, "dom", [(i, (i + by) % devices) for i in range(devices)])

    def swap(array, groups):
        return lax.all_to_all(array, "dom", split_axis=0, concat_axis=0, axis_index_groups=groups, tiled=True)

    def exchange(*messages):
        return [shift(m, -o) for m, o in zip(messages, partner_offsets(devices))]

    small, aux, asks, group, one = prepare(
        outward_face_normals,
        largest_wave_speed[None],
        element_cluster_index[None],
        element_new_slot[None],
        neighbours,
        face_rotation_codes,
        q,
        jac,
        devices,
    )
    asks = lax.all_gather(asks, "dom", axis=0, tiled=False)
    stride = devices // GROUPS
    group = swap(group, [[r + stride * j for j in range(GROUPS)] for r in range(stride)])
    one = shift(one, 1)
    w_pred, w_own, w_lift, w_table = make_weights(deriv_mats, stiff_mats, face_eval, face_lift)
    weights = [w_pred, w_own, w_lift, w_table]

    padded, gathered = scratch_of(WIDE)
    packed_shape = jax.ShapeDtypeStruct((2 * PACK, count), bf16)
    field_shape = jax.ShapeDtypeStruct((NV, NBP, count), f32)
    far = pltpu.VMEM((2 * PACK, FAR), bf16)
    first, slow = pl.pallas_call(
        first_kernel,
        grid=(steps,),
        in_specs=[Q_SPEC, J_SPEC, whole_spec(w_pred)],
        out_specs=[X_SPEC, F_SPEC],
        out_shape=[packed_shape, field_shape],
        scratch_shapes=[padded],
        compiler_params=PARAMS,
        name="first",
    )(q, jac, w_pred)

    q_moved, jac_moved, small_moved, aux_moved, asks_moved = unpack(group, one, devices)
    messages = exchange(*answer(answer_kernel, MESSAGE1, devices, [asks, asks_moved], [first]))

    base, second = pl.pallas_call(
        middle_kernel,
        grid=(steps,),
        in_specs=[Q_SPEC, J_SPEC, S_SPEC, F_SPEC, X_SPEC, N_SPEC, A_SPEC]
        + [rows_spec(m) for m in messages]
        + [whole_spec(w) for w in weights],
        out_specs=[F_SPEC, X_SPEC],
        out_shape=[field_shape, packed_shape],
        scratch_shapes=[padded, gathered, far],
        compiler_params=PARAMS,
        name="middle",
    )(q, jac, small, slow, first, first, aux, *messages, *weights)

    messages = exchange(*answer(answer_again_kernel, 3 * REQ, devices, [asks, *messages], [first, second]))

    new_state = pl.pallas_call(
        last_kernel,
        grid=(steps,),
        in_specs=[F_SPEC, J_SPEC, S_SPEC, X_SPEC, N_SPEC, A_SPEC]
        + [rows_spec(m) for m in messages]
        + [whole_spec(w) for w in weights[1:]],
        out_specs=Q_SPEC,
        out_shape=jax.ShapeDtypeStruct((NV, NB, PARTITION_SLOTS), f32),
        scratch_shapes=[gathered, far],
        compiler_params=PARAMS,
        name="last",
    )(base, jac, small, second, second, aux, *messages, *weights[1:])

    return pl.pallas_call(
        moved_kernel,
        grid=(1,),
        in_specs=[whole_spec(a) for a in (q_moved, jac_moved, small_moved, aux_moved)]
        + [N_SPEC, N_SPEC]
        + [whole_spec(m) for m in messages]
        + [whole_spec(w) for w in weights]
        + [pl.BlockSpec(memory_space=pl.ANY)],
        out_specs=pl.BlockSpec((NV, NB, LANES), lambda i: (0, 0, count // LANES)),
        out_shape=jax.ShapeDtypeStruct((NV, NB, PARTITION_SLOTS), f32),
        scratch_shapes=scratch_of(LANES),
        input_output_aliases={6 + PARTNERS + 4: 0},
        compiler_params=PARAMS,
        name="moved",
    )(q_moved, jac_moved, small_moved, aux_moved, first, second, *messages, *weights, new_state)


def solution(mesh):
    placed = (
        P(None, None, "dom"),
        P(None, None, None, "dom"),
        P(None, None, "dom"),
        P("dom"),
        P("dom"),
        P("dom"),
        P(None, "dom"),
        P(None, "dom"),
        P(),
        P(),
        P(),
        P(),
    )
    return jax.shard_map(
        per_device, mesh=mesh, in_specs=placed, out_specs=P(None, None, "dom"), check_vma=False
    )
```

```python
import math

import jax
import jax.numpy as jnp
from jax import lax
from jax.experimental import pallas as pl
from jax.experimental.pallas import tpu as pltpu
from jax.sharding import PartitionSpec as P

NV = 9
NB = 20
NBP = 24
NQ = 16
NORDER = 4
GROUPS = 8
CSZ = 16
KEEP = 896
PARTITION_SLOTS = 1152
REQ = 32
PARTNERS = 9
ASKS = 16
LANES = 128
WIDE = 256
ROWS = 216
PACK = 192
MSG = 256
FAR = 384
RECORD = 768
SMALL = 24
MESSAGE1 = REQ + 8

step_fast = 0.25
exact = lax.Precision.HIGHEST
f32 = jnp.float32
bf16 = jnp.bfloat16
i32 = jnp.int32

SPEED, CLUSTER, LINK, ORIENT, OCCUPIED = 12, 13, 14, 18, 22

PARAMS = pltpu.CompilerParams(vmem_limit_bytes=60 << 20)


def coefficients(lower, upper):
    return [
        (upper ** (degree + 1) - lower ** (degree + 1)) / math.factorial(degree + 1)
        for degree in range(NORDER)
    ]


FIRST = coefficients(0.0, step_fast)
SECOND = coefficients(step_fast, 2.0 * step_fast)


def partner_offsets(devices):
    return [1, 2, 3, 4, -1, -2, -3, -4, devices // 2]


def packed_row(quantity, basis):
    group, member = quantity // 3, quantity % 3
    inside = 16 * member + basis if basis < 16 else 48 + 4 * member + (basis - 16)
    return 64 * group + inside


def pack_three(members):
    a, b, c = members
    tail = a[16:24] + pltpu.roll(b[16:24], 4, 0)
    return jnp.concatenate([a[:16], b[:16], c[:16], tail, c[16:24]], axis=0)


def split(values):
    high = values.astype(bf16)
    low = (values - high.astype(f32)).astype(bf16)
    return high, low


def stacked(high, low):
    return jnp.concatenate([high, low, high], axis=0)


def dot(a, b):
    return jnp.dot(a, b, preferred_element_type=f32)


def dot_last(a, b):
    return lax.dot_general(a, b, (((1,), (1,)), ((), ())), preferred_element_type=f32)


def iota(shape, axis):
    return lax.broadcasted_iota(i32, shape, axis)


def one_hot(condition):
    return jnp.where(condition, 1.0, 0.0).astype(bf16)


def weights_kernel(deriv, stiff, evals, lift, evals_flat, w_pred, w_own, w_lift, w_table, square):
    def turned(matrix, rows, columns):
        square[...] = jnp.zeros((LANES, LANES), f32)
        square[:rows, :columns] = matrix
        return square[...].T[:NBP]

    column = iota((LANES, PACK), 1) & 63
    member = jnp.where(column < 48, column >> 4, (column - 48) >> 2)
    basis = jnp.where(column < 48, column & 15, 16 + (column & 3))
    spread = one_hot(iota((LANES, PACK), 0) == jnp.where(member < 3, basis, -1))
    member = member[:NBP]
    part = iota((NBP, PACK), 1)

    def three(matrix):
        high, low = split(turned(matrix, NB, NB))
        row = jnp.where(part < 128, dot(high, spread), dot(low, spread))
        return [jnp.where(member == inner, row, 0.0) for inner in range(3)]

    blocks = []
    for axis in range(3):
        blocks += three(-deriv[axis])
    w_pred[...] = jnp.concatenate(blocks, axis=0).astype(bf16)

    own = [
        jnp.dot(evals[3 * face], lift[face], precision=exact, preferred_element_type=f32) for face in range(4)
    ]
    blocks = []
    for matrix in [stiff[axis] for axis in range(3)] + own + [own[0] + own[1] + own[2] + own[3]]:
        blocks += three(matrix if len(blocks) < 9 else -0.5 * matrix)
    w_own[...] = jnp.concatenate(blocks, axis=0).astype(bf16)

    column = iota((LANES, 144), 1)
    spread = one_hot(iota((LANES, 144), 0) == (column & 15))
    column = column[:NBP]
    block = column >> 4
    member = block - jnp.where(column >= 96, 6, jnp.where(column >= 48, 3, 0))
    for face in range(4):
        high, low = split(turned(lift[face], NQ, NB))
        row = jnp.where(column < 96, dot(high, spread), dot(low, spread))
        rows = [jnp.where(member == inner, -0.5 * row, 0.0) for inner in range(3)]
        w_lift[face] = jnp.concatenate(rows + [-r for r in rows], axis=0).astype(bf16)

    flat = evals_flat[...]
    high = flat.astype(bf16).astype(f32)
    low = flat - high
    source = jnp.concatenate([high, low, jnp.zeros((96, 384), f32)], axis=0)
    w_table[...] = source.T[:320, :32].astype(bf16)


def make_weights(deriv, stiff, evals, lift):
    flat = jnp.pad(evals.reshape(12, NB * NQ), ((0, 4), (0, 384 - NB * NQ)))
    return pl.pallas_call(
        weights_kernel,
        out_shape=(
            jax.ShapeDtypeStruct((ROWS, PACK), bf16),
            jax.ShapeDtypeStruct((576, PACK), bf16),
            jax.ShapeDtypeStruct((4, 144, 144), bf16),
            jax.ShapeDtypeStruct((320, 32), bf16),
        ),
        scratch_shapes=[pltpu.VMEM((LANES, LANES), f32)],
        compiler_params=PARAMS,
        name="weights",
    )(deriv, stiff, evals, lift, flat)


def find_links(devices, tiles, small, aux, from_top):
    me = lax.axis_index("dom").astype(f32)
    row = iota((ASKS, LANES), 0).astype(f32)
    up_to = one_hot(iota((LANES, LANES), 0) <= iota((LANES, LANES), 1))
    request = (iota((LANES, LANES), 0) & (REQ - 1)).astype(f32)
    carry = jnp.zeros((ASKS, 1), f32)
    wanted = jnp.zeros((2 * ASKS, LANES), f32)
    for tile in range(tiles):
        at = slice(tile * LANES, (tile + 1) * LANES)
        occupied = small[OCCUPIED : OCCUPIED + 1, at] > 0.5
        target = jnp.full((1, LANES), -1.0, f32)
        slots = jnp.zeros((1, LANES), f32)
        for face in range(4):
            link = small[LINK + face : LINK + face + 1, at]
            owner = jnp.floor((link + 0.5) * (1.0 / PARTITION_SLOTS))
            slot = link - owner * PARTITION_SLOTS
            near = owner == me
            aux[face : face + 1, at] = jnp.where(near, slot, -1.0).astype(i32)
            away = occupied & jnp.logical_not(near)
            target = jnp.where(away, owner, target)
            slots = jnp.where(away, slot, slots)
        far = target - me
        far = jnp.where(far < 0, far + devices, far)
        partner = jnp.where(far <= 4, far - 1.0, jnp.where(far >= devices - 4, devices + 3.0 - far, 8.0))
        partner = jnp.where(target >= 0, partner, -1.0)
        named = jnp.where(row == partner, 1.0, 0.0)
        prefix = dot(named.astype(bf16), up_to) + carry
        carry = carry + jnp.sum(named, axis=1, keepdims=True)
        rank = jnp.sum(named * prefix, axis=0, keepdims=True) - 1.0
        if from_top:
            rank = REQ - 1.0 - rank
        aux[4:5, at] = jnp.where(target >= 0, partner * REQ + rank, -1.0).astype(i32)
        aux[5:8, at] = jnp.zeros((3, LANES), i32)
        ask = slots + 1.0
        high = jnp.floor(ask * (1.0 / 32)) * 32.0
        both = jnp.concatenate([named * high, named * (ask - high)], axis=0).astype(bf16)
        wanted = wanted + dot_last(both, one_hot(request == rank))
    return wanted[:ASKS] + wanted[ASKS:]


def prepare_kernel(devices, tiles, normals, speed, cluster, slot, links, orient, q, jac, small, aux, asks, group, one):
    me = lax.axis_index("dom")
    for face in range(4):
        small[3 * face : 3 * face + 3, :] = normals[face]
    small[SPEED : SPEED + 1, :] = speed[...]
    small[CLUSTER : CLUSTER + 1, :] = cluster[...].astype(f32)
    small[LINK : LINK + 4, :] = links[...].astype(f32)
    small[ORIENT : ORIENT + 4, :] = orient[...].astype(f32)
    where = slot[...]
    stays = (where >= me * PARTITION_SLOTS) & (where < (me + 1) * PARTITION_SLOTS)
    small[OCCUPIED : OCCUPIED + 1, :] = jnp.where(stays, 1.0, 0.0)
    small[OCCUPIED + 1 : SMALL, :] = jnp.zeros((1, tiles * LANES), f32)
    wanted = find_links(devices, tiles, small, aux, False)
    asks[...] = jnp.zeros((devices, 1, LANES), f32)
    for k, offset in enumerate(partner_offsets(devices)):
        asks[lax.rem(me + offset + devices, devices)] = wanted[k : k + 1]

    zero4 = jnp.zeros((4, LANES), f32)
    zero7 = jnp.zeros((7, LANES), f32)
    pieces = []
    for p in range(NV):
        pieces += [q[p], zero4]
    for d in range(3):
        for p in range(NV):
            pieces += [jac[d, p], zero7]
    fields = small[:, KEEP:]
    row = iota(fields.shape, 0)
    pieces.append(jnp.where(row == OCCUPIED, 1.0 - fields, fields))
    pieces.append(jnp.zeros((96, LANES), f32))
    whole = jnp.concatenate(pieces, axis=0)
    turned = jnp.concatenate([whole[c : c + LANES].T for c in range(0, RECORD, LANES)], axis=1)
    one[...] = turned[:CSZ]
    position = me // (devices // GROUPS)
    for g in range(GROUPS):
        group[lax.rem(position + g, GROUPS)] = turned[g * CSZ : (g + 1) * CSZ]


def prepare(normals, speed, cluster, slot, links, orient, q, jac, devices):
    count = q.shape[2]

    def body(*refs):
        prepare_kernel(devices, count // LANES, *refs)

    last = KEEP // LANES
    return pl.pallas_call(
        body,
        grid=(1,),
        in_specs=[
            whole_spec(normals),
            whole_spec(speed),
            whole_spec(cluster),
            whole_spec(slot),
            whole_spec(links),
            whole_spec(orient),
            pl.BlockSpec((NV, NB, LANES), lambda i: (0, 0, last)),
            pl.BlockSpec((3, NV, NV, LANES), lambda i: (0, 0, 0, last)),
        ],
        out_specs=[
            pl.BlockSpec((SMALL, count), lambda i: (0, 0)),
            pl.BlockSpec((8, count), lambda i: (0, 0)),
            pl.BlockSpec((devices, 1, LANES), lambda i: (0, 0, 0)),
            pl.BlockSpec((GROUPS, CSZ, RECORD), lambda i: (0, 0, 0)),
            pl.BlockSpec((CSZ, RECORD), lambda i: (0, 0)),
        ],
        out_shape=[
            jax.ShapeDtypeStruct((SMALL, count), f32),
            jax.ShapeDtypeStruct((8, count), i32),
            jax.ShapeDtypeStruct((devices, 1, LANES), f32),
            jax.ShapeDtypeStruct((GROUPS, CSZ, RECORD), f32),
            jax.ShapeDtypeStruct((CSZ, RECORD), f32),
        ],
        compiler_params=PARAMS,
        name="prepare",
    )(normals, speed, cluster, slot, links, orient, q, jac)


def unpack_kernel(devices, group, one, q, jac, small, aux, asks):
    position = lax.axis_index("dom") // (devices // GROUPS)
    rows = [one[...]]
    for g in range(1, GROUPS):
        rows.append(group[lax.rem(position - g + GROUPS, GROUPS)])
    whole = jnp.concatenate(rows, axis=0)
    turned = jnp.concatenate([whole[:, c : c + LANES].T for c in range(0, RECORD, LANES)], axis=0)
    for p in range(NV):
        q[p] = turned[p * NBP : p * NBP + NB]
    for d in range(3):
        for p in range(NV):
            at = ROWS + (d * NV + p) * 16
            jac[d, p] = turned[at : at + NV]
    at = ROWS + 3 * NV * 16
    small[...] = turned[at : at + SMALL]
    asks[...] = find_links(devices, 1, small, aux, True)


def unpack(group, one, devices):
    def body(*refs):
        unpack_kernel(devices, *refs)

    return pl.pallas_call(
        body,
        out_shape=[
            jax.ShapeDtypeStruct((NV, NB, LANES), f32),
            jax.ShapeDtypeStruct((3, NV, NV, LANES), f32),
            jax.ShapeDtypeStruct((SMALL, LANES), f32),
            jax.ShapeDtypeStruct((8, LANES), i32),
            jax.ShapeDtypeStruct((ASKS, LANES), f32),
        ],
        compiler_params=PARAMS,
        name="unpack",
    )(group, one)


def picked(requests, fields):
    lane = iota((1, LANES), 1)
    tiles = []
    for at in range(0, 12, 4):
        four = [requests[min(at + n, PARTNERS - 1)] for n in range(4)]
        tiles.append(
            jnp.where(lane < 32, four[0], jnp.where(lane < 64, four[1], jnp.where(lane < 96, four[2], four[3])))
        )
    slots = (iota((KEEP, FAR), 0) + 1).astype(f32)
    return dot(fields, one_hot(slots == jnp.concatenate(tiles, axis=1)))


def message_rows(both):
    value = both[:PACK] + both[PACK:]
    return jnp.concatenate([value, jnp.zeros((MSG - PACK, FAR), f32)], axis=0).T


def back(k):
    return k if k == PARTNERS - 1 else (k + 4) % 8


def requests_here(devices, asks):
    me = lax.axis_index("dom")
    peers = [lax.rem(me - o + devices, devices) for o in partner_offsets(devices)]
    return [asks[p] for p in peers]


def answer_kernel(devices, asks, moved, field, *outs):
    rows = message_rows(picked(requests_here(devices, asks), field[...]))
    for k, out in enumerate(outs):
        out[:REQ] = rows[k * REQ : (k + 1) * REQ]
        out[REQ:, :LANES] = jnp.broadcast_to(moved[back(k) : back(k) + 1, :], (8, LANES))
        out[REQ:, LANES:] = jnp.zeros((8, MSG - LANES), f32)


def answer_again_kernel(devices, asks, *refs):
    got, (field, later), outs = refs[:PARTNERS], refs[PARTNERS : PARTNERS + 2], refs[PARTNERS + 2 :]
    moved = [got[back(k)][REQ : REQ + 1, :LANES] for k in range(PARTNERS)]
    every = [a + b for a, b in zip(requests_here(devices, asks), moved)]
    rows = message_rows(picked(every, later[...]))
    rows_first = message_rows(picked(moved, field[...]))
    for k, out in enumerate(outs):
        at = slice(k * REQ, (k + 1) * REQ)
        out[:REQ] = rows[at]
        out[REQ:] = rows_first[at]


def answer(body, rows, devices, arrays, fields):
    def kernel(*refs):
        body(devices, *refs)

    return pl.pallas_call(
        kernel,
        grid=(1,),
        in_specs=[whole_spec(a) for a in arrays]
        + [pl.BlockSpec((2 * PACK, KEEP), lambda i: (0, 0))] * len(fields),
        out_specs=[pl.BlockSpec((rows, MSG), lambda i: (0, 0))] * PARTNERS,
        out_shape=[jax.ShapeDtypeStruct((rows, MSG), f32)] * PARTNERS,
        compiler_params=PARAMS,
        name="answer",
    )(*arrays, *fields)


def far_table(part, messages):
    rows = [m[part * REQ : (part + 1) * REQ, :] for m in messages]
    rows.append(jnp.zeros((FAR - PARTNERS * REQ, MSG), f32))
    turned = jnp.concatenate(rows, axis=0).T[:PACK]
    return jnp.concatenate(split(turned), axis=0)


def lanes(tile):
    return slice(tile * LANES, (tile + 1) * LANES)


def jacobian_apply(jac, tile, parts):
    result = [None] * NV
    for group in range(3):
        for d in range(3):
            for inner in range(3):
                q = 3 * group + inner
                value = parts(d, q)
                for p in range(NV):
                    term = jac[d, p, q : q + 1, lanes(tile)] * value
                    result[p] = term if result[p] is None else result[p] + term
    return result


def packed_split(fields, group):
    packed = [pack_three(tile[3 * group : 3 * group + 3]) for tile in fields]
    return split(jnp.concatenate(packed, axis=1))


def split_fields(fields):
    pairs = [packed_split(fields, group) for group in range(3)]
    return jnp.concatenate([a for a, _ in pairs] + [b for _, b in pairs], axis=0)


def predict(start, jac, w_pred, scales):
    tiles = range(len(start))
    sums = [[[s[0] * x for x in tile] for tile in start] for s in scales]
    now = start
    for degree in range(1, NORDER):
        turned = [dot(w_pred, stacked(*packed_split(now, group))) for group in range(3)]
        now = [
            jacobian_apply(
                jac, t, lambda d, q: turned[q // 3][d * 72 + (q % 3) * NBP : d * 72 + (q % 3) * NBP + NBP, lanes(t)]
            )
            for t in tiles
        ]
        sums = [
            [[a + s[degree] * x for a, x in zip(total[t], now[t])] for t in tiles] for total, s in zip(sums, scales)
        ]
    return sums


def update(own, near, far, small, aux, jac, w_own, w_lift, w_table, gathered):
    count = own.shape[1]
    tiles = range(count // LANES)
    place = aux[4:5, :]
    both = dot(far, one_hot(iota((FAR, count), 0) == place))
    remote = both[:PACK] + both[PACK:]
    slots = iota((KEEP, count), 0)
    codes = iota((16, count), 0).astype(f32)

    def gather(face):
        index = aux[face : face + 1, :]
        both = dot(near, one_hot(slots == index))
        take_far = (index < 0) & (place >= 0)
        gathered[face] = both[:PACK] + both[PACK:] + jnp.where(take_far, remote, 0.0)
        code = one_hot(codes == small[ORIENT + face : ORIENT + face + 1, :])
        return dot(w_table, jnp.concatenate([code, code], axis=0))

    table = gather(0)
    mine = []
    for group in range(3):
        rows = slice(64 * group, 64 * group + 64)
        lower = slice(PACK + 64 * group, PACK + 64 * group + 64)
        mine.append(dot(w_own, stacked(own[rows], own[lower])))

    def of_own(block, q, t):
        at = block * 72 + (q % 3) * NBP
        return mine[q // 3][at : at + NBP, lanes(t)]

    volume = [[[of_own(d, q, t) for q in range(NV)] for d in range(3)] for t in tiles]
    upwind = [[of_own(7, q, t) for q in range(NV)] for t in tiles]
    for face in range(4):
        now = table
        if face < 3:
            table = gather(face + 1)
        outers = []
        for t in tiles:
            outer = [None] * NV
            for b in range(NB):
                values = now[b * NQ : (b + 1) * NQ, lanes(t)]
                for p in range(NV):
                    at = packed_row(p, b)
                    term = gathered[face, at : at + 1, lanes(t)] * values
                    outer[p] = term if outer[p] is None else outer[p] + term
            outers.append(outer)
        for group in range(3):
            joined = [jnp.concatenate(outer[3 * group : 3 * group + 3], axis=0) for outer in outers]
            lifted = dot(w_lift[face], stacked(*split(jnp.concatenate(joined, axis=1))))
            for t in tiles:
                for inner in range(3):
                    q = 3 * group + inner
                    at = inner * NBP
                    mixed = lifted[at : at + NBP, lanes(t)] + of_own(3 + face, q, t)
                    upwind[t][q] = upwind[t][q] + lifted[72 + at : 72 + at + NBP, lanes(t)]
                    for d in range(3):
                        normal = small[3 * face + d : 3 * face + d + 1, lanes(t)]
                        volume[t][d][q] = volume[t][d][q] + normal * mixed
    result = []
    for t in tiles:
        change = jacobian_apply(jac, t, lambda d, q: volume[t][d][q])
        speed = small[SPEED : SPEED + 1, lanes(t)]
        result.append([c + speed * u for c, u in zip(change, upwind[t])])
    return result


def load_state(q, padded):
    padded[:, NB:NBP, :] = jnp.zeros((NV, NBP - NB, padded.shape[2]), f32)
    for p in range(NV):
        padded[p, :NB, :] = q[p]
    return load_field(padded)


def load_field(ref):
    return [[ref[p, :, lanes(t)] for p in range(NV)] for t in range(ref.shape[2] // LANES)]


def store_field(ref, field):
    for t, tile in enumerate(field):
        for p in range(NV):
            ref[p, :, lanes(t)] = tile[p]


def store_result(out, base, change, small):
    for t in range(len(base)):
        occupied = small[OCCUPIED : OCCUPIED + 1, lanes(t)] > 0.5
        for p in range(NV):
            out[p, :, lanes(t)] = jnp.where(occupied, base[t][p] + change[t][p], 0.0)[:NB]


def first_kernel(q, jac, w_pred, packed, slow, padded):
    first, later = predict(load_state(q, padded), jac, w_pred[...], [FIRST, SECOND])
    packed[...] = split_fields(first)
    store_field(slow, later)


def middle_step(start, jac, small, slow, own, near, far, aux, weights, gathered):
    w_pred, w_own, w_lift, w_table = weights
    change = update(own, near, far, small, aux, jac, w_own, w_lift, w_table, gathered)
    base, midway, second = [], [], []
    fast = [small[CLUSTER : CLUSTER + 1, lanes(t)] < 0.5 for t in range(len(start))]
    for t in range(len(start)):
        base.append([a + b for a, b in zip(start[t], change[t])])
        midway.append([jnp.where(fast[t], a, b) for a, b in zip(base[t], start[t])])
    (later,) = predict(midway, jac, w_pred, [FIRST])
    for t in range(len(start)):
        second.append([jnp.where(fast[t], a, b) for a, b in zip(later[t], slow[t])])
    return base, split_fields(second)


def middle_kernel(q, jac, small, slow, own, near, aux, *refs):
    messages = refs[:PARTNERS]
    w_pred, w_own, w_lift, w_table, base, packed, padded, gathered, far = refs[PARTNERS:]

    @pl.when(pl.program_id(0) == 0)
    def _():
        far[...] = far_table(0, messages)

    weights = (w_pred[...], w_own[...], w_lift, w_table[...])
    now, second = middle_step(
        load_state(q, padded), jac, small, load_field(slow), own[...], near[...], far[...], aux, weights, gathered
    )
    store_field(base, now)
    packed[...] = second


def last_kernel(base, jac, small, own, near, aux, *refs):
    messages = refs[:PARTNERS]
    w_own, w_lift, w_table, out, gathered, far = refs[PARTNERS:]

    @pl.when(pl.program_id(0) == 0)
    def _():
        far[...] = far_table(0, messages)

    change = update(
        own[...], near[...], far[...], small, aux, jac, w_own[...], w_lift, w_table[...], gathered
    )
    store_result(out, load_field(base), change, small)


def moved_kernel(q, jac, small, aux, near, later, *refs):
    messages = refs[:PARTNERS]
    w_pred, w_own, w_lift, w_table, _, out, padded, gathered = refs[PARTNERS:]
    weights = (w_pred[...], w_own[...], w_lift, w_table[...])
    start = load_state(q, padded)
    first, slow = predict(start, jac, weights[0], [FIRST, SECOND])
    base, second = middle_step(
        start, jac, small, slow, split_fields(first), near[...], far_table(1, messages), aux, weights, gathered
    )
    change = update(
        second, later[...], far_table(0, messages), small, aux, jac, *weights[1:], gathered
    )
    store_result(out, base, change, small)


def whole_spec(array):
    rank = array.ndim
    return pl.BlockSpec(array.shape, lambda i: (0,) * rank)


def lane_spec(*lead):
    rank = len(lead)
    return pl.BlockSpec(lead + (WIDE,), lambda i: (0,) * rank + (i,))


def rows_spec(message):
    lead = message.shape[:-2]
    rank = message.ndim
    return pl.BlockSpec(lead + (REQ, MSG), lambda i: (0,) * rank)


Q_SPEC = lane_spec(NV, NB)
J_SPEC = lane_spec(3, NV, NV)
S_SPEC = lane_spec(SMALL)
A_SPEC = lane_spec(8)
F_SPEC = lane_spec(NV, NBP)
X_SPEC = lane_spec(2 * PACK)
N_SPEC = pl.BlockSpec((2 * PACK, KEEP), lambda i: (0, 0))


def scratch_of(width):
    return pltpu.VMEM((NV, NBP, width), f32), pltpu.VMEM((4, PACK, width), f32)


def per_device(
    element_freedom_values,
    scaled_jacobian_matrices,
    outward_face_normals,
    largest_wave_speed,
    element_cluster_index,
    element_new_slot,
    neighbours,
    face_rotation_codes,
    deriv_mats,
    stiff_mats,
    face_eval,
    face_lift,
):
    count = element_freedom_values.shape[2]
    steps = count // WIDE
    devices = lax.axis_size("dom")
    q, jac = element_freedom_values, scaled_jacobian_matrices

    def shift(array, by):
        return lax.ppermute(array, "dom", [(i, (i + by) % devices) for i in range(devices)])

    def swap(array, groups):
        return lax.all_to_all(array, "dom", split_axis=0, concat_axis=0, axis_index_groups=groups, tiled=True)

    def exchange(*messages):
        return [shift(m, -o) for m, o in zip(messages, partner_offsets(devices))]

    small, aux, asks, group, one = prepare(
        outward_face_normals,
        largest_wave_speed[None],
        element_cluster_index[None],
        element_new_slot[None],
        neighbours,
        face_rotation_codes,
        q,
        jac,
        devices,
    )
    asks = swap(asks, None)
    asks, group, one = lax.optimization_barrier((asks, group, one))
    stride = devices // GROUPS
    group = swap(group, [[r + stride * j for j in range(GROUPS)] for r in range(stride)])
    one = shift(one, 1)
    w_pred, w_own, w_lift, w_table = make_weights(deriv_mats, stiff_mats, face_eval, face_lift)
    weights = [w_pred, w_own, w_lift, w_table]

    padded, gathered = scratch_of(WIDE)
    packed_shape = jax.ShapeDtypeStruct((2 * PACK, count), bf16)
    field_shape = jax.ShapeDtypeStruct((NV, NBP, count), f32)
    far = pltpu.VMEM((2 * PACK, FAR), bf16)
    first, slow = pl.pallas_call(
        first_kernel,
        grid=(steps,),
        in_specs=[Q_SPEC, J_SPEC, whole_spec(w_pred)],
        out_specs=[X_SPEC, F_SPEC],
        out_shape=[packed_shape, field_shape],
        scratch_shapes=[padded],
        compiler_params=PARAMS,
        name="first",
    )(q, jac, w_pred)

    q_moved, jac_moved, small_moved, aux_moved, asks_moved = unpack(group, one, devices)
    messages = exchange(*answer(answer_kernel, MESSAGE1, devices, [asks, asks_moved], [first]))

    base, second = pl.pallas_call(
        middle_kernel,
        grid=(steps,),
        in_specs=[Q_SPEC, J_SPEC, S_SPEC, F_SPEC, X_SPEC, N_SPEC, A_SPEC]
        + [rows_spec(m) for m in messages]
        + [whole_spec(w) for w in weights],
        out_specs=[F_SPEC, X_SPEC],
        out_shape=[field_shape, packed_shape],
        scratch_shapes=[padded, gathered, far],
        compiler_params=PARAMS,
        name="middle",
    )(q, jac, small, slow, first, first, aux, *messages, *weights)

    messages = exchange(*answer(answer_again_kernel, 2 * REQ, devices, [asks, *messages], [first, second]))

    new_state = pl.pallas_call(
        last_kernel,
        grid=(steps,),
        in_specs=[F_SPEC, J_SPEC, S_SPEC, X_SPEC, N_SPEC, A_SPEC]
        + [rows_spec(m) for m in messages]
        + [whole_spec(w) for w in weights[1:]],
        out_specs=Q_SPEC,
        out_shape=jax.ShapeDtypeStruct((NV, NB, PARTITION_SLOTS), f32),
        scratch_shapes=[gathered, far],
        compiler_params=PARAMS,
        name="last",
    )(base, jac, small, second, second, aux, *messages, *weights[1:])

    return pl.pallas_call(
        moved_kernel,
        grid=(1,),
        in_specs=[whole_spec(a) for a in (q_moved, jac_moved, small_moved, aux_moved)]
        + [N_SPEC, N_SPEC]
        + [whole_spec(m) for m in messages]
        + [whole_spec(w) for w in weights]
        + [pl.BlockSpec(memory_space=pl.ANY)],
        out_specs=pl.BlockSpec((NV, NB, LANES), lambda i: (0, 0, count // LANES)),
        out_shape=jax.ShapeDtypeStruct((NV, NB, PARTITION_SLOTS), f32),
        scratch_shapes=scratch_of(LANES),
        input_output_aliases={6 + PARTNERS + 4: 0},
        compiler_params=PARAMS,
        name="moved",
    )(q_moved, jac_moved, small_moved, aux_moved, first, second, *messages, *weights, new_state)


def solution(mesh):
    placed = (
        P(None, None, "dom"),
        P(None, None, None, "dom"),
        P(None, None, "dom"),
        P("dom"),
        P("dom"),
        P("dom"),
        P(None, "dom"),
        P(None, "dom"),
        P(),
        P(),
        P(),
        P(),
    )
    return jax.shard_map(
        per_device, mesh=mesh, in_specs=placed, out_specs=P(None, None, "dom"), check_vma=False
    )
```

```python
import math

import jax
import jax.numpy as jnp
from jax import lax
from jax.experimental import pallas as pl
from jax.experimental.pallas import tpu as pltpu
from jax.sharding import PartitionSpec as P

NV = 9
NB = 20
NBP = 24
NQ = 16
NORDER = 4
GROUPS = 8
CSZ = 16
KEEP = 896
PARTITION_SLOTS = 1152
REQ = 32
PARTNERS = 9
ASKS = 16
LANES = 128
WIDE = 256
ROWS = 216
JAC_END = ROWS + 4 * NV * NV
PACK = 192
MSG = 256
FAR = 384
RECORD = 640
SMALL = 24
MESSAGE1 = REQ + 8

step_fast = 0.25
exact = lax.Precision.HIGHEST
f32 = jnp.float32
bf16 = jnp.bfloat16
i32 = jnp.int32

SPEED, CLUSTER, LINK, ORIENT, OCCUPIED = 12, 13, 14, 18, 22

PARAMS = pltpu.CompilerParams(vmem_limit_bytes=60 << 20)


def coefficients(lower, upper):
    return [
        (upper ** (degree + 1) - lower ** (degree + 1)) / math.factorial(degree + 1)
        for degree in range(NORDER)
    ]


FIRST = coefficients(0.0, step_fast)
SECOND = coefficients(step_fast, 2.0 * step_fast)


def partner_offsets(devices):
    return [1, 2, 3, 4, -1, -2, -3, -4, devices // 2]


def packed_row(quantity, basis):
    group, member = quantity // 3, quantity % 3
    inside = 16 * member + basis if basis < 16 else 48 + 4 * member + (basis - 16)
    return 64 * group + inside


def pack_three(members):
    a, b, c = members
    tail = a[16:24] + pltpu.roll(b[16:24], 4, 0)
    return jnp.concatenate([a[:16], b[:16], c[:16], tail, c[16:24]], axis=0)


def split(values):
    high = values.astype(bf16)
    low = (values - high.astype(f32)).astype(bf16)
    return high, low


def stacked(high, low):
    return jnp.concatenate([high, low, high], axis=0)


def dot(a, b):
    return jnp.dot(a, b, preferred_element_type=f32)


def dot_last(a, b):
    return lax.dot_general(a, b, (((1,), (1,)), ((), ())), preferred_element_type=f32)


def iota(shape, axis):
    return lax.broadcasted_iota(i32, shape, axis)


def one_hot(condition):
    return jnp.where(condition, 1.0, 0.0).astype(bf16)


def make_weights(deriv, stiff, evals, lift, w_pred, w_own, w_lift, w_table, square):
    def turned(matrix, rows, columns):
        square[...] = jnp.zeros((LANES, LANES), f32)
        square[:rows, :columns] = matrix
        return square[...].T[:NBP]

    column = iota((LANES, PACK), 1) & 63
    member = jnp.where(column < 48, column >> 4, (column - 48) >> 2)
    basis = jnp.where(column < 48, column & 15, 16 + (column & 3))
    spread = one_hot(iota((LANES, PACK), 0) == jnp.where(member < 3, basis, -1))
    member = member[:NBP]
    part = iota((NBP, PACK), 1)

    def three(matrix):
        high, low = split(turned(matrix, NB, NB))
        row = jnp.where(part < 128, dot(high, spread), dot(low, spread))
        return [jnp.where(member == inner, row, 0.0) for inner in range(3)]

    blocks = []
    for axis in range(3):
        blocks += three(-deriv[axis])
    w_pred[...] = jnp.concatenate(blocks, axis=0).astype(bf16)

    own = [
        lax.dot_general(
            evals[48 * face : 48 * face + NQ, :],
            lift[face],
            (((0,), (0,)), ((), ())),
            precision=exact,
            preferred_element_type=f32,
        )
        for face in range(4)
    ]
    blocks = []
    for matrix in [stiff[axis] for axis in range(3)] + own + [own[0] + own[1] + own[2] + own[3]]:
        blocks += three(matrix if len(blocks) < 9 else -0.5 * matrix)
    w_own[...] = jnp.concatenate(blocks, axis=0).astype(bf16)

    column = iota((LANES, 144), 1)
    spread = one_hot(iota((LANES, 144), 0) == (column & 15))
    column = column[:NBP]
    block = column >> 4
    member = block - jnp.where(column >= 96, 6, jnp.where(column >= 48, 3, 0))
    for face in range(4):
        high, low = split(turned(lift[face], NQ, NB))
        row = jnp.where(column < 96, dot(high, spread), dot(low, spread))
        rows = [jnp.where(member == inner, -0.5 * row, 0.0) for inner in range(3)]
        w_lift[face] = jnp.concatenate(rows + [-r for r in rows], axis=0).astype(bf16)

    basis_of = one_hot((iota((320, NB), 0) >> 4) == iota((320, NB), 1))
    keep = (iota((320, PACK), 0) & 15) == (iota((320, PACK), 1) & 15)
    code_of = one_hot((iota((PACK, 16), 0) >> 4) == iota((PACK, 16), 1))
    halves = []
    for part_of in split(evals[...]):
        halves.append(dot(jnp.where(keep, dot_last(basis_of, part_of), 0.0).astype(bf16), code_of))
    w_table[:, :16] = halves[0].astype(bf16)
    w_table[:, 16:] = halves[1].astype(bf16)


def find_links(devices, tiles, small, aux, from_top):
    me = lax.axis_index("dom").astype(f32)
    row = iota((ASKS, LANES), 0).astype(f32)
    up_to = one_hot(iota((LANES, LANES), 0) <= iota((LANES, LANES), 1))
    request = (iota((LANES, LANES), 0) & (REQ - 1)).astype(f32)
    carry = jnp.zeros((ASKS, 1), f32)
    wanted = jnp.zeros((2 * ASKS, LANES), f32)
    for tile in range(tiles):
        at = slice(tile * LANES, (tile + 1) * LANES)
        occupied = small[OCCUPIED : OCCUPIED + 1, at] > 0.5
        target = jnp.full((1, LANES), -1.0, f32)
        slots = jnp.zeros((1, LANES), f32)
        for face in range(4):
            link = small[LINK + face : LINK + face + 1, at]
            owner = jnp.floor((link + 0.5) * (1.0 / PARTITION_SLOTS))
            slot = link - owner * PARTITION_SLOTS
            near = owner == me
            aux[face : face + 1, at] = jnp.where(near, slot, -1.0).astype(i32)
            away = occupied & jnp.logical_not(near)
            target = jnp.where(away, owner, target)
            slots = jnp.where(away, slot, slots)
        far = target - me
        far = jnp.where(far < 0, far + devices, far)
        partner = jnp.where(far <= 4, far - 1.0, jnp.where(far >= devices - 4, devices + 3.0 - far, 8.0))
        partner = jnp.where(target >= 0, partner, -1.0)
        named = jnp.where(row == partner, 1.0, 0.0)
        prefix = dot(named.astype(bf16), up_to) + carry
        carry = carry + jnp.sum(named, axis=1, keepdims=True)
        rank = jnp.sum(named * prefix, axis=0, keepdims=True) - 1.0
        if from_top:
            rank = REQ - 1.0 - rank
        aux[4:5, at] = jnp.where(target >= 0, partner * REQ + rank, -1.0).astype(i32)
        aux[5:8, at] = jnp.zeros((3, LANES), i32)
        ask = slots + 1.0
        high = jnp.floor(ask * (1.0 / 32)) * 32.0
        both = jnp.concatenate([named * high, named * (ask - high)], axis=0).astype(bf16)
        wanted = wanted + dot_last(both, one_hot(request == rank))
    return wanted[:ASKS] + wanted[ASKS:]


def prepare_kernel(devices, tiles, normals, speed, cluster, slot, links, orient, q, jac, small, aux, asks, group, one, record):
    me = lax.axis_index("dom")
    for face in range(4):
        small[3 * face : 3 * face + 3, :] = jnp.concatenate([normals[d, face : face + 1, :] for d in range(3)], axis=0)
    small[SPEED : SPEED + 1, :] = speed[...]
    small[CLUSTER : CLUSTER + 1, :] = cluster[...].astype(f32)
    small[LINK : LINK + 4, :] = links[...].astype(f32)
    small[ORIENT : ORIENT + 4, :] = orient[...].astype(f32)
    where = slot[...]
    stays = (where >= me * PARTITION_SLOTS) & (where < (me + 1) * PARTITION_SLOTS)
    small[OCCUPIED : OCCUPIED + 1, :] = jnp.where(stays, 1.0, 0.0)
    small[OCCUPIED + 1 : SMALL, :] = jnp.zeros((1, tiles * LANES), f32)
    wanted = find_links(devices, tiles, small, aux, False)
    asks[...] = jnp.zeros((devices, 1, LANES), f32)
    for k, offset in enumerate(partner_offsets(devices)):
        asks[lax.rem(me + offset + devices, devices)] = wanted[k : k + 1]

    record[...] = jnp.zeros((RECORD, LANES), f32)
    for p in range(NV):
        record[p * NBP : p * NBP + NB] = q[p]
        for inner in range(NV):
            at = ROWS + 4 * (p * NV + inner)
            record[at : at + 3] = jac[p, inner]
    fields = small[:, KEEP:]
    row = iota(fields.shape, 0)
    record[JAC_END : JAC_END + SMALL] = jnp.where(row == OCCUPIED, 1.0 - fields, fields)
    whole = record[...]
    turned = jnp.concatenate([whole[c : c + LANES].T for c in range(0, RECORD, LANES)], axis=1)
    one[...] = turned[:CSZ]
    position = me // (devices // GROUPS)
    for g in range(GROUPS):
        group[lax.rem(position + g, GROUPS)] = turned[g * CSZ : (g + 1) * CSZ]


def prepare(normals, speed, cluster, slot, links, orient, q, jac, devices):
    count = q.shape[2]

    def body(*refs):
        prepare_kernel(devices, count // LANES, *refs)

    last = KEEP // LANES
    return pl.pallas_call(
        body,
        grid=(1,),
        in_specs=[
            whole_spec(normals),
            whole_spec(speed),
            whole_spec(cluster),
            whole_spec(slot),
            whole_spec(links),
            whole_spec(orient),
            pl.BlockSpec((NV, NB, LANES), lambda i: (0, 0, last)),
            pl.BlockSpec((NV, NV, 3, LANES), lambda i: (0, 0, 0, last)),
        ],
        out_specs=[
            pl.BlockSpec((SMALL, count), lambda i: (0, 0)),
            pl.BlockSpec((8, count), lambda i: (0, 0)),
            pl.BlockSpec((devices, 1, LANES), lambda i: (0, 0, 0)),
            pl.BlockSpec((GROUPS, CSZ, RECORD), lambda i: (0, 0, 0)),
            pl.BlockSpec((CSZ, RECORD), lambda i: (0, 0)),
        ],
        out_shape=[
            jax.ShapeDtypeStruct((SMALL, count), f32),
            jax.ShapeDtypeStruct((8, count), i32),
            jax.ShapeDtypeStruct((devices, 1, LANES), f32),
            jax.ShapeDtypeStruct((GROUPS, CSZ, RECORD), f32),
            jax.ShapeDtypeStruct((CSZ, RECORD), f32),
        ],
        scratch_shapes=[pltpu.VMEM((RECORD, LANES), f32)],
        compiler_params=PARAMS,
        name="prepare",
    )(normals, speed, cluster, slot, links, orient, q, jac)


def unpack(devices, group, one, q, jac, small, aux):
    position = lax.axis_index("dom") // (devices // GROUPS)
    rows = [one[...]]
    for g in range(1, GROUPS):
        rows.append(group[lax.rem(position - g + GROUPS, GROUPS)])
    whole = jnp.concatenate(rows, axis=0)
    turned = jnp.concatenate([whole[:, c : c + LANES].T for c in range(0, RECORD, LANES)], axis=0)
    for p in range(NV):
        q[p] = turned[p * NBP : p * NBP + NB]
        for inner in range(NV):
            at = ROWS + 4 * (p * NV + inner)
            jac[p, inner] = turned[at : at + 3]
    small[...] = turned[JAC_END : JAC_END + SMALL]
    return find_links(devices, 1, small, aux, True)


OUT_BLOCKS = {1: (0, 0), 4: (0, 1), -2: (0, 2), -1: (1, 0), -4: (1, 1), 2: (1, 2), 3: (2, 0), -3: (3, 0)}
IN_BLOCKS = {-1: (0, 0), 1: (1, 0), -3: (2, 0), -4: (2, 1), -2: (2, 2), 3: (3, 0), 4: (3, 1), 2: (3, 2)}


def put(outs, rows, k, devices):
    if k == PARTNERS - 1:
        return outs[4], 0
    array, block = OUT_BLOCKS[-partner_offsets(devices)[k]]
    return outs[array], block * rows


def take(messages, k, devices):
    if k == PARTNERS - 1:
        return messages[4], 0
    array, block = IN_BLOCKS[partner_offsets(devices)[k]]
    rows = messages[4].shape[0]
    return messages[array], block * rows


def picked(requests, fields):
    lane = iota((1, LANES), 1)
    tiles = []
    for at in range(0, 12, 4):
        four = [requests[min(at + n, PARTNERS - 1)] for n in range(4)]
        tiles.append(
            jnp.where(lane < 32, four[0], jnp.where(lane < 64, four[1], jnp.where(lane < 96, four[2], four[3])))
        )
    slots = (iota((KEEP, FAR), 0) + 1).astype(f32)
    return dot(fields, one_hot(slots == jnp.concatenate(tiles, axis=1)))


def message_rows(both):
    value = both[:PACK] + both[PACK:]
    return jnp.concatenate([value, jnp.zeros((MSG - PACK, FAR), f32)], axis=0).T


def back(k):
    return k if k == PARTNERS - 1 else (k + 4) % 8


def requests_here(devices, asks):
    me = lax.axis_index("dom")
    peers = [lax.rem(me - o + devices, devices) for o in partner_offsets(devices)]
    return [asks[p] for p in peers]


def unpack_kernel(devices, group, one, asks, field, q, jac, small, aux, *outs):
    moved = unpack(devices, group, one, q, jac, small, aux)
    rows = message_rows(picked(requests_here(devices, asks), field[...]))
    for k in range(PARTNERS):
        out, at = put(outs, MESSAGE1, k, devices)
        out[at : at + REQ] = rows[k * REQ : (k + 1) * REQ]
        out[at + REQ : at + MESSAGE1, :LANES] = jnp.broadcast_to(moved[back(k) : back(k) + 1, :], (8, LANES))
        out[at + REQ : at + MESSAGE1, LANES:] = jnp.zeros((8, MSG - LANES), f32)


def answer_again(devices, asks, got, field, later, outs):
    moved = []
    for k in range(PARTNERS):
        message, at = take(got, back(k), devices)
        moved.append(message[at + REQ : at + REQ + 1, :LANES])
    every = [a + b for a, b in zip(requests_here(devices, asks), moved)]
    rows = message_rows(picked(every, later))
    rows_first = message_rows(picked(moved, field))
    for k in range(PARTNERS):
        out, at = put(outs, 2 * REQ, k, devices)
        out[at : at + REQ] = rows[k * REQ : (k + 1) * REQ]
        out[at + REQ : at + 2 * REQ] = rows_first[k * REQ : (k + 1) * REQ]


def relay_kernel(got_plus, got_minus, own_plus, own_minus, on_plus, on_minus):
    rows = own_plus.shape[0]
    block = [slice(b * rows, (b + 1) * rows) for b in range(3)]
    on_plus[block[0]] = own_plus[...]
    on_plus[block[1]] = got_plus[block[1]]
    on_plus[block[2]] = got_minus[block[2]]
    on_minus[block[0]] = own_minus[...]
    on_minus[block[1]] = got_minus[block[1]]
    on_minus[block[2]] = got_plus[block[2]]


def message_shapes(rows):
    return [jax.ShapeDtypeStruct((rows * blocks, MSG), f32) for blocks in (3, 3, 1, 1, 1)]


def far_table(devices, part, messages):
    rows = []
    for k in range(PARTNERS):
        message, at = take(messages, k, devices)
        rows.append(message[at + part * REQ : at + (part + 1) * REQ, :])
    rows.append(jnp.zeros((FAR - PARTNERS * REQ, MSG), f32))
    turned = jnp.concatenate(rows, axis=0).T[:PACK]
    return jnp.concatenate(split(turned), axis=0)


def lanes(tile):
    return slice(tile * LANES, (tile + 1) * LANES)


def jacobian_apply(jac, tile, parts):
    result = [None] * NV
    for group in range(3):
        for d in range(3):
            for inner in range(3):
                q = 3 * group + inner
                value = parts(d, q)
                for p in range(NV):
                    term = jac[p, q, d : d + 1, lanes(tile)] * value
                    result[p] = term if result[p] is None else result[p] + term
    return result


def packed_split(fields, group):
    packed = [pack_three(tile[3 * group : 3 * group + 3]) for tile in fields]
    return split(jnp.concatenate(packed, axis=1))


def split_fields(fields):
    pairs = [packed_split(fields, group) for group in range(3)]
    return jnp.concatenate([a for a, _ in pairs] + [b for _, b in pairs], axis=0)


def predict(start, jac, w_pred, scales):
    tiles = range(len(start))
    sums = [[[s[0] * x for x in tile] for tile in start] for s in scales]
    now = start
    for degree in range(1, NORDER):
        turned = [dot(w_pred, stacked(*packed_split(now, group))) for group in range(3)]
        now = [
            jacobian_apply(
                jac, t, lambda d, q: turned[q // 3][d * 72 + (q % 3) * NBP : d * 72 + (q % 3) * NBP + NBP, lanes(t)]
            )
            for t in tiles
        ]
        sums = [
            [[a + s[degree] * x for a, x in zip(total[t], now[t])] for t in tiles] for total, s in zip(sums, scales)
        ]
    return sums


def update(own, near, far, small, aux, jac, w_own, w_lift, w_table, gathered):
    count = own.shape[1]
    tiles = range(count // LANES)
    place = aux[4:5, :]
    both = dot(far, one_hot(iota((FAR, count), 0) == place))
    remote = both[:PACK] + both[PACK:]
    slots = iota((KEEP, count), 0)
    codes = iota((16, count), 0).astype(f32)

    def gather(face):
        index = aux[face : face + 1, :]
        both = dot(near[...], one_hot(slots == index))
        take_far = (index < 0) & (place >= 0)
        gathered[face, :, :count] = both[:PACK] + both[PACK:] + jnp.where(take_far, remote, 0.0)
        code = one_hot(codes == small[ORIENT + face : ORIENT + face + 1, :])
        return dot(w_table, jnp.concatenate([code, code], axis=0))

    table = gather(0)
    mine = []
    for group in range(3):
        rows = slice(64 * group, 64 * group + 64)
        lower = slice(PACK + 64 * group, PACK + 64 * group + 64)
        mine.append(dot(w_own, stacked(own[rows], own[lower])))

    def of_own(block, q, t):
        at = block * 72 + (q % 3) * NBP
        return mine[q // 3][at : at + NBP, lanes(t)]

    volume = [[[of_own(d, q, t) for q in range(NV)] for d in range(3)] for t in tiles]
    upwind = [[of_own(7, q, t) for q in range(NV)] for t in tiles]
    for face in range(4):
        now = table
        if face < 3:
            table = gather(face + 1)
        outers = []
        for t in tiles:
            outer = [None] * NV
            for b in range(NB):
                values = now[b * NQ : (b + 1) * NQ, lanes(t)]
                for p in range(NV):
                    at = packed_row(p, b)
                    term = gathered[face, at : at + 1, lanes(t)] * values
                    outer[p] = term if outer[p] is None else outer[p] + term
            outers.append(outer)
        for group in range(3):
            joined = [jnp.concatenate(outer[3 * group : 3 * group + 3], axis=0) for outer in outers]
            lifted = dot(w_lift[face], stacked(*split(jnp.concatenate(joined, axis=1))))
            for t in tiles:
                for inner in range(3):
                    q = 3 * group + inner
                    at = inner * NBP
                    mixed = lifted[at : at + NBP, lanes(t)] + of_own(3 + face, q, t)
                    upwind[t][q] = upwind[t][q] + lifted[72 + at : 72 + at + NBP, lanes(t)]
                    for d in range(3):
                        normal = small[3 * face + d : 3 * face + d + 1, lanes(t)]
                        volume[t][d][q] = volume[t][d][q] + normal * mixed
    result = []
    for t in tiles:
        change = jacobian_apply(jac, t, lambda d, q: volume[t][d][q])
        speed = small[SPEED : SPEED + 1, lanes(t)]
        result.append([c + speed * u for c, u in zip(change, upwind[t])])
    return result


def load_state(q, padded):
    padded[:, NB:NBP, :] = jnp.zeros((NV, NBP - NB, padded.shape[2]), f32)
    for p in range(NV):
        padded[p, :NB, :] = q[p]
    return load_field(padded)


def load_field(ref):
    return [[ref[p, :, lanes(t)] for p in range(NV)] for t in range(ref.shape[2] // LANES)]


def store_field(ref, field):
    for t, tile in enumerate(field):
        for p in range(NV):
            ref[p, :, lanes(t)] = tile[p]


def store_result(out, base, change, small):
    for t in range(len(base)):
        occupied = small[OCCUPIED : OCCUPIED + 1, lanes(t)] > 0.5
        for p in range(NV):
            out[p, :, lanes(t)] = jnp.where(occupied, base[t][p] + change[t][p], 0.0)[:NB]


def first_kernel(q, jac, deriv, stiff, evals, lift, packed, slow, w_pred, w_own, w_lift, w_table, padded, square):
    @pl.when(pl.program_id(0) == 0)
    def _():
        make_weights(deriv, stiff, evals, lift, w_pred, w_own, w_lift, w_table, square)

    first, later = predict(load_state(q, padded), jac, w_pred[...], [FIRST, SECOND])
    packed[...] = split_fields(first)
    store_field(slow, later)


def middle_step(start, jac, small, slow, own, near, far, aux, weights, gathered):
    w_pred, w_own, w_lift, w_table = weights
    change = update(own, near, far, small, aux, jac, w_own, w_lift, w_table, gathered)
    base, midway, second = [], [], []
    fast = [small[CLUSTER : CLUSTER + 1, lanes(t)] < 0.5 for t in range(len(start))]
    for t in range(len(start)):
        base.append([a + b for a, b in zip(start[t], change[t])])
        midway.append([jnp.where(fast[t], a, b) for a, b in zip(base[t], start[t])])
    (later,) = predict(midway, jac, w_pred, [FIRST])
    for t in range(len(start)):
        second.append([jnp.where(fast[t], a, b) for a, b in zip(later[t], slow[t])])
    return base, split_fields(second)


def middle_kernel(devices, steps, q, jac, small, slow, own, near, aux, asks, *refs):
    messages = refs[:5]
    w_pred, w_own, w_lift, w_table, base, packed, *outs, padded, gathered, far = refs[5:]
    step = pl.program_id(0)

    @pl.when(step == 0)
    def _():
        far[...] = far_table(devices, 0, messages)

    weights = (w_pred[...], w_own[...], w_lift, w_table[...])
    now, second = middle_step(
        load_state(q, padded), jac, small, load_field(slow), own[...], near, far[...], aux, weights, gathered
    )
    store_field(base, now)
    packed[:, pl.ds(pl.multiple_of(step * WIDE, WIDE), WIDE)] = second

    @pl.when(step == steps - 1)
    def _():
        answer_again(devices, asks, messages, near[...], packed[:, :KEEP], outs)


def last_kernel(
    devices, steps, base, jac, small, own, later, aux, q_moved, jac_moved, small_moved, aux_moved, near, *refs
):
    messages = refs[:5]
    w_pred, w_own, w_lift, w_table, out, padded, gathered, far = refs[5:]
    step = pl.program_id(0)

    @pl.when(step == 0)
    def _():
        far[...] = far_table(devices, 0, messages)

    @pl.when(step < steps)
    def _():
        change = update(
            own[...], later, far[...], small, aux, jac, w_own[...], w_lift, w_table[...], gathered
        )
        store_result(out, load_field(base), change, small)

    @pl.when(step == steps)
    def _():
        weights = (w_pred[...], w_own[...], w_lift, w_table[...])
        start = load_state(q_moved, padded)
        first, slow = predict(start, jac_moved, weights[0], [FIRST, SECOND])
        now, second = middle_step(
            start, jac_moved, small_moved, slow, split_fields(first), near, far_table(devices, 1, messages), aux_moved,
            weights, gathered,
        )
        change = update(second, later, far[...], small_moved, aux_moved, jac_moved, *weights[1:], gathered)
        store_result(out, now, change, small_moved)


def whole_spec(array):
    rank = array.ndim
    return pl.BlockSpec(array.shape, lambda i: (0,) * rank)


def lane_spec(*lead, last=None):
    rank = len(lead)
    if last is None:
        return pl.BlockSpec(lead + (WIDE,), lambda i: (0,) * rank + (i,))
    return pl.BlockSpec(lead + (WIDE,), lambda i: (0,) * rank + (jnp.minimum(i, last),))


Q_SPEC = lane_spec(NV, NB)
J_SPEC = lane_spec(NV, NV, 3)
S_SPEC = lane_spec(SMALL)
A_SPEC = lane_spec(8)
F_SPEC = lane_spec(NV, NBP)
X_SPEC = lane_spec(2 * PACK)
N_SPEC = pl.BlockSpec((2 * PACK, KEEP), lambda i: (0, 0))


def scratch_of(width):
    return pltpu.VMEM((NV, NBP, width), f32), pltpu.VMEM((4, PACK, width), f32)


def per_device(
    element_freedom_values,
    scaled_jacobian_matrices,
    outward_face_normals,
    largest_wave_speed,
    element_cluster_index,
    element_new_slot,
    neighbours,
    face_rotation_codes,
    deriv_mats,
    stiff_mats,
    face_eval,
    face_lift,
):
    count = element_freedom_values.shape[2]
    steps = count // WIDE
    devices = lax.axis_size("dom")
    q = element_freedom_values
    jac = jnp.transpose(scaled_jacobian_matrices, (1, 2, 0, 3))

    def shift(array, by):
        return lax.ppermute(array, "dom", [(i, (i + by) % devices) for i in range(devices)])

    def swap(array, groups):
        return lax.all_to_all(array, "dom", split_axis=0, concat_axis=0, axis_index_groups=groups, tiled=True)

    def exchange(plus, minus, own_plus, own_minus, half):
        got_plus, got_minus, half = shift(plus, 1), shift(minus, -1), shift(half, devices // 2)
        on_plus, on_minus = pl.pallas_call(
            relay_kernel,
            out_shape=[jax.ShapeDtypeStruct(plus.shape, f32)] * 2,
            compiler_params=pltpu.CompilerParams(vmem_limit_bytes=4 << 20),
            name="relay",
        )(got_plus, got_minus, own_plus, own_minus)
        return got_plus, got_minus, shift(on_plus, 3), shift(on_minus, -3), half

    def on_ring(body):
        def kernel(*refs):
            body(devices, *refs)

        return kernel

    small, aux, asks, group, one = prepare(
        jnp.transpose(outward_face_normals, (1, 0, 2)),
        largest_wave_speed[None],
        element_cluster_index[None],
        element_new_slot[None],
        neighbours,
        face_rotation_codes,
        q,
        jac,
        devices,
    )
    asks = swap(asks, None)
    asks, group, one = lax.optimization_barrier((asks, group, one))
    stride = devices // GROUPS
    group = swap(group, [[r + stride * j for j in range(GROUPS)] for r in range(stride)])
    one = shift(one, 1)
    padded, gathered = scratch_of(WIDE)
    packed_shape = jax.ShapeDtypeStruct((2 * PACK, count), bf16)
    field_shape = jax.ShapeDtypeStruct((NV, NBP, count), f32)
    far = pltpu.VMEM((2 * PACK, FAR), bf16)
    weight_shapes = [
        jax.ShapeDtypeStruct((ROWS, PACK), bf16),
        jax.ShapeDtypeStruct((576, PACK), bf16),
        jax.ShapeDtypeStruct((4, 144, 144), bf16),
        jax.ShapeDtypeStruct((320, 32), bf16),
    ]
    evals = jnp.transpose(face_eval, (0, 2, 1)).reshape(12 * NQ, NB)
    matrices = [deriv_mats, stiff_mats, evals, face_lift]
    first, slow, *weights = pl.pallas_call(
        first_kernel,
        grid=(steps,),
        in_specs=[Q_SPEC, J_SPEC] + [whole_spec(m) for m in matrices],
        out_specs=[X_SPEC, F_SPEC] + [whole_spec(w) for w in weight_shapes],
        out_shape=[packed_shape, field_shape] + weight_shapes,
        scratch_shapes=[padded, pltpu.VMEM((LANES, LANES), f32)],
        compiler_params=PARAMS,
        name="first",
    )(q, jac, *matrices)

    moved_shapes = [
        jax.ShapeDtypeStruct((NV, NB, LANES), f32),
        jax.ShapeDtypeStruct((NV, NV, 3, LANES), f32),
        jax.ShapeDtypeStruct((SMALL, LANES), f32),
        jax.ShapeDtypeStruct((8, LANES), i32),
    ]
    out_shape = moved_shapes + message_shapes(MESSAGE1)
    *moved, m0, m1, m2, m3, m4 = pl.pallas_call(
        on_ring(unpack_kernel),
        grid=(1,),
        in_specs=[whole_spec(a) for a in (group, one, asks)] + [N_SPEC],
        out_specs=[whole_spec(o) for o in out_shape],
        out_shape=out_shape,
        compiler_params=PARAMS,
        name="unpack",
    )(group, one, asks, first)
    messages = exchange(m0, m1, m2, m3, m4)

    def middle(*refs):
        middle_kernel(devices, steps, *refs)

    out_shape = [field_shape, packed_shape] + message_shapes(2 * REQ)
    base, second, *answers = pl.pallas_call(
        middle,
        grid=(steps,),
        in_specs=[Q_SPEC, J_SPEC, S_SPEC, F_SPEC, X_SPEC, N_SPEC, A_SPEC, whole_spec(asks)]
        + [whole_spec(a) for a in (*messages, *weights)],
        out_specs=[F_SPEC] + [whole_spec(o) for o in out_shape[1:]],
        out_shape=out_shape,
        scratch_shapes=[padded, gathered, far],
        compiler_params=PARAMS,
        name="middle",
    )(q, jac, small, slow, first, first, aux, asks, *messages, *weights)
    messages = exchange(*answers)

    def last(*refs):
        last_kernel(devices, steps, *refs)

    end = steps - 1
    return pl.pallas_call(
        last,
        grid=(steps + 1,),
        in_specs=[
            lane_spec(NV, NBP, last=end),
            lane_spec(NV, NV, 3, last=end),
            lane_spec(SMALL, last=end),
            lane_spec(2 * PACK, last=end),
            N_SPEC,
            lane_spec(8, last=end),
        ]
        + [whole_spec(a) for a in moved]
        + [N_SPEC]
        + [whole_spec(a) for a in (*messages, *weights)],
        out_specs=Q_SPEC,
        out_shape=jax.ShapeDtypeStruct((NV, NB, PARTITION_SLOTS), f32),
        scratch_shapes=[scratch_of(LANES)[0], gathered, far],
        compiler_params=PARAMS,
        name="last",
    )(base, jac, small, second, second, aux, *moved, first, *messages, *weights)


def solution(mesh):
    placed = (
        P(None, None, "dom"),
        P(None, None, None, "dom"),
        P(None, None, "dom"),
        P("dom"),
        P("dom"),
        P("dom"),
        P(None, "dom"),
        P(None, "dom"),
        P(),
        P(),
        P(),
        P(),
    )
    return jax.shard_map(
        per_device, mesh=mesh, in_specs=placed, out_specs=P(None, None, "dom"), check_vma=False
    )
```

```python
import math

import jax
import jax.numpy as jnp
from jax import lax
from jax.experimental import pallas as pl
from jax.experimental.pallas import tpu as pltpu
from jax.sharding import PartitionSpec as P

NV = 9
NB = 20
NBP = 24
NQ = 16
NORDER = 4
GROUPS = 8
CSZ = 16
KEEP = 896
PARTITION_SLOTS = 1152
REQ = 32
PARTNERS = 9
ASKS = 16
LANES = 128
WIDE = 256
ROWS = 216
JAC_END = ROWS + 4 * NV * NV
PACK = 192
MSG = 256
FAR = 384
RECORD = 640
SMALL = 24
MESSAGE1 = REQ + 8

step_fast = 0.25
exact = lax.Precision.HIGHEST
f32 = jnp.float32
bf16 = jnp.bfloat16
i32 = jnp.int32

SPEED, CLUSTER, LINK, ORIENT, OCCUPIED = 12, 13, 14, 18, 22

PARAMS = pltpu.CompilerParams(vmem_limit_bytes=60 << 20)


def coefficients(lower, upper):
    return [
        (upper ** (degree + 1) - lower ** (degree + 1)) / math.factorial(degree + 1)
        for degree in range(NORDER)
    ]


FIRST = coefficients(0.0, step_fast)
SECOND = coefficients(step_fast, 2.0 * step_fast)


def partner_offsets(devices):
    return [1, 2, 3, 4, -1, -2, -3, -4, devices // 2]


def packed_row(quantity, basis):
    group, member = quantity // 3, quantity % 3
    inside = 16 * member + basis if basis < 16 else 48 + 4 * member + (basis - 16)
    return 64 * group + inside


def pack_three(members):
    a, b, c = members
    tail = a[16:24] + pltpu.roll(b[16:24], 4, 0)
    return jnp.concatenate([a[:16], b[:16], c[:16], tail, c[16:24]], axis=0)


def split(values):
    high = values.astype(bf16)
    low = (values - high.astype(f32)).astype(bf16)
    return high, low


def stacked(high, low):
    return jnp.concatenate([high, low, high], axis=0)


def dot(a, b):
    return jnp.dot(a, b, preferred_element_type=f32)


def dot_last(a, b):
    return lax.dot_general(a, b, (((1,), (1,)), ((), ())), preferred_element_type=f32)


def iota(shape, axis):
    return lax.broadcasted_iota(i32, shape, axis)


def one_hot(condition):
    return jnp.where(condition, 1.0, 0.0).astype(bf16)


def make_weights(deriv, stiff, evals, lift, w_pred, w_own, w_lift, w_table, w_far, square):
    def turned(matrix, rows, columns):
        square[...] = jnp.zeros((LANES, LANES), f32)
        square[:rows, :columns] = matrix
        return square[...].T[:NBP]

    column = iota((LANES, PACK), 1) & 63
    member = jnp.where(column < 48, column >> 4, (column - 48) >> 2)
    basis = jnp.where(column < 48, column & 15, 16 + (column & 3))
    spread = one_hot(iota((LANES, PACK), 0) == jnp.where(member < 3, basis, -1))
    member = member[:NBP]
    part = iota((NBP, PACK), 1)

    def three(matrix):
        high, low = split(turned(matrix, NB, NB))
        row = jnp.where(part < 128, dot(high, spread), dot(low, spread))
        return [jnp.where(member == inner, row, 0.0) for inner in range(3)]

    blocks = []
    for axis in range(3):
        blocks += three(-deriv[axis])
    w_pred[...] = jnp.concatenate(blocks, axis=0).astype(bf16)

    own = [
        lax.dot_general(
            evals[48 * face : 48 * face + NQ, :],
            lift[face],
            (((0,), (0,)), ((), ())),
            precision=exact,
            preferred_element_type=f32,
        )
        for face in range(4)
    ]
    blocks = []
    for matrix in [stiff[axis] for axis in range(3)] + own + [own[0] + own[1] + own[2] + own[3]]:
        blocks += three(matrix if len(blocks) < 9 else -0.5 * matrix)
    w_own[...] = jnp.concatenate(blocks, axis=0).astype(bf16)

    column = iota((LANES, 144), 1)
    spread = one_hot(iota((LANES, 144), 0) == (column & 15))
    column = column[:NBP]
    block = column >> 4
    member = block - jnp.where(column >= 96, 6, jnp.where(column >= 48, 3, 0))
    every = []
    for face in range(4):
        high, low = split(turned(lift[face], NQ, NB))
        row = jnp.where(column < 96, dot(high, spread), dot(low, spread))
        rows = [jnp.where(member == inner, -0.5 * row, 0.0) for inner in range(3)]
        w_lift[face] = jnp.concatenate(rows + [-r for r in rows], axis=0).astype(bf16)
        every += rows
    w_far[...] = jnp.concatenate(every, axis=0).astype(bf16)

    basis_of = one_hot((iota((320, NB), 0) >> 4) == iota((320, NB), 1))
    keep = (iota((320, PACK), 0) & 15) == (iota((320, PACK), 1) & 15)
    code_of = one_hot((iota((PACK, 16), 0) >> 4) == iota((PACK, 16), 1))
    halves = []
    for part_of in split(evals[...]):
        halves.append(dot(jnp.where(keep, dot_last(basis_of, part_of), 0.0).astype(bf16), code_of))
    w_table[:, :16] = halves[0].astype(bf16)
    w_table[:, 16:] = halves[1].astype(bf16)


def find_links(devices, tiles, small, aux, from_top):
    me = lax.axis_index("dom").astype(f32)
    row = iota((ASKS, LANES), 0).astype(f32)
    up_to = one_hot(iota((LANES, LANES), 0) <= iota((LANES, LANES), 1))
    request = (iota((LANES, LANES), 0) & (REQ - 1)).astype(f32)
    carry = jnp.zeros((ASKS, 1), f32)
    wanted = jnp.zeros((2 * ASKS, LANES), f32)
    for tile in range(tiles):
        at = slice(tile * LANES, (tile + 1) * LANES)
        occupied = small[OCCUPIED : OCCUPIED + 1, at] > 0.5
        target = jnp.full((1, LANES), -1.0, f32)
        slots = jnp.zeros((1, LANES), f32)
        for face in range(4):
            link = small[LINK + face : LINK + face + 1, at]
            owner = jnp.floor((link + 0.5) * (1.0 / PARTITION_SLOTS))
            slot = link - owner * PARTITION_SLOTS
            near = owner == me
            aux[face : face + 1, at] = jnp.where(near, slot, -1.0).astype(i32)
            away = occupied & jnp.logical_not(near)
            target = jnp.where(away, owner, target)
            slots = jnp.where(away, slot, slots)
        far = target - me
        far = jnp.where(far < 0, far + devices, far)
        partner = jnp.where(far <= 4, far - 1.0, jnp.where(far >= devices - 4, devices + 3.0 - far, 8.0))
        partner = jnp.where(target >= 0, partner, -1.0)
        named = jnp.where(row == partner, 1.0, 0.0)
        prefix = dot(named.astype(bf16), up_to) + carry
        carry = carry + jnp.sum(named, axis=1, keepdims=True)
        rank = jnp.sum(named * prefix, axis=0, keepdims=True) - 1.0
        if from_top:
            rank = REQ - 1.0 - rank
        aux[4:5, at] = jnp.where(target >= 0, partner * REQ + rank, -1.0).astype(i32)
        aux[5:8, at] = jnp.zeros((3, LANES), i32)
        ask = slots + 1.0
        high = jnp.floor(ask * (1.0 / 32)) * 32.0
        both = jnp.concatenate([named * high, named * (ask - high)], axis=0).astype(bf16)
        wanted = wanted + dot_last(both, one_hot(request == rank))
    return wanted[:ASKS] + wanted[ASKS:]


def prepare_kernel(devices, tiles, normals, speed, cluster, slot, links, orient, q, jac, small, aux, asks, group, one, record):
    me = lax.axis_index("dom")
    for face in range(4):
        small[3 * face : 3 * face + 3, :] = jnp.concatenate([normals[d, face : face + 1, :] for d in range(3)], axis=0)
    small[SPEED : SPEED + 1, :] = speed[...]
    small[CLUSTER : CLUSTER + 1, :] = cluster[...].astype(f32)
    small[LINK : LINK + 4, :] = links[...].astype(f32)
    small[ORIENT : ORIENT + 4, :] = orient[...].astype(f32)
    where = slot[...]
    stays = (where >= me * PARTITION_SLOTS) & (where < (me + 1) * PARTITION_SLOTS)
    small[OCCUPIED : OCCUPIED + 1, :] = jnp.where(stays, 1.0, 0.0)
    small[OCCUPIED + 1 : SMALL, :] = jnp.zeros((1, tiles * LANES), f32)
    wanted = find_links(devices, tiles, small, aux, False)
    asks[...] = jnp.zeros((devices, 1, LANES), f32)
    for k, offset in enumerate(partner_offsets(devices)):
        asks[lax.rem(me + offset + devices, devices)] = wanted[k : k + 1]

    record[...] = jnp.zeros((RECORD, LANES), f32)
    for p in range(NV):
        record[p * NBP : p * NBP + NB] = q[p]
        for inner in range(NV):
            at = ROWS + 4 * (p * NV + inner)
            record[at : at + 3] = jac[p, inner]
    fields = small[:, KEEP:]
    row = iota(fields.shape, 0)
    record[JAC_END : JAC_END + SMALL] = jnp.where(row == OCCUPIED, 1.0 - fields, fields)
    whole = record[...]
    turned = jnp.concatenate([whole[c : c + LANES].T for c in range(0, RECORD, LANES)], axis=1)
    one[...] = turned[:CSZ]
    position = me // (devices // GROUPS)
    for g in range(GROUPS):
        group[lax.rem(position + g, GROUPS)] = turned[g * CSZ : (g + 1) * CSZ]


def prepare(normals, speed, cluster, slot, links, orient, q, jac, devices):
    count = q.shape[2]

    def body(*refs):
        prepare_kernel(devices, count // LANES, *refs)

    last = KEEP // LANES
    return pl.pallas_call(
        body,
        grid=(1,),
        in_specs=[
            whole_spec(normals),
            whole_spec(speed),
            whole_spec(cluster),
            whole_spec(slot),
            whole_spec(links),
            whole_spec(orient),
            pl.BlockSpec((NV, NB, LANES), lambda i: (0, 0, last)),
            pl.BlockSpec((NV, NV, 3, LANES), lambda i: (0, 0, 0, last)),
        ],
        out_specs=[
            pl.BlockSpec((SMALL, count), lambda i: (0, 0)),
            pl.BlockSpec((8, count), lambda i: (0, 0)),
            pl.BlockSpec((devices, 1, LANES), lambda i: (0, 0, 0)),
            pl.BlockSpec((GROUPS, CSZ, RECORD), lambda i: (0, 0, 0)),
            pl.BlockSpec((CSZ, RECORD), lambda i: (0, 0)),
        ],
        out_shape=[
            jax.ShapeDtypeStruct((SMALL, count), f32),
            jax.ShapeDtypeStruct((8, count), i32),
            jax.ShapeDtypeStruct((devices, 1, LANES), f32),
            jax.ShapeDtypeStruct((GROUPS, CSZ, RECORD), f32),
            jax.ShapeDtypeStruct((CSZ, RECORD), f32),
        ],
        scratch_shapes=[pltpu.VMEM((RECORD, LANES), f32)],
        compiler_params=PARAMS,
        name="prepare",
    )(normals, speed, cluster, slot, links, orient, q, jac)


def unpack(devices, group, one, q, jac, small, aux):
    position = lax.axis_index("dom") // (devices // GROUPS)
    rows = [one[...]]
    for g in range(1, GROUPS):
        rows.append(group[lax.rem(position - g + GROUPS, GROUPS)])
    whole = jnp.concatenate(rows, axis=0)
    turned = jnp.concatenate([whole[:, c : c + LANES].T for c in range(0, RECORD, LANES)], axis=0)
    for p in range(NV):
        q[p] = turned[p * NBP : p * NBP + NB]
        for inner in range(NV):
            at = ROWS + 4 * (p * NV + inner)
            jac[p, inner] = turned[at : at + 3]
    small[...] = turned[JAC_END : JAC_END + SMALL]
    return find_links(devices, 1, small, aux, True)


OUT_BLOCKS = {1: (0, 0), 4: (0, 1), -2: (0, 2), -1: (1, 0), -4: (1, 1), 2: (1, 2), 3: (2, 0), -3: (3, 0)}
IN_BLOCKS = {-1: (0, 0), 1: (1, 0), -3: (2, 0), -4: (2, 1), -2: (2, 2), 3: (3, 0), 4: (3, 1), 2: (3, 2)}


def put(outs, rows, k, devices):
    if k == PARTNERS - 1:
        return outs[4], 0
    array, block = OUT_BLOCKS[-partner_offsets(devices)[k]]
    return outs[array], block * rows


def take(messages, k, devices):
    if k == PARTNERS - 1:
        return messages[4], 0
    array, block = IN_BLOCKS[partner_offsets(devices)[k]]
    rows = messages[4].shape[0]
    return messages[array], block * rows


def picked(requests, fields):
    lane = iota((1, LANES), 1)
    tiles = []
    for at in range(0, 12, 4):
        four = [requests[min(at + n, PARTNERS - 1)] for n in range(4)]
        tiles.append(
            jnp.where(lane < 32, four[0], jnp.where(lane < 64, four[1], jnp.where(lane < 96, four[2], four[3])))
        )
    slots = (iota((KEEP, FAR), 0) + 1).astype(f32)
    return dot(fields, one_hot(slots == jnp.concatenate(tiles, axis=1)))


def message_rows(both):
    value = both[:PACK] + both[PACK:]
    return jnp.concatenate([value, jnp.zeros((MSG - PACK, FAR), f32)], axis=0).T


def back(k):
    return k if k == PARTNERS - 1 else (k + 4) % 8


def requests_here(devices, asks):
    me = lax.axis_index("dom")
    peers = [lax.rem(me - o + devices, devices) for o in partner_offsets(devices)]
    return [asks[p] for p in peers]


def unpack_kernel(devices, group, one, asks, field, q, jac, small, aux, *outs):
    moved = unpack(devices, group, one, q, jac, small, aux)
    rows = message_rows(picked(requests_here(devices, asks), field[...]))
    for k in range(PARTNERS):
        out, at = put(outs, MESSAGE1, k, devices)
        out[at : at + REQ] = rows[k * REQ : (k + 1) * REQ]
        out[at + REQ : at + MESSAGE1, :LANES] = jnp.broadcast_to(moved[back(k) : back(k) + 1, :], (8, LANES))
        out[at + REQ : at + MESSAGE1, LANES:] = jnp.zeros((8, MSG - LANES), f32)


def answer_again(devices, asks, got, field, later, outs):
    moved = []
    for k in range(PARTNERS):
        message, at = take(got, back(k), devices)
        moved.append(message[at + REQ : at + REQ + 1, :LANES])
    every = [a + b for a, b in zip(requests_here(devices, asks), moved)]
    rows = message_rows(picked(every, later))
    rows_first = message_rows(picked(moved, field))
    for k in range(PARTNERS):
        out, at = put(outs, 2 * REQ, k, devices)
        out[at : at + REQ] = rows[k * REQ : (k + 1) * REQ]
        out[at + REQ : at + 2 * REQ] = rows_first[k * REQ : (k + 1) * REQ]


def relay_kernel(got_plus, got_minus, own_plus, own_minus, on_plus, on_minus):
    rows = own_plus.shape[0]
    block = [slice(b * rows, (b + 1) * rows) for b in range(3)]
    on_plus[block[0]] = own_plus[...]
    on_plus[block[1]] = got_plus[block[1]]
    on_plus[block[2]] = got_minus[block[2]]
    on_minus[block[0]] = own_minus[...]
    on_minus[block[1]] = got_minus[block[1]]
    on_minus[block[2]] = got_plus[block[2]]


def message_shapes(rows):
    return [jax.ShapeDtypeStruct((rows * blocks, MSG), f32) for blocks in (3, 3, 1, 1, 1)]


def far_table(devices, part, messages):
    rows = []
    for k in range(PARTNERS):
        message, at = take(messages, k, devices)
        rows.append(message[at + part * REQ : at + (part + 1) * REQ, :])
    rows.append(jnp.zeros((FAR - PARTNERS * REQ, MSG), f32))
    turned = jnp.concatenate(rows, axis=0).T[:PACK]
    return jnp.concatenate(split(turned), axis=0)


def lanes(tile):
    return slice(tile * LANES, (tile + 1) * LANES)


def jacobian_apply(jac, tile, parts):
    result = [None] * NV
    for group in range(3):
        for d in range(3):
            for inner in range(3):
                q = 3 * group + inner
                value = parts(d, q)
                for p in range(NV):
                    term = jac[p, q, d : d + 1, lanes(tile)] * value
                    result[p] = term if result[p] is None else result[p] + term
    return result


def packed_split(fields, group):
    packed = [pack_three(tile[3 * group : 3 * group + 3]) for tile in fields]
    return split(jnp.concatenate(packed, axis=1))


def split_fields(fields):
    pairs = [packed_split(fields, group) for group in range(3)]
    return jnp.concatenate([a for a, _ in pairs] + [b for _, b in pairs], axis=0)


def predict(start, jac, w_pred, scales):
    tiles = range(len(start))
    sums = [[[s[0] * x for x in tile] for tile in start] for s in scales]
    now = start
    for degree in range(1, NORDER):
        turned = [dot(w_pred, stacked(*packed_split(now, group))) for group in range(3)]
        now = [
            jacobian_apply(
                jac, t, lambda d, q: turned[q // 3][d * 72 + (q % 3) * NBP : d * 72 + (q % 3) * NBP + NBP, lanes(t)]
            )
            for t in tiles
        ]
        sums = [
            [[a + s[degree] * x for a, x in zip(total[t], now[t])] for t in tiles] for total, s in zip(sums, scales)
        ]
    return sums


def face_products(gathered, at_face, table, tiles):
    outers = []
    for t in tiles:
        outer = [None] * NV
        for b in range(NB):
            values = table[b * NQ : (b + 1) * NQ, lanes(t)]
            for p in range(NV):
                at = packed_row(p, b)
                term = gathered[at_face, at : at + 1, lanes(t)] * values
                outer[p] = term if outer[p] is None else outer[p] + term
        outers.append(outer)
    return [
        stacked(*split(jnp.concatenate([jnp.concatenate(o[3 * g : 3 * g + 3], axis=0) for o in outers], axis=1)))
        for g in range(3)
    ]


def table_of(code, w_table):
    hot = one_hot(iota((16, code.shape[1]), 0).astype(f32) == code)
    return dot(w_table, jnp.concatenate([hot, hot], axis=0))


def near_part(own, near, small, aux, w_own, w_lift, w_table, gathered):
    count = own.shape[1]
    tiles = range(count // LANES)
    slots = iota((KEEP, count), 0)

    def gather(face):
        both = dot(near[...], one_hot(slots == aux[face : face + 1, :]))
        gathered[face, :, :count] = both[:PACK] + both[PACK:]
        return table_of(small[ORIENT + face : ORIENT + face + 1, :], w_table)

    table = gather(0)
    mine = []
    for group in range(3):
        rows = slice(64 * group, 64 * group + 64)
        lower = slice(PACK + 64 * group, PACK + 64 * group + 64)
        mine.append(dot(w_own, stacked(own[rows], own[lower])))

    def of_own(block, q, t):
        at = block * 72 + (q % 3) * NBP
        return mine[q // 3][at : at + NBP, lanes(t)]

    volume = [[[of_own(d, q, t) for q in range(NV)] for d in range(3)] for t in tiles]
    upwind = [[of_own(7, q, t) for q in range(NV)] for t in tiles]
    for face in range(4):
        now = table
        if face < 3:
            table = gather(face + 1)
        for group, points in enumerate(face_products(gathered, face, now, tiles)):
            lifted = dot(w_lift[face], points)
            for t in tiles:
                for inner in range(3):
                    q = 3 * group + inner
                    at = inner * NBP
                    mixed = lifted[at : at + NBP, lanes(t)] + of_own(3 + face, q, t)
                    upwind[t][q] = upwind[t][q] + lifted[72 + at : 72 + at + NBP, lanes(t)]
                    for d in range(3):
                        normal = small[3 * face + d : 3 * face + d + 1, lanes(t)]
                        volume[t][d][q] = volume[t][d][q] + normal * mixed
    return volume, upwind


def update(parts, far, small, aux, jac, w_far, w_table, gathered):
    volume, upwind = parts
    tiles = range(len(volume))
    count = len(volume) * LANES
    place = aux[4:5, :]
    both = dot(far, one_hot(iota((FAR, count), 0) == place))
    gathered[0, :, :count] = both[:PACK] + both[PACK:]
    masks = [jnp.where((aux[face : face + 1, :] < 0) & (place >= 0), 1.0, 0.0) for face in range(4)]
    code = masks[0] * small[ORIENT : ORIENT + 1, :]
    normals = [masks[0] * small[d : d + 1, :] for d in range(3)]
    for face in range(1, 4):
        code = code + masks[face] * small[ORIENT + face : ORIENT + face + 1, :]
        normals = [n + masks[face] * small[3 * face + d : 3 * face + d + 1, :] for d, n in enumerate(normals)]
    changes = [[None] * NV for t in tiles]
    volume = [[list(v) for v in tile] for tile in volume]
    upwind = [list(tile) for tile in upwind]
    for group, points in enumerate(face_products(gathered, 0, table_of(code, w_table), tiles)):
        lifted = dot(w_far, points)
        for t in tiles:
            for inner in range(3):
                q = 3 * group + inner
                mixed = None
                for face in range(4):
                    at = 72 * face + inner * NBP
                    term = masks[face][:, lanes(t)] * lifted[at : at + NBP, lanes(t)]
                    mixed = term if mixed is None else mixed + term
                upwind[t][q] = upwind[t][q] - mixed
                for d in range(3):
                    volume[t][d][q] = volume[t][d][q] + normals[d][:, lanes(t)] * mixed
    for t in tiles:
        change = jacobian_apply(jac, t, lambda d, q: volume[t][d][q])
        speed = small[SPEED : SPEED + 1, lanes(t)]
        changes[t] = [c + speed * u for c, u in zip(change, upwind[t])]
    return changes


def store_parts(ref, parts):
    volume, upwind = parts
    for t in range(len(volume)):
        for q in range(NV):
            for d in range(3):
                ref[d * NV + q, :, lanes(t)] = volume[t][d][q]
            ref[3 * NV + q, :, lanes(t)] = upwind[t][q]


def load_parts(ref):
    tiles = range(ref.shape[2] // LANES)
    volume = [[[ref[d * NV + q, :, lanes(t)] for q in range(NV)] for d in range(3)] for t in tiles]
    return volume, [[ref[3 * NV + q, :, lanes(t)] for q in range(NV)] for t in tiles]


def load_state(q, padded):
    padded[:, NB:NBP, :] = jnp.zeros((NV, NBP - NB, padded.shape[2]), f32)
    for p in range(NV):
        padded[p, :NB, :] = q[p]
    return load_field(padded)


def load_field(ref):
    return [[ref[p, :, lanes(t)] for p in range(NV)] for t in range(ref.shape[2] // LANES)]


def store_field(ref, field):
    for t, tile in enumerate(field):
        for p in range(NV):
            ref[p, :, lanes(t)] = tile[p]


def store_result(out, base, change, small):
    for t in range(len(base)):
        occupied = small[OCCUPIED : OCCUPIED + 1, lanes(t)] > 0.5
        for p in range(NV):
            out[p, :, lanes(t)] = jnp.where(occupied, base[t][p] + change[t][p], 0.0)[:NB]


def first_kernel(q, jac, deriv, stiff, evals, lift, packed, slow, w_pred, w_own, w_lift, w_table, w_far, padded, square):
    @pl.when(pl.program_id(0) == 0)
    def _():
        make_weights(deriv, stiff, evals, lift, w_pred, w_own, w_lift, w_table, w_far, square)

    first, later = predict(load_state(q, padded), jac, w_pred[...], [FIRST, SECOND])
    packed[...] = split_fields(first)
    store_field(slow, later)


def near_kernel(own, near, small, aux, w_own, w_lift, w_table, *refs):
    parts, gathered = refs[-2:]
    store_parts(parts, near_part(own[...], near, small, aux, w_own[...], w_lift, w_table[...], gathered))


def middle_step(start, parts, jac, small, slow, far, aux, w_pred, w_far, w_table, gathered):
    change = update(parts, far, small, aux, jac, w_far, w_table, gathered)
    base, midway, second = [], [], []
    fast = [small[CLUSTER : CLUSTER + 1, lanes(t)] < 0.5 for t in range(len(start))]
    for t in range(len(start)):
        base.append([a + b for a, b in zip(start[t], change[t])])
        midway.append([jnp.where(fast[t], a, b) for a, b in zip(base[t], start[t])])
    (later,) = predict(midway, jac, w_pred, [FIRST])
    for t in range(len(start)):
        second.append([jnp.where(fast[t], a, b) for a, b in zip(later[t], slow[t])])
    return base, split_fields(second)


def middle_kernel(devices, steps, q, jac, small, slow, parts, near, aux, asks, *refs):
    messages = refs[:5]
    w_pred, w_far, w_table, base, packed, *outs, padded, gathered, far = refs[5:]
    step = pl.program_id(0)

    @pl.when(step == 0)
    def _():
        far[...] = far_table(devices, 0, messages)

    now, second = middle_step(
        load_state(q, padded), load_parts(parts), jac, small, load_field(slow), far[...], aux,
        w_pred[...], w_far[...], w_table[...], gathered,
    )
    store_field(base, now)
    packed[:, pl.ds(pl.multiple_of(step * WIDE, WIDE), WIDE)] = second

    @pl.when(step == steps - 1)
    def _():
        answer_again(devices, asks, messages, near[...], packed[:, :KEEP], outs)


def last_kernel(
    devices, steps, base, jac, small, parts, aux, q_moved, jac_moved, small_moved, aux_moved, near, later, *refs
):
    messages = refs[:5]
    w_pred, w_own, w_lift, w_table, w_far, out, padded, gathered, far = refs[5:]
    step = pl.program_id(0)

    @pl.when(step == 0)
    def _():
        far[...] = far_table(devices, 0, messages)

    @pl.when(step < steps)
    def _():
        change = update(load_parts(parts), far[...], small, aux, jac, w_far[...], w_table[...], gathered)
        store_result(out, load_field(base), change, small)

    @pl.when(step == steps)
    def _():
        start = load_state(q_moved, padded)
        first, slow = predict(start, jac_moved, w_pred[...], [FIRST, SECOND])
        of_near = w_own[...], w_lift, w_table[...]
        own = near_part(split_fields(first), near, small_moved, aux_moved, *of_near, gathered)
        now, second = middle_step(
            start, own, jac_moved, small_moved, slow, far_table(devices, 1, messages), aux_moved,
            w_pred[...], w_far[...], w_table[...], gathered,
        )
        own = near_part(second, later, small_moved, aux_moved, *of_near, gathered)
        change = update(own, far[...], small_moved, aux_moved, jac_moved, w_far[...], w_table[...], gathered)
        store_result(out, now, change, small_moved)


def whole_spec(array):
    rank = array.ndim
    return pl.BlockSpec(array.shape, lambda i: (0,) * rank)


def lane_spec(*lead, last=None):
    rank = len(lead)
    if last is None:
        return pl.BlockSpec(lead + (WIDE,), lambda i: (0,) * rank + (i,))
    return pl.BlockSpec(lead + (WIDE,), lambda i: (0,) * rank + (jnp.minimum(i, last),))


Q_SPEC = lane_spec(NV, NB)
J_SPEC = lane_spec(NV, NV, 3)
S_SPEC = lane_spec(SMALL)
A_SPEC = lane_spec(8)
F_SPEC = lane_spec(NV, NBP)
X_SPEC = lane_spec(2 * PACK)
N_SPEC = pl.BlockSpec((2 * PACK, KEEP), lambda i: (0, 0))


def scratch_of(width):
    return pltpu.VMEM((NV, NBP, width), f32), pltpu.VMEM((4, PACK, width), f32)


def per_device(
    element_freedom_values,
    scaled_jacobian_matrices,
    outward_face_normals,
    largest_wave_speed,
    element_cluster_index,
    element_new_slot,
    neighbours,
    face_rotation_codes,
    deriv_mats,
    stiff_mats,
    face_eval,
    face_lift,
):
    count = element_freedom_values.shape[2]
    steps = count // WIDE
    devices = lax.axis_size("dom")
    q = element_freedom_values
    jac = jnp.transpose(scaled_jacobian_matrices, (1, 2, 0, 3))

    def shift(array, by):
        return lax.ppermute(array, "dom", [(i, (i + by) % devices) for i in range(devices)])

    def swap(array, groups):
        return lax.all_to_all(array, "dom", split_axis=0, concat_axis=0, axis_index_groups=groups, tiled=True)

    def on_ring(body):
        def kernel(*refs):
            body(devices, *refs)

        return kernel

    small, aux, asks, group, one = prepare(
        jnp.transpose(outward_face_normals, (1, 0, 2)),
        largest_wave_speed[None],
        element_cluster_index[None],
        element_new_slot[None],
        neighbours,
        face_rotation_codes,
        q,
        jac,
        devices,
    )
    asks = swap(asks, None)
    asks, group, one = lax.optimization_barrier((asks, group, one))
    stride = devices // GROUPS
    group = swap(group, [[r + stride * j for j in range(GROUPS)] for r in range(stride)])
    one = shift(one, 1)
    padded, gathered = scratch_of(WIDE)
    packed_shape = jax.ShapeDtypeStruct((2 * PACK, count), bf16)
    field_shape = jax.ShapeDtypeStruct((NV, NBP, count), f32)
    far = pltpu.VMEM((2 * PACK, FAR), bf16)
    weight_shapes = [
        jax.ShapeDtypeStruct((ROWS, PACK), bf16),
        jax.ShapeDtypeStruct((576, PACK), bf16),
        jax.ShapeDtypeStruct((4, 144, 144), bf16),
        jax.ShapeDtypeStruct((320, 32), bf16),
        jax.ShapeDtypeStruct((288, 144), bf16),
    ]
    evals = jnp.transpose(face_eval, (0, 2, 1)).reshape(12 * NQ, NB)
    matrices = [deriv_mats, stiff_mats, evals, face_lift]
    first, slow, w_pred, w_own, w_lift, w_table, w_far = pl.pallas_call(
        first_kernel,
        grid=(steps,),
        in_specs=[Q_SPEC, J_SPEC] + [whole_spec(m) for m in matrices],
        out_specs=[X_SPEC, F_SPEC] + [whole_spec(w) for w in weight_shapes],
        out_shape=[packed_shape, field_shape] + weight_shapes,
        scratch_shapes=[padded, pltpu.VMEM((LANES, LANES), f32)],
        compiler_params=PARAMS,
        name="first",
    )(q, jac, *matrices)

    moved_shapes = [
        jax.ShapeDtypeStruct((NV, NB, LANES), f32),
        jax.ShapeDtypeStruct((NV, NV, 3, LANES), f32),
        jax.ShapeDtypeStruct((SMALL, LANES), f32),
        jax.ShapeDtypeStruct((8, LANES), i32),
    ]
    out_shape = moved_shapes + message_shapes(MESSAGE1)
    *moved, m0, m1, m2, m3, m4 = pl.pallas_call(
        on_ring(unpack_kernel),
        grid=(1,),
        in_specs=[whole_spec(a) for a in (group, one, asks)] + [N_SPEC],
        out_specs=[whole_spec(o) for o in out_shape],
        out_shape=out_shape,
        compiler_params=PARAMS,
        name="unpack",
    )(group, one, asks, first)
    of_near = [w_own, w_lift, w_table]
    parts_shape = jax.ShapeDtypeStruct((4 * NV, NBP, count), f32)

    def near_steps(field, begin, number, parts):
        def spec(*lead):
            rank = len(lead)
            return pl.BlockSpec(lead + (WIDE,), lambda i: (0,) * rank + (i + begin,))

        return pl.pallas_call(
            near_kernel,
            grid=(number,),
            in_specs=[spec(2 * PACK), N_SPEC, spec(SMALL), spec(8)]
            + [whole_spec(w) for w in of_near]
            + [pl.BlockSpec(memory_space=pl.ANY)] * len(parts),
            out_specs=spec(4 * NV, NBP),
            out_shape=parts_shape,
            scratch_shapes=[gathered],
            input_output_aliases={7: 0} if parts else {},
            cost_estimate=pl.CostEstimate(flops=int(2e9) * number, bytes_accessed=4 << 20, transcendentals=0),
            compiler_params=PARAMS,
            name="near",
        )(field, field, small, aux, *of_near, *parts)

    def exchange_beside(answers, field):
        half = steps // 2
        plus, minus, own_plus, own_minus, opposite = answers
        got_plus, got_minus, opposite = shift(plus, 1), shift(minus, -1), shift(opposite, devices // 2)
        parts = near_steps(field, 0, half, [])
        got_plus, got_minus, opposite, parts = lax.optimization_barrier((got_plus, got_minus, opposite, parts))
        on_plus, on_minus = pl.pallas_call(
            relay_kernel,
            out_shape=[jax.ShapeDtypeStruct(plus.shape, f32)] * 2,
            compiler_params=pltpu.CompilerParams(vmem_limit_bytes=4 << 20),
            name="relay",
        )(got_plus, got_minus, own_plus, own_minus)
        on_plus, on_minus = shift(on_plus, 3), shift(on_minus, -3)
        parts = near_steps(field, half, steps - half, [parts])
        return (got_plus, got_minus, on_plus, on_minus, opposite), parts

    messages, parts = exchange_beside((m0, m1, m2, m3, m4), first)

    def middle(*refs):
        middle_kernel(devices, steps, *refs)

    P_SPEC = lane_spec(4 * NV, NBP)
    weights = [w_pred, w_far, w_table]
    out_shape = [field_shape, packed_shape] + message_shapes(2 * REQ)
    base, second, *answers = pl.pallas_call(
        middle,
        grid=(steps,),
        in_specs=[Q_SPEC, J_SPEC, S_SPEC, F_SPEC, P_SPEC, N_SPEC, A_SPEC, whole_spec(asks)]
        + [whole_spec(a) for a in (*messages, *weights)],
        out_specs=[F_SPEC] + [whole_spec(o) for o in out_shape[1:]],
        out_shape=out_shape,
        scratch_shapes=[padded, gathered, far],
        compiler_params=PARAMS,
        name="middle",
    )(q, jac, small, slow, parts, first, aux, asks, *messages, *weights)
    messages, parts = exchange_beside(answers, second)

    def last(*refs):
        last_kernel(devices, steps, *refs)

    end = steps - 1
    weights = [w_pred, w_own, w_lift, w_table, w_far]
    return pl.pallas_call(
        last,
        grid=(steps + 1,),
        in_specs=[
            lane_spec(NV, NBP, last=end),
            lane_spec(NV, NV, 3, last=end),
            lane_spec(SMALL, last=end),
            lane_spec(4 * NV, NBP, last=end),
            lane_spec(8, last=end),
        ]
        + [whole_spec(a) for a in moved]
        + [N_SPEC, N_SPEC]
        + [whole_spec(a) for a in (*messages, *weights)],
        out_specs=Q_SPEC,
        out_shape=jax.ShapeDtypeStruct((NV, NB, PARTITION_SLOTS), f32),
        scratch_shapes=[scratch_of(LANES)[0], gathered, far],
        compiler_params=PARAMS,
        name="last",
    )(base, jac, small, parts, aux, *moved, first, second, *messages, *weights)


def solution(mesh):
    placed = (
        P(None, None, "dom"),
        P(None, None, None, "dom"),
        P(None, None, "dom"),
        P("dom"),
        P("dom"),
        P("dom"),
        P(None, "dom"),
        P(None, "dom"),
        P(),
        P(),
        P(),
        P(),
    )
    return jax.shard_map(
        per_device, mesh=mesh, in_specs=placed, out_specs=P(None, None, "dom"), check_vma=False
    )
```

```python
import math

import jax
import jax.numpy as jnp
from jax import lax
from jax.experimental import pallas as pl
from jax.experimental.pallas import tpu as pltpu
from jax.sharding import PartitionSpec as P

NV = 9
NB = 20
NBP = 24
NQ = 16
NORDER = 4
GROUPS = 8
CSZ = 16
KEEP = 896
PARTITION_SLOTS = 1152
REQ = 32
PARTNERS = 9
ASKS = 16
LANES = 128
WIDE = 256
BOTH = 512
ROWS = 216
JAC_END = ROWS + 4 * NV * NV
PACK = 192
MSG = 256
FAR = 384
RECORD = 640
SMALL = 24
MESSAGE1 = REQ + 8

step_fast = 0.25
exact = lax.Precision.HIGHEST
f32 = jnp.float32
bf16 = jnp.bfloat16
i32 = jnp.int32

SPEED, CLUSTER, LINK, ORIENT, OCCUPIED = 12, 13, 14, 18, 22

PARAMS = pltpu.CompilerParams(vmem_limit_bytes=20 << 20)


def coefficients(lower, upper):
    return [
        (upper ** (degree + 1) - lower ** (degree + 1)) / math.factorial(degree + 1)
        for degree in range(NORDER)
    ]


FIRST = coefficients(0.0, step_fast)
SECOND = coefficients(step_fast, 2.0 * step_fast)


def partner_offsets(devices):
    return [1, 2, 3, 4, -1, -2, -3, -4, devices // 2]


def packed_row(quantity, basis):
    group, member = quantity // 3, quantity % 3
    inside = 16 * member + basis if basis < 16 else 48 + 4 * member + (basis - 16)
    return 64 * group + inside


def pack_three(members):
    a, b, c = members
    tail = a[16:24] + pltpu.roll(b[16:24], 4, 0)
    return jnp.concatenate([a[:16], b[:16], c[:16], tail, c[16:24]], axis=0)


def split(values):
    high = values.astype(bf16)
    low = (values - high.astype(f32)).astype(bf16)
    return high, low


def stacked(high, low):
    return jnp.concatenate([high, low, high], axis=0)


def dot(a, b):
    return jnp.dot(a, b, preferred_element_type=f32)


def dot_last(a, b):
    return lax.dot_general(a, b, (((1,), (1,)), ((), ())), preferred_element_type=f32)


def iota(shape, axis):
    return lax.broadcasted_iota(i32, shape, axis)


def one_hot(condition):
    return jnp.where(condition, 1.0, 0.0).astype(bf16)


def make_weights(deriv, stiff, evals, lift, w_pred, w_own, w_lift, w_table, w_far, square):
    def turned(matrix, rows, columns):
        square[...] = jnp.zeros((LANES, LANES), f32)
        square[:rows, :columns] = matrix
        return square[...].T[:NBP]

    column = iota((LANES, PACK), 1) & 63
    member = jnp.where(column < 48, column >> 4, (column - 48) >> 2)
    basis = jnp.where(column < 48, column & 15, 16 + (column & 3))
    spread = one_hot(iota((LANES, PACK), 0) == jnp.where(member < 3, basis, -1))
    member = member[:NBP]
    part = iota((NBP, PACK), 1)

    def three(matrix):
        high, low = split(turned(matrix, NB, NB))
        row = jnp.where(part < 128, dot(high, spread), dot(low, spread))
        return [jnp.where(member == inner, row, 0.0) for inner in range(3)]

    blocks = []
    for axis in range(3):
        blocks += three(-deriv[axis])
    w_pred[...] = jnp.concatenate(blocks, axis=0).astype(bf16)

    own = [
        lax.dot_general(
            evals[48 * face : 48 * face + NQ, :],
            lift[face],
            (((0,), (0,)), ((), ())),
            precision=exact,
            preferred_element_type=f32,
        )
        for face in range(4)
    ]
    blocks = []
    for matrix in [stiff[axis] for axis in range(3)] + own + [own[0] + own[1] + own[2] + own[3]]:
        blocks += three(matrix if len(blocks) < 9 else -0.5 * matrix)
    w_own[...] = jnp.concatenate(blocks, axis=0).astype(bf16)

    column = iota((LANES, 144), 1)
    spread = one_hot(iota((LANES, 144), 0) == (column & 15))
    column = column[:NBP]
    block = column >> 4
    member = block - jnp.where(column >= 96, 6, jnp.where(column >= 48, 3, 0))
    every = []
    for face in range(4):
        high, low = split(turned(lift[face], NQ, NB))
        row = jnp.where(column < 96, dot(high, spread), dot(low, spread))
        rows = [jnp.where(member == inner, -0.5 * row, 0.0) for inner in range(3)]
        w_lift[face] = jnp.concatenate(rows + [-r for r in rows], axis=0).astype(bf16)
        every += rows
    w_far[...] = jnp.concatenate(every, axis=0).astype(bf16)

    basis_of = one_hot((iota((320, NB), 0) >> 4) == iota((320, NB), 1))
    keep = (iota((320, PACK), 0) & 15) == (iota((320, PACK), 1) & 15)
    code_of = one_hot((iota((PACK, 16), 0) >> 4) == iota((PACK, 16), 1))
    halves = []
    for part_of in split(evals[...]):
        halves.append(dot(jnp.where(keep, dot_last(basis_of, part_of), 0.0).astype(bf16), code_of))
    w_table[:, :16] = halves[0].astype(bf16)
    w_table[:, 16:] = halves[1].astype(bf16)


def find_links(devices, tiles, small, aux, from_top):
    me = lax.axis_index("dom").astype(f32)
    row = iota((ASKS, LANES), 0).astype(f32)
    up_to = one_hot(iota((LANES, LANES), 0) <= iota((LANES, LANES), 1))
    request = (iota((LANES, LANES), 0) & (REQ - 1)).astype(f32)
    carry = jnp.zeros((ASKS, 1), f32)
    wanted = jnp.zeros((2 * ASKS, LANES), f32)
    for tile in range(tiles):
        at = slice(tile * LANES, (tile + 1) * LANES)
        occupied = small[OCCUPIED : OCCUPIED + 1, at] > 0.5
        target = jnp.full((1, LANES), -1.0, f32)
        slots = jnp.zeros((1, LANES), f32)
        for face in range(4):
            link = small[LINK + face : LINK + face + 1, at]
            owner = jnp.floor((link + 0.5) * (1.0 / PARTITION_SLOTS))
            slot = link - owner * PARTITION_SLOTS
            near = owner == me
            aux[face : face + 1, at] = jnp.where(near, slot, -1.0).astype(i32)
            away = occupied & jnp.logical_not(near)
            target = jnp.where(away, owner, target)
            slots = jnp.where(away, slot, slots)
        far = target - me
        far = jnp.where(far < 0, far + devices, far)
        partner = jnp.where(far <= 4, far - 1.0, jnp.where(far >= devices - 4, devices + 3.0 - far, 8.0))
        partner = jnp.where(target >= 0, partner, -1.0)
        named = jnp.where(row == partner, 1.0, 0.0)
        prefix = dot(named.astype(bf16), up_to) + carry
        carry = carry + jnp.sum(named, axis=1, keepdims=True)
        rank = jnp.sum(named * prefix, axis=0, keepdims=True) - 1.0
        if from_top:
            rank = REQ - 1.0 - rank
        aux[4:5, at] = jnp.where(target >= 0, partner * REQ + rank, -1.0).astype(i32)
        aux[5:8, at] = jnp.zeros((3, LANES), i32)
        ask = slots + 1.0
        high = jnp.floor(ask * (1.0 / 32)) * 32.0
        both = jnp.concatenate([named * high, named * (ask - high)], axis=0).astype(bf16)
        wanted = wanted + dot_last(both, one_hot(request == rank))
    return wanted[:ASKS] + wanted[ASKS:]


def prepare_kernel(devices, tiles, normals, speed, cluster, slot, links, orient, q, jac, small, aux, asks, group, one, record):
    me = lax.axis_index("dom")
    for face in range(4):
        small[3 * face : 3 * face + 3, :] = jnp.concatenate([normals[d, face : face + 1, :] for d in range(3)], axis=0)
    small[SPEED : SPEED + 1, :] = speed[...]
    small[CLUSTER : CLUSTER + 1, :] = cluster[...].astype(f32)
    small[LINK : LINK + 4, :] = links[...].astype(f32)
    small[ORIENT : ORIENT + 4, :] = orient[...].astype(f32)
    where = slot[...]
    stays = (where >= me * PARTITION_SLOTS) & (where < (me + 1) * PARTITION_SLOTS)
    small[OCCUPIED : OCCUPIED + 1, :] = jnp.where(stays, 1.0, 0.0)
    small[OCCUPIED + 1 : SMALL, :] = jnp.zeros((1, tiles * LANES), f32)
    wanted = find_links(devices, tiles, small, aux, False)
    asks[...] = jnp.zeros((devices, 1, LANES), f32)
    for k, offset in enumerate(partner_offsets(devices)):
        asks[lax.rem(me + offset + devices, devices)] = wanted[k : k + 1]

    record[...] = jnp.zeros((RECORD, LANES), f32)
    for p in range(NV):
        record[p * NBP : p * NBP + NB] = q[p]
        for inner in range(NV):
            at = ROWS + 4 * (p * NV + inner)
            record[at : at + 3] = jac[p, inner]
    fields = small[:, KEEP:]
    row = iota(fields.shape, 0)
    record[JAC_END : JAC_END + SMALL] = jnp.where(row == OCCUPIED, 1.0 - fields, fields)
    whole = record[...]
    turned = jnp.concatenate([whole[c : c + LANES].T for c in range(0, RECORD, LANES)], axis=1)
    one[...] = turned[:CSZ]
    position = me // (devices // GROUPS)
    for g in range(GROUPS):
        group[lax.rem(position + g, GROUPS)] = turned[g * CSZ : (g + 1) * CSZ]


def prepare(normals, speed, cluster, slot, links, orient, q, jac, devices):
    count = q.shape[2]

    def body(*refs):
        prepare_kernel(devices, count // LANES, *refs)

    last = KEEP // LANES
    return pl.pallas_call(
        body,
        grid=(1,),
        in_specs=[
            whole_spec(normals),
            whole_spec(speed),
            whole_spec(cluster),
            whole_spec(slot),
            whole_spec(links),
            whole_spec(orient),
            pl.BlockSpec((NV, NB, LANES), lambda i: (0, 0, last)),
            pl.BlockSpec((NV, NV, 3, LANES), lambda i: (0, 0, 0, last)),
        ],
        out_specs=[
            pl.BlockSpec((SMALL, count), lambda i: (0, 0)),
            pl.BlockSpec((8, count), lambda i: (0, 0)),
            pl.BlockSpec((devices, 1, LANES), lambda i: (0, 0, 0)),
            pl.BlockSpec((GROUPS, CSZ, RECORD), lambda i: (0, 0, 0)),
            pl.BlockSpec((CSZ, RECORD), lambda i: (0, 0)),
        ],
        out_shape=[
            jax.ShapeDtypeStruct((SMALL, count), f32),
            jax.ShapeDtypeStruct((8, count), i32),
            jax.ShapeDtypeStruct((devices, 1, LANES), f32),
            jax.ShapeDtypeStruct((GROUPS, CSZ, RECORD), f32),
            jax.ShapeDtypeStruct((CSZ, RECORD), f32),
        ],
        scratch_shapes=[pltpu.VMEM((RECORD, LANES), f32)],
        compiler_params=PARAMS,
        name="prepare",
    )(normals, speed, cluster, slot, links, orient, q, jac)


def unpack(devices, group, one, q, jac, small, aux):
    position = lax.axis_index("dom") // (devices // GROUPS)
    rows = [one[...]]
    for g in range(1, GROUPS):
        rows.append(group[lax.rem(position - g + GROUPS, GROUPS)])
    whole = jnp.concatenate(rows, axis=0)
    turned = jnp.concatenate([whole[:, c : c + LANES].T for c in range(0, RECORD, LANES)], axis=0)
    for p in range(NV):
        q[p] = turned[p * NBP : p * NBP + NB]
        for inner in range(NV):
            at = ROWS + 4 * (p * NV + inner)
            jac[p, inner] = turned[at : at + 3]
    small[...] = turned[JAC_END : JAC_END + SMALL]
    return find_links(devices, 1, small, aux, True)


OUT_BLOCKS = {1: (0, 0), 4: (0, 1), -2: (0, 2), -1: (1, 0), -4: (1, 1), 2: (1, 2), 3: (2, 0), -3: (3, 0)}
IN_BLOCKS = {-1: (0, 0), 1: (1, 0), -3: (2, 0), -4: (2, 1), -2: (2, 2), 3: (3, 0), 4: (3, 1), 2: (3, 2)}


def put(outs, rows, k, devices):
    if k == PARTNERS - 1:
        return outs[4], 0
    array, block = OUT_BLOCKS[-partner_offsets(devices)[k]]
    return outs[array], block * rows


def take(messages, k, devices):
    if k == PARTNERS - 1:
        return messages[4], 0
    array, block = IN_BLOCKS[partner_offsets(devices)[k]]
    rows = messages[4].shape[0]
    return messages[array], block * rows


def picked(requests, fields):
    lane = iota((1, LANES), 1)
    tiles = []
    for at in range(0, 12, 4):
        four = [requests[min(at + n, PARTNERS - 1)] for n in range(4)]
        tiles.append(
            jnp.where(lane < 32, four[0], jnp.where(lane < 64, four[1], jnp.where(lane < 96, four[2], four[3])))
        )
    slots = (iota((KEEP, FAR), 0) + 1).astype(f32)
    return dot(fields, one_hot(slots == jnp.concatenate(tiles, axis=1)))


def message_rows(both):
    value = both[:PACK] + both[PACK:]
    return jnp.concatenate([value, jnp.zeros((MSG - PACK, FAR), f32)], axis=0).T


def back(k):
    return k if k == PARTNERS - 1 else (k + 4) % 8


def requests_here(devices, asks):
    me = lax.axis_index("dom")
    peers = [lax.rem(me - o + devices, devices) for o in partner_offsets(devices)]
    return [asks[p] for p in peers]


def unpack_kernel(devices, group, one, asks, field, q, jac, small, aux, *outs):
    moved = unpack(devices, group, one, q, jac, small, aux)
    rows = message_rows(picked(requests_here(devices, asks), field[...]))
    for k in range(PARTNERS):
        out, at = put(outs, MESSAGE1, k, devices)
        out[at : at + REQ] = rows[k * REQ : (k + 1) * REQ]
        out[at + REQ : at + MESSAGE1, :LANES] = jnp.broadcast_to(moved[back(k) : back(k) + 1, :], (8, LANES))
        out[at + REQ : at + MESSAGE1, LANES:] = jnp.zeros((8, MSG - LANES), f32)


def answer_again(devices, asks, got, field, later, outs):
    moved = []
    for k in range(PARTNERS):
        message, at = take(got, back(k), devices)
        moved.append(message[at + REQ : at + REQ + 1, :LANES])
    every = [a + b for a, b in zip(requests_here(devices, asks), moved)]
    rows = message_rows(picked(every, later))
    rows_first = message_rows(picked(moved, field))
    for k in range(PARTNERS):
        out, at = put(outs, 2 * REQ, k, devices)
        out[at : at + REQ] = rows[k * REQ : (k + 1) * REQ]
        out[at + REQ : at + 2 * REQ] = rows_first[k * REQ : (k + 1) * REQ]


def relay_kernel(got_plus, got_minus, own_plus, own_minus, on_plus, on_minus):
    rows = own_plus.shape[0]
    block = [slice(b * rows, (b + 1) * rows) for b in range(3)]
    on_plus[block[0]] = own_plus[...]
    on_plus[block[1]] = got_plus[block[1]]
    on_plus[block[2]] = got_minus[block[2]]
    on_minus[block[0]] = own_minus[...]
    on_minus[block[1]] = got_minus[block[1]]
    on_minus[block[2]] = got_plus[block[2]]


def message_shapes(rows):
    return [jax.ShapeDtypeStruct((rows * blocks, MSG), f32) for blocks in (3, 3, 1, 1, 1)]


def far_table(devices, part, messages):
    rows = []
    for k in range(PARTNERS):
        message, at = take(messages, k, devices)
        rows.append(message[at + part * REQ : at + (part + 1) * REQ, :])
    rows.append(jnp.zeros((FAR - PARTNERS * REQ, MSG), f32))
    turned = jnp.concatenate(rows, axis=0).T[:PACK]
    return jnp.concatenate(split(turned), axis=0)


def take_turns(*chains):
    results = [None] * len(chains)
    going = list(range(len(chains)))
    while going:
        for n in list(going):
            try:
                next(chains[n])
            except StopIteration as stop:
                results[n] = stop.value
                going.remove(n)
    return results


def alone(chain):
    return take_turns(chain)[0]


class Window:
    def __init__(self, ref, begin, width):
        self.ref, self.begin = ref, begin
        self.shape = tuple(ref.shape[:-1]) + (width,)

    def _at(self, index):
        rank = len(self.shape)
        if index is Ellipsis:
            index = ()
        index = index if isinstance(index, tuple) else (index,)
        index = index + (slice(None),) * (rank - len(index))
        low, high, _ = index[-1].indices(self.shape[-1])
        return index[:-1] + (slice(self.begin + low, self.begin + high),)

    def __getitem__(self, index):
        return self.ref[self._at(index)]

    def __setitem__(self, index, value):
        self.ref[self._at(index)] = value


def lanes(tile):
    return slice(tile * LANES, (tile + 1) * LANES)


def jacobian_apply(jac, tile, parts):
    result = [None] * NV
    for group in range(3):
        for d in range(3):
            for inner in range(3):
                q = 3 * group + inner
                value = parts(d, q)
                for p in range(NV):
                    term = jac[p, q, d : d + 1, lanes(tile)] * value
                    result[p] = term if result[p] is None else result[p] + term
    return result


def packed_split(fields, group):
    packed = [pack_three(tile[3 * group : 3 * group + 3]) for tile in fields]
    return split(jnp.concatenate(packed, axis=1))


def split_fields(fields):
    pairs = [packed_split(fields, group) for group in range(3)]
    return jnp.concatenate([a for a, _ in pairs] + [b for _, b in pairs], axis=0)


def predict_chain(start, jac, w_pred, scales):
    tiles = range(len(start))
    sums = [[[s[0] * x for x in tile] for tile in start] for s in scales]
    now = start
    for degree in range(1, NORDER):
        turned = [dot(w_pred, stacked(*packed_split(now, group))) for group in range(3)]
        yield
        now = [
            jacobian_apply(
                jac, t, lambda d, q: turned[q // 3][d * 72 + (q % 3) * NBP : d * 72 + (q % 3) * NBP + NBP, lanes(t)]
            )
            for t in tiles
        ]
        sums = [
            [[a + s[degree] * x for a, x in zip(total[t], now[t])] for t in tiles] for total, s in zip(sums, scales)
        ]
    return sums


def predict(*args):
    return alone(predict_chain(*args))


def face_products(gathered, at_face, table, tiles):
    outers = []
    for t in tiles:
        outer = [None] * NV
        for b in range(NB):
            values = table[b * NQ : (b + 1) * NQ, lanes(t)]
            for p in range(NV):
                at = packed_row(p, b)
                term = gathered[at_face, at : at + 1, lanes(t)] * values
                outer[p] = term if outer[p] is None else outer[p] + term
        outers.append(outer)
    return [
        stacked(*split(jnp.concatenate([jnp.concatenate(o[3 * g : 3 * g + 3], axis=0) for o in outers], axis=1)))
        for g in range(3)
    ]


def table_of(code, w_table):
    hot = one_hot(iota((16, code.shape[1]), 0).astype(f32) == code)
    return dot(w_table, jnp.concatenate([hot, hot], axis=0))


def near_chain(own, near, small, aux, w_own, w_lift, w_table, gathered):
    count = own.shape[1]
    tiles = range(count // LANES)
    slots = iota((KEEP, count), 0).astype(jnp.int16)

    def gather(face):
        index = jnp.broadcast_to(aux[face : face + 1, :], (16, count)).astype(jnp.int16)
        index = jnp.concatenate([index] * (KEEP // 16), axis=0)
        both = dot(near[...], jnp.where(slots == index, jnp.ones((), bf16), jnp.zeros((), bf16)))
        gathered[face, :, :count] = both[:PACK] + both[PACK:]
        return table_of(small[ORIENT + face : ORIENT + face + 1, :], w_table)

    table = gather(0)
    mine = []
    for group in range(3):
        rows = slice(64 * group, 64 * group + 64)
        lower = slice(PACK + 64 * group, PACK + 64 * group + 64)
        mine.append(dot(w_own, stacked(own[rows], own[lower])))

    def of_own(block, q, t):
        at = block * 72 + (q % 3) * NBP
        return mine[q // 3][at : at + NBP, lanes(t)]

    yield
    volume = [[[of_own(d, q, t) for q in range(NV)] for d in range(3)] for t in tiles]
    upwind = [[of_own(7, q, t) for q in range(NV)] for t in tiles]
    for face in range(4):
        now = table
        if face < 3:
            table = gather(face + 1)
            yield
        for group, points in enumerate(face_products(gathered, face, now, tiles)):
            lifted = dot(w_lift[face], points)
            for t in tiles:
                for inner in range(3):
                    q = 3 * group + inner
                    at = inner * NBP
                    mixed = lifted[at : at + NBP, lanes(t)] + of_own(3 + face, q, t)
                    upwind[t][q] = upwind[t][q] + lifted[72 + at : 72 + at + NBP, lanes(t)]
                    for d in range(3):
                        normal = small[3 * face + d : 3 * face + d + 1, lanes(t)]
                        volume[t][d][q] = volume[t][d][q] + normal * mixed
    return volume, upwind


def near_part(*args):
    return alone(near_chain(*args))


def update(parts, far, small, aux, jac, w_far, w_table, gathered):
    volume, upwind = parts
    tiles = range(len(volume))
    count = len(volume) * LANES
    place = aux[4:5, :]
    both = dot(far, one_hot(iota((FAR, count), 0) == place))
    gathered[0, :, :count] = both[:PACK] + both[PACK:]
    masks = [jnp.where((aux[face : face + 1, :] < 0) & (place >= 0), 1.0, 0.0) for face in range(4)]
    code = masks[0] * small[ORIENT : ORIENT + 1, :]
    normals = [masks[0] * small[d : d + 1, :] for d in range(3)]
    for face in range(1, 4):
        code = code + masks[face] * small[ORIENT + face : ORIENT + face + 1, :]
        normals = [n + masks[face] * small[3 * face + d : 3 * face + d + 1, :] for d, n in enumerate(normals)]
    changes = [[None] * NV for t in tiles]
    volume = [[list(v) for v in tile] for tile in volume]
    upwind = [list(tile) for tile in upwind]
    for group, points in enumerate(face_products(gathered, 0, table_of(code, w_table), tiles)):
        lifted = dot(w_far, points)
        for t in tiles:
            for inner in range(3):
                q = 3 * group + inner
                mixed = None
                for face in range(4):
                    at = 72 * face + inner * NBP
                    term = masks[face][:, lanes(t)] * lifted[at : at + NBP, lanes(t)]
                    mixed = term if mixed is None else mixed + term
                upwind[t][q] = upwind[t][q] - mixed
                for d in range(3):
                    volume[t][d][q] = volume[t][d][q] + normals[d][:, lanes(t)] * mixed
    for t in tiles:
        change = jacobian_apply(jac, t, lambda d, q: volume[t][d][q])
        speed = small[SPEED : SPEED + 1, lanes(t)]
        changes[t] = [c + speed * u for c, u in zip(change, upwind[t])]
    return changes


def store_parts(ref, parts):
    volume, upwind = parts
    for t in range(len(volume)):
        for q in range(NV):
            for d in range(3):
                ref[d * NV + q, :, lanes(t)] = volume[t][d][q]
            ref[3 * NV + q, :, lanes(t)] = upwind[t][q]


def load_parts(ref):
    tiles = range(ref.shape[2] // LANES)
    volume = [[[ref[d * NV + q, :, lanes(t)] for q in range(NV)] for d in range(3)] for t in tiles]
    return volume, [[ref[3 * NV + q, :, lanes(t)] for q in range(NV)] for t in tiles]


def load_state(q, padded):
    padded[:, NB:NBP, :] = jnp.zeros((NV, NBP - NB, padded.shape[2]), f32)
    for p in range(NV):
        padded[p, :NB, :] = q[p]
    return load_field(padded)


def load_field(ref):
    return [[ref[p, :, lanes(t)] for p in range(NV)] for t in range(ref.shape[2] // LANES)]


def store_field(ref, field):
    for t, tile in enumerate(field):
        for p in range(NV):
            ref[p, :, lanes(t)] = tile[p]


def store_result(out, base, change, small):
    for t in range(len(base)):
        occupied = small[OCCUPIED : OCCUPIED + 1, lanes(t)] > 0.5
        for p in range(NV):
            out[p, :, lanes(t)] = jnp.where(occupied, base[t][p] + change[t][p], 0.0)[:NB]


def first_half_kernel(q, jac, deriv, stiff, evals, lift, packed, slow, w_pred, w_own, w_lift, w_table, w_far, padded, square):
    make_weights(deriv, stiff, evals, lift, w_pred, w_own, w_lift, w_table, w_far, square)
    first_fields(q, jac, w_pred, packed, slow, padded)


def second_half_kernel(q, jac, w_pred, _, __, packed, slow, padded):
    first_fields(q, jac, w_pred, packed, slow, padded)


def first_fields(q, jac, w_pred, packed, slow, padded):
    weights = w_pred[...]
    windows = [[Window(r, begin, WIDE) for r in (q, jac, packed, slow, padded)] for begin in range(0, BOTH, WIDE)]
    chains = [predict_chain(load_state(w[0], w[4]), w[1], weights, [FIRST, SECOND]) for w in windows]
    for (_, _, packed, slow, _), (first, later) in zip(windows, take_turns(*chains)):
        packed[...] = split_fields(first)
        store_field(slow, later)


def near_kernel(own, near, small, aux, w_own, w_lift, w_table, *refs):
    parts, gathered = refs[-2:]
    weights = w_own[...], w_lift, w_table[...]
    chains = []
    for begin in range(0, BOTH, WIDE):
        window = [Window(r, begin, WIDE) for r in (own, small, aux, gathered)]
        chains.append(near_chain(window[0][...], near, window[1], window[2], *weights, window[3]))
    for begin, values in zip(range(0, BOTH, WIDE), take_turns(*chains)):
        store_parts(Window(parts, begin, WIDE), values)


def middle_step(start, parts, jac, small, slow, far, aux, w_pred, w_far, w_table, gathered):
    change = update(parts, far, small, aux, jac, w_far, w_table, gathered)
    base, midway, second = [], [], []
    fast = [small[CLUSTER : CLUSTER + 1, lanes(t)] < 0.5 for t in range(len(start))]
    for t in range(len(start)):
        base.append([a + b for a, b in zip(start[t], change[t])])
        midway.append([jnp.where(fast[t], a, b) for a, b in zip(base[t], start[t])])
    (later,) = predict(midway, jac, w_pred, [FIRST])
    for t in range(len(start)):
        second.append([jnp.where(fast[t], a, b) for a, b in zip(later[t], slow[t])])
    return base, split_fields(second)


def middle_kernel(devices, steps, q, jac, small, slow, parts, near, aux, asks, *refs):
    messages = refs[:5]
    w_pred, w_far, w_table, base, packed, *outs, padded, gathered, far = refs[5:]
    step = pl.program_id(0)

    @pl.when(step == 0)
    def _():
        far[...] = far_table(devices, 0, messages)

    now, second = middle_step(
        load_state(q, padded), load_parts(parts), jac, small, load_field(slow), far[...], aux,
        w_pred[...], w_far[...], w_table[...], gathered,
    )
    store_field(base, now)
    packed[:, pl.ds(pl.multiple_of(step * WIDE, WIDE), WIDE)] = second

    @pl.when(step == steps - 1)
    def _():
        answer_again(devices, asks, messages, near[...], packed[:, :KEEP], outs)


def last_kernel(
    devices, steps, base, jac, small, parts, aux, q_moved, jac_moved, small_moved, aux_moved, near, later, *refs
):
    messages = refs[:5]
    w_pred, w_own, w_lift, w_table, w_far, out, padded, gathered, far = refs[5:]
    step = pl.program_id(0)

    @pl.when(step == 0)
    def _():
        far[...] = far_table(devices, 0, messages)

    @pl.when(step < steps)
    def _():
        change = update(load_parts(parts), far[...], small, aux, jac, w_far[...], w_table[...], gathered)
        store_result(out, load_field(base), change, small)

    @pl.when(step == steps)
    def _():
        start = load_state(q_moved, padded)
        first, slow = predict(start, jac_moved, w_pred[...], [FIRST, SECOND])
        of_near = w_own[...], w_lift, w_table[...]
        own = near_part(split_fields(first), near, small_moved, aux_moved, *of_near, gathered)
        now, second = middle_step(
            start, own, jac_moved, small_moved, slow, far_table(devices, 1, messages), aux_moved,
            w_pred[...], w_far[...], w_table[...], gathered,
        )
        own = near_part(second, later, small_moved, aux_moved, *of_near, gathered)
        change = update(own, far[...], small_moved, aux_moved, jac_moved, w_far[...], w_table[...], gathered)
        store_result(out, now, change, small_moved)


def whole_spec(array):
    rank = array.ndim
    return pl.BlockSpec(array.shape, lambda i: (0,) * rank)


def lane_spec(*lead, last=None):
    rank = len(lead)
    if last is None:
        return pl.BlockSpec(lead + (WIDE,), lambda i: (0,) * rank + (i,))
    return pl.BlockSpec(lead + (WIDE,), lambda i: (0,) * rank + (jnp.minimum(i, last),))


Q_SPEC = lane_spec(NV, NB)
J_SPEC = lane_spec(NV, NV, 3)
S_SPEC = lane_spec(SMALL)
A_SPEC = lane_spec(8)
F_SPEC = lane_spec(NV, NBP)
X_SPEC = lane_spec(2 * PACK)
N_SPEC = pl.BlockSpec((2 * PACK, KEEP), lambda i: (0, 0))


def scratch_of(width):
    return pltpu.VMEM((NV, NBP, width), f32), pltpu.VMEM((4, PACK, width), f32)


def per_device(
    element_freedom_values,
    scaled_jacobian_matrices,
    outward_face_normals,
    largest_wave_speed,
    element_cluster_index,
    element_new_slot,
    neighbours,
    face_rotation_codes,
    deriv_mats,
    stiff_mats,
    face_eval,
    face_lift,
):
    count = element_freedom_values.shape[2]
    steps = count // WIDE
    devices = lax.axis_size("dom")
    q = element_freedom_values
    jac = jnp.transpose(scaled_jacobian_matrices, (1, 2, 0, 3))

    def shift(array, by):
        return lax.ppermute(array, "dom", [(i, (i + by) % devices) for i in range(devices)])

    def swap(array, groups):
        return lax.all_to_all(array, "dom", split_axis=0, concat_axis=0, axis_index_groups=groups, tiled=True)

    def on_ring(body):
        def kernel(*refs):
            body(devices, *refs)

        return kernel

    small, aux, asks, group, one = prepare(
        jnp.transpose(outward_face_normals, (1, 0, 2)),
        largest_wave_speed[None],
        element_cluster_index[None],
        element_new_slot[None],
        neighbours,
        face_rotation_codes,
        q,
        jac,
        devices,
    )
    asks = swap(asks, None)
    padded, gathered = scratch_of(WIDE)
    packed_shape = jax.ShapeDtypeStruct((2 * PACK, count), bf16)
    field_shape = jax.ShapeDtypeStruct((NV, NBP, count), f32)
    far = pltpu.VMEM((2 * PACK, FAR), bf16)
    weight_shapes = [
        jax.ShapeDtypeStruct((ROWS, PACK), bf16),
        jax.ShapeDtypeStruct((576, PACK), bf16),
        jax.ShapeDtypeStruct((4, 144, 144), bf16),
        jax.ShapeDtypeStruct((320, 32), bf16),
        jax.ShapeDtypeStruct((288, 144), bf16),
    ]
    evals = jnp.transpose(face_eval, (0, 2, 1)).reshape(12 * NQ, NB)
    matrices = [deriv_mats, stiff_mats, evals, face_lift]
    halves = count // BOTH

    def part_spec(begin, *lead):
        rank = len(lead)
        return pl.BlockSpec(lead + (BOTH,), lambda i: (0,) * rank + (i + begin,))

    def first_specs(begin):
        return [part_spec(begin, NV, NB), part_spec(begin, NV, NV, 3)], [
            part_spec(begin, 2 * PACK),
            part_spec(begin, NV, NBP),
        ]

    ins, outs = first_specs(0)
    twice = scratch_of(BOTH)
    first, slow, w_pred, w_own, w_lift, w_table, w_far = pl.pallas_call(
        first_half_kernel,
        grid=(1,),
        in_specs=ins + [whole_spec(m) for m in matrices],
        out_specs=outs + [whole_spec(w) for w in weight_shapes],
        out_shape=[packed_shape, field_shape] + weight_shapes,
        scratch_shapes=[twice[0], pltpu.VMEM((LANES, LANES), f32)],
        cost_estimate=pl.CostEstimate(flops=int(4e9), bytes_accessed=4 << 20, transcendentals=0),
        compiler_params=PARAMS,
        name="first",
    )(q, jac, *matrices)
    asks, group, one, first, slow = lax.optimization_barrier((asks, group, one, first, slow))
    stride = devices // GROUPS
    group = swap(group, [[r + stride * j for j in range(GROUPS)] for r in range(stride)])
    one = shift(one, 1)
    ins, outs = first_specs(1)
    first, slow = pl.pallas_call(
        second_half_kernel,
        grid=(halves - 1,),
        in_specs=ins + [whole_spec(w_pred)] + [pl.BlockSpec(memory_space=pl.ANY)] * 2,
        out_specs=outs,
        out_shape=[packed_shape, field_shape],
        scratch_shapes=[twice[0]],
        input_output_aliases={3: 0, 4: 1},
        cost_estimate=pl.CostEstimate(flops=int(4e9), bytes_accessed=4 << 20, transcendentals=0),
        compiler_params=PARAMS,
        name="first",
    )(q, jac, w_pred, first, slow)

    moved_shapes = [
        jax.ShapeDtypeStruct((NV, NB, LANES), f32),
        jax.ShapeDtypeStruct((NV, NV, 3, LANES), f32),
        jax.ShapeDtypeStruct((SMALL, LANES), f32),
        jax.ShapeDtypeStruct((8, LANES), i32),
    ]
    out_shape = moved_shapes + message_shapes(MESSAGE1)
    *moved, m0, m1, m2, m3, m4 = pl.pallas_call(
        on_ring(unpack_kernel),
        grid=(1,),
        in_specs=[whole_spec(a) for a in (group, one, asks)] + [N_SPEC],
        out_specs=[whole_spec(o) for o in out_shape],
        out_shape=out_shape,
        compiler_params=PARAMS,
        name="unpack",
    )(group, one, asks, first)
    of_near = [w_own, w_lift, w_table]
    parts_shape = jax.ShapeDtypeStruct((4 * NV, NBP, count), f32)

    def near_steps(field, begin, number, parts):
        def spec(*lead):
            return part_spec(begin, *lead)

        return pl.pallas_call(
            near_kernel,
            grid=(number,),
            in_specs=[spec(2 * PACK), N_SPEC, spec(SMALL), spec(8)]
            + [whole_spec(w) for w in of_near]
            + [pl.BlockSpec(memory_space=pl.ANY)] * len(parts),
            out_specs=spec(4 * NV, NBP),
            out_shape=parts_shape,
            scratch_shapes=[twice[1]],
            input_output_aliases={7: 0} if parts else {},
            cost_estimate=pl.CostEstimate(flops=int(4e9) * number, bytes_accessed=4 << 20, transcendentals=0),
            compiler_params=PARAMS,
            name="near",
        )(field, field, small, aux, *of_near, *parts)

    def exchange_beside(answers, field):
        half = halves // 2
        plus, minus, own_plus, own_minus, opposite = answers
        got_plus, got_minus, opposite = shift(plus, 1), shift(minus, -1), shift(opposite, devices // 2)
        parts = near_steps(field, 0, half, [])
        got_plus, got_minus, opposite, parts = lax.optimization_barrier((got_plus, got_minus, opposite, parts))
        on_plus, on_minus = pl.pallas_call(
            relay_kernel,
            out_shape=[jax.ShapeDtypeStruct(plus.shape, f32)] * 2,
            compiler_params=pltpu.CompilerParams(vmem_limit_bytes=4 << 20),
            name="relay",
        )(got_plus, got_minus, own_plus, own_minus)
        on_plus, on_minus = shift(on_plus, 3), shift(on_minus, -3)
        parts = near_steps(field, half, halves - half, [parts])
        return (got_plus, got_minus, on_plus, on_minus, opposite), parts

    messages, parts = exchange_beside((m0, m1, m2, m3, m4), first)

    def middle(*refs):
        middle_kernel(devices, steps, *refs)

    P_SPEC = lane_spec(4 * NV, NBP)
    weights = [w_pred, w_far, w_table]
    out_shape = [field_shape, packed_shape] + message_shapes(2 * REQ)
    base, second, *answers = pl.pallas_call(
        middle,
        grid=(steps,),
        in_specs=[Q_SPEC, J_SPEC, S_SPEC, F_SPEC, P_SPEC, N_SPEC, A_SPEC, whole_spec(asks)]
        + [whole_spec(a) for a in (*messages, *weights)],
        out_specs=[F_SPEC] + [whole_spec(o) for o in out_shape[1:]],
        out_shape=out_shape,
        scratch_shapes=[padded, gathered, far],
        compiler_params=PARAMS,
        name="middle",
    )(q, jac, small, slow, parts, first, aux, asks, *messages, *weights)
    messages, parts = exchange_beside(answers, second)

    def last(*refs):
        last_kernel(devices, steps, *refs)

    end = steps - 1
    weights = [w_pred, w_own, w_lift, w_table, w_far]
    return pl.pallas_call(
        last,
        grid=(steps + 1,),
        in_specs=[
            lane_spec(NV, NBP, last=end),
            lane_spec(NV, NV, 3, last=end),
            lane_spec(SMALL, last=end),
            lane_spec(4 * NV, NBP, last=end),
            lane_spec(8, last=end),
        ]
        + [whole_spec(a) for a in moved]
        + [N_SPEC, N_SPEC]
        + [whole_spec(a) for a in (*messages, *weights)],
        out_specs=Q_SPEC,
        out_shape=jax.ShapeDtypeStruct((NV, NB, PARTITION_SLOTS), f32),
        scratch_shapes=[scratch_of(LANES)[0], gathered, far],
        compiler_params=PARAMS,
        name="last",
    )(base, jac, small, parts, aux, *moved, first, second, *messages, *weights)


def solution(mesh):
    placed = (
        P(None, None, "dom"),
        P(None, None, None, "dom"),
        P(None, None, "dom"),
        P("dom"),
        P("dom"),
        P("dom"),
        P(None, "dom"),
        P(None, "dom"),
        P(),
        P(),
        P(),
        P(),
    )
    return jax.shard_map(
        per_device, mesh=mesh, in_specs=placed, out_specs=P(None, None, "dom"), check_vma=False
    )
```

```python
import math

import jax
import jax.numpy as jnp
from jax import lax
from jax.experimental import pallas as pl
from jax.experimental.pallas import tpu as pltpu
from jax.sharding import PartitionSpec as P

NV = 9
NB = 20
NBP = 24
NQ = 16
NORDER = 4
GROUPS = 8
CSZ = 16
KEEP = 896
PARTITION_SLOTS = 1152
REQ = 32
PARTNERS = 9
ASKS = 16
LANES = 128
WIDE = 256
BOTH = 512
ROWS = 216
JAC_END = ROWS + 4 * NV * NV
PACK = 192
MSG = 256
FAR = 384
RECORD = 640
SMALL = 24
MESSAGE1 = REQ + 8

step_fast = 0.25
exact = lax.Precision.HIGHEST
f32 = jnp.float32
bf16 = jnp.bfloat16
i32 = jnp.int32

SPEED, CLUSTER, LINK, ORIENT, OCCUPIED = 12, 13, 14, 18, 22

PARAMS = pltpu.CompilerParams(vmem_limit_bytes=60 << 20)


def coefficients(lower, upper):
    return [
        (upper ** (degree + 1) - lower ** (degree + 1)) / math.factorial(degree + 1)
        for degree in range(NORDER)
    ]


FIRST = coefficients(0.0, step_fast)
SECOND = coefficients(step_fast, 2.0 * step_fast)


def partner_offsets(devices):
    return [1, 2, 3, 4, -1, -2, -3, -4, devices // 2]


def packed_row(quantity, basis):
    group, member = quantity // 3, quantity % 3
    inside = 16 * member + basis if basis < 16 else 48 + 4 * member + (basis - 16)
    return 64 * group + inside


def pack_three(members):
    a, b, c = members
    tail = a[16:24] + pltpu.roll(b[16:24], 4, 0)
    return jnp.concatenate([a[:16], b[:16], c[:16], tail, c[16:24]], axis=0)


def split(values):
    high = values.astype(bf16)
    low = (values - high.astype(f32)).astype(bf16)
    return high, low


def stacked(high, low):
    return jnp.concatenate([high, low, high], axis=0)


def dot(a, b):
    return jnp.dot(a, b, preferred_element_type=f32)


def dot_last(a, b):
    return lax.dot_general(a, b, (((1,), (1,)), ((), ())), preferred_element_type=f32)


def iota(shape, axis):
    return lax.broadcasted_iota(i32, shape, axis)


def one_hot(condition):
    return jnp.where(condition, 1.0, 0.0).astype(bf16)


def make_weights(deriv, stiff, evals, lift, w_pred, w_own, w_lift, w_table, w_far, square):
    def turned(matrix, rows, columns):
        square[...] = jnp.zeros((LANES, LANES), f32)
        square[:rows, :columns] = matrix
        return square[...].T[:NBP]

    column = iota((LANES, PACK), 1) & 63
    member = jnp.where(column < 48, column >> 4, (column - 48) >> 2)
    basis = jnp.where(column < 48, column & 15, 16 + (column & 3))
    spread = one_hot(iota((LANES, PACK), 0) == jnp.where(member < 3, basis, -1))
    member = member[:NBP]
    part = iota((NBP, PACK), 1)

    def three(matrix):
        high, low = split(turned(matrix, NB, NB))
        row = jnp.where(part < 128, dot(high, spread), dot(low, spread))
        return [jnp.where(member == inner, row, 0.0) for inner in range(3)]

    blocks = []
    for axis in range(3):
        blocks += three(-deriv[axis])
    w_pred[...] = jnp.concatenate(blocks, axis=0).astype(bf16)

    own = [
        lax.dot_general(
            evals[48 * face : 48 * face + NQ, :],
            lift[face],
            (((0,), (0,)), ((), ())),
            precision=exact,
            preferred_element_type=f32,
        )
        for face in range(4)
    ]
    blocks = []
    for matrix in [stiff[axis] for axis in range(3)] + own + [own[0] + own[1] + own[2] + own[3]]:
        blocks += three(matrix if len(blocks) < 9 else -0.5 * matrix)
    w_own[...] = jnp.concatenate(blocks, axis=0).astype(bf16)

    column = iota((LANES, 144), 1)
    spread = one_hot(iota((LANES, 144), 0) == (column & 15))
    column = column[:NBP]
    block = column >> 4
    member = block - jnp.where(column >= 96, 6, jnp.where(column >= 48, 3, 0))
    every = []
    for face in range(4):
        high, low = split(turned(lift[face], NQ, NB))
        row = jnp.where(column < 96, dot(high, spread), dot(low, spread))
        rows = [jnp.where(member == inner, -0.5 * row, 0.0) for inner in range(3)]
        w_lift[face] = jnp.concatenate(rows + [-r for r in rows], axis=0).astype(bf16)
        every += rows
    w_far[...] = jnp.concatenate(every, axis=0).astype(bf16)

    basis_of = one_hot((iota((320, NB), 0) >> 4) == iota((320, NB), 1))
    keep = (iota((320, PACK), 0) & 15) == (iota((320, PACK), 1) & 15)
    code_of = one_hot((iota((PACK, 16), 0) >> 4) == iota((PACK, 16), 1))
    halves = []
    for part_of in split(evals[...]):
        halves.append(dot(jnp.where(keep, dot_last(basis_of, part_of), 0.0).astype(bf16), code_of))
    w_table[:, :16] = halves[0].astype(bf16)
    w_table[:, 16:] = halves[1].astype(bf16)


def find_links(devices, tiles, small, aux, from_top):
    me = lax.axis_index("dom").astype(f32)
    row = iota((ASKS, LANES), 0).astype(f32)
    up_to = one_hot(iota((LANES, LANES), 0) <= iota((LANES, LANES), 1))
    request = (iota((LANES, LANES), 0) & (REQ - 1)).astype(f32)
    carry = jnp.zeros((ASKS, 1), f32)
    wanted = jnp.zeros((2 * ASKS, LANES), f32)
    for tile in range(tiles):
        at = slice(tile * LANES, (tile + 1) * LANES)
        occupied = small[OCCUPIED : OCCUPIED + 1, at] > 0.5
        target = jnp.full((1, LANES), -1.0, f32)
        slots = jnp.zeros((1, LANES), f32)
        for face in range(4):
            link = small[LINK + face : LINK + face + 1, at]
            owner = jnp.floor((link + 0.5) * (1.0 / PARTITION_SLOTS))
            slot = link - owner * PARTITION_SLOTS
            near = owner == me
            aux[face : face + 1, at] = jnp.where(near, slot, -1.0).astype(i32)
            away = occupied & jnp.logical_not(near)
            target = jnp.where(away, owner, target)
            slots = jnp.where(away, slot, slots)
        far = target - me
        far = jnp.where(far < 0, far + devices, far)
        partner = jnp.where(far <= 4, far - 1.0, jnp.where(far >= devices - 4, devices + 3.0 - far, 8.0))
        partner = jnp.where(target >= 0, partner, -1.0)
        named = jnp.where(row == partner, 1.0, 0.0)
        prefix = dot(named.astype(bf16), up_to) + carry
        carry = carry + jnp.sum(named, axis=1, keepdims=True)
        rank = jnp.sum(named * prefix, axis=0, keepdims=True) - 1.0
        if from_top:
            rank = REQ - 1.0 - rank
        aux[4:5, at] = jnp.where(target >= 0, partner * REQ + rank, -1.0).astype(i32)
        aux[5:8, at] = jnp.zeros((3, LANES), i32)
        ask = slots + 1.0
        high = jnp.floor(ask * (1.0 / 32)) * 32.0
        both = jnp.concatenate([named * high, named * (ask - high)], axis=0).astype(bf16)
        wanted = wanted + dot_last(both, one_hot(request == rank))
    return wanted[:ASKS] + wanted[ASKS:]


def prepare_kernel(devices, tiles, normals, speed, cluster, slot, links, orient, q, jac, small, aux, asks, group, one, record):
    me = lax.axis_index("dom")
    for face in range(4):
        small[3 * face : 3 * face + 3, :] = jnp.concatenate([normals[d, face : face + 1, :] for d in range(3)], axis=0)
    small[SPEED : SPEED + 1, :] = speed[...]
    small[CLUSTER : CLUSTER + 1, :] = cluster[...].astype(f32)
    small[LINK : LINK + 4, :] = links[...].astype(f32)
    small[ORIENT : ORIENT + 4, :] = orient[...].astype(f32)
    where = slot[...]
    stays = (where >= me * PARTITION_SLOTS) & (where < (me + 1) * PARTITION_SLOTS)
    small[OCCUPIED : OCCUPIED + 1, :] = jnp.where(stays, 1.0, 0.0)
    small[OCCUPIED + 1 : SMALL, :] = jnp.zeros((1, tiles * LANES), f32)
    wanted = find_links(devices, tiles, small, aux, False)
    asks[...] = jnp.zeros((devices, 1, LANES), f32)
    for k, offset in enumerate(partner_offsets(devices)):
        asks[lax.rem(me + offset + devices, devices)] = wanted[k : k + 1]

    record[...] = jnp.zeros((RECORD, LANES), f32)
    for p in range(NV):
        record[p * NBP : p * NBP + NB] = q[p]
        for inner in range(NV):
            at = ROWS + 4 * (p * NV + inner)
            record[at : at + 3] = jac[p, inner]
    fields = small[:, KEEP:]
    row = iota(fields.shape, 0)
    record[JAC_END : JAC_END + SMALL] = jnp.where(row == OCCUPIED, 1.0 - fields, fields)
    whole = record[...]
    turned = jnp.concatenate([whole[c : c + LANES].T for c in range(0, RECORD, LANES)], axis=1)
    one[...] = turned[:CSZ]
    position = me // (devices // GROUPS)
    for g in range(GROUPS):
        group[lax.rem(position + g, GROUPS)] = turned[g * CSZ : (g + 1) * CSZ]


def prepare(normals, speed, cluster, slot, links, orient, q, jac, devices):
    count = q.shape[2]

    def body(*refs):
        prepare_kernel(devices, count // LANES, *refs)

    last = KEEP // LANES
    return pl.pallas_call(
        body,
        grid=(1,),
        in_specs=[
            whole_spec(normals),
            whole_spec(speed),
            whole_spec(cluster),
            whole_spec(slot),
            whole_spec(links),
            whole_spec(orient),
            pl.BlockSpec((NV, NB, LANES), lambda i: (0, 0, last)),
            pl.BlockSpec((NV, NV, 3, LANES), lambda i: (0, 0, 0, last)),
        ],
        out_specs=[
            pl.BlockSpec((SMALL, count), lambda i: (0, 0)),
            pl.BlockSpec((8, count), lambda i: (0, 0)),
            pl.BlockSpec((devices, 1, LANES), lambda i: (0, 0, 0)),
            pl.BlockSpec((GROUPS, CSZ, RECORD), lambda i: (0, 0, 0)),
            pl.BlockSpec((CSZ, RECORD), lambda i: (0, 0)),
        ],
        out_shape=[
            jax.ShapeDtypeStruct((SMALL, count), f32),
            jax.ShapeDtypeStruct((8, count), i32),
            jax.ShapeDtypeStruct((devices, 1, LANES), f32),
            jax.ShapeDtypeStruct((GROUPS, CSZ, RECORD), f32),
            jax.ShapeDtypeStruct((CSZ, RECORD), f32),
        ],
        scratch_shapes=[pltpu.VMEM((RECORD, LANES), f32)],
        compiler_params=PARAMS,
        name="prepare",
    )(normals, speed, cluster, slot, links, orient, q, jac)


def unpack(devices, group, one, q, jac, small, aux):
    position = lax.axis_index("dom") // (devices // GROUPS)
    rows = [one[...]]
    for g in range(1, GROUPS):
        rows.append(group[lax.rem(position - g + GROUPS, GROUPS)])
    whole = jnp.concatenate(rows, axis=0)
    turned = jnp.concatenate([whole[:, c : c + LANES].T for c in range(0, RECORD, LANES)], axis=0)
    for p in range(NV):
        q[p] = turned[p * NBP : p * NBP + NB]
        for inner in range(NV):
            at = ROWS + 4 * (p * NV + inner)
            jac[p, inner] = turned[at : at + 3]
    small[...] = turned[JAC_END : JAC_END + SMALL]
    return find_links(devices, 1, small, aux, True)


OUT_BLOCKS = {1: (0, 0), 4: (0, 1), -2: (0, 2), -1: (1, 0), -4: (1, 1), 2: (1, 2), 3: (2, 0), -3: (3, 0)}
IN_BLOCKS = {-1: (0, 0), 1: (1, 0), -3: (2, 0), -4: (2, 1), -2: (2, 2), 3: (3, 0), 4: (3, 1), 2: (3, 2)}


def put(outs, rows, k, devices):
    if k == PARTNERS - 1:
        return outs[4], 0
    array, block = OUT_BLOCKS[-partner_offsets(devices)[k]]
    return outs[array], block * rows


def take(messages, k, devices):
    if k == PARTNERS - 1:
        return messages[4], 0
    array, block = IN_BLOCKS[partner_offsets(devices)[k]]
    rows = messages[4].shape[0]
    return messages[array], block * rows


def picked(requests, fields):
    lane = iota((1, LANES), 1)
    tiles = []
    for at in range(0, 12, 4):
        four = [requests[min(at + n, PARTNERS - 1)] for n in range(4)]
        tiles.append(
            jnp.where(lane < 32, four[0], jnp.where(lane < 64, four[1], jnp.where(lane < 96, four[2], four[3])))
        )
    slots = (iota((KEEP, FAR), 0) + 1).astype(f32)
    return dot(fields, one_hot(slots == jnp.concatenate(tiles, axis=1)))


def message_rows(both):
    value = both[:PACK] + both[PACK:]
    return jnp.concatenate([value, jnp.zeros((MSG - PACK, FAR), f32)], axis=0).T


def back(k):
    return k if k == PARTNERS - 1 else (k + 4) % 8


def requests_here(devices, asks):
    me = lax.axis_index("dom")
    peers = [lax.rem(me - o + devices, devices) for o in partner_offsets(devices)]
    return [asks[p] for p in peers]


def unpack_kernel(devices, group, one, asks, field, q, jac, small, aux, *outs):
    moved = unpack(devices, group, one, q, jac, small, aux)
    rows = message_rows(picked(requests_here(devices, asks), field[...]))
    for k in range(PARTNERS):
        out, at = put(outs, MESSAGE1, k, devices)
        out[at : at + REQ] = rows[k * REQ : (k + 1) * REQ]
        out[at + REQ : at + MESSAGE1, :LANES] = jnp.broadcast_to(moved[back(k) : back(k) + 1, :], (8, LANES))
        out[at + REQ : at + MESSAGE1, LANES:] = jnp.zeros((8, MSG - LANES), f32)


def answer_again(devices, asks, got, field, later, outs):
    moved = []
    for k in range(PARTNERS):
        message, at = take(got, back(k), devices)
        moved.append(message[at + REQ : at + REQ + 1, :LANES])
    every = [a + b for a, b in zip(requests_here(devices, asks), moved)]
    rows = message_rows(picked(every, later))
    rows_first = message_rows(picked(moved, field))
    for k in range(PARTNERS):
        out, at = put(outs, 2 * REQ, k, devices)
        out[at : at + REQ] = rows[k * REQ : (k + 1) * REQ]
        out[at + REQ : at + 2 * REQ] = rows_first[k * REQ : (k + 1) * REQ]


def relay_kernel(got_plus, got_minus, own_plus, own_minus, on_plus, on_minus):
    rows = own_plus.shape[0]
    block = [slice(b * rows, (b + 1) * rows) for b in range(3)]
    on_plus[block[0]] = own_plus[...]
    on_plus[block[1]] = got_plus[block[1]]
    on_plus[block[2]] = got_minus[block[2]]
    on_minus[block[0]] = own_minus[...]
    on_minus[block[1]] = got_minus[block[1]]
    on_minus[block[2]] = got_plus[block[2]]


def message_shapes(rows):
    return [jax.ShapeDtypeStruct((rows * blocks, MSG), f32) for blocks in (3, 3, 1, 1, 1)]


def far_table(devices, part, messages):
    rows = []
    for k in range(PARTNERS):
        message, at = take(messages, k, devices)
        rows.append(message[at + part * REQ : at + (part + 1) * REQ, :])
    rows.append(jnp.zeros((FAR - PARTNERS * REQ, MSG), f32))
    turned = jnp.concatenate(rows, axis=0).T[:PACK]
    return jnp.concatenate(split(turned), axis=0)


def take_turns(*chains):
    results = [None] * len(chains)
    going = list(range(len(chains)))
    while going:
        for n in list(going):
            try:
                next(chains[n])
            except StopIteration as stop:
                results[n] = stop.value
                going.remove(n)
    return results


def alone(chain):
    return take_turns(chain)[0]


class Window:
    def __init__(self, ref, begin, width):
        self.ref, self.begin = ref, begin
        self.shape = tuple(ref.shape[:-1]) + (width,)

    def _at(self, index):
        rank = len(self.shape)
        if index is Ellipsis:
            index = ()
        index = index if isinstance(index, tuple) else (index,)
        index = index + (slice(None),) * (rank - len(index))
        low, high, _ = index[-1].indices(self.shape[-1])
        return index[:-1] + (slice(self.begin + low, self.begin + high),)

    def __getitem__(self, index):
        return self.ref[self._at(index)]

    def __setitem__(self, index, value):
        self.ref[self._at(index)] = value


def lanes(tile):
    return slice(tile * LANES, (tile + 1) * LANES)


def jacobian_apply(jac, tile, parts):
    result = [None] * NV
    for group in range(3):
        for d in range(3):
            for inner in range(3):
                q = 3 * group + inner
                value = parts(d, q)
                for p in range(NV):
                    term = jac[p, q, d : d + 1, lanes(tile)] * value
                    result[p] = term if result[p] is None else result[p] + term
    return result


def packed_split(fields, group):
    packed = [pack_three(tile[3 * group : 3 * group + 3]) for tile in fields]
    return split(jnp.concatenate(packed, axis=1))


def split_fields(fields):
    pairs = [packed_split(fields, group) for group in range(3)]
    return jnp.concatenate([a for a, _ in pairs] + [b for _, b in pairs], axis=0)


def predict_chain(start, jac, w_pred, scales):
    tiles = range(len(start))
    sums = [[[s[0] * x for x in tile] for tile in start] for s in scales]
    now = start
    for degree in range(1, NORDER):
        turned = [dot(w_pred, stacked(*packed_split(now, group))) for group in range(3)]
        yield
        now = [
            jacobian_apply(
                jac, t, lambda d, q: turned[q // 3][d * 72 + (q % 3) * NBP : d * 72 + (q % 3) * NBP + NBP, lanes(t)]
            )
            for t in tiles
        ]
        sums = [
            [[a + s[degree] * x for a, x in zip(total[t], now[t])] for t in tiles] for total, s in zip(sums, scales)
        ]
    return sums


def predict(*args):
    return alone(predict_chain(*args))


def face_products(gathered, at_face, table, tiles):
    outers = []
    for t in tiles:
        outer = [None] * NV
        for b in range(NB):
            values = table[b * NQ : (b + 1) * NQ, lanes(t)]
            for p in range(NV):
                at = packed_row(p, b)
                term = gathered[at_face, at : at + 1, lanes(t)] * values
                outer[p] = term if outer[p] is None else outer[p] + term
        outers.append(outer)
    return [
        stacked(*split(jnp.concatenate([jnp.concatenate(o[3 * g : 3 * g + 3], axis=0) for o in outers], axis=1)))
        for g in range(3)
    ]


def table_of(code, w_table):
    hot = one_hot(iota((16, code.shape[1]), 0).astype(f32) == code)
    return dot(w_table, jnp.concatenate([hot, hot], axis=0))


def near_chain(own, near, small, aux, w_own, w_lift, w_table, gathered):
    count = own.shape[1]
    tiles = range(count // LANES)
    slots = iota((KEEP, count), 0).astype(jnp.int16)

    def gather(face):
        index = jnp.broadcast_to(aux[face : face + 1, :], (16, count)).astype(jnp.int16)
        index = jnp.concatenate([index] * (KEEP // 16), axis=0)
        both = dot(near[...], jnp.where(slots == index, jnp.ones((), bf16), jnp.zeros((), bf16)))
        gathered[face, :, :count] = both[:PACK] + both[PACK:]
        return table_of(small[ORIENT + face : ORIENT + face + 1, :], w_table)

    table = gather(0)
    mine = []
    for group in range(3):
        rows = slice(64 * group, 64 * group + 64)
        lower = slice(PACK + 64 * group, PACK + 64 * group + 64)
        mine.append(dot(w_own, stacked(own[rows], own[lower])))

    def of_own(block, q, t):
        at = block * 72 + (q % 3) * NBP
        return mine[q // 3][at : at + NBP, lanes(t)]

    yield
    volume = [[[of_own(d, q, t) for q in range(NV)] for d in range(3)] for t in tiles]
    upwind = [[of_own(7, q, t) for q in range(NV)] for t in tiles]
    for face in range(4):
        now = table
        if face < 3:
            table = gather(face + 1)
            yield
        for group, points in enumerate(face_products(gathered, face, now, tiles)):
            lifted = dot(w_lift[face], points)
            for t in tiles:
                for inner in range(3):
                    q = 3 * group + inner
                    at = inner * NBP
                    mixed = lifted[at : at + NBP, lanes(t)] + of_own(3 + face, q, t)
                    upwind[t][q] = upwind[t][q] + lifted[72 + at : 72 + at + NBP, lanes(t)]
                    for d in range(3):
                        normal = small[3 * face + d : 3 * face + d + 1, lanes(t)]
                        volume[t][d][q] = volume[t][d][q] + normal * mixed
    return volume, upwind


def near_part(*args):
    return alone(near_chain(*args))


def update_chain(parts, far, small, aux, jac, w_far, w_table, gathered):
    volume, upwind = parts
    tiles = range(len(volume))
    count = len(volume) * LANES
    place = aux[4:5, :]
    both = dot(far, one_hot(iota((FAR, count), 0) == place))
    gathered[0, :, :count] = both[:PACK] + both[PACK:]
    masks = [jnp.where((aux[face : face + 1, :] < 0) & (place >= 0), 1.0, 0.0) for face in range(4)]
    code = masks[0] * small[ORIENT : ORIENT + 1, :]
    normals = [masks[0] * small[d : d + 1, :] for d in range(3)]
    for face in range(1, 4):
        code = code + masks[face] * small[ORIENT + face : ORIENT + face + 1, :]
        normals = [n + masks[face] * small[3 * face + d : 3 * face + d + 1, :] for d, n in enumerate(normals)]
    changes = [[None] * NV for t in tiles]
    table = table_of(code, w_table)
    yield
    volume = [[list(v) for v in tile] for tile in volume]
    upwind = [list(tile) for tile in upwind]
    for group, points in enumerate(face_products(gathered, 0, table, tiles)):
        lifted = dot(w_far, points)
        for t in tiles:
            for inner in range(3):
                q = 3 * group + inner
                mixed = None
                for face in range(4):
                    at = 72 * face + inner * NBP
                    term = masks[face][:, lanes(t)] * lifted[at : at + NBP, lanes(t)]
                    mixed = term if mixed is None else mixed + term
                upwind[t][q] = upwind[t][q] - mixed
                for d in range(3):
                    volume[t][d][q] = volume[t][d][q] + normals[d][:, lanes(t)] * mixed
    for t in tiles:
        change = jacobian_apply(jac, t, lambda d, q: volume[t][d][q])
        speed = small[SPEED : SPEED + 1, lanes(t)]
        changes[t] = [c + speed * u for c, u in zip(change, upwind[t])]
    return changes


def update(*args):
    return alone(update_chain(*args))


def store_parts(ref, parts):
    volume, upwind = parts
    for t in range(len(volume)):
        for q in range(NV):
            for d in range(3):
                ref[d * NV + q, :, lanes(t)] = volume[t][d][q]
            ref[3 * NV + q, :, lanes(t)] = upwind[t][q]


def load_parts(ref):
    tiles = range(ref.shape[2] // LANES)
    volume = [[[ref[d * NV + q, :, lanes(t)] for q in range(NV)] for d in range(3)] for t in tiles]
    return volume, [[ref[3 * NV + q, :, lanes(t)] for q in range(NV)] for t in tiles]


def load_state(q, padded):
    padded[:, NB:NBP, :] = jnp.zeros((NV, NBP - NB, padded.shape[2]), f32)
    for p in range(NV):
        padded[p, :NB, :] = q[p]
    return load_field(padded)


def load_field(ref):
    return [[ref[p, :, lanes(t)] for p in range(NV)] for t in range(ref.shape[2] // LANES)]


def store_field(ref, field):
    for t, tile in enumerate(field):
        for p in range(NV):
            ref[p, :, lanes(t)] = tile[p]


def store_result(out, base, change, small):
    for t in range(len(base)):
        occupied = small[OCCUPIED : OCCUPIED + 1, lanes(t)] > 0.5
        for p in range(NV):
            out[p, :, lanes(t)] = jnp.where(occupied, base[t][p] + change[t][p], 0.0)[:NB]


def first_half_kernel(q, jac, deriv, stiff, evals, lift, packed, slow, w_pred, w_own, w_lift, w_table, w_far, padded, square):
    make_weights(deriv, stiff, evals, lift, w_pred, w_own, w_lift, w_table, w_far, square)
    first_fields(q, jac, w_pred, packed, slow, padded)


def second_half_kernel(q, jac, w_pred, _, __, packed, slow, padded):
    first_fields(q, jac, w_pred, packed, slow, padded)


def first_fields(q, jac, w_pred, packed, slow, padded):
    weights = w_pred[...]
    windows = [[Window(r, begin, WIDE) for r in (q, jac, packed, slow, padded)] for begin in range(0, BOTH, WIDE)]
    chains = [predict_chain(load_state(w[0], w[4]), w[1], weights, [FIRST, SECOND]) for w in windows]
    for (_, _, packed, slow, _), (first, later) in zip(windows, take_turns(*chains)):
        packed[...] = split_fields(first)
        store_field(slow, later)


def near_kernel(own, near, small, aux, w_own, w_lift, w_table, *refs):
    parts, gathered = refs[-2:]
    weights = w_own[...], w_lift, w_table[...]
    chains = []
    for begin in range(0, BOTH, WIDE):
        window = [Window(r, begin, WIDE) for r in (own, small, aux, gathered)]
        chains.append(near_chain(window[0][...], near, window[1], window[2], *weights, window[3]))
    for begin, values in zip(range(0, BOTH, WIDE), take_turns(*chains)):
        store_parts(Window(parts, begin, WIDE), values)


def middle_chain(start, parts, jac, small, slow, far, aux, w_pred, w_far, w_table, gathered):
    change = yield from update_chain(parts, far, small, aux, jac, w_far, w_table, gathered)
    base, midway, second = [], [], []
    fast = [small[CLUSTER : CLUSTER + 1, lanes(t)] < 0.5 for t in range(len(start))]
    for t in range(len(start)):
        base.append([a + b for a, b in zip(start[t], change[t])])
        midway.append([jnp.where(fast[t], a, b) for a, b in zip(base[t], start[t])])
    (later,) = yield from predict_chain(midway, jac, w_pred, [FIRST])
    for t in range(len(start)):
        second.append([jnp.where(fast[t], a, b) for a, b in zip(later[t], slow[t])])
    return base, split_fields(second)


def middle_step(*args):
    return alone(middle_chain(*args))


def middle_kernel(devices, steps, q, jac, small, slow, parts, near, aux, asks, *refs):
    messages = refs[:5]
    w_pred, w_far, w_table, base, packed, *outs, padded, gathered, far = refs[5:]
    step = pl.program_id(0)

    @pl.when(step == 0)
    def _():
        far[...] = far_table(devices, 0, messages)

    weights = w_pred[...], w_far[...], w_table[...]
    table = far[...]
    chains, bases = [], []
    for begin in range(0, BOTH, WIDE):
        w = [Window(r, begin, WIDE) for r in (q, padded, parts, jac, small, slow, aux, gathered, base)]
        state = load_state(w[0], w[1])
        chains.append(
            middle_chain(state, load_parts(w[2]), w[3], w[4], load_field(w[5]), table, w[6], *weights, w[7])
        )
        bases.append(w[8])
    results = take_turns(*chains)
    for window, (now, _) in zip(bases, results):
        store_field(window, now)
    second = jnp.concatenate([values for _, values in results], axis=1)
    packed[:, pl.ds(pl.multiple_of(step * BOTH, BOTH), BOTH)] = second

    @pl.when(step == steps - 1)
    def _():
        answer_again(devices, asks, messages, near[...], packed[:, :KEEP], outs)


def last_kernel(
    devices, steps, base, jac, small, parts, aux, q_moved, jac_moved, small_moved, aux_moved, near, later, *refs
):
    messages = refs[:5]
    w_pred, w_own, w_lift, w_table, w_far, out, padded, gathered, far = refs[5:]
    step = pl.program_id(0)

    @pl.when(step == 0)
    def _():
        far[...] = far_table(devices, 0, messages)

    @pl.when(step < steps)
    def _():
        change = update(load_parts(parts), far[...], small, aux, jac, w_far[...], w_table[...], gathered)
        store_result(out, load_field(base), change, small)

    @pl.when(step == steps)
    def _():
        start = load_state(q_moved, padded)
        first, slow = predict(start, jac_moved, w_pred[...], [FIRST, SECOND])
        of_near = w_own[...], w_lift, w_table[...]
        own = near_part(split_fields(first), near, small_moved, aux_moved, *of_near, gathered)
        now, second = middle_step(
            start, own, jac_moved, small_moved, slow, far_table(devices, 1, messages), aux_moved,
            w_pred[...], w_far[...], w_table[...], gathered,
        )
        own = near_part(second, later, small_moved, aux_moved, *of_near, gathered)
        change = update(own, far[...], small_moved, aux_moved, jac_moved, w_far[...], w_table[...], gathered)
        store_result(out, now, change, small_moved)


def whole_spec(array):
    rank = array.ndim
    return pl.BlockSpec(array.shape, lambda i: (0,) * rank)


def lane_spec(*lead, last=None):
    rank = len(lead)
    if last is None:
        return pl.BlockSpec(lead + (WIDE,), lambda i: (0,) * rank + (i,))
    return pl.BlockSpec(lead + (WIDE,), lambda i: (0,) * rank + (jnp.minimum(i, last),))


Q_SPEC = lane_spec(NV, NB)
J_SPEC = lane_spec(NV, NV, 3)
S_SPEC = lane_spec(SMALL)
A_SPEC = lane_spec(8)
F_SPEC = lane_spec(NV, NBP)
X_SPEC = lane_spec(2 * PACK)
N_SPEC = pl.BlockSpec((2 * PACK, KEEP), lambda i: (0, 0))


def scratch_of(width):
    return pltpu.VMEM((NV, NBP, width), f32), pltpu.VMEM((4, PACK, width), f32)


def per_device(
    element_freedom_values,
    scaled_jacobian_matrices,
    outward_face_normals,
    largest_wave_speed,
    element_cluster_index,
    element_new_slot,
    neighbours,
    face_rotation_codes,
    deriv_mats,
    stiff_mats,
    face_eval,
    face_lift,
):
    count = element_freedom_values.shape[2]
    steps = count // WIDE
    devices = lax.axis_size("dom")
    q = element_freedom_values
    jac = jnp.transpose(scaled_jacobian_matrices, (1, 2, 0, 3))

    def shift(array, by):
        return lax.ppermute(array, "dom", [(i, (i + by) % devices) for i in range(devices)])

    def swap(array, groups):
        return lax.all_to_all(array, "dom", split_axis=0, concat_axis=0, axis_index_groups=groups, tiled=True)

    def on_ring(body):
        def kernel(*refs):
            body(devices, *refs)

        return kernel

    small, aux, asks, group, one = prepare(
        jnp.transpose(outward_face_normals, (1, 0, 2)),
        largest_wave_speed[None],
        element_cluster_index[None],
        element_new_slot[None],
        neighbours,
        face_rotation_codes,
        q,
        jac,
        devices,
    )
    asks = swap(asks, None)
    padded, gathered = scratch_of(WIDE)
    packed_shape = jax.ShapeDtypeStruct((2 * PACK, count), bf16)
    field_shape = jax.ShapeDtypeStruct((NV, NBP, count), f32)
    far = pltpu.VMEM((2 * PACK, FAR), bf16)
    weight_shapes = [
        jax.ShapeDtypeStruct((ROWS, PACK), bf16),
        jax.ShapeDtypeStruct((576, PACK), bf16),
        jax.ShapeDtypeStruct((4, 144, 144), bf16),
        jax.ShapeDtypeStruct((320, 32), bf16),
        jax.ShapeDtypeStruct((288, 144), bf16),
    ]
    evals = jnp.transpose(face_eval, (0, 2, 1)).reshape(12 * NQ, NB)
    matrices = [deriv_mats, stiff_mats, evals, face_lift]
    halves = count // BOTH

    def part_spec(begin, *lead):
        rank = len(lead)
        return pl.BlockSpec(lead + (BOTH,), lambda i: (0,) * rank + (i + begin,))

    def first_specs(begin):
        return [part_spec(begin, NV, NB), part_spec(begin, NV, NV, 3)], [
            part_spec(begin, 2 * PACK),
            part_spec(begin, NV, NBP),
        ]

    ins, outs = first_specs(0)
    twice = scratch_of(BOTH)
    first, slow, w_pred, w_own, w_lift, w_table, w_far = pl.pallas_call(
        first_half_kernel,
        grid=(1,),
        in_specs=ins + [whole_spec(m) for m in matrices],
        out_specs=outs + [whole_spec(w) for w in weight_shapes],
        out_shape=[packed_shape, field_shape] + weight_shapes,
        scratch_shapes=[twice[0], pltpu.VMEM((LANES, LANES), f32)],
        cost_estimate=pl.CostEstimate(flops=int(4e9), bytes_accessed=4 << 20, transcendentals=0),
        compiler_params=PARAMS,
        name="first",
    )(q, jac, *matrices)
    asks, group, one, first, slow = lax.optimization_barrier((asks, group, one, first, slow))
    stride = devices // GROUPS
    group = swap(group, [[r + stride * j for j in range(GROUPS)] for r in range(stride)])
    one = shift(one, 1)
    ins, outs = first_specs(1)
    first, slow = pl.pallas_call(
        second_half_kernel,
        grid=(halves - 1,),
        in_specs=ins + [whole_spec(w_pred)] + [pl.BlockSpec(memory_space=pl.ANY)] * 2,
        out_specs=outs,
        out_shape=[packed_shape, field_shape],
        scratch_shapes=[twice[0]],
        input_output_aliases={3: 0, 4: 1},
        cost_estimate=pl.CostEstimate(flops=int(4e9), bytes_accessed=4 << 20, transcendentals=0),
        compiler_params=PARAMS,
        name="first",
    )(q, jac, w_pred, first, slow)

    moved_shapes = [
        jax.ShapeDtypeStruct((NV, NB, LANES), f32),
        jax.ShapeDtypeStruct((NV, NV, 3, LANES), f32),
        jax.ShapeDtypeStruct((SMALL, LANES), f32),
        jax.ShapeDtypeStruct((8, LANES), i32),
    ]
    out_shape = moved_shapes + message_shapes(MESSAGE1)
    *moved, m0, m1, m2, m3, m4 = pl.pallas_call(
        on_ring(unpack_kernel),
        grid=(1,),
        in_specs=[whole_spec(a) for a in (group, one, asks)] + [N_SPEC],
        out_specs=[whole_spec(o) for o in out_shape],
        out_shape=out_shape,
        compiler_params=PARAMS,
        name="unpack",
    )(group, one, asks, first)
    of_near = [w_own, w_lift, w_table]
    parts_shape = jax.ShapeDtypeStruct((4 * NV, NBP, count), f32)

    def near_steps(field, begin, number, parts):
        def spec(*lead):
            return part_spec(begin, *lead)

        return pl.pallas_call(
            near_kernel,
            grid=(number,),
            in_specs=[spec(2 * PACK), N_SPEC, spec(SMALL), spec(8)]
            + [whole_spec(w) for w in of_near]
            + [pl.BlockSpec(memory_space=pl.ANY)] * len(parts),
            out_specs=spec(4 * NV, NBP),
            out_shape=parts_shape,
            scratch_shapes=[twice[1]],
            input_output_aliases={7: 0} if parts else {},
            cost_estimate=pl.CostEstimate(flops=int(4e9) * number, bytes_accessed=4 << 20, transcendentals=0),
            compiler_params=PARAMS,
            name="near",
        )(field, field, small, aux, *of_near, *parts)

    def exchange_beside(answers, field):
        half = halves // 2
        plus, minus, own_plus, own_minus, opposite = answers
        got_plus, got_minus, opposite = shift(plus, 1), shift(minus, -1), shift(opposite, devices // 2)
        parts = near_steps(field, 0, half, [])
        got_plus, got_minus, opposite, parts = lax.optimization_barrier((got_plus, got_minus, opposite, parts))
        on_plus, on_minus = pl.pallas_call(
            relay_kernel,
            out_shape=[jax.ShapeDtypeStruct(plus.shape, f32)] * 2,
            compiler_params=pltpu.CompilerParams(vmem_limit_bytes=4 << 20),
            name="relay",
        )(got_plus, got_minus, own_plus, own_minus)
        on_plus, on_minus = shift(on_plus, 3), shift(on_minus, -3)
        parts = near_steps(field, half, halves - half, [parts])
        return (got_plus, got_minus, on_plus, on_minus, opposite), parts

    messages, parts = exchange_beside((m0, m1, m2, m3, m4), first)

    def middle(*refs):
        middle_kernel(devices, halves, *refs)

    weights = [w_pred, w_far, w_table]
    out_shape = [field_shape, packed_shape] + message_shapes(2 * REQ)
    base, second, *answers = pl.pallas_call(
        middle,
        grid=(halves,),
        in_specs=[
            part_spec(0, NV, NB),
            part_spec(0, NV, NV, 3),
            part_spec(0, SMALL),
            part_spec(0, NV, NBP),
            part_spec(0, 4 * NV, NBP),
            N_SPEC,
            part_spec(0, 8),
            whole_spec(asks),
        ]
        + [whole_spec(a) for a in (*messages, *weights)],
        out_specs=[part_spec(0, NV, NBP)] + [whole_spec(o) for o in out_shape[1:]],
        out_shape=out_shape,
        scratch_shapes=[*twice, far],
        compiler_params=PARAMS,
        name="middle",
    )(q, jac, small, slow, parts, first, aux, asks, *messages, *weights)
    messages, parts = exchange_beside(answers, second)

    def last(*refs):
        last_kernel(devices, steps, *refs)

    end = steps - 1
    weights = [w_pred, w_own, w_lift, w_table, w_far]
    return pl.pallas_call(
        last,
        grid=(steps + 1,),
        in_specs=[
            lane_spec(NV, NBP, last=end),
            lane_spec(NV, NV, 3, last=end),
            lane_spec(SMALL, last=end),
            lane_spec(4 * NV, NBP, last=end),
            lane_spec(8, last=end),
        ]
        + [whole_spec(a) for a in moved]
        + [N_SPEC, N_SPEC]
        + [whole_spec(a) for a in (*messages, *weights)],
        out_specs=Q_SPEC,
        out_shape=jax.ShapeDtypeStruct((NV, NB, PARTITION_SLOTS), f32),
        scratch_shapes=[scratch_of(LANES)[0], gathered, far],
        compiler_params=PARAMS,
        name="last",
    )(base, jac, small, parts, aux, *moved, first, second, *messages, *weights)


def solution(mesh):
    placed = (
        P(None, None, "dom"),
        P(None, None, None, "dom"),
        P(None, None, "dom"),
        P("dom"),
        P("dom"),
        P("dom"),
        P(None, "dom"),
        P(None, "dom"),
        P(),
        P(),
        P(),
        P(),
    )
    return jax.shard_map(
        per_device, mesh=mesh, in_specs=placed, out_specs=P(None, None, "dom"), check_vma=False
    )
```

```python
import math

import jax
import jax.numpy as jnp
from jax import lax
from jax.experimental import pallas as pl
from jax.experimental.pallas import tpu as pltpu
from jax.sharding import PartitionSpec as P

NV = 9
NB = 20
NBP = 24
NQ = 16
NORDER = 4
GROUPS = 8
CSZ = 16
KEEP = 896
PARTITION_SLOTS = 1152
REQ = 32
PARTNERS = 9
ASKS = 16
LANES = 128
WIDE = 256
BOTH = 512
ROWS = 216
JAC_END = ROWS + 4 * NV * NV
PACK = 192
MSG = 256
FAR = 384
RECORD = 640
SMALL = 24
MESSAGE1 = REQ + 8

step_fast = 0.25
exact = lax.Precision.HIGHEST
f32 = jnp.float32
bf16 = jnp.bfloat16
i32 = jnp.int32

SPEED, CLUSTER, LINK, ORIENT, OCCUPIED = 12, 13, 14, 18, 22

MOST = pltpu.CompilerParams(vmem_limit_bytes=60 << 20)
PARAMS = pltpu.CompilerParams(vmem_limit_bytes=20 << 20)


def coefficients(lower, upper):
    return [
        (upper ** (degree + 1) - lower ** (degree + 1)) / math.factorial(degree + 1)
        for degree in range(NORDER)
    ]


FIRST = coefficients(0.0, step_fast)
SECOND = coefficients(step_fast, 2.0 * step_fast)


def partner_offsets(devices):
    return [1, 2, 3, 4, -1, -2, -3, -4, devices // 2]


def packed_row(quantity, basis):
    group, member = quantity // 3, quantity % 3
    inside = 16 * member + basis if basis < 16 else 48 + 4 * member + (basis - 16)
    return 64 * group + inside


def pack_three(members):
    a, b, c = members
    tail = a[16:24] + pltpu.roll(b[16:24], 4, 0)
    return jnp.concatenate([a[:16], b[:16], c[:16], tail, c[16:24]], axis=0)


def split(values):
    high = values.astype(bf16)
    low = (values - high.astype(f32)).astype(bf16)
    return high, low


def stacked(high, low):
    return jnp.concatenate([high, low, high], axis=0)


def dot(a, b):
    return jnp.dot(a, b, preferred_element_type=f32)


def dot_last(a, b):
    return lax.dot_general(a, b, (((1,), (1,)), ((), ())), preferred_element_type=f32)


def iota(shape, axis):
    return lax.broadcasted_iota(i32, shape, axis)


def one_hot(condition):
    return jnp.where(condition, 1.0, 0.0).astype(bf16)


def make_weights(deriv, stiff, evals, lift, w_pred, w_own, w_lift, w_table, w_far, square):
    def turned(matrix, rows, columns):
        square[...] = jnp.zeros((LANES, LANES), f32)
        square[:rows, :columns] = matrix
        return square[...].T[:NBP]

    column = iota((LANES, PACK), 1) & 63
    member = jnp.where(column < 48, column >> 4, (column - 48) >> 2)
    basis = jnp.where(column < 48, column & 15, 16 + (column & 3))
    spread = one_hot(iota((LANES, PACK), 0) == jnp.where(member < 3, basis, -1))
    member = member[:NBP]
    part = iota((NBP, PACK), 1)

    def three(matrix):
        high, low = split(turned(matrix, NB, NB))
        row = jnp.where(part < 128, dot(high, spread), dot(low, spread))
        return [jnp.where(member == inner, row, 0.0) for inner in range(3)]

    blocks = []
    for axis in range(3):
        blocks += three(-deriv[axis])
    w_pred[...] = jnp.concatenate(blocks, axis=0).astype(bf16)

    own = [
        lax.dot_general(
            evals[48 * face : 48 * face + NQ, :],
            lift[face],
            (((0,), (0,)), ((), ())),
            precision=exact,
            preferred_element_type=f32,
        )
        for face in range(4)
    ]
    blocks = []
    for matrix in [stiff[axis] for axis in range(3)] + own + [own[0] + own[1] + own[2] + own[3]]:
        blocks += three(matrix if len(blocks) < 9 else -0.5 * matrix)
    w_own[...] = jnp.concatenate(blocks, axis=0).astype(bf16)

    column = iota((LANES, 144), 1)
    spread = one_hot(iota((LANES, 144), 0) == (column & 15))
    column = column[:NBP]
    block = column >> 4
    member = block - jnp.where(column >= 96, 6, jnp.where(column >= 48, 3, 0))
    every = []
    for face in range(4):
        high, low = split(turned(lift[face], NQ, NB))
        row = jnp.where(column < 96, dot(high, spread), dot(low, spread))
        rows = [jnp.where(member == inner, -0.5 * row, 0.0) for inner in range(3)]
        w_lift[face] = jnp.concatenate(rows + [-r for r in rows], axis=0).astype(bf16)
        every += rows
    w_far[...] = jnp.concatenate(every, axis=0).astype(bf16)

    basis_of = one_hot((iota((320, NB), 0) >> 4) == iota((320, NB), 1))
    keep = (iota((320, PACK), 0) & 15) == (iota((320, PACK), 1) & 15)
    code_of = one_hot((iota((PACK, 16), 0) >> 4) == iota((PACK, 16), 1))
    halves = []
    for part_of in split(evals[...]):
        halves.append(dot(jnp.where(keep, dot_last(basis_of, part_of), 0.0).astype(bf16), code_of))
    w_table[:, :16] = halves[0].astype(bf16)
    w_table[:, 16:] = halves[1].astype(bf16)


def find_links(devices, tiles, small, aux, from_top):
    me = lax.axis_index("dom").astype(f32)
    row = iota((ASKS, LANES), 0).astype(f32)
    up_to = one_hot(iota((LANES, LANES), 0) <= iota((LANES, LANES), 1))
    request = (iota((LANES, LANES), 0) & (REQ - 1)).astype(f32)
    carry = jnp.zeros((ASKS, 1), f32)
    wanted = jnp.zeros((2 * ASKS, LANES), f32)
    for tile in range(tiles):
        at = slice(tile * LANES, (tile + 1) * LANES)
        occupied = small[OCCUPIED : OCCUPIED + 1, at] > 0.5
        target = jnp.full((1, LANES), -1.0, f32)
        slots = jnp.zeros((1, LANES), f32)
        for face in range(4):
            link = small[LINK + face : LINK + face + 1, at]
            owner = jnp.floor((link + 0.5) * (1.0 / PARTITION_SLOTS))
            slot = link - owner * PARTITION_SLOTS
            near = owner == me
            aux[face : face + 1, at] = jnp.where(near, slot, -1.0).astype(i32)
            away = occupied & jnp.logical_not(near)
            target = jnp.where(away, owner, target)
            slots = jnp.where(away, slot, slots)
        far = target - me
        far = jnp.where(far < 0, far + devices, far)
        partner = jnp.where(far <= 4, far - 1.0, jnp.where(far >= devices - 4, devices + 3.0 - far, 8.0))
        partner = jnp.where(target >= 0, partner, -1.0)
        named = jnp.where(row == partner, 1.0, 0.0)
        prefix = dot(named.astype(bf16), up_to) + carry
        carry = carry + jnp.sum(named, axis=1, keepdims=True)
        rank = jnp.sum(named * prefix, axis=0, keepdims=True) - 1.0
        if from_top:
            rank = REQ - 1.0 - rank
        aux[4:5, at] = jnp.where(target >= 0, partner * REQ + rank, -1.0).astype(i32)
        aux[5:8, at] = jnp.zeros((3, LANES), i32)
        ask = slots + 1.0
        high = jnp.floor(ask * (1.0 / 32)) * 32.0
        both = jnp.concatenate([named * high, named * (ask - high)], axis=0).astype(bf16)
        wanted = wanted + dot_last(both, one_hot(request == rank))
    return wanted[:ASKS] + wanted[ASKS:]


def prepare_kernel(devices, tiles, normals, speed, cluster, slot, links, orient, q, jac, small, aux, asks, group, one, record):
    me = lax.axis_index("dom")
    for face in range(4):
        small[3 * face : 3 * face + 3, :] = jnp.concatenate([normals[d, face : face + 1, :] for d in range(3)], axis=0)
    small[SPEED : SPEED + 1, :] = speed[...]
    small[CLUSTER : CLUSTER + 1, :] = cluster[...].astype(f32)
    small[LINK : LINK + 4, :] = links[...].astype(f32)
    small[ORIENT : ORIENT + 4, :] = orient[...].astype(f32)
    where = slot[...]
    stays = (where >= me * PARTITION_SLOTS) & (where < (me + 1) * PARTITION_SLOTS)
    small[OCCUPIED : OCCUPIED + 1, :] = jnp.where(stays, 1.0, 0.0)
    small[OCCUPIED + 1 : SMALL, :] = jnp.zeros((1, tiles * LANES), f32)
    wanted = find_links(devices, tiles, small, aux, False)
    asks[...] = jnp.zeros((devices, 1, LANES), f32)
    for k, offset in enumerate(partner_offsets(devices)):
        asks[lax.rem(me + offset + devices, devices)] = wanted[k : k + 1]

    record[...] = jnp.zeros((RECORD, LANES), f32)
    for p in range(NV):
        record[p * NBP : p * NBP + NB] = q[p]
        for inner in range(NV):
            at = ROWS + 4 * (p * NV + inner)
            record[at : at + 3] = jac[p, inner]
    fields = small[:, KEEP:]
    row = iota(fields.shape, 0)
    record[JAC_END : JAC_END + SMALL] = jnp.where(row == OCCUPIED, 1.0 - fields, fields)
    whole = record[...]
    turned = jnp.concatenate([whole[c : c + LANES].T for c in range(0, RECORD, LANES)], axis=1)
    one[...] = turned[:CSZ]
    position = me // (devices // GROUPS)
    for g in range(GROUPS):
        group[lax.rem(position + g, GROUPS)] = turned[g * CSZ : (g + 1) * CSZ]


def prepare(normals, speed, cluster, slot, links, orient, q, jac, devices):
    count = q.shape[2]

    def body(*refs):
        prepare_kernel(devices, count // LANES, *refs)

    last = KEEP // LANES
    return pl.pallas_call(
        body,
        grid=(1,),
        in_specs=[
            whole_spec(normals),
            whole_spec(speed),
            whole_spec(cluster),
            whole_spec(slot),
            whole_spec(links),
            whole_spec(orient),
            pl.BlockSpec((NV, NB, LANES), lambda i: (0, 0, last)),
            pl.BlockSpec((NV, NV, 3, LANES), lambda i: (0, 0, 0, last)),
        ],
        out_specs=[
            pl.BlockSpec((SMALL, count), lambda i: (0, 0)),
            pl.BlockSpec((8, count), lambda i: (0, 0)),
            pl.BlockSpec((devices, 1, LANES), lambda i: (0, 0, 0)),
            pl.BlockSpec((GROUPS, CSZ, RECORD), lambda i: (0, 0, 0)),
            pl.BlockSpec((CSZ, RECORD), lambda i: (0, 0)),
        ],
        out_shape=[
            jax.ShapeDtypeStruct((SMALL, count), f32),
            jax.ShapeDtypeStruct((8, count), i32),
            jax.ShapeDtypeStruct((devices, 1, LANES), f32),
            jax.ShapeDtypeStruct((GROUPS, CSZ, RECORD), f32),
            jax.ShapeDtypeStruct((CSZ, RECORD), f32),
        ],
        scratch_shapes=[pltpu.VMEM((RECORD, LANES), f32)],
        compiler_params=MOST,
        name="prepare",
    )(normals, speed, cluster, slot, links, orient, q, jac)


def unpack(devices, group, one, q, jac, small, aux):
    position = lax.axis_index("dom") // (devices // GROUPS)
    rows = [one[...]]
    for g in range(1, GROUPS):
        rows.append(group[lax.rem(position - g + GROUPS, GROUPS)])
    whole = jnp.concatenate(rows, axis=0)
    turned = jnp.concatenate([whole[:, c : c + LANES].T for c in range(0, RECORD, LANES)], axis=0)
    for p in range(NV):
        q[p] = turned[p * NBP : p * NBP + NB]
        for inner in range(NV):
            at = ROWS + 4 * (p * NV + inner)
            jac[p, inner] = turned[at : at + 3]
    small[...] = turned[JAC_END : JAC_END + SMALL]
    return find_links(devices, 1, small, aux, True)


OUT_BLOCKS = {1: (0, 0), 4: (0, 1), -2: (0, 2), -1: (1, 0), -4: (1, 1), 2: (1, 2), 3: (2, 0), -3: (3, 0)}
IN_BLOCKS = {-1: (0, 0), 1: (1, 0), -3: (2, 0), -4: (2, 1), -2: (2, 2), 3: (3, 0), 4: (3, 1), 2: (3, 2)}


def put(outs, rows, k, devices):
    if k == PARTNERS - 1:
        return outs[4], 0
    array, block = OUT_BLOCKS[-partner_offsets(devices)[k]]
    return outs[array], block * rows


def take(messages, k, devices):
    if k == PARTNERS - 1:
        return messages[4], 0
    array, block = IN_BLOCKS[partner_offsets(devices)[k]]
    rows = messages[4].shape[0]
    return messages[array], block * rows


def picked(requests, fields):
    lane = iota((1, LANES), 1)
    tiles = []
    for at in range(0, 12, 4):
        four = [requests[min(at + n, PARTNERS - 1)] for n in range(4)]
        tiles.append(
            jnp.where(lane < 32, four[0], jnp.where(lane < 64, four[1], jnp.where(lane < 96, four[2], four[3])))
        )
    slots = (iota((KEEP, FAR), 0) + 1).astype(f32)
    return dot(fields, one_hot(slots == jnp.concatenate(tiles, axis=1)))


def message_rows(both):
    value = both[:PACK] + both[PACK:]
    return jnp.concatenate([value, jnp.zeros((MSG - PACK, FAR), f32)], axis=0).T


def back(k):
    return k if k == PARTNERS - 1 else (k + 4) % 8


def requests_here(devices, asks):
    me = lax.axis_index("dom")
    peers = [lax.rem(me - o + devices, devices) for o in partner_offsets(devices)]
    return [asks[p] for p in peers]


def unpack_kernel(devices, group, one, asks, field, q, jac, small, aux, *outs):
    moved = unpack(devices, group, one, q, jac, small, aux)
    rows = message_rows(picked(requests_here(devices, asks), field[...]))
    for k in range(PARTNERS):
        out, at = put(outs, MESSAGE1, k, devices)
        out[at : at + REQ] = rows[k * REQ : (k + 1) * REQ]
        out[at + REQ : at + MESSAGE1, :LANES] = jnp.broadcast_to(moved[back(k) : back(k) + 1, :], (8, LANES))
        out[at + REQ : at + MESSAGE1, LANES:] = jnp.zeros((8, MSG - LANES), f32)


def answer_again(devices, asks, got, field, later, outs):
    moved = []
    for k in range(PARTNERS):
        message, at = take(got, back(k), devices)
        moved.append(message[at + REQ : at + REQ + 1, :LANES])
    every = [a + b for a, b in zip(requests_here(devices, asks), moved)]
    rows = message_rows(picked(every, later))
    rows_first = message_rows(picked(moved, field))
    for k in range(PARTNERS):
        out, at = put(outs, 2 * REQ, k, devices)
        out[at : at + REQ] = rows[k * REQ : (k + 1) * REQ]
        out[at + REQ : at + 2 * REQ] = rows_first[k * REQ : (k + 1) * REQ]


def relay_kernel(got_plus, got_minus, own_plus, own_minus, on_plus, on_minus):
    rows = own_plus.shape[0]
    block = [slice(b * rows, (b + 1) * rows) for b in range(3)]
    on_plus[block[0]] = own_plus[...]
    on_plus[block[1]] = got_plus[block[1]]
    on_plus[block[2]] = got_minus[block[2]]
    on_minus[block[0]] = own_minus[...]
    on_minus[block[1]] = got_minus[block[1]]
    on_minus[block[2]] = got_plus[block[2]]


def message_shapes(rows):
    return [jax.ShapeDtypeStruct((rows * blocks, MSG), f32) for blocks in (3, 3, 1, 1, 1)]


def far_table(devices, part, messages):
    rows = []
    for k in range(PARTNERS):
        message, at = take(messages, k, devices)
        rows.append(message[at + part * REQ : at + (part + 1) * REQ, :])
    rows.append(jnp.zeros((FAR - PARTNERS * REQ, MSG), f32))
    turned = jnp.concatenate(rows, axis=0).T[:PACK]
    return jnp.concatenate(split(turned), axis=0)


def take_turns(*chains):
    results = [None] * len(chains)
    going = list(range(len(chains)))
    while going:
        for n in list(going):
            try:
                next(chains[n])
            except StopIteration as stop:
                results[n] = stop.value
                going.remove(n)
    return results


def alone(chain):
    return take_turns(chain)[0]


class Window:
    def __init__(self, ref, begin, width):
        self.ref, self.begin = ref, begin
        self.shape = tuple(ref.shape[:-1]) + (width,)

    def _at(self, index):
        rank = len(self.shape)
        if index is Ellipsis:
            index = ()
        index = index if isinstance(index, tuple) else (index,)
        index = index + (slice(None),) * (rank - len(index))
        low, high, _ = index[-1].indices(self.shape[-1])
        return index[:-1] + (slice(self.begin + low, self.begin + high),)

    def __getitem__(self, index):
        return self.ref[self._at(index)]

    def __setitem__(self, index, value):
        self.ref[self._at(index)] = value


def lanes(tile):
    return slice(tile * LANES, (tile + 1) * LANES)


def jacobian_apply(jac, tile, parts):
    result = [None] * NV
    for group in range(3):
        for d in range(3):
            for inner in range(3):
                q = 3 * group + inner
                value = parts(d, q)
                for p in range(NV):
                    term = jac[p, q, d : d + 1, lanes(tile)] * value
                    result[p] = term if result[p] is None else result[p] + term
    return result


def packed_split(fields, group):
    packed = [pack_three(tile[3 * group : 3 * group + 3]) for tile in fields]
    return split(jnp.concatenate(packed, axis=1))


def split_fields(fields):
    pairs = [packed_split(fields, group) for group in range(3)]
    return jnp.concatenate([a for a, _ in pairs] + [b for _, b in pairs], axis=0)


def predict_chain(start, jac, w_pred, scales):
    tiles = range(len(start))
    sums = [[[s[0] * x for x in tile] for tile in start] for s in scales]
    now = start
    for degree in range(1, NORDER):
        turned = [dot(w_pred, stacked(*packed_split(now, group))) for group in range(3)]
        yield
        now = [
            jacobian_apply(
                jac, t, lambda d, q: turned[q // 3][d * 72 + (q % 3) * NBP : d * 72 + (q % 3) * NBP + NBP, lanes(t)]
            )
            for t in tiles
        ]
        sums = [
            [[a + s[degree] * x for a, x in zip(total[t], now[t])] for t in tiles] for total, s in zip(sums, scales)
        ]
    return sums


def predict(*args):
    return alone(predict_chain(*args))


def face_products(gathered, at_face, table, tiles):
    outers = []
    for t in tiles:
        outer = [None] * NV
        for b in range(NB):
            values = table[b * NQ : (b + 1) * NQ, lanes(t)]
            for p in range(NV):
                at = packed_row(p, b)
                term = gathered[at_face, at : at + 1, lanes(t)] * values
                outer[p] = term if outer[p] is None else outer[p] + term
        outers.append(outer)
    return [
        stacked(*split(jnp.concatenate([jnp.concatenate(o[3 * g : 3 * g + 3], axis=0) for o in outers], axis=1)))
        for g in range(3)
    ]


def table_of(code, w_table):
    hot = one_hot(iota((16, code.shape[1]), 0).astype(f32) == code)
    return dot(w_table, jnp.concatenate([hot, hot], axis=0))


def near_chain(own, near, small, aux, w_own, w_lift, w_table, gathered):
    count = own.shape[1]
    tiles = range(count // LANES)
    slots = iota((KEEP, count), 0).astype(jnp.int16)

    def gather(face):
        index = jnp.broadcast_to(aux[face : face + 1, :], (16, count)).astype(jnp.int16)
        index = jnp.concatenate([index] * (KEEP // 16), axis=0)
        both = dot(near[...], jnp.where(slots == index, jnp.ones((), bf16), jnp.zeros((), bf16)))
        gathered[face, :, :count] = both[:PACK] + both[PACK:]
        return table_of(small[ORIENT + face : ORIENT + face + 1, :], w_table)

    table = gather(0)
    mine = []
    for group in range(3):
        rows = slice(64 * group, 64 * group + 64)
        lower = slice(PACK + 64 * group, PACK + 64 * group + 64)
        mine.append(dot(w_own, stacked(own[rows], own[lower])))

    def of_own(block, q, t):
        at = block * 72 + (q % 3) * NBP
        return mine[q // 3][at : at + NBP, lanes(t)]

    yield
    volume = [[[of_own(d, q, t) for q in range(NV)] for d in range(3)] for t in tiles]
    upwind = [[of_own(7, q, t) for q in range(NV)] for t in tiles]
    for face in range(4):
        now = table
        if face < 3:
            table = gather(face + 1)
            yield
        for group, points in enumerate(face_products(gathered, face, now, tiles)):
            lifted = dot(w_lift[face], points)
            for t in tiles:
                for inner in range(3):
                    q = 3 * group + inner
                    at = inner * NBP
                    mixed = lifted[at : at + NBP, lanes(t)] + of_own(3 + face, q, t)
                    upwind[t][q] = upwind[t][q] + lifted[72 + at : 72 + at + NBP, lanes(t)]
                    for d in range(3):
                        normal = small[3 * face + d : 3 * face + d + 1, lanes(t)]
                        volume[t][d][q] = volume[t][d][q] + normal * mixed
    return volume, upwind


def near_part(*args):
    return alone(near_chain(*args))


def update_chain(parts, far, small, aux, jac, w_far, w_table, gathered):
    volume, upwind = parts
    tiles = range(len(volume))
    count = len(volume) * LANES
    place = aux[4:5, :]
    both = dot(far, one_hot(iota((FAR, count), 0) == place))
    gathered[0, :, :count] = both[:PACK] + both[PACK:]
    masks = [jnp.where((aux[face : face + 1, :] < 0) & (place >= 0), 1.0, 0.0) for face in range(4)]
    code = masks[0] * small[ORIENT : ORIENT + 1, :]
    normals = [masks[0] * small[d : d + 1, :] for d in range(3)]
    for face in range(1, 4):
        code = code + masks[face] * small[ORIENT + face : ORIENT + face + 1, :]
        normals = [n + masks[face] * small[3 * face + d : 3 * face + d + 1, :] for d, n in enumerate(normals)]
    changes = [[None] * NV for t in tiles]
    table = table_of(code, w_table)
    yield
    volume = [[list(v) for v in tile] for tile in volume]
    upwind = [list(tile) for tile in upwind]
    for group, points in enumerate(face_products(gathered, 0, table, tiles)):
        lifted = dot(w_far, points)
        for t in tiles:
            for inner in range(3):
                q = 3 * group + inner
                mixed = None
                for face in range(4):
                    at = 72 * face + inner * NBP
                    term = masks[face][:, lanes(t)] * lifted[at : at + NBP, lanes(t)]
                    mixed = term if mixed is None else mixed + term
                upwind[t][q] = upwind[t][q] - mixed
                for d in range(3):
                    volume[t][d][q] = volume[t][d][q] + normals[d][:, lanes(t)] * mixed
    for t in tiles:
        change = jacobian_apply(jac, t, lambda d, q: volume[t][d][q])
        speed = small[SPEED : SPEED + 1, lanes(t)]
        changes[t] = [c + speed * u for c, u in zip(change, upwind[t])]
    return changes


def update(*args):
    return alone(update_chain(*args))


def store_parts(ref, parts):
    volume, upwind = parts
    for t in range(len(volume)):
        for q in range(NV):
            for d in range(3):
                ref[d * NV + q, :, lanes(t)] = volume[t][d][q]
            ref[3 * NV + q, :, lanes(t)] = upwind[t][q]


def load_parts(ref):
    tiles = range(ref.shape[2] // LANES)
    volume = [[[ref[d * NV + q, :, lanes(t)] for q in range(NV)] for d in range(3)] for t in tiles]
    return volume, [[ref[3 * NV + q, :, lanes(t)] for q in range(NV)] for t in tiles]


def load_state(q, padded):
    padded[:, NB:NBP, :] = jnp.zeros((NV, NBP - NB, padded.shape[2]), f32)
    for p in range(NV):
        padded[p, :NB, :] = q[p]
    return load_field(padded)


def load_field(ref):
    return [[ref[p, :, lanes(t)] for p in range(NV)] for t in range(ref.shape[2] // LANES)]


def store_field(ref, field):
    for t, tile in enumerate(field):
        for p in range(NV):
            ref[p, :, lanes(t)] = tile[p]


def store_result(out, base, change, small):
    for t in range(len(base)):
        occupied = small[OCCUPIED : OCCUPIED + 1, lanes(t)] > 0.5
        for p in range(NV):
            out[p, :, lanes(t)] = jnp.where(occupied, base[t][p] + change[t][p], 0.0)[:NB]


def first_kernel(q, jac, deriv, stiff, evals, lift, packed, slow, w_pred, w_own, w_lift, w_table, w_far, padded, square):
    @pl.when(pl.program_id(0) == 0)
    def _():
        make_weights(deriv, stiff, evals, lift, w_pred, w_own, w_lift, w_table, w_far, square)

    first_fields(q, jac, w_pred, packed, slow, padded)


def first_fields(q, jac, w_pred, packed, slow, padded):
    weights = w_pred[...]
    windows = [[Window(r, begin, WIDE) for r in (q, jac, packed, slow, padded)] for begin in range(0, BOTH, WIDE)]
    chains = [predict_chain(load_state(w[0], w[4]), w[1], weights, [FIRST, SECOND]) for w in windows]
    for (_, _, packed, slow, _), (first, later) in zip(windows, take_turns(*chains)):
        packed[...] = split_fields(first)
        store_field(slow, later)


def near_kernel(own, near, small, aux, w_own, w_lift, w_table, *refs):
    parts, gathered = refs[-2:]
    weights = w_own[...], w_lift, w_table[...]
    chains = []
    for begin in range(0, BOTH, WIDE):
        window = [Window(r, begin, WIDE) for r in (own, small, aux, gathered)]
        chains.append(near_chain(window[0][...], near, window[1], window[2], *weights, window[3]))
    for begin, values in zip(range(0, BOTH, WIDE), take_turns(*chains)):
        store_parts(Window(parts, begin, WIDE), values)


def middle_chain(start, parts, jac, small, slow, far, aux, w_pred, w_far, w_table, gathered):
    change = yield from update_chain(parts, far, small, aux, jac, w_far, w_table, gathered)
    base, midway, second = [], [], []
    fast = [small[CLUSTER : CLUSTER + 1, lanes(t)] < 0.5 for t in range(len(start))]
    for t in range(len(start)):
        base.append([a + b for a, b in zip(start[t], change[t])])
        midway.append([jnp.where(fast[t], a, b) for a, b in zip(base[t], start[t])])
    (later,) = yield from predict_chain(midway, jac, w_pred, [FIRST])
    for t in range(len(start)):
        second.append([jnp.where(fast[t], a, b) for a, b in zip(later[t], slow[t])])
    return base, split_fields(second)


def middle_step(*args):
    return alone(middle_chain(*args))


def middle_kernel(devices, steps, q, jac, small, slow, parts, near, aux, asks, *refs):
    messages = refs[:5]
    w_pred, w_far, w_table, base, packed, *outs, padded, gathered, far = refs[5:]
    step = pl.program_id(0)

    @pl.when(step == 0)
    def _():
        far[...] = far_table(devices, 0, messages)

    weights = w_pred[...], w_far[...], w_table[...]
    table = far[...]
    chains, bases = [], []
    for begin in range(0, BOTH, WIDE):
        w = [Window(r, begin, WIDE) for r in (q, padded, parts, jac, small, slow, aux, gathered, base)]
        state = load_state(w[0], w[1])
        chains.append(
            middle_chain(state, load_parts(w[2]), w[3], w[4], load_field(w[5]), table, w[6], *weights, w[7])
        )
        bases.append(w[8])
    results = take_turns(*chains)
    for window, (now, _) in zip(bases, results):
        store_field(window, now)
    second = jnp.concatenate([values for _, values in results], axis=1)
    packed[:, pl.ds(pl.multiple_of(step * BOTH, BOTH), BOTH)] = second

    @pl.when(step == steps - 1)
    def _():
        answer_again(devices, asks, messages, near[...], packed[:, :KEEP], outs)


def last_kernel(
    devices, steps, base, jac, small, parts, aux, q_moved, jac_moved, small_moved, aux_moved, near, later, *refs
):
    messages = refs[:5]
    w_pred, w_own, w_lift, w_table, w_far, out, padded, gathered, far = refs[5:]
    step = pl.program_id(0)

    @pl.when(step == 0)
    def _():
        far[...] = far_table(devices, 0, messages)

    @pl.when(step < steps)
    def _():
        change = update(load_parts(parts), far[...], small, aux, jac, w_far[...], w_table[...], gathered)
        store_result(out, load_field(base), change, small)

    @pl.when(step == steps)
    def _():
        start = load_state(q_moved, padded)
        first, slow = predict(start, jac_moved, w_pred[...], [FIRST, SECOND])
        of_near = w_own[...], w_lift, w_table[...]
        own = near_part(split_fields(first), near, small_moved, aux_moved, *of_near, gathered)
        now, second = middle_step(
            start, own, jac_moved, small_moved, slow, far_table(devices, 1, messages), aux_moved,
            w_pred[...], w_far[...], w_table[...], gathered,
        )
        own = near_part(second, later, small_moved, aux_moved, *of_near, gathered)
        change = update(own, far[...], small_moved, aux_moved, jac_moved, w_far[...], w_table[...], gathered)
        store_result(out, now, change, small_moved)


def whole_spec(array):
    rank = array.ndim
    return pl.BlockSpec(array.shape, lambda i: (0,) * rank)


def lane_spec(*lead, last=None):
    rank = len(lead)
    if last is None:
        return pl.BlockSpec(lead + (WIDE,), lambda i: (0,) * rank + (i,))
    return pl.BlockSpec(lead + (WIDE,), lambda i: (0,) * rank + (jnp.minimum(i, last),))


Q_SPEC = lane_spec(NV, NB)
J_SPEC = lane_spec(NV, NV, 3)
S_SPEC = lane_spec(SMALL)
A_SPEC = lane_spec(8)
F_SPEC = lane_spec(NV, NBP)
X_SPEC = lane_spec(2 * PACK)
N_SPEC = pl.BlockSpec((2 * PACK, KEEP), lambda i: (0, 0))


def scratch_of(width):
    return pltpu.VMEM((NV, NBP, width), f32), pltpu.VMEM((4, PACK, width), f32)


def per_device(
    element_freedom_values,
    scaled_jacobian_matrices,
    outward_face_normals,
    largest_wave_speed,
    element_cluster_index,
    element_new_slot,
    neighbours,
    face_rotation_codes,
    deriv_mats,
    stiff_mats,
    face_eval,
    face_lift,
):
    count = element_freedom_values.shape[2]
    steps = count // WIDE
    devices = lax.axis_size("dom")
    q = element_freedom_values
    jac = jnp.transpose(scaled_jacobian_matrices, (1, 2, 0, 3))

    def shift(array, by):
        return lax.ppermute(array, "dom", [(i, (i + by) % devices) for i in range(devices)])

    def swap(array, groups):
        return lax.all_to_all(array, "dom", split_axis=0, concat_axis=0, axis_index_groups=groups, tiled=True)

    def on_ring(body):
        def kernel(*refs):
            body(devices, *refs)

        return kernel

    small, aux, asks, group, one = prepare(
        jnp.transpose(outward_face_normals, (1, 0, 2)),
        largest_wave_speed[None],
        element_cluster_index[None],
        element_new_slot[None],
        neighbours,
        face_rotation_codes,
        q,
        jac,
        devices,
    )
    asks = swap(asks, None)
    asks, group, one = lax.optimization_barrier((asks, group, one))
    stride = devices // GROUPS
    group = swap(group, [[r + stride * j for j in range(GROUPS)] for r in range(stride)])
    one = shift(one, 1)
    padded, gathered = scratch_of(WIDE)
    packed_shape = jax.ShapeDtypeStruct((2 * PACK, count), bf16)
    field_shape = jax.ShapeDtypeStruct((NV, NBP, count), f32)
    far = pltpu.VMEM((2 * PACK, FAR), bf16)
    weight_shapes = [
        jax.ShapeDtypeStruct((ROWS, PACK), bf16),
        jax.ShapeDtypeStruct((576, PACK), bf16),
        jax.ShapeDtypeStruct((4, 144, 144), bf16),
        jax.ShapeDtypeStruct((320, 32), bf16),
        jax.ShapeDtypeStruct((288, 144), bf16),
    ]
    evals = jnp.transpose(face_eval, (0, 2, 1)).reshape(12 * NQ, NB)
    matrices = [deriv_mats, stiff_mats, evals, face_lift]
    halves = count // BOTH

    def part_spec(begin, *lead):
        rank = len(lead)
        return pl.BlockSpec(lead + (BOTH,), lambda i: (0,) * rank + (i + begin,))

    twice = scratch_of(BOTH)
    first, slow, w_pred, w_own, w_lift, w_table, w_far = pl.pallas_call(
        first_kernel,
        grid=(halves,),
        in_specs=[part_spec(0, NV, NB), part_spec(0, NV, NV, 3)] + [whole_spec(m) for m in matrices],
        out_specs=[part_spec(0, 2 * PACK), part_spec(0, NV, NBP)] + [whole_spec(w) for w in weight_shapes],
        out_shape=[packed_shape, field_shape] + weight_shapes,
        scratch_shapes=[twice[0], pltpu.VMEM((LANES, LANES), f32)],
        compiler_params=MOST,
        name="first",
    )(q, jac, *matrices)

    moved_shapes = [
        jax.ShapeDtypeStruct((NV, NB, LANES), f32),
        jax.ShapeDtypeStruct((NV, NV, 3, LANES), f32),
        jax.ShapeDtypeStruct((SMALL, LANES), f32),
        jax.ShapeDtypeStruct((8, LANES), i32),
    ]
    out_shape = moved_shapes + message_shapes(MESSAGE1)
    *moved, m0, m1, m2, m3, m4 = pl.pallas_call(
        on_ring(unpack_kernel),
        grid=(1,),
        in_specs=[whole_spec(a) for a in (group, one, asks)] + [N_SPEC],
        out_specs=[whole_spec(o) for o in out_shape],
        out_shape=out_shape,
        compiler_params=MOST,
        name="unpack",
    )(group, one, asks, first)
    of_near = [w_own, w_lift, w_table]
    parts_shape = jax.ShapeDtypeStruct((4 * NV, NBP, count), f32)

    def near_steps(field, begin, number, parts):
        def spec(*lead):
            return part_spec(begin, *lead)

        return pl.pallas_call(
            near_kernel,
            grid=(number,),
            in_specs=[spec(2 * PACK), N_SPEC, spec(SMALL), spec(8)]
            + [whole_spec(w) for w in of_near]
            + [pl.BlockSpec(memory_space=pl.ANY)] * len(parts),
            out_specs=spec(4 * NV, NBP),
            out_shape=parts_shape,
            scratch_shapes=[twice[1]],
            input_output_aliases={7: 0} if parts else {},
            cost_estimate=pl.CostEstimate(flops=int(4e9) * number, bytes_accessed=4 << 20, transcendentals=0),
            compiler_params=PARAMS,
            name="near",
        )(field, field, small, aux, *of_near, *parts)

    def exchange_beside(answers, field):
        half = halves // 2
        plus, minus, own_plus, own_minus, opposite = answers
        got_plus, got_minus, opposite = shift(plus, 1), shift(minus, -1), shift(opposite, devices // 2)
        parts = near_steps(field, 0, half, [])
        got_plus, got_minus, opposite, parts = lax.optimization_barrier((got_plus, got_minus, opposite, parts))
        on_plus, on_minus = pl.pallas_call(
            relay_kernel,
            out_shape=[jax.ShapeDtypeStruct(plus.shape, f32)] * 2,
            compiler_params=pltpu.CompilerParams(vmem_limit_bytes=4 << 20),
            name="relay",
        )(got_plus, got_minus, own_plus, own_minus)
        on_plus, on_minus = shift(on_plus, 3), shift(on_minus, -3)
        parts = near_steps(field, half, halves - half, [parts])
        return (got_plus, got_minus, on_plus, on_minus, opposite), parts

    messages, parts = exchange_beside((m0, m1, m2, m3, m4), first)

    def middle(*refs):
        middle_kernel(devices, halves, *refs)

    weights = [w_pred, w_far, w_table]
    out_shape = [field_shape, packed_shape] + message_shapes(2 * REQ)
    base, second, *answers = pl.pallas_call(
        middle,
        grid=(halves,),
        in_specs=[
            part_spec(0, NV, NB),
            part_spec(0, NV, NV, 3),
            part_spec(0, SMALL),
            part_spec(0, NV, NBP),
            part_spec(0, 4 * NV, NBP),
            N_SPEC,
            part_spec(0, 8),
            whole_spec(asks),
        ]
        + [whole_spec(a) for a in (*messages, *weights)],
        out_specs=[part_spec(0, NV, NBP)] + [whole_spec(o) for o in out_shape[1:]],
        out_shape=out_shape,
        scratch_shapes=[*twice, far],
        compiler_params=PARAMS,
        name="middle",
    )(q, jac, small, slow, parts, first, aux, asks, *messages, *weights)
    messages, parts = exchange_beside(answers, second)

    def last(*refs):
        last_kernel(devices, steps, *refs)

    end = steps - 1
    weights = [w_pred, w_own, w_lift, w_table, w_far]
    return pl.pallas_call(
        last,
        grid=(steps + 1,),
        in_specs=[
            lane_spec(NV, NBP, last=end),
            lane_spec(NV, NV, 3, last=end),
            lane_spec(SMALL, last=end),
            lane_spec(4 * NV, NBP, last=end),
            lane_spec(8, last=end),
        ]
        + [whole_spec(a) for a in moved]
        + [N_SPEC, N_SPEC]
        + [whole_spec(a) for a in (*messages, *weights)],
        out_specs=Q_SPEC,
        out_shape=jax.ShapeDtypeStruct((NV, NB, PARTITION_SLOTS), f32),
        scratch_shapes=[scratch_of(LANES)[0], gathered, far],
        compiler_params=PARAMS,
        name="last",
    )(base, jac, small, parts, aux, *moved, first, second, *messages, *weights)


def solution(mesh):
    placed = (
        P(None, None, "dom"),
        P(None, None, None, "dom"),
        P(None, None, "dom"),
        P("dom"),
        P("dom"),
        P("dom"),
        P(None, "dom"),
        P(None, "dom"),
        P(),
        P(),
        P(),
        P(),
    )
    return jax.shard_map(
        per_device, mesh=mesh, in_specs=placed, out_specs=P(None, None, "dom"), check_vma=False
    )
```

```python
import math

import jax
import jax.numpy as jnp
from jax import lax
from jax.experimental import pallas as pl
from jax.experimental.pallas import tpu as pltpu
from jax.sharding import PartitionSpec as P

NV = 9
NB = 20
NBP = 24
NQ = 16
NORDER = 4
GROUPS = 8
CSZ = 16
KEEP = 896
PARTITION_SLOTS = 1152
REQ = 32
PARTNERS = 9
ASKS = 16
LANES = 128
WIDE = 256
BOTH = 512
ROWS = 216
JAC_END = ROWS + 4 * NV * NV
PACK = 192
MSG = 256
FAR = 384
RECORD = 640
SMALL = 24
MESSAGE1 = REQ + 8

step_fast = 0.25
exact = lax.Precision.HIGHEST
f32 = jnp.float32
bf16 = jnp.bfloat16
i32 = jnp.int32

SPEED, CLUSTER, LINK, ORIENT, OCCUPIED = 12, 13, 14, 18, 22

MOST = pltpu.CompilerParams(vmem_limit_bytes=60 << 20)
PARAMS = pltpu.CompilerParams(vmem_limit_bytes=20 << 20)


def coefficients(lower, upper):
    return [
        (upper ** (degree + 1) - lower ** (degree + 1)) / math.factorial(degree + 1)
        for degree in range(NORDER)
    ]


FIRST = coefficients(0.0, step_fast)
SECOND = coefficients(step_fast, 2.0 * step_fast)


def partner_offsets(devices):
    return [1, 2, 3, 4, -1, -2, -3, -4, devices // 2]


def packed_row(quantity, basis):
    group, member = quantity // 3, quantity % 3
    inside = 16 * member + basis if basis < 16 else 48 + 4 * member + (basis - 16)
    return 64 * group + inside


def pack_three(members):
    a, b, c = members
    tail = a[16:24] + pltpu.roll(b[16:24], 4, 0)
    return jnp.concatenate([a[:16], b[:16], c[:16], tail, c[16:24]], axis=0)


def split(values):
    high = values.astype(bf16)
    low = (values - high.astype(f32)).astype(bf16)
    return high, low


def stacked(high, low):
    return jnp.concatenate([high, low, high], axis=0)


def dot(a, b):
    return jnp.dot(a, b, preferred_element_type=f32)


def dot_last(a, b):
    return lax.dot_general(a, b, (((1,), (1,)), ((), ())), preferred_element_type=f32)


def iota(shape, axis):
    return lax.broadcasted_iota(i32, shape, axis)


def one_hot(condition):
    return jnp.where(condition, 1.0, 0.0).astype(bf16)


def make_weights(deriv, stiff, evals, lift, w_pred, w_own, w_lift, w_table, w_far, square):
    def turned(matrix, rows, columns):
        square[...] = jnp.zeros((LANES, LANES), f32)
        square[:rows, :columns] = matrix
        return square[...].T[:NBP]

    column = iota((LANES, PACK), 1) & 63
    member = jnp.where(column < 48, column >> 4, (column - 48) >> 2)
    basis = jnp.where(column < 48, column & 15, 16 + (column & 3))
    spread = one_hot(iota((LANES, PACK), 0) == jnp.where(member < 3, basis, -1))
    member = member[:NBP]
    part = iota((NBP, PACK), 1)

    def three(matrix):
        high, low = split(turned(matrix, NB, NB))
        row = jnp.where(part < 128, dot(high, spread), dot(low, spread))
        return [jnp.where(member == inner, row, 0.0) for inner in range(3)]

    blocks = []
    for axis in range(3):
        blocks += three(-deriv[axis])
    w_pred[...] = jnp.concatenate(blocks, axis=0).astype(bf16)

    own = [
        lax.dot_general(
            evals[48 * face : 48 * face + NQ, :],
            lift[face],
            (((0,), (0,)), ((), ())),
            precision=exact,
            preferred_element_type=f32,
        )
        for face in range(4)
    ]
    blocks = []
    for matrix in [stiff[axis] for axis in range(3)] + own + [own[0] + own[1] + own[2] + own[3]]:
        blocks += three(matrix if len(blocks) < 9 else -0.5 * matrix)
    w_own[...] = jnp.concatenate(blocks, axis=0).astype(bf16)

    column = iota((LANES, 144), 1)
    spread = one_hot(iota((LANES, 144), 0) == (column & 15))
    column = column[:NBP]
    block = column >> 4
    member = block - jnp.where(column >= 96, 6, jnp.where(column >= 48, 3, 0))
    every = []
    for face in range(4):
        high, low = split(turned(lift[face], NQ, NB))
        row = jnp.where(column < 96, dot(high, spread), dot(low, spread))
        rows = [jnp.where(member == inner, -0.5 * row, 0.0) for inner in range(3)]
        w_lift[face] = jnp.concatenate(rows + [-r for r in rows], axis=0).astype(bf16)
        every += rows
    w_far[...] = jnp.concatenate(every, axis=0).astype(bf16)

    basis_of = one_hot((iota((320, NB), 0) >> 4) == iota((320, NB), 1))
    keep = (iota((320, PACK), 0) & 15) == (iota((320, PACK), 1) & 15)
    code_of = one_hot((iota((PACK, 16), 0) >> 4) == iota((PACK, 16), 1))
    halves = []
    for part_of in split(evals[...]):
        halves.append(dot(jnp.where(keep, dot_last(basis_of, part_of), 0.0).astype(bf16), code_of))
    w_table[:, :16] = halves[0].astype(bf16)
    w_table[:, 16:] = halves[1].astype(bf16)


def find_links(devices, tiles, small, aux, from_top):
    me = lax.axis_index("dom").astype(f32)
    row = iota((ASKS, LANES), 0).astype(f32)
    up_to = one_hot(iota((LANES, LANES), 0) <= iota((LANES, LANES), 1))
    request = (iota((LANES, LANES), 0) & (REQ - 1)).astype(f32)
    carry = jnp.zeros((ASKS, 1), f32)
    wanted = jnp.zeros((2 * ASKS, LANES), f32)
    for tile in range(tiles):
        at = slice(tile * LANES, (tile + 1) * LANES)
        occupied = small[OCCUPIED : OCCUPIED + 1, at] > 0.5
        target = jnp.full((1, LANES), -1.0, f32)
        slots = jnp.zeros((1, LANES), f32)
        for face in range(4):
            link = small[LINK + face : LINK + face + 1, at]
            owner = jnp.floor((link + 0.5) * (1.0 / PARTITION_SLOTS))
            slot = link - owner * PARTITION_SLOTS
            near = owner == me
            aux[face : face + 1, at] = jnp.where(near, slot, -1.0).astype(i32)
            away = occupied & jnp.logical_not(near)
            target = jnp.where(away, owner, target)
            slots = jnp.where(away, slot, slots)
        far = target - me
        far = jnp.where(far < 0, far + devices, far)
        partner = jnp.where(far <= 4, far - 1.0, jnp.where(far >= devices - 4, devices + 3.0 - far, 8.0))
        partner = jnp.where(target >= 0, partner, -1.0)
        named = jnp.where(row == partner, 1.0, 0.0)
        prefix = dot(named.astype(bf16), up_to) + carry
        carry = carry + jnp.sum(named, axis=1, keepdims=True)
        rank = jnp.sum(named * prefix, axis=0, keepdims=True) - 1.0
        if from_top:
            rank = REQ - 1.0 - rank
        aux[4:5, at] = jnp.where(target >= 0, partner * REQ + rank, -1.0).astype(i32)
        aux[5:8, at] = jnp.zeros((3, LANES), i32)
        ask = slots + 1.0
        high = jnp.floor(ask * (1.0 / 32)) * 32.0
        both = jnp.concatenate([named * high, named * (ask - high)], axis=0).astype(bf16)
        wanted = wanted + dot_last(both, one_hot(request == rank))
    return wanted[:ASKS] + wanted[ASKS:]


def prepare_kernel(devices, tiles, normals, speed, cluster, slot, links, orient, q, jac, small, aux, asks, group, one, record):
    me = lax.axis_index("dom")
    for face in range(4):
        small[3 * face : 3 * face + 3, :] = jnp.concatenate([normals[d, face : face + 1, :] for d in range(3)], axis=0)
    small[SPEED : SPEED + 1, :] = speed[...]
    small[CLUSTER : CLUSTER + 1, :] = cluster[...].astype(f32)
    small[LINK : LINK + 4, :] = links[...].astype(f32)
    small[ORIENT : ORIENT + 4, :] = orient[...].astype(f32)
    where = slot[...]
    stays = (where >= me * PARTITION_SLOTS) & (where < (me + 1) * PARTITION_SLOTS)
    small[OCCUPIED : OCCUPIED + 1, :] = jnp.where(stays, 1.0, 0.0)
    small[OCCUPIED + 1 : SMALL, :] = jnp.zeros((1, tiles * LANES), f32)
    wanted = find_links(devices, tiles, small, aux, False)
    asks[...] = jnp.zeros((devices, 1, LANES), f32)
    for k, offset in enumerate(partner_offsets(devices)):
        asks[lax.rem(me + offset + devices, devices)] = wanted[k : k + 1]

    record[...] = jnp.zeros((RECORD, LANES), f32)
    for p in range(NV):
        record[p * NBP : p * NBP + NB] = q[p]
        for inner in range(NV):
            at = ROWS + 4 * (p * NV + inner)
            record[at : at + 3] = jac[p, inner]
    fields = small[:, KEEP:]
    row = iota(fields.shape, 0)
    record[JAC_END : JAC_END + SMALL] = jnp.where(row == OCCUPIED, 1.0 - fields, fields)
    whole = record[...]
    turned = jnp.concatenate([whole[c : c + LANES].T for c in range(0, RECORD, LANES)], axis=1)
    one[...] = turned[:CSZ]
    position = me // (devices // GROUPS)
    for g in range(GROUPS):
        group[lax.rem(position + g, GROUPS)] = turned[g * CSZ : (g + 1) * CSZ]


def prepare(normals, speed, cluster, slot, links, orient, q, jac, devices):
    count = q.shape[2]

    def body(*refs):
        prepare_kernel(devices, count // LANES, *refs)

    last = KEEP // LANES
    return pl.pallas_call(
        body,
        grid=(1,),
        in_specs=[
            whole_spec(normals),
            whole_spec(speed),
            whole_spec(cluster),
            whole_spec(slot),
            whole_spec(links),
            whole_spec(orient),
            pl.BlockSpec((NV, NB, LANES), lambda i: (0, 0, last)),
            pl.BlockSpec((NV, NV, 3, LANES), lambda i: (0, 0, 0, last)),
        ],
        out_specs=[
            pl.BlockSpec((SMALL, count), lambda i: (0, 0)),
            pl.BlockSpec((8, count), lambda i: (0, 0)),
            pl.BlockSpec((devices, 1, LANES), lambda i: (0, 0, 0)),
            pl.BlockSpec((GROUPS, CSZ, RECORD), lambda i: (0, 0, 0)),
            pl.BlockSpec((CSZ, RECORD), lambda i: (0, 0)),
        ],
        out_shape=[
            jax.ShapeDtypeStruct((SMALL, count), f32),
            jax.ShapeDtypeStruct((8, count), i32),
            jax.ShapeDtypeStruct((devices, 1, LANES), f32),
            jax.ShapeDtypeStruct((GROUPS, CSZ, RECORD), f32),
            jax.ShapeDtypeStruct((CSZ, RECORD), f32),
        ],
        scratch_shapes=[pltpu.VMEM((RECORD, LANES), f32)],
        compiler_params=MOST,
        name="prepare",
    )(normals, speed, cluster, slot, links, orient, q, jac)


def unpack(devices, group, one, q, jac, small, aux):
    position = lax.axis_index("dom") // (devices // GROUPS)
    rows = [one[...]]
    for g in range(1, GROUPS):
        rows.append(group[lax.rem(position - g + GROUPS, GROUPS)])
    whole = jnp.concatenate(rows, axis=0)
    turned = jnp.concatenate([whole[:, c : c + LANES].T for c in range(0, RECORD, LANES)], axis=0)
    for p in range(NV):
        q[p] = turned[p * NBP : p * NBP + NB]
        for inner in range(NV):
            at = ROWS + 4 * (p * NV + inner)
            jac[p, inner] = turned[at : at + 3]
    small[...] = turned[JAC_END : JAC_END + SMALL]
    return find_links(devices, 1, small, aux, True)


OUT_BLOCKS = {1: (0, 0), 4: (0, 1), -2: (0, 2), -1: (1, 0), -4: (1, 1), 2: (1, 2), 3: (2, 0), -3: (3, 0)}
IN_BLOCKS = {-1: (0, 0), 1: (1, 0), -3: (2, 0), -4: (2, 1), -2: (2, 2), 3: (3, 0), 4: (3, 1), 2: (3, 2)}


def put(outs, rows, k, devices):
    if k == PARTNERS - 1:
        return outs[4], 0
    array, block = OUT_BLOCKS[-partner_offsets(devices)[k]]
    return outs[array], block * rows


def take(messages, k, devices):
    if k == PARTNERS - 1:
        return messages[4], 0
    array, block = IN_BLOCKS[partner_offsets(devices)[k]]
    rows = messages[4].shape[0]
    return messages[array], block * rows


def picked(requests, fields):
    lane = iota((1, LANES), 1)
    tiles = []
    for at in range(0, 12, 4):
        four = [requests[min(at + n, PARTNERS - 1)] for n in range(4)]
        tiles.append(
            jnp.where(lane < 32, four[0], jnp.where(lane < 64, four[1], jnp.where(lane < 96, four[2], four[3])))
        )
    slots = (iota((KEEP, FAR), 0) + 1).astype(f32)
    return dot(fields, one_hot(slots == jnp.concatenate(tiles, axis=1)))


def message_rows(both):
    value = both[:PACK] + both[PACK:]
    return jnp.concatenate([value, jnp.zeros((MSG - PACK, FAR), f32)], axis=0).T


def back(k):
    return k if k == PARTNERS - 1 else (k + 4) % 8


def requests_here(devices, asks):
    me = lax.axis_index("dom")
    peers = [lax.rem(me - o + devices, devices) for o in partner_offsets(devices)]
    return [asks[p] for p in peers]


def unpack_kernel(devices, group, one, asks, field, q, jac, small, aux, *outs):
    moved = unpack(devices, group, one, q, jac, small, aux)
    rows = message_rows(picked(requests_here(devices, asks), field[...]))
    for k in range(PARTNERS):
        out, at = put(outs, MESSAGE1, k, devices)
        out[at : at + REQ] = rows[k * REQ : (k + 1) * REQ]
        out[at + REQ : at + MESSAGE1, :LANES] = jnp.broadcast_to(moved[back(k) : back(k) + 1, :], (8, LANES))
        out[at + REQ : at + MESSAGE1, LANES:] = jnp.zeros((8, MSG - LANES), f32)


def answer_again(devices, asks, got, field, later, outs):
    moved = []
    for k in range(PARTNERS):
        message, at = take(got, back(k), devices)
        moved.append(message[at + REQ : at + REQ + 1, :LANES])
    every = [a + b for a, b in zip(requests_here(devices, asks), moved)]
    rows = message_rows(picked(every, later))
    rows_first = message_rows(picked(moved, field))
    for k in range(PARTNERS):
        out, at = put(outs, 2 * REQ, k, devices)
        out[at : at + REQ] = rows[k * REQ : (k + 1) * REQ]
        out[at + REQ : at + 2 * REQ] = rows_first[k * REQ : (k + 1) * REQ]


def relay_kernel(got_plus, got_minus, own_plus, own_minus, on_plus, on_minus):
    rows = own_plus.shape[0]
    block = [slice(b * rows, (b + 1) * rows) for b in range(3)]
    on_plus[block[0]] = own_plus[...]
    on_plus[block[1]] = got_plus[block[1]]
    on_plus[block[2]] = got_minus[block[2]]
    on_minus[block[0]] = own_minus[...]
    on_minus[block[1]] = got_minus[block[1]]
    on_minus[block[2]] = got_plus[block[2]]


def message_shapes(rows):
    return [jax.ShapeDtypeStruct((rows * blocks, MSG), f32) for blocks in (3, 3, 1, 1, 1)]


def far_table(devices, part, messages):
    rows = []
    for k in range(PARTNERS):
        message, at = take(messages, k, devices)
        rows.append(message[at + part * REQ : at + (part + 1) * REQ, :])
    rows.append(jnp.zeros((FAR - PARTNERS * REQ, MSG), f32))
    turned = jnp.concatenate(rows, axis=0).T[:PACK]
    return jnp.concatenate(split(turned), axis=0)


def take_turns(*chains):
    results = [None] * len(chains)
    going = list(range(len(chains)))
    while going:
        for n in list(going):
            try:
                next(chains[n])
            except StopIteration as stop:
                results[n] = stop.value
                going.remove(n)
    return results


def alone(chain):
    return take_turns(chain)[0]


class Window:
    def __init__(self, ref, begin, width):
        self.ref, self.begin = ref, begin
        self.shape = tuple(ref.shape[:-1]) + (width,)

    def _at(self, index):
        rank = len(self.shape)
        if index is Ellipsis:
            index = ()
        index = index if isinstance(index, tuple) else (index,)
        index = index + (slice(None),) * (rank - len(index))
        low, high, _ = index[-1].indices(self.shape[-1])
        return index[:-1] + (slice(self.begin + low, self.begin + high),)

    def __getitem__(self, index):
        return self.ref[self._at(index)]

    def __setitem__(self, index, value):
        self.ref[self._at(index)] = value


def lanes(tile):
    return slice(tile * LANES, (tile + 1) * LANES)


def jacobian_apply(jac, tile, parts):
    result = [None] * NV
    for group in range(3):
        for d in range(3):
            for inner in range(3):
                q = 3 * group + inner
                value = parts(d, q)
                for p in range(NV):
                    term = jac[p, q, d : d + 1, lanes(tile)] * value
                    result[p] = term if result[p] is None else result[p] + term
    return result


def packed_split(fields, group):
    packed = [pack_three(tile[3 * group : 3 * group + 3]) for tile in fields]
    return split(jnp.concatenate(packed, axis=1))


def split_fields(fields):
    pairs = [packed_split(fields, group) for group in range(3)]
    return jnp.concatenate([a for a, _ in pairs] + [b for _, b in pairs], axis=0)


def predict(chains, w_pred):
    for state, _, sums in chains:
        for ref, scale in sums:
            for p in range(NV):
                ref[p] = scale[0] * state[p]

    def degree_step(degree, carry):
        turned = []
        for state, _, _ in chains:
            now = load_field(state)
            turned.append([dot(w_pred[...], stacked(*packed_split(now, group))) for group in range(3)])
        for (state, jac, sums), of in zip(chains, turned):
            scales = [jnp.where(degree == 1, s[1], jnp.where(degree == 2, s[2], s[3])) for _, s in sums]
            for t in range(state.shape[2] // LANES):
                at = lanes(t)
                result = jacobian_apply(
                    jac, t, lambda d, q: of[q // 3][d * 72 + (q % 3) * NBP : d * 72 + (q % 3) * NBP + NBP, at]
                )
                for p in range(NV):
                    state[p, :, at] = result[p]
                    for (ref, _), scale in zip(sums, scales):
                        ref[p, :, at] = ref[p, :, at] + scale * result[p]
        return carry

    lax.fori_loop(1, NORDER, degree_step, 0)


def face_products(gathered, table, tiles):
    outers = []
    for t in tiles:
        outer = [None] * NV
        for b in range(NB):
            values = table[b * NQ : (b + 1) * NQ, lanes(t)]
            for p in range(NV):
                at = packed_row(p, b)
                term = gathered[at : at + 1, lanes(t)] * values
                outer[p] = term if outer[p] is None else outer[p] + term
        outers.append(outer)
    return [
        stacked(*split(jnp.concatenate([jnp.concatenate(o[3 * g : 3 * g + 3], axis=0) for o in outers], axis=1)))
        for g in range(3)
    ]


def table_of(code, w_table):
    hot = one_hot(iota((16, code.shape[1]), 0).astype(f32) == code)
    return dot(w_table, jnp.concatenate([hot, hot], axis=0))


class NearChain:
    def __init__(self, near, weights, small, aux, gathered, table, by_face, parts):
        self.near, self.small, self.aux, self.gathered, self.table = near, small, aux, gathered, table
        self.by_face, self.parts = by_face, parts
        self.w_own, self.w_lift, self.w_table = weights
        self.count = aux.shape[-1]
        self.tiles = range(self.count // LANES)

    def begin(self, own):
        for group in range(3):
            rows = slice(64 * group, 64 * group + 64)
            lower = slice(PACK + 64 * group, PACK + 64 * group + 64)
            mine = dot(self.w_own[...], stacked(own[rows], own[lower]))
            for inner in range(3):
                q = 3 * group + inner
                of = [mine[72 * block + NBP * inner : 72 * block + NBP * inner + NBP] for block in range(8)]
                for d in range(3):
                    self.parts[d * NV + q] = of[d]
                for face in range(4):
                    self.by_face[face, q] = of[3 + face]
                self.parts[3 * NV + q] = of[7]

    def gather(self, face):
        count = self.count
        slots = iota((KEEP, count), 0).astype(jnp.int16)
        index = jnp.broadcast_to(self.aux[pl.ds(face, 1), :], (16, count)).astype(jnp.int16)
        index = jnp.concatenate([index] * (KEEP // 16), axis=0)
        both = dot(self.near[...], jnp.where(slots == index, jnp.ones((), bf16), jnp.zeros((), bf16)))
        self.gathered[...] = both[:PACK] + both[PACK:]
        self.table[...] = table_of(self.small[pl.ds(ORIENT + face, 1), :], self.w_table[...])

    def products(self, face):
        normals = [self.small[pl.ds(3 * face + d, 1), :] for d in range(3)]
        for group, points in enumerate(face_products(self.gathered, self.table, self.tiles)):
            lifted = dot(self.w_lift[face], points)
            for inner in range(3):
                q = 3 * group + inner
                at = inner * NBP
                mixed = lifted[at : at + NBP] + self.by_face[face, q]
                self.parts[3 * NV + q] = self.parts[3 * NV + q] + lifted[72 + at : 72 + at + NBP]
                for d in range(3):
                    self.parts[d * NV + q] = self.parts[d * NV + q] + normals[d] * mixed


def near_part(chains, owns):
    chains[0].gather(0)
    for chain, own in zip(chains, owns):
        chain.begin(own)

    def face_step(face, carry):
        for other in chains[1:]:
            other.gather(face)
        chains[0].products(face)
        chains[0].gather((face + 1) & 3)
        for other in chains[1:]:
            other.products(face)
        return carry

    lax.fori_loop(0, 4, face_step, 0)


def update_chain(parts, far, small, aux, jac, w_far, w_table, gathered):
    volume, upwind = parts
    tiles = range(len(volume))
    count = len(volume) * LANES
    place = aux[4:5, :]
    both = dot(far, one_hot(iota((FAR, count), 0) == place))
    gathered[...] = both[:PACK] + both[PACK:]
    masks = [jnp.where((aux[face : face + 1, :] < 0) & (place >= 0), 1.0, 0.0) for face in range(4)]
    code = masks[0] * small[ORIENT : ORIENT + 1, :]
    normals = [masks[0] * small[d : d + 1, :] for d in range(3)]
    for face in range(1, 4):
        code = code + masks[face] * small[ORIENT + face : ORIENT + face + 1, :]
        normals = [n + masks[face] * small[3 * face + d : 3 * face + d + 1, :] for d, n in enumerate(normals)]
    changes = [[None] * NV for t in tiles]
    table = table_of(code, w_table)
    yield
    volume = [[list(v) for v in tile] for tile in volume]
    upwind = [list(tile) for tile in upwind]
    for group, points in enumerate(face_products(gathered, table, tiles)):
        lifted = dot(w_far, points)
        for t in tiles:
            for inner in range(3):
                q = 3 * group + inner
                mixed = None
                for face in range(4):
                    at = 72 * face + inner * NBP
                    term = masks[face][:, lanes(t)] * lifted[at : at + NBP, lanes(t)]
                    mixed = term if mixed is None else mixed + term
                upwind[t][q] = upwind[t][q] - mixed
                for d in range(3):
                    volume[t][d][q] = volume[t][d][q] + normals[d][:, lanes(t)] * mixed
    for t in tiles:
        change = jacobian_apply(jac, t, lambda d, q: volume[t][d][q])
        speed = small[SPEED : SPEED + 1, lanes(t)]
        changes[t] = [c + speed * u for c, u in zip(change, upwind[t])]
    return changes


def update(*args):
    return alone(update_chain(*args))


def load_parts(ref):
    tiles = range(ref.shape[2] // LANES)
    volume = [[[ref[d * NV + q, :, lanes(t)] for q in range(NV)] for d in range(3)] for t in tiles]
    return volume, [[ref[3 * NV + q, :, lanes(t)] for q in range(NV)] for t in tiles]


def load_state(q, padded):
    padded[:, NB:NBP, :] = jnp.zeros((NV, NBP - NB, padded.shape[2]), f32)
    for p in range(NV):
        padded[p, :NB, :] = q[p]
    return load_field(padded)


def load_field(ref):
    return [[ref[p, :, lanes(t)] for p in range(NV)] for t in range(ref.shape[2] // LANES)]


def store_field(ref, field):
    for t, tile in enumerate(field):
        for p in range(NV):
            ref[p, :, lanes(t)] = tile[p]


def store_result(out, base, change, small):
    for t in range(len(base)):
        occupied = small[OCCUPIED : OCCUPIED + 1, lanes(t)] > 0.5
        for p in range(NV):
            out[p, :, lanes(t)] = jnp.where(occupied, base[t][p] + change[t][p], 0.0)[:NB]


def first_kernel(
    q, jac, deriv, stiff, evals, lift, packed, slow, w_pred, w_own, w_lift, w_table, w_far, padded, sums, square
):
    @pl.when(pl.program_id(0) == 0)
    def _():
        make_weights(deriv, stiff, evals, lift, w_pred, w_own, w_lift, w_table, w_far, square)

    load_state(q, padded)
    chains = []
    for begin in range(0, BOTH, WIDE):
        state, jacobians, early, late = [Window(r, begin, WIDE) for r in (padded, jac, sums, slow)]
        chains.append((state, jacobians, [(early, FIRST), (late, SECOND)]))
    predict(chains, w_pred)
    packed[...] = split_fields(load_field(sums))


def near_kernel(own, near, small, aux, w_own, w_lift, w_table, *refs):
    parts, gathered, table, by_face = refs[-4:]
    chains, owns = [], []
    for begin in range(0, BOTH, WIDE):
        windows = [Window(r, begin, WIDE) for r in (small, aux, gathered, table, by_face, parts)]
        chains.append(NearChain(near, (w_own, w_lift, w_table), *windows))
        owns.append(Window(own, begin, WIDE))
    near_part(chains, owns)


def middle_steps(chains, far, w_pred, w_far, w_table):
    updates = []
    for _, parts, jac, small, _, aux, gathered, _, _, _ in chains:
        updates.append(update_chain(load_parts(parts), far, small, aux, jac, w_far, w_table, gathered))
    for chain, change in zip(chains, take_turns(*updates)):
        q, _, _, small, _, _, _, base, state, _ = chain
        start = load_state(q, state)
        for t in range(len(start)):
            fast = small[CLUSTER : CLUSTER + 1, lanes(t)] < 0.5
            for p in range(NV):
                now = start[t][p] + change[t][p]
                base[p, :, lanes(t)] = now
                state[p, :, lanes(t)] = jnp.where(fast, now, start[t][p])
    predict([(chain[8], chain[2], [(chain[9], FIRST)]) for chain in chains], w_pred)
    results = []
    for _, _, _, small, slow, _, _, _, _, sums in chains:
        second = []
        for t, (late, later) in enumerate(zip(load_field(slow), load_field(sums))):
            fast = small[CLUSTER : CLUSTER + 1, lanes(t)] < 0.5
            second.append([jnp.where(fast, a, b) for a, b in zip(later, late)])
        results.append(split_fields(second))
    return results


def middle_kernel(devices, steps, q, jac, small, slow, parts, near, aux, asks, *refs):
    messages = refs[:5]
    w_pred, w_far, w_table, base, packed, *outs, padded, sums, gathered, far = refs[5:]
    step = pl.program_id(0)

    @pl.when(step == 0)
    def _():
        far[...] = far_table(devices, 0, messages)

    refs = (q, parts, jac, small, slow, aux, gathered, base, padded, sums)
    chains = [[Window(r, begin, WIDE) for r in refs] for begin in range(0, BOTH, WIDE)]
    second = jnp.concatenate(middle_steps(chains, far[...], w_pred, w_far[...], w_table[...]), axis=1)
    packed[:, pl.ds(pl.multiple_of(step * BOTH, BOTH), BOTH)] = second

    @pl.when(step == steps - 1)
    def _():
        answer_again(devices, asks, messages, near[...], packed[:, :KEEP], outs)


def last_kernel(
    devices, steps, base, jac, small, parts, aux, q_moved, jac_moved, small_moved, aux_moved, near, later, *refs
):
    messages = refs[:5]
    w_pred, w_own, w_lift, w_table, w_far, out, gathered, far = refs[5:13]
    padded, gathered_moved, table, by_face, parts_moved, early, late, now = refs[13:]
    step = pl.program_id(0)

    @pl.when(step == 0)
    def _():
        far[...] = far_table(devices, 0, messages)

    @pl.when(step < steps)
    def _():
        change = update(load_parts(parts), far[...], small, aux, jac, w_far[...], w_table[...], gathered)
        store_result(out, load_field(base), change, small)

    @pl.when(step == steps)
    def _():
        load_state(q_moved, padded)
        predict([(padded, jac_moved, [(early, FIRST), (late, SECOND)])], w_pred)
        chain = NearChain(
            near, (w_own, w_lift, w_table), small_moved, aux_moved, gathered_moved, table, by_face, parts_moved
        )
        near_part([chain], [split_fields(load_field(early))])
        fields = (q_moved, parts_moved, jac_moved, small_moved, late, aux_moved, gathered_moved, now, padded, early)
        far_first = far_table(devices, 1, messages)
        (second,) = middle_steps([fields], far_first, w_pred, w_far[...], w_table[...])
        chain.near = later
        near_part([chain], [second])
        change = update(
            load_parts(parts_moved), far[...], small_moved, aux_moved, jac_moved, w_far[...], w_table[...],
            gathered_moved,
        )
        store_result(out, load_field(now), change, small_moved)


def whole_spec(array):
    rank = array.ndim
    return pl.BlockSpec(array.shape, lambda i: (0,) * rank)


def lane_spec(*lead, last=None):
    rank = len(lead)
    if last is None:
        return pl.BlockSpec(lead + (WIDE,), lambda i: (0,) * rank + (i,))
    return pl.BlockSpec(lead + (WIDE,), lambda i: (0,) * rank + (jnp.minimum(i, last),))


Q_SPEC = lane_spec(NV, NB)
J_SPEC = lane_spec(NV, NV, 3)
S_SPEC = lane_spec(SMALL)
A_SPEC = lane_spec(8)
F_SPEC = lane_spec(NV, NBP)
X_SPEC = lane_spec(2 * PACK)
N_SPEC = pl.BlockSpec((2 * PACK, KEEP), lambda i: (0, 0))


def padded_scratch(width):
    return pltpu.VMEM((NV, NBP, width), f32)


def gathered_scratch(width):
    return pltpu.VMEM((PACK, width), f32)


def near_scratch(width):
    return [gathered_scratch(width), pltpu.VMEM((320, width), f32), pltpu.VMEM((4, NV, NBP, width), f32)]


def per_device(
    element_freedom_values,
    scaled_jacobian_matrices,
    outward_face_normals,
    largest_wave_speed,
    element_cluster_index,
    element_new_slot,
    neighbours,
    face_rotation_codes,
    deriv_mats,
    stiff_mats,
    face_eval,
    face_lift,
):
    count = element_freedom_values.shape[2]
    steps = count // WIDE
    devices = lax.axis_size("dom")
    q = element_freedom_values
    jac = jnp.transpose(scaled_jacobian_matrices, (1, 2, 0, 3))

    def shift(array, by):
        return lax.ppermute(array, "dom", [(i, (i + by) % devices) for i in range(devices)])

    def swap(array, groups):
        return lax.all_to_all(array, "dom", split_axis=0, concat_axis=0, axis_index_groups=groups, tiled=True)

    def on_ring(body):
        def kernel(*refs):
            body(devices, *refs)

        return kernel

    small, aux, asks, group, one = prepare(
        jnp.transpose(outward_face_normals, (1, 0, 2)),
        largest_wave_speed[None],
        element_cluster_index[None],
        element_new_slot[None],
        neighbours,
        face_rotation_codes,
        q,
        jac,
        devices,
    )
    asks = swap(asks, None)
    asks, group, one = lax.optimization_barrier((asks, group, one))
    stride = devices // GROUPS
    group = swap(group, [[r + stride * j for j in range(GROUPS)] for r in range(stride)])
    one = shift(one, 1)
    packed_shape = jax.ShapeDtypeStruct((2 * PACK, count), bf16)
    field_shape = jax.ShapeDtypeStruct((NV, NBP, count), f32)
    far = pltpu.VMEM((2 * PACK, FAR), bf16)
    weight_shapes = [
        jax.ShapeDtypeStruct((ROWS, PACK), bf16),
        jax.ShapeDtypeStruct((576, PACK), bf16),
        jax.ShapeDtypeStruct((4, 144, 144), bf16),
        jax.ShapeDtypeStruct((320, 32), bf16),
        jax.ShapeDtypeStruct((288, 144), bf16),
    ]
    evals = jnp.transpose(face_eval, (0, 2, 1)).reshape(12 * NQ, NB)
    matrices = [deriv_mats, stiff_mats, evals, face_lift]
    halves = count // BOTH

    def part_spec(begin, *lead):
        rank = len(lead)
        return pl.BlockSpec(lead + (BOTH,), lambda i: (0,) * rank + (i + begin,))

    first, slow, w_pred, w_own, w_lift, w_table, w_far = pl.pallas_call(
        first_kernel,
        grid=(halves,),
        in_specs=[part_spec(0, NV, NB), part_spec(0, NV, NV, 3)] + [whole_spec(m) for m in matrices],
        out_specs=[part_spec(0, 2 * PACK), part_spec(0, NV, NBP)] + [whole_spec(w) for w in weight_shapes],
        out_shape=[packed_shape, field_shape] + weight_shapes,
        scratch_shapes=[padded_scratch(BOTH), padded_scratch(BOTH), pltpu.VMEM((LANES, LANES), f32)],
        compiler_params=MOST,
        name="first",
    )(q, jac, *matrices)

    moved_shapes = [
        jax.ShapeDtypeStruct((NV, NB, LANES), f32),
        jax.ShapeDtypeStruct((NV, NV, 3, LANES), f32),
        jax.ShapeDtypeStruct((SMALL, LANES), f32),
        jax.ShapeDtypeStruct((8, LANES), i32),
    ]
    out_shape = moved_shapes + message_shapes(MESSAGE1)
    *moved, m0, m1, m2, m3, m4 = pl.pallas_call(
        on_ring(unpack_kernel),
        grid=(1,),
        in_specs=[whole_spec(a) for a in (group, one, asks)] + [N_SPEC],
        out_specs=[whole_spec(o) for o in out_shape],
        out_shape=out_shape,
        compiler_params=MOST,
        name="unpack",
    )(group, one, asks, first)
    of_near = [w_own, w_lift, w_table]
    parts_shape = jax.ShapeDtypeStruct((4 * NV, NBP, count), f32)

    def near_steps(field, begin, number, parts):
        def spec(*lead):
            return part_spec(begin, *lead)

        return pl.pallas_call(
            near_kernel,
            grid=(number,),
            in_specs=[spec(2 * PACK), N_SPEC, spec(SMALL), spec(8)]
            + [whole_spec(w) for w in of_near]
            + [pl.BlockSpec(memory_space=pl.ANY)] * len(parts),
            out_specs=spec(4 * NV, NBP),
            out_shape=parts_shape,
            scratch_shapes=near_scratch(BOTH),
            input_output_aliases={7: 0} if parts else {},
            cost_estimate=pl.CostEstimate(flops=int(4e9) * number, bytes_accessed=4 << 20, transcendentals=0),
            compiler_params=PARAMS,
            name="near",
        )(field, field, small, aux, *of_near, *parts)

    def exchange_beside(answers, field):
        half = halves // 2
        plus, minus, own_plus, own_minus, opposite = answers
        got_plus, got_minus, opposite = shift(plus, 1), shift(minus, -1), shift(opposite, devices // 2)
        parts = near_steps(field, 0, half, [])
        got_plus, got_minus, opposite, parts = lax.optimization_barrier((got_plus, got_minus, opposite, parts))
        on_plus, on_minus = pl.pallas_call(
            relay_kernel,
            out_shape=[jax.ShapeDtypeStruct(plus.shape, f32)] * 2,
            compiler_params=pltpu.CompilerParams(vmem_limit_bytes=4 << 20),
            name="relay",
        )(got_plus, got_minus, own_plus, own_minus)
        on_plus, on_minus = shift(on_plus, 3), shift(on_minus, -3)
        parts = near_steps(field, half, halves - half, [parts])
        return (got_plus, got_minus, on_plus, on_minus, opposite), parts

    messages, parts = exchange_beside((m0, m1, m2, m3, m4), first)

    def middle(*refs):
        middle_kernel(devices, halves, *refs)

    weights = [w_pred, w_far, w_table]
    out_shape = [field_shape, packed_shape] + message_shapes(2 * REQ)
    base, second, *answers = pl.pallas_call(
        middle,
        grid=(halves,),
        in_specs=[
            part_spec(0, NV, NB),
            part_spec(0, NV, NV, 3),
            part_spec(0, SMALL),
            part_spec(0, NV, NBP),
            part_spec(0, 4 * NV, NBP),
            N_SPEC,
            part_spec(0, 8),
            whole_spec(asks),
        ]
        + [whole_spec(a) for a in (*messages, *weights)],
        out_specs=[part_spec(0, NV, NBP)] + [whole_spec(o) for o in out_shape[1:]],
        out_shape=out_shape,
        scratch_shapes=[padded_scratch(BOTH), padded_scratch(BOTH), gathered_scratch(BOTH), far],
        compiler_params=PARAMS,
        name="middle",
    )(q, jac, small, slow, parts, first, aux, asks, *messages, *weights)
    messages, parts = exchange_beside(answers, second)

    def last(*refs):
        last_kernel(devices, steps, *refs)

    end = steps - 1
    weights = [w_pred, w_own, w_lift, w_table, w_far]
    return pl.pallas_call(
        last,
        grid=(steps + 1,),
        in_specs=[
            lane_spec(NV, NBP, last=end),
            lane_spec(NV, NV, 3, last=end),
            lane_spec(SMALL, last=end),
            lane_spec(4 * NV, NBP, last=end),
            lane_spec(8, last=end),
        ]
        + [whole_spec(a) for a in moved]
        + [N_SPEC, N_SPEC]
        + [whole_spec(a) for a in (*messages, *weights)],
        out_specs=Q_SPEC,
        out_shape=jax.ShapeDtypeStruct((NV, NB, PARTITION_SLOTS), f32),
        scratch_shapes=[
            gathered_scratch(WIDE),
            far,
            padded_scratch(LANES),
            *near_scratch(LANES),
            pltpu.VMEM((4 * NV, NBP, LANES), f32),
            *[padded_scratch(LANES)] * 3,
        ],
        compiler_params=PARAMS,
        name="last",
    )(base, jac, small, parts, aux, *moved, first, second, *messages, *weights)


def solution(mesh):
    placed = (
        P(None, None, "dom"),
        P(None, None, None, "dom"),
        P(None, None, "dom"),
        P("dom"),
        P("dom"),
        P("dom"),
        P(None, "dom"),
        P(None, "dom"),
        P(),
        P(),
        P(),
        P(),
    )
    return jax.shard_map(
        per_device, mesh=mesh, in_specs=placed, out_specs=P(None, None, "dom"), check_vma=False
    )
```

```python
import math

import jax
import jax.numpy as jnp
from jax import lax
from jax.experimental import pallas as pl
from jax.experimental.pallas import tpu as pltpu
from jax.sharding import PartitionSpec as P

NV = 9
NB = 20
NBP = 24
NQ = 16
NORDER = 4
GROUPS = 8
CSZ = 16
KEEP = 896
PARTITION_SLOTS = 1152
REQ = 32
PARTNERS = 9
ASKS = 16
LANES = 128
WIDE = 256
BOTH = 512
ROWS = 216
JAC_END = ROWS + 4 * NV * NV
PACK = 192
MSG = 256
FAR = 384
RECORD = 640
SMALL = 24
MESSAGE1 = REQ + 8

step_fast = 0.25
exact = lax.Precision.HIGHEST
f32 = jnp.float32
bf16 = jnp.bfloat16
i32 = jnp.int32

SPEED, CLUSTER, LINK, ORIENT, OCCUPIED = 12, 13, 14, 18, 22

MOST = pltpu.CompilerParams(vmem_limit_bytes=60 << 20)
PARAMS = pltpu.CompilerParams(vmem_limit_bytes=20 << 20)


def coefficients(lower, upper):
    return [
        (upper ** (degree + 1) - lower ** (degree + 1)) / math.factorial(degree + 1)
        for degree in range(NORDER)
    ]


FIRST = coefficients(0.0, step_fast)
SECOND = coefficients(step_fast, 2.0 * step_fast)


def partner_offsets(devices):
    return [1, 2, 3, 4, -1, -2, -3, -4, devices // 2]


def packed_row(quantity, basis):
    group, member = quantity // 3, quantity % 3
    inside = 16 * member + basis if basis < 16 else 48 + 4 * member + (basis - 16)
    return 64 * group + inside


def pack_three(members):
    a, b, c = members
    tail = a[16:24] + pltpu.roll(b[16:24], 4, 0)
    return jnp.concatenate([a[:16], b[:16], c[:16], tail, c[16:24]], axis=0)


def split(values):
    high = values.astype(bf16)
    low = (values - high.astype(f32)).astype(bf16)
    return high, low


def stacked(high, low):
    return jnp.concatenate([high, low, high], axis=0)


def dot(a, b):
    return jnp.dot(a, b, preferred_element_type=f32)


def dot_last(a, b):
    return lax.dot_general(a, b, (((1,), (1,)), ((), ())), preferred_element_type=f32)


def iota(shape, axis):
    return lax.broadcasted_iota(i32, shape, axis)


def one_hot(condition):
    return jnp.where(condition, 1.0, 0.0).astype(bf16)


def make_weights(deriv, stiff, evals, lift, w_pred, w_own, w_lift, w_table, w_far, square):
    def turned(matrix, rows, columns):
        square[...] = jnp.zeros((LANES, LANES), f32)
        square[:rows, :columns] = matrix
        return square[...].T[:NBP]

    column = iota((LANES, PACK), 1) & 63
    member = jnp.where(column < 48, column >> 4, (column - 48) >> 2)
    basis = jnp.where(column < 48, column & 15, 16 + (column & 3))
    spread = one_hot(iota((LANES, PACK), 0) == jnp.where(member < 3, basis, -1))
    member = member[:NBP]
    part = iota((NBP, PACK), 1)

    def three(matrix):
        high, low = split(turned(matrix, NB, NB))
        row = jnp.where(part < 128, dot(high, spread), dot(low, spread))
        return [jnp.where(member == inner, row, 0.0) for inner in range(3)]

    blocks = []
    for axis in range(3):
        blocks += three(-deriv[axis])
    w_pred[...] = jnp.concatenate(blocks, axis=0).astype(bf16)

    own = [
        lax.dot_general(
            evals[48 * face : 48 * face + NQ, :],
            lift[face],
            (((0,), (0,)), ((), ())),
            precision=exact,
            preferred_element_type=f32,
        )
        for face in range(4)
    ]
    blocks = []
    for matrix in [stiff[axis] for axis in range(3)] + own + [own[0] + own[1] + own[2] + own[3]]:
        blocks += three(matrix if len(blocks) < 9 else -0.5 * matrix)
    w_own[...] = jnp.concatenate(blocks, axis=0).astype(bf16)

    column = iota((LANES, 144), 1)
    spread = one_hot(iota((LANES, 144), 0) == (column & 15))
    column = column[:NBP]
    block = column >> 4
    member = block - jnp.where(column >= 96, 6, jnp.where(column >= 48, 3, 0))
    every = []
    for face in range(4):
        high, low = split(turned(lift[face], NQ, NB))
        row = jnp.where(column < 96, dot(high, spread), dot(low, spread))
        rows = [jnp.where(member == inner, -0.5 * row, 0.0) for inner in range(3)]
        w_lift[face] = jnp.concatenate(rows + [-r for r in rows], axis=0).astype(bf16)
        every += rows
    w_far[...] = jnp.concatenate(every, axis=0).astype(bf16)

    basis_of = one_hot((iota((320, NB), 0) >> 4) == iota((320, NB), 1))
    keep = (iota((320, PACK), 0) & 15) == (iota((320, PACK), 1) & 15)
    code_of = one_hot((iota((PACK, 16), 0) >> 4) == iota((PACK, 16), 1))
    halves = []
    for part_of in split(evals[...]):
        halves.append(dot(jnp.where(keep, dot_last(basis_of, part_of), 0.0).astype(bf16), code_of))
    w_table[:, :16] = halves[0].astype(bf16)
    w_table[:, 16:] = halves[1].astype(bf16)


def find_links(devices, tiles, small, aux, from_top):
    me = lax.axis_index("dom").astype(f32)
    row = iota((ASKS, LANES), 0).astype(f32)
    up_to = one_hot(iota((LANES, LANES), 0) <= iota((LANES, LANES), 1))
    request = (iota((LANES, LANES), 0) & (REQ - 1)).astype(f32)
    carry = jnp.zeros((ASKS, 1), f32)
    wanted = jnp.zeros((2 * ASKS, LANES), f32)
    for tile in range(tiles):
        at = slice(tile * LANES, (tile + 1) * LANES)
        occupied = small[OCCUPIED : OCCUPIED + 1, at] > 0.5
        target = jnp.full((1, LANES), -1.0, f32)
        slots = jnp.zeros((1, LANES), f32)
        for face in range(4):
            link = small[LINK + face : LINK + face + 1, at]
            owner = jnp.floor((link + 0.5) * (1.0 / PARTITION_SLOTS))
            slot = link - owner * PARTITION_SLOTS
            near = owner == me
            aux[face : face + 1, at] = jnp.where(near, slot, -1.0).astype(i32)
            away = occupied & jnp.logical_not(near)
            target = jnp.where(away, owner, target)
            slots = jnp.where(away, slot, slots)
        far = target - me
        far = jnp.where(far < 0, far + devices, far)
        partner = jnp.where(far <= 4, far - 1.0, jnp.where(far >= devices - 4, devices + 3.0 - far, 8.0))
        partner = jnp.where(target >= 0, partner, -1.0)
        named = jnp.where(row == partner, 1.0, 0.0)
        prefix = dot(named.astype(bf16), up_to) + carry
        carry = carry + jnp.sum(named, axis=1, keepdims=True)
        rank = jnp.sum(named * prefix, axis=0, keepdims=True) - 1.0
        if from_top:
            rank = REQ - 1.0 - rank
        aux[4:5, at] = jnp.where(target >= 0, partner * REQ + rank, -1.0).astype(i32)
        aux[5:8, at] = jnp.zeros((3, LANES), i32)
        ask = slots + 1.0
        high = jnp.floor(ask * (1.0 / 32)) * 32.0
        both = jnp.concatenate([named * high, named * (ask - high)], axis=0).astype(bf16)
        wanted = wanted + dot_last(both, one_hot(request == rank))
    return wanted[:ASKS] + wanted[ASKS:]


def prepare_kernel(devices, tiles, normals, speed, cluster, slot, links, orient, q, jac, small, aux, asks, group, one, record):
    me = lax.axis_index("dom")
    for face in range(4):
        small[3 * face : 3 * face + 3, :] = jnp.concatenate([normals[d, face : face + 1, :] for d in range(3)], axis=0)
    small[SPEED : SPEED + 1, :] = speed[...]
    small[CLUSTER : CLUSTER + 1, :] = cluster[...].astype(f32)
    small[LINK : LINK + 4, :] = links[...].astype(f32)
    small[ORIENT : ORIENT + 4, :] = orient[...].astype(f32)
    where = slot[...]
    stays = (where >= me * PARTITION_SLOTS) & (where < (me + 1) * PARTITION_SLOTS)
    small[OCCUPIED : OCCUPIED + 1, :] = jnp.where(stays, 1.0, 0.0)
    small[OCCUPIED + 1 : SMALL, :] = jnp.zeros((1, tiles * LANES), f32)
    wanted = find_links(devices, tiles, small, aux, False)
    asks[...] = jnp.zeros((devices, 1, LANES), f32)
    for k, offset in enumerate(partner_offsets(devices)):
        asks[lax.rem(me + offset + devices, devices)] = wanted[k : k + 1]

    record[...] = jnp.zeros((RECORD, LANES), f32)
    for p in range(NV):
        record[p * NBP : p * NBP + NB] = q[p]
        for inner in range(NV):
            at = ROWS + 4 * (p * NV + inner)
            record[at : at + 3] = jac[p, inner]
    fields = small[:, KEEP:]
    row = iota(fields.shape, 0)
    record[JAC_END : JAC_END + SMALL] = jnp.where(row == OCCUPIED, 1.0 - fields, fields)
    whole = record[...]
    turned = jnp.concatenate([whole[c : c + LANES].T for c in range(0, RECORD, LANES)], axis=1)
    one[...] = turned[:CSZ]
    position = me // (devices // GROUPS)
    for g in range(GROUPS):
        group[lax.rem(position + g, GROUPS)] = turned[g * CSZ : (g + 1) * CSZ]


def prepare(normals, speed, cluster, slot, links, orient, q, jac, devices):
    count = q.shape[2]

    def body(*refs):
        prepare_kernel(devices, count // LANES, *refs)

    last = KEEP // LANES
    return pl.pallas_call(
        body,
        grid=(1,),
        in_specs=[
            whole_spec(normals),
            whole_spec(speed),
            whole_spec(cluster),
            whole_spec(slot),
            whole_spec(links),
            whole_spec(orient),
            pl.BlockSpec((NV, NB, LANES), lambda i: (0, 0, last)),
            pl.BlockSpec((NV, NV, 3, LANES), lambda i: (0, 0, 0, last)),
        ],
        out_specs=[
            pl.BlockSpec((SMALL, count), lambda i: (0, 0)),
            pl.BlockSpec((8, count), lambda i: (0, 0)),
            pl.BlockSpec((devices, 1, LANES), lambda i: (0, 0, 0)),
            pl.BlockSpec((GROUPS, CSZ, RECORD), lambda i: (0, 0, 0)),
            pl.BlockSpec((CSZ, RECORD), lambda i: (0, 0)),
        ],
        out_shape=[
            jax.ShapeDtypeStruct((SMALL, count), f32),
            jax.ShapeDtypeStruct((8, count), i32),
            jax.ShapeDtypeStruct((devices, 1, LANES), f32),
            jax.ShapeDtypeStruct((GROUPS, CSZ, RECORD), f32),
            jax.ShapeDtypeStruct((CSZ, RECORD), f32),
        ],
        scratch_shapes=[pltpu.VMEM((RECORD, LANES), f32)],
        compiler_params=MOST,
        name="prepare",
    )(normals, speed, cluster, slot, links, orient, q, jac)


def unpack(devices, group, one, q, jac, small, aux):
    position = lax.axis_index("dom") // (devices // GROUPS)
    rows = [one[...]]
    for g in range(1, GROUPS):
        rows.append(group[lax.rem(position - g + GROUPS, GROUPS)])
    whole = jnp.concatenate(rows, axis=0)
    turned = jnp.concatenate([whole[:, c : c + LANES].T for c in range(0, RECORD, LANES)], axis=0)
    for p in range(NV):
        q[p] = turned[p * NBP : p * NBP + NB]
        for inner in range(NV):
            at = ROWS + 4 * (p * NV + inner)
            jac[p, inner] = turned[at : at + 3]
    small[...] = turned[JAC_END : JAC_END + SMALL]
    return find_links(devices, 1, small, aux, True)


OUT_BLOCKS = {1: (0, 0), 4: (0, 1), -2: (0, 2), -1: (1, 0), -4: (1, 1), 2: (1, 2), 3: (2, 0), -3: (3, 0)}
IN_BLOCKS = {-1: (0, 0), 1: (1, 0), -3: (2, 0), -4: (2, 1), -2: (2, 2), 3: (3, 0), 4: (3, 1), 2: (3, 2)}


def put(outs, rows, k, devices):
    if k == PARTNERS - 1:
        return outs[4], 0
    array, block = OUT_BLOCKS[-partner_offsets(devices)[k]]
    return outs[array], block * rows


def take(messages, k, devices):
    if k == PARTNERS - 1:
        return messages[4], 0
    array, block = IN_BLOCKS[partner_offsets(devices)[k]]
    rows = messages[4].shape[0]
    return messages[array], block * rows


def picked(requests, fields):
    lane = iota((1, LANES), 1)
    tiles = []
    for at in range(0, 12, 4):
        four = [requests[min(at + n, PARTNERS - 1)] for n in range(4)]
        tiles.append(
            jnp.where(lane < 32, four[0], jnp.where(lane < 64, four[1], jnp.where(lane < 96, four[2], four[3])))
        )
    slots = (iota((KEEP, FAR), 0) + 1).astype(f32)
    return dot(fields, one_hot(slots == jnp.concatenate(tiles, axis=1)))


def message_rows(both):
    value = both[:PACK] + both[PACK:]
    return jnp.concatenate([value, jnp.zeros((MSG - PACK, FAR), f32)], axis=0).T


def back(k):
    return k if k == PARTNERS - 1 else (k + 4) % 8


def requests_here(devices, asks):
    me = lax.axis_index("dom")
    peers = [lax.rem(me - o + devices, devices) for o in partner_offsets(devices)]
    return [asks[p] for p in peers]


def unpack_kernel(devices, group, one, asks, field, q, jac, small, aux, *outs):
    moved = unpack(devices, group, one, q, jac, small, aux)
    rows = message_rows(picked(requests_here(devices, asks), field[...]))
    for k in range(PARTNERS):
        out, at = put(outs, MESSAGE1, k, devices)
        out[at : at + REQ] = rows[k * REQ : (k + 1) * REQ]
        out[at + REQ : at + MESSAGE1, :LANES] = jnp.broadcast_to(moved[back(k) : back(k) + 1, :], (8, LANES))
        out[at + REQ : at + MESSAGE1, LANES:] = jnp.zeros((8, MSG - LANES), f32)


def answer_again(devices, asks, got, field, later, outs):
    moved = []
    for k in range(PARTNERS):
        message, at = take(got, back(k), devices)
        moved.append(message[at + REQ : at + REQ + 1, :LANES])
    every = [a + b for a, b in zip(requests_here(devices, asks), moved)]
    rows = message_rows(picked(every, later))
    rows_first = message_rows(picked(moved, field))
    for k in range(PARTNERS):
        out, at = put(outs, 2 * REQ, k, devices)
        out[at : at + REQ] = rows[k * REQ : (k + 1) * REQ]
        out[at + REQ : at + 2 * REQ] = rows_first[k * REQ : (k + 1) * REQ]


def relay_kernel(got_plus, got_minus, own_plus, own_minus, on_plus, on_minus):
    rows = own_plus.shape[0]
    block = [slice(b * rows, (b + 1) * rows) for b in range(3)]
    on_plus[block[0]] = own_plus[...]
    on_plus[block[1]] = got_plus[block[1]]
    on_plus[block[2]] = got_minus[block[2]]
    on_minus[block[0]] = own_minus[...]
    on_minus[block[1]] = got_minus[block[1]]
    on_minus[block[2]] = got_plus[block[2]]


def message_shapes(rows):
    return [jax.ShapeDtypeStruct((rows * blocks, MSG), f32) for blocks in (3, 3, 1, 1, 1)]


def far_table(devices, part, messages):
    rows = []
    for k in range(PARTNERS):
        message, at = take(messages, k, devices)
        rows.append(message[at + part * REQ : at + (part + 1) * REQ, :])
    rows.append(jnp.zeros((FAR - PARTNERS * REQ, MSG), f32))
    turned = jnp.concatenate(rows, axis=0).T[:PACK]
    return jnp.concatenate(split(turned), axis=0)


def take_turns(*chains):
    results = [None] * len(chains)
    going = list(range(len(chains)))
    while going:
        for n in list(going):
            try:
                next(chains[n])
            except StopIteration as stop:
                results[n] = stop.value
                going.remove(n)
    return results


def alone(chain):
    return take_turns(chain)[0]


class Window:
    def __init__(self, ref, begin, width):
        self.ref, self.begin = ref, begin
        self.shape = tuple(ref.shape[:-1]) + (width,)

    def _at(self, index):
        rank = len(self.shape)
        if index is Ellipsis:
            index = ()
        index = index if isinstance(index, tuple) else (index,)
        index = index + (slice(None),) * (rank - len(index))
        low, high, _ = index[-1].indices(self.shape[-1])
        return index[:-1] + (slice(self.begin + low, self.begin + high),)

    def __getitem__(self, index):
        return self.ref[self._at(index)]

    def __setitem__(self, index, value):
        self.ref[self._at(index)] = value


def lanes(tile):
    return slice(tile * LANES, (tile + 1) * LANES)


def jacobian_apply(jac, tile, parts):
    result = [None] * NV
    for group in range(3):
        for d in range(3):
            for inner in range(3):
                q = 3 * group + inner
                value = parts(d, q)
                for p in range(NV):
                    term = jac[p, q, d : d + 1, lanes(tile)] * value
                    result[p] = term if result[p] is None else result[p] + term
    return result


def packed_split(fields, group):
    packed = [pack_three(tile[3 * group : 3 * group + 3]) for tile in fields]
    return split(jnp.concatenate(packed, axis=1))


def split_fields(fields):
    pairs = [packed_split(fields, group) for group in range(3)]
    return jnp.concatenate([a for a, _ in pairs] + [b for _, b in pairs], axis=0)


def predict(chains, w_pred):
    for state, _, sums in chains:
        for ref, scale in sums:
            for p in range(NV):
                ref[p] = scale[0] * state[p]

    def degree_step(degree, carry):
        turned = []
        for state, _, _ in chains:
            now = load_field(state)
            turned.append([dot(w_pred[...], stacked(*packed_split(now, group))) for group in range(3)])
        for (state, jac, sums), of in zip(chains, turned):
            scales = [jnp.where(degree == 1, s[1], jnp.where(degree == 2, s[2], s[3])) for _, s in sums]
            for t in range(state.shape[2] // LANES):
                at = lanes(t)
                result = jacobian_apply(
                    jac, t, lambda d, q: of[q // 3][d * 72 + (q % 3) * NBP : d * 72 + (q % 3) * NBP + NBP, at]
                )
                for p in range(NV):
                    state[p, :, at] = result[p]
                    for (ref, _), scale in zip(sums, scales):
                        ref[p, :, at] = ref[p, :, at] + scale * result[p]
        return carry

    lax.fori_loop(1, NORDER, degree_step, 0)


def face_products(gathered, table, tiles):
    outers = []
    for t in tiles:
        outer = [None] * NV
        for b in range(NB):
            values = table[b * NQ : (b + 1) * NQ, lanes(t)]
            for p in range(NV):
                at = packed_row(p, b)
                term = gathered[at : at + 1, lanes(t)] * values
                outer[p] = term if outer[p] is None else outer[p] + term
        outers.append(outer)
    return [
        stacked(*split(jnp.concatenate([jnp.concatenate(o[3 * g : 3 * g + 3], axis=0) for o in outers], axis=1)))
        for g in range(3)
    ]


def table_of(code, w_table):
    hot = one_hot(iota((16, code.shape[1]), 0).astype(f32) == code)
    return dot(w_table, jnp.concatenate([hot, hot], axis=0))


class NearChain:
    def __init__(self, near, weights, small, aux, gathered, table, by_face, parts):
        self.near, self.small, self.aux, self.gathered, self.table = near, small, aux, gathered, table
        self.by_face, self.parts = by_face, parts
        self.w_own, self.w_lift, self.w_table = weights
        self.count = aux.shape[-1]
        self.tiles = range(self.count // LANES)

    def begin(self, own):
        for group in range(3):
            rows = slice(64 * group, 64 * group + 64)
            lower = slice(PACK + 64 * group, PACK + 64 * group + 64)
            mine = dot(self.w_own[...], stacked(own[rows], own[lower]))
            for inner in range(3):
                q = 3 * group + inner
                of = [mine[72 * block + NBP * inner : 72 * block + NBP * inner + NBP] for block in range(8)]
                for d in range(3):
                    self.parts[d * NV + q] = of[d]
                for face in range(4):
                    self.by_face[face, q] = of[3 + face]
                self.parts[3 * NV + q] = of[7]

    def gather(self, face):
        count = self.count
        slots = iota((KEEP, count), 0).astype(jnp.int16)
        index = jnp.broadcast_to(self.aux[pl.ds(face, 1), :], (16, count)).astype(jnp.int16)
        index = jnp.concatenate([index] * (KEEP // 16), axis=0)
        both = dot(self.near[...], jnp.where(slots == index, jnp.ones((), bf16), jnp.zeros((), bf16)))
        self.gathered[...] = both[:PACK] + both[PACK:]
        self.table[...] = table_of(self.small[pl.ds(ORIENT + face, 1), :], self.w_table[...])

    def products(self, face):
        normals = [self.small[pl.ds(3 * face + d, 1), :] for d in range(3)]
        for group, points in enumerate(face_products(self.gathered, self.table, self.tiles)):
            lifted = dot(self.w_lift[face], points)
            for inner in range(3):
                q = 3 * group + inner
                at = inner * NBP
                mixed = lifted[at : at + NBP] + self.by_face[face, q]
                self.parts[3 * NV + q] = self.parts[3 * NV + q] + lifted[72 + at : 72 + at + NBP]
                for d in range(3):
                    self.parts[d * NV + q] = self.parts[d * NV + q] + normals[d] * mixed


def near_part(chains, owns):
    chains[0].gather(0)
    for chain, own in zip(chains, owns):
        chain.begin(own)

    def two_faces(pair, carry):
        for face in (2 * pair, 2 * pair + 1):
            for other in chains[1:]:
                other.gather(face)
            chains[0].products(face)
            chains[0].gather((face + 1) & 3)
            for other in chains[1:]:
                other.products(face)
        return carry

    lax.fori_loop(0, 2, two_faces, 0)


def update_chain(parts, far, small, aux, jac, w_far, w_table, gathered):
    volume, upwind = parts
    tiles = range(len(volume))
    count = len(volume) * LANES
    place = aux[4:5, :]
    both = dot(far, one_hot(iota((FAR, count), 0) == place))
    gathered[...] = both[:PACK] + both[PACK:]
    masks = [jnp.where((aux[face : face + 1, :] < 0) & (place >= 0), 1.0, 0.0) for face in range(4)]
    code = masks[0] * small[ORIENT : ORIENT + 1, :]
    normals = [masks[0] * small[d : d + 1, :] for d in range(3)]
    for face in range(1, 4):
        code = code + masks[face] * small[ORIENT + face : ORIENT + face + 1, :]
        normals = [n + masks[face] * small[3 * face + d : 3 * face + d + 1, :] for d, n in enumerate(normals)]
    changes = [[None] * NV for t in tiles]
    table = table_of(code, w_table)
    yield
    volume = [[list(v) for v in tile] for tile in volume]
    upwind = [list(tile) for tile in upwind]
    for group, points in enumerate(face_products(gathered, table, tiles)):
        lifted = dot(w_far, points)
        for t in tiles:
            for inner in range(3):
                q = 3 * group + inner
                mixed = None
                for face in range(4):
                    at = 72 * face + inner * NBP
                    term = masks[face][:, lanes(t)] * lifted[at : at + NBP, lanes(t)]
                    mixed = term if mixed is None else mixed + term
                upwind[t][q] = upwind[t][q] - mixed
                for d in range(3):
                    volume[t][d][q] = volume[t][d][q] + normals[d][:, lanes(t)] * mixed
    for t in tiles:
        change = jacobian_apply(jac, t, lambda d, q: volume[t][d][q])
        speed = small[SPEED : SPEED + 1, lanes(t)]
        changes[t] = [c + speed * u for c, u in zip(change, upwind[t])]
    return changes


def update(*args):
    return alone(update_chain(*args))


def load_parts(ref):
    tiles = range(ref.shape[2] // LANES)
    volume = [[[ref[d * NV + q, :, lanes(t)] for q in range(NV)] for d in range(3)] for t in tiles]
    return volume, [[ref[3 * NV + q, :, lanes(t)] for q in range(NV)] for t in tiles]


def load_state(q, padded):
    padded[:, NB:NBP, :] = jnp.zeros((NV, NBP - NB, padded.shape[2]), f32)
    for p in range(NV):
        padded[p, :NB, :] = q[p]
    return load_field(padded)


def load_field(ref):
    return [[ref[p, :, lanes(t)] for p in range(NV)] for t in range(ref.shape[2] // LANES)]


def store_field(ref, field):
    for t, tile in enumerate(field):
        for p in range(NV):
            ref[p, :, lanes(t)] = tile[p]


def store_result(out, base, change, small):
    for t in range(len(base)):
        occupied = small[OCCUPIED : OCCUPIED + 1, lanes(t)] > 0.5
        for p in range(NV):
            out[p, :, lanes(t)] = jnp.where(occupied, base[t][p] + change[t][p], 0.0)[:NB]


def first_kernel(
    q, jac, deriv, stiff, evals, lift, packed, slow, w_pred, w_own, w_lift, w_table, w_far, padded, sums, square
):
    @pl.when(pl.program_id(0) == 0)
    def _():
        make_weights(deriv, stiff, evals, lift, w_pred, w_own, w_lift, w_table, w_far, square)

    load_state(q, padded)
    chains = []
    for begin in range(0, BOTH, WIDE):
        state, jacobians, early, late = [Window(r, begin, WIDE) for r in (padded, jac, sums, slow)]
        chains.append((state, jacobians, [(early, FIRST), (late, SECOND)]))
    predict(chains, w_pred)
    packed[...] = split_fields(load_field(sums))


def near_kernel(own, near, small, aux, w_own, w_lift, w_table, *refs):
    parts, gathered, table, by_face = refs[-4:]
    chains, owns = [], []
    for begin in range(0, BOTH, WIDE):
        windows = [Window(r, begin, WIDE) for r in (small, aux, gathered, table, by_face, parts)]
        chains.append(NearChain(near, (w_own, w_lift, w_table), *windows))
        owns.append(Window(own, begin, WIDE))
    near_part(chains, owns)


def middle_steps(chains, far, w_pred, w_far, w_table):
    updates = []
    for _, parts, jac, small, _, aux, gathered, _, _, _ in chains:
        updates.append(update_chain(load_parts(parts), far, small, aux, jac, w_far, w_table, gathered))
    for chain, change in zip(chains, take_turns(*updates)):
        q, _, _, small, _, _, _, base, state, _ = chain
        start = load_state(q, state)
        for t in range(len(start)):
            fast = small[CLUSTER : CLUSTER + 1, lanes(t)] < 0.5
            for p in range(NV):
                now = start[t][p] + change[t][p]
                base[p, :, lanes(t)] = now
                state[p, :, lanes(t)] = jnp.where(fast, now, start[t][p])
    predict([(chain[8], chain[2], [(chain[9], FIRST)]) for chain in chains], w_pred)
    results = []
    for _, _, _, small, slow, _, _, _, _, sums in chains:
        second = []
        for t, (late, later) in enumerate(zip(load_field(slow), load_field(sums))):
            fast = small[CLUSTER : CLUSTER + 1, lanes(t)] < 0.5
            second.append([jnp.where(fast, a, b) for a, b in zip(later, late)])
        results.append(split_fields(second))
    return results


def middle_kernel(devices, steps, q, jac, small, slow, parts, near, aux, asks, *refs):
    messages = refs[:5]
    w_pred, w_far, w_table, base, packed, *outs, padded, sums, gathered, far = refs[5:]
    step = pl.program_id(0)

    @pl.when(step == 0)
    def _():
        far[...] = far_table(devices, 0, messages)

    refs = (q, parts, jac, small, slow, aux, gathered, base, padded, sums)
    chains = [[Window(r, begin, WIDE) for r in refs] for begin in range(0, BOTH, WIDE)]
    second = jnp.concatenate(middle_steps(chains, far[...], w_pred, w_far[...], w_table[...]), axis=1)
    packed[:, pl.ds(pl.multiple_of(step * BOTH, BOTH), BOTH)] = second

    @pl.when(step == steps - 1)
    def _():
        answer_again(devices, asks, messages, near[...], packed[:, :KEEP], outs)


def last_kernel(
    devices, steps, base, jac, small, parts, aux, q_moved, jac_moved, small_moved, aux_moved, near, later, *refs
):
    messages = refs[:5]
    w_pred, w_own, w_lift, w_table, w_far, out, gathered, far = refs[5:13]
    padded, gathered_moved, table, by_face, parts_moved, early, late, now = refs[13:]
    step = pl.program_id(0)

    @pl.when(step == 0)
    def _():
        far[...] = far_table(devices, 0, messages)

    @pl.when(step < steps)
    def _():
        table_far = far[...]
        chains, stores = [], []
        for begin in range(0, BOTH, WIDE):
            w = [Window(r, begin, WIDE) for r in (parts, small, aux, jac, gathered, out, base)]
            chains.append(
                update_chain(load_parts(w[0]), table_far, w[1], w[2], w[3], w_far[...], w_table[...], w[4])
            )
            stores.append((w[5], w[6], w[1]))
        for (to, start, fields), change in zip(stores, take_turns(*chains)):
            store_result(to, load_field(start), change, fields)

    @pl.when(step == steps)
    def _():
        load_state(q_moved, padded)
        predict([(padded, jac_moved, [(early, FIRST), (late, SECOND)])], w_pred)
        chain = NearChain(
            near, (w_own, w_lift, w_table), small_moved, aux_moved, gathered_moved, table, by_face, parts_moved
        )
        near_part([chain], [split_fields(load_field(early))])
        fields = (q_moved, parts_moved, jac_moved, small_moved, late, aux_moved, gathered_moved, now, padded, early)
        far_first = far_table(devices, 1, messages)
        (second,) = middle_steps([fields], far_first, w_pred, w_far[...], w_table[...])
        chain.near = later
        near_part([chain], [second])
        change = update(
            load_parts(parts_moved), far[...], small_moved, aux_moved, jac_moved, w_far[...], w_table[...],
            gathered_moved,
        )
        store_result(out, load_field(now), change, small_moved)


def whole_spec(array):
    rank = array.ndim
    return pl.BlockSpec(array.shape, lambda i: (0,) * rank)


def lane_spec(*lead, last=None):
    rank = len(lead)
    if last is None:
        return pl.BlockSpec(lead + (WIDE,), lambda i: (0,) * rank + (i,))
    return pl.BlockSpec(lead + (BOTH,), lambda i: (0,) * rank + (jnp.minimum(i, last),))


Q_SPEC = lane_spec(NV, NB)
J_SPEC = lane_spec(NV, NV, 3)
S_SPEC = lane_spec(SMALL)
A_SPEC = lane_spec(8)
F_SPEC = lane_spec(NV, NBP)
X_SPEC = lane_spec(2 * PACK)
N_SPEC = pl.BlockSpec((2 * PACK, KEEP), lambda i: (0, 0))


def padded_scratch(width):
    return pltpu.VMEM((NV, NBP, width), f32)


def gathered_scratch(width):
    return pltpu.VMEM((PACK, width), f32)


def near_scratch(width):
    return [gathered_scratch(width), pltpu.VMEM((320, width), f32), pltpu.VMEM((4, NV, NBP, width), f32)]


def per_device(
    element_freedom_values,
    scaled_jacobian_matrices,
    outward_face_normals,
    largest_wave_speed,
    element_cluster_index,
    element_new_slot,
    neighbours,
    face_rotation_codes,
    deriv_mats,
    stiff_mats,
    face_eval,
    face_lift,
):
    count = element_freedom_values.shape[2]
    steps = count // WIDE
    devices = lax.axis_size("dom")
    q = element_freedom_values
    jac = jnp.transpose(scaled_jacobian_matrices, (1, 2, 0, 3))

    def shift(array, by):
        return lax.ppermute(array, "dom", [(i, (i + by) % devices) for i in range(devices)])

    def swap(array, groups):
        return lax.all_to_all(array, "dom", split_axis=0, concat_axis=0, axis_index_groups=groups, tiled=True)

    def on_ring(body):
        def kernel(*refs):
            body(devices, *refs)

        return kernel

    small, aux, asks, group, one = prepare(
        jnp.transpose(outward_face_normals, (1, 0, 2)),
        largest_wave_speed[None],
        element_cluster_index[None],
        element_new_slot[None],
        neighbours,
        face_rotation_codes,
        q,
        jac,
        devices,
    )
    asks = swap(asks, None)
    asks, group, one = lax.optimization_barrier((asks, group, one))
    stride = devices // GROUPS
    group = swap(group, [[r + stride * j for j in range(GROUPS)] for r in range(stride)])
    one = shift(one, 1)
    packed_shape = jax.ShapeDtypeStruct((2 * PACK, count), bf16)
    field_shape = jax.ShapeDtypeStruct((NV, NBP, count), f32)
    far = pltpu.VMEM((2 * PACK, FAR), bf16)
    weight_shapes = [
        jax.ShapeDtypeStruct((ROWS, PACK), bf16),
        jax.ShapeDtypeStruct((576, PACK), bf16),
        jax.ShapeDtypeStruct((4, 144, 144), bf16),
        jax.ShapeDtypeStruct((320, 32), bf16),
        jax.ShapeDtypeStruct((288, 144), bf16),
    ]
    evals = jnp.transpose(face_eval, (0, 2, 1)).reshape(12 * NQ, NB)
    matrices = [deriv_mats, stiff_mats, evals, face_lift]
    halves = count // BOTH

    def part_spec(begin, *lead):
        rank = len(lead)
        return pl.BlockSpec(lead + (BOTH,), lambda i: (0,) * rank + (i + begin,))

    first, slow, w_pred, w_own, w_lift, w_table, w_far = pl.pallas_call(
        first_kernel,
        grid=(halves,),
        in_specs=[part_spec(0, NV, NB), part_spec(0, NV, NV, 3)] + [whole_spec(m) for m in matrices],
        out_specs=[part_spec(0, 2 * PACK), part_spec(0, NV, NBP)] + [whole_spec(w) for w in weight_shapes],
        out_shape=[packed_shape, field_shape] + weight_shapes,
        scratch_shapes=[padded_scratch(BOTH), padded_scratch(BOTH), pltpu.VMEM((LANES, LANES), f32)],
        compiler_params=MOST,
        name="first",
    )(q, jac, *matrices)

    moved_shapes = [
        jax.ShapeDtypeStruct((NV, NB, LANES), f32),
        jax.ShapeDtypeStruct((NV, NV, 3, LANES), f32),
        jax.ShapeDtypeStruct((SMALL, LANES), f32),
        jax.ShapeDtypeStruct((8, LANES), i32),
    ]
    out_shape = moved_shapes + message_shapes(MESSAGE1)
    *moved, m0, m1, m2, m3, m4 = pl.pallas_call(
        on_ring(unpack_kernel),
        grid=(1,),
        in_specs=[whole_spec(a) for a in (group, one, asks)] + [N_SPEC],
        out_specs=[whole_spec(o) for o in out_shape],
        out_shape=out_shape,
        compiler_params=MOST,
        name="unpack",
    )(group, one, asks, first)
    of_near = [w_own, w_lift, w_table]
    parts_shape = jax.ShapeDtypeStruct((4 * NV, NBP, count), f32)

    def near_steps(field, begin, number, parts):
        def spec(*lead):
            return part_spec(begin, *lead)

        return pl.pallas_call(
            near_kernel,
            grid=(number,),
            in_specs=[spec(2 * PACK), N_SPEC, spec(SMALL), spec(8)]
            + [whole_spec(w) for w in of_near]
            + [pl.BlockSpec(memory_space=pl.ANY)] * len(parts),
            out_specs=spec(4 * NV, NBP),
            out_shape=parts_shape,
            scratch_shapes=near_scratch(BOTH),
            input_output_aliases={7: 0} if parts else {},
            cost_estimate=pl.CostEstimate(flops=int(4e9) * number, bytes_accessed=4 << 20, transcendentals=0),
            compiler_params=PARAMS,
            name="near",
        )(field, field, small, aux, *of_near, *parts)

    def exchange_beside(answers, field):
        half = halves // 2
        plus, minus, own_plus, own_minus, opposite = answers
        got_plus, got_minus, opposite = shift(plus, 1), shift(minus, -1), shift(opposite, devices // 2)
        parts = near_steps(field, 0, half, [])
        got_plus, got_minus, opposite, parts = lax.optimization_barrier((got_plus, got_minus, opposite, parts))
        on_plus, on_minus = pl.pallas_call(
            relay_kernel,
            out_shape=[jax.ShapeDtypeStruct(plus.shape, f32)] * 2,
            compiler_params=pltpu.CompilerParams(vmem_limit_bytes=4 << 20),
            name="relay",
        )(got_plus, got_minus, own_plus, own_minus)
        on_plus, on_minus = shift(on_plus, 3), shift(on_minus, -3)
        parts = near_steps(field, half, halves - half, [parts])
        return (got_plus, got_minus, on_plus, on_minus, opposite), parts

    messages, parts = exchange_beside((m0, m1, m2, m3, m4), first)

    def middle(*refs):
        middle_kernel(devices, halves, *refs)

    weights = [w_pred, w_far, w_table]
    out_shape = [field_shape, packed_shape] + message_shapes(2 * REQ)
    base, second, *answers = pl.pallas_call(
        middle,
        grid=(halves,),
        in_specs=[
            part_spec(0, NV, NB),
            part_spec(0, NV, NV, 3),
            part_spec(0, SMALL),
            part_spec(0, NV, NBP),
            part_spec(0, 4 * NV, NBP),
            N_SPEC,
            part_spec(0, 8),
            whole_spec(asks),
        ]
        + [whole_spec(a) for a in (*messages, *weights)],
        out_specs=[part_spec(0, NV, NBP)] + [whole_spec(o) for o in out_shape[1:]],
        out_shape=out_shape,
        scratch_shapes=[padded_scratch(BOTH), padded_scratch(BOTH), gathered_scratch(BOTH), far],
        compiler_params=PARAMS,
        name="middle",
    )(q, jac, small, slow, parts, first, aux, asks, *messages, *weights)
    messages, parts = exchange_beside(answers, second)

    def last(*refs):
        last_kernel(devices, halves, *refs)

    end = halves - 1
    weights = [w_pred, w_own, w_lift, w_table, w_far]
    return pl.pallas_call(
        last,
        grid=(halves + 1,),
        in_specs=[
            lane_spec(NV, NBP, last=end),
            lane_spec(NV, NV, 3, last=end),
            lane_spec(SMALL, last=end),
            lane_spec(4 * NV, NBP, last=end),
            lane_spec(8, last=end),
        ]
        + [whole_spec(a) for a in moved]
        + [N_SPEC, N_SPEC]
        + [whole_spec(a) for a in (*messages, *weights)],
        out_specs=part_spec(0, NV, NB),
        out_shape=jax.ShapeDtypeStruct((NV, NB, PARTITION_SLOTS), f32),
        scratch_shapes=[
            gathered_scratch(BOTH),
            far,
            padded_scratch(LANES),
            *near_scratch(LANES),
            pltpu.VMEM((4 * NV, NBP, LANES), f32),
            *[padded_scratch(LANES)] * 3,
        ],
        compiler_params=PARAMS,
        name="last",
    )(base, jac, small, parts, aux, *moved, first, second, *messages, *weights)


def solution(mesh):
    placed = (
        P(None, None, "dom"),
        P(None, None, None, "dom"),
        P(None, None, "dom"),
        P("dom"),
        P("dom"),
        P("dom"),
        P(None, "dom"),
        P(None, "dom"),
        P(),
        P(),
        P(),
        P(),
    )
    return jax.shard_map(
        per_device, mesh=mesh, in_specs=placed, out_specs=P(None, None, "dom"), check_vma=False
    )
```

```python
import math

import jax
import jax.numpy as jnp
from jax import lax
from jax.experimental import pallas as pl
from jax.experimental.pallas import tpu as pltpu
from jax.sharding import PartitionSpec as P

NV = 9
NB = 20
NBP = 24
NQ = 16
NORDER = 4
GROUPS = 8
CSZ = 16
KEEP = 896
PARTITION_SLOTS = 1152
REQ = 32
PARTNERS = 9
ASKS = 16
LANES = 128
WIDE = 256
BOTH = 512
ROWS = 216
JAC_END = ROWS + 4 * NV * NV
PACK = 192
MSG = 256
FAR = 384
RECORD = 640
SMALL = 24
MESSAGE1 = REQ + 8
LIFT_AT, TABLE_AT, NEAR_ROWS = 576, 1152, 1472

step_fast = 0.25
exact = lax.Precision.HIGHEST
f32 = jnp.float32
bf16 = jnp.bfloat16
i32 = jnp.int32

SPEED, CLUSTER, LINK, ORIENT, OCCUPIED = 12, 13, 14, 18, 22

MOST = pltpu.CompilerParams(vmem_limit_bytes=60 << 20)
PARAMS = pltpu.CompilerParams(vmem_limit_bytes=20 << 20)


def coefficients(lower, upper):
    return [
        (upper ** (degree + 1) - lower ** (degree + 1)) / math.factorial(degree + 1)
        for degree in range(NORDER)
    ]


FIRST = coefficients(0.0, step_fast)
SECOND = coefficients(step_fast, 2.0 * step_fast)


def partner_offsets(devices):
    return [1, 2, 3, 4, -1, -2, -3, -4, devices // 2]


def packed_row(quantity, basis):
    group, member = quantity // 3, quantity % 3
    inside = 16 * member + basis if basis < 16 else 48 + 4 * member + (basis - 16)
    return 64 * group + inside


def pack_three(members):
    a, b, c = members
    tail = a[16:24] + pltpu.roll(b[16:24], 4, 0)
    return jnp.concatenate([a[:16], b[:16], c[:16], tail, c[16:24]], axis=0)


def split(values):
    high = values.astype(bf16)
    low = (values - high.astype(f32)).astype(bf16)
    return high, low


def stacked(high, low):
    return jnp.concatenate([high, low, high], axis=0)


def dot(a, b):
    return jnp.dot(a, b, preferred_element_type=f32)


def dot_last(a, b):
    return lax.dot_general(a, b, (((1,), (1,)), ((), ())), preferred_element_type=f32)


def iota(shape, axis):
    return lax.broadcasted_iota(i32, shape, axis)


def one_hot(condition):
    return jnp.where(condition, 1.0, 0.0).astype(bf16)


def make_weights(deriv, stiff, evals, lift, w_pred, w_near, w_far, square):
    def turned(matrix, rows, columns):
        square[...] = jnp.zeros((LANES, LANES), f32)
        square[:rows, :columns] = matrix
        return square[...].T[:NBP]

    column = iota((LANES, PACK), 1) & 63
    member = jnp.where(column < 48, column >> 4, (column - 48) >> 2)
    basis = jnp.where(column < 48, column & 15, 16 + (column & 3))
    spread = one_hot(iota((LANES, PACK), 0) == jnp.where(member < 3, basis, -1))
    member = member[:NBP]
    part = iota((NBP, PACK), 1)

    def three(matrix):
        high, low = split(turned(matrix, NB, NB))
        row = jnp.where(part < 128, dot(high, spread), dot(low, spread))
        return [jnp.where(member == inner, row, 0.0) for inner in range(3)]

    blocks = []
    for axis in range(3):
        blocks += three(-deriv[axis])
    w_pred[...] = jnp.concatenate(blocks, axis=0).astype(bf16)

    own = [
        lax.dot_general(
            evals[48 * face : 48 * face + NQ, :],
            lift[face],
            (((0,), (0,)), ((), ())),
            precision=exact,
            preferred_element_type=f32,
        )
        for face in range(4)
    ]
    blocks = []
    for matrix in [stiff[axis] for axis in range(3)] + own + [own[0] + own[1] + own[2] + own[3]]:
        blocks += three(matrix if len(blocks) < 9 else -0.5 * matrix)
    w_near[:LIFT_AT, :] = jnp.concatenate(blocks, axis=0).astype(bf16)

    column = iota((LANES, 144), 1)
    spread = one_hot(iota((LANES, 144), 0) == (column & 15))
    column = column[:NBP]
    block = column >> 4
    member = block - jnp.where(column >= 96, 6, jnp.where(column >= 48, 3, 0))
    every = []
    for face in range(4):
        high, low = split(turned(lift[face], NQ, NB))
        row = jnp.where(column < 96, dot(high, spread), dot(low, spread))
        rows = [jnp.where(member == inner, -0.5 * row, 0.0) for inner in range(3)]
        at = LIFT_AT + 144 * face
        w_near[at : at + 144, :144] = jnp.concatenate(rows + [-r for r in rows], axis=0).astype(bf16)
        every += rows
    w_far[...] = jnp.concatenate(every, axis=0).astype(bf16)

    basis_of = one_hot((iota((320, NB), 0) >> 4) == iota((320, NB), 1))
    keep = (iota((320, PACK), 0) & 15) == (iota((320, PACK), 1) & 15)
    code_of = one_hot((iota((PACK, 16), 0) >> 4) == iota((PACK, 16), 1))
    halves = []
    for part_of in split(evals[...]):
        halves.append(dot(jnp.where(keep, dot_last(basis_of, part_of), 0.0).astype(bf16), code_of))
    w_near[TABLE_AT:, :32] = jnp.concatenate(halves, axis=1).astype(bf16)


def find_links(devices, tiles, small, aux, from_top):
    me = lax.axis_index("dom").astype(f32)
    row = iota((ASKS, LANES), 0).astype(f32)
    up_to = one_hot(iota((LANES, LANES), 0) <= iota((LANES, LANES), 1))
    request = (iota((LANES, LANES), 0) & (REQ - 1)).astype(f32)
    carry = jnp.zeros((ASKS, 1), f32)
    wanted = jnp.zeros((2 * ASKS, LANES), f32)
    for tile in range(tiles):
        at = slice(tile * LANES, (tile + 1) * LANES)
        occupied = small[OCCUPIED : OCCUPIED + 1, at] > 0.5
        target = jnp.full((1, LANES), -1.0, f32)
        slots = jnp.zeros((1, LANES), f32)
        for face in range(4):
            link = small[LINK + face : LINK + face + 1, at]
            owner = jnp.floor((link + 0.5) * (1.0 / PARTITION_SLOTS))
            slot = link - owner * PARTITION_SLOTS
            near = owner == me
            aux[face : face + 1, at] = jnp.where(near, slot, -1.0).astype(i32)
            away = occupied & jnp.logical_not(near)
            target = jnp.where(away, owner, target)
            slots = jnp.where(away, slot, slots)
        far = target - me
        far = jnp.where(far < 0, far + devices, far)
        partner = jnp.where(far <= 4, far - 1.0, jnp.where(far >= devices - 4, devices + 3.0 - far, 8.0))
        partner = jnp.where(target >= 0, partner, -1.0)
        named = jnp.where(row == partner, 1.0, 0.0)
        prefix = dot(named.astype(bf16), up_to) + carry
        carry = carry + jnp.sum(named, axis=1, keepdims=True)
        rank = jnp.sum(named * prefix, axis=0, keepdims=True) - 1.0
        if from_top:
            rank = REQ - 1.0 - rank
        aux[4:5, at] = jnp.where(target >= 0, partner * REQ + rank, -1.0).astype(i32)
        aux[5:8, at] = jnp.zeros((3, LANES), i32)
        ask = slots + 1.0
        high = jnp.floor(ask * (1.0 / 32)) * 32.0
        both = jnp.concatenate([named * high, named * (ask - high)], axis=0).astype(bf16)
        wanted = wanted + dot_last(both, one_hot(request == rank))
    return wanted[:ASKS] + wanted[ASKS:]


def prepare_kernel(devices, tiles, normals, speed, cluster, slot, links, orient, q, jac, small, aux, asks, group, one, record):
    me = lax.axis_index("dom")
    for face in range(4):
        small[3 * face : 3 * face + 3, :] = jnp.concatenate([normals[d, face : face + 1, :] for d in range(3)], axis=0)
    small[SPEED : SPEED + 1, :] = speed[...]
    small[CLUSTER : CLUSTER + 1, :] = cluster[...].astype(f32)
    small[LINK : LINK + 4, :] = links[...].astype(f32)
    small[ORIENT : ORIENT + 4, :] = orient[...].astype(f32)
    where = slot[...]
    stays = (where >= me * PARTITION_SLOTS) & (where < (me + 1) * PARTITION_SLOTS)
    small[OCCUPIED : OCCUPIED + 1, :] = jnp.where(stays, 1.0, 0.0)
    small[OCCUPIED + 1 : SMALL, :] = jnp.zeros((1, tiles * LANES), f32)
    wanted = find_links(devices, tiles, small, aux, False)
    asks[...] = jnp.zeros((devices, 1, LANES), f32)
    for k, offset in enumerate(partner_offsets(devices)):
        asks[lax.rem(me + offset + devices, devices)] = wanted[k : k + 1]

    record[...] = jnp.zeros((RECORD, LANES), f32)
    for p in range(NV):
        record[p * NBP : p * NBP + NB] = q[p]
        for inner in range(NV):
            at = ROWS + 4 * (p * NV + inner)
            record[at : at + 3] = jac[p, inner]
    fields = small[:, KEEP:]
    row = iota(fields.shape, 0)
    record[JAC_END : JAC_END + SMALL] = jnp.where(row == OCCUPIED, 1.0 - fields, fields)
    whole = record[...]
    turned = jnp.concatenate([whole[c : c + LANES].T for c in range(0, RECORD, LANES)], axis=1)
    one[...] = turned[:CSZ]
    position = me // (devices // GROUPS)
    for g in range(GROUPS):
        group[lax.rem(position + g, GROUPS)] = turned[g * CSZ : (g + 1) * CSZ]


def prepare(normals, speed, cluster, slot, links, orient, q, jac, devices):
    count = q.shape[2]

    def body(*refs):
        prepare_kernel(devices, count // LANES, *refs)

    last = KEEP // LANES
    return pl.pallas_call(
        body,
        grid=(1,),
        in_specs=[
            whole_spec(normals),
            whole_spec(speed),
            whole_spec(cluster),
            whole_spec(slot),
            whole_spec(links),
            whole_spec(orient),
            pl.BlockSpec((NV, NB, LANES), lambda i: (0, 0, last)),
            pl.BlockSpec((NV, NV, 3, LANES), lambda i: (0, 0, 0, last)),
        ],
        out_specs=[
            pl.BlockSpec((SMALL, count), lambda i: (0, 0)),
            pl.BlockSpec((8, count), lambda i: (0, 0)),
            pl.BlockSpec((devices, 1, LANES), lambda i: (0, 0, 0)),
            pl.BlockSpec((GROUPS, CSZ, RECORD), lambda i: (0, 0, 0)),
            pl.BlockSpec((CSZ, RECORD), lambda i: (0, 0)),
        ],
        out_shape=[
            jax.ShapeDtypeStruct((SMALL, count), f32),
            jax.ShapeDtypeStruct((8, count), i32),
            jax.ShapeDtypeStruct((devices, 1, LANES), f32),
            jax.ShapeDtypeStruct((GROUPS, CSZ, RECORD), f32),
            jax.ShapeDtypeStruct((CSZ, RECORD), f32),
        ],
        scratch_shapes=[pltpu.VMEM((RECORD, LANES), f32)],
        compiler_params=MOST,
        name="prepare",
    )(normals, speed, cluster, slot, links, orient, q, jac)


def unpack(devices, group, one, q, jac, small, aux):
    position = lax.axis_index("dom") // (devices // GROUPS)
    rows = [one[...]]
    for g in range(1, GROUPS):
        rows.append(group[lax.rem(position - g + GROUPS, GROUPS)])
    whole = jnp.concatenate(rows, axis=0)
    turned = jnp.concatenate([whole[:, c : c + LANES].T for c in range(0, RECORD, LANES)], axis=0)
    for p in range(NV):
        q[p] = turned[p * NBP : p * NBP + NB]
        for inner in range(NV):
            at = ROWS + 4 * (p * NV + inner)
            jac[p, inner] = turned[at : at + 3]
    small[...] = turned[JAC_END : JAC_END + SMALL]
    return find_links(devices, 1, small, aux, True)


OUT_BLOCKS = {1: (0, 0), 4: (0, 1), -2: (0, 2), -1: (1, 0), -4: (1, 1), 2: (1, 2), 3: (2, 0), -3: (3, 0)}
IN_BLOCKS = {-1: (0, 0), 1: (1, 0), -3: (2, 0), -4: (2, 1), -2: (2, 2), 3: (3, 0), 4: (3, 1), 2: (3, 2)}


def put(outs, rows, k, devices):
    if k == PARTNERS - 1:
        return outs[4], 0
    array, block = OUT_BLOCKS[-partner_offsets(devices)[k]]
    return outs[array], block * rows


def take(messages, k, devices):
    if k == PARTNERS - 1:
        return messages[4], 0
    array, block = IN_BLOCKS[partner_offsets(devices)[k]]
    rows = messages[4].shape[0]
    return messages[array], block * rows


def picked(requests, fields):
    lane = iota((1, LANES), 1)
    tiles = []
    for at in range(0, 12, 4):
        four = [requests[min(at + n, PARTNERS - 1)] for n in range(4)]
        tiles.append(
            jnp.where(lane < 32, four[0], jnp.where(lane < 64, four[1], jnp.where(lane < 96, four[2], four[3])))
        )
    slots = (iota((KEEP, FAR), 0) + 1).astype(f32)
    return dot(fields, one_hot(slots == jnp.concatenate(tiles, axis=1)))


def message_rows(both):
    value = both[:PACK] + both[PACK:]
    return jnp.concatenate([value, jnp.zeros((MSG - PACK, FAR), f32)], axis=0).T


def back(k):
    return k if k == PARTNERS - 1 else (k + 4) % 8


def requests_here(devices, asks):
    me = lax.axis_index("dom")
    peers = [lax.rem(me - o + devices, devices) for o in partner_offsets(devices)]
    return [asks[p] for p in peers]


def unpack_kernel(devices, group, one, asks, field, q, jac, small, aux, *outs):
    moved = unpack(devices, group, one, q, jac, small, aux)
    rows = message_rows(picked(requests_here(devices, asks), field[...]))
    for k in range(PARTNERS):
        out, at = put(outs, MESSAGE1, k, devices)
        out[at : at + REQ] = rows[k * REQ : (k + 1) * REQ]
        out[at + REQ : at + MESSAGE1, :LANES] = jnp.broadcast_to(moved[back(k) : back(k) + 1, :], (8, LANES))
        out[at + REQ : at + MESSAGE1, LANES:] = jnp.zeros((8, MSG - LANES), f32)


def answer_again(devices, asks, got, field, later, outs):
    moved = []
    for k in range(PARTNERS):
        message, at = take(got, back(k), devices)
        moved.append(message[at + REQ : at + REQ + 1, :LANES])
    every = [a + b for a, b in zip(requests_here(devices, asks), moved)]
    rows = message_rows(picked(every, later))
    rows_first = message_rows(picked(moved, field))
    for k in range(PARTNERS):
        out, at = put(outs, 2 * REQ, k, devices)
        out[at : at + REQ] = rows[k * REQ : (k + 1) * REQ]
        out[at + REQ : at + 2 * REQ] = rows_first[k * REQ : (k + 1) * REQ]


def relay_kernel(got_plus, got_minus, own_plus, own_minus, on_plus, on_minus):
    rows = own_plus.shape[0]
    block = [slice(b * rows, (b + 1) * rows) for b in range(3)]
    on_plus[block[0]] = own_plus[...]
    on_plus[block[1]] = got_plus[block[1]]
    on_plus[block[2]] = got_minus[block[2]]
    on_minus[block[0]] = own_minus[...]
    on_minus[block[1]] = got_minus[block[1]]
    on_minus[block[2]] = got_plus[block[2]]


def message_shapes(rows):
    return [jax.ShapeDtypeStruct((rows * blocks, MSG), f32) for blocks in (3, 3, 1, 1, 1)]


def far_table(devices, part, messages):
    rows = []
    for k in range(PARTNERS):
        message, at = take(messages, k, devices)
        rows.append(message[at + part * REQ : at + (part + 1) * REQ, :])
    rows.append(jnp.zeros((FAR - PARTNERS * REQ, MSG), f32))
    turned = jnp.concatenate(rows, axis=0).T[:PACK]
    return jnp.concatenate(split(turned), axis=0)


def take_turns(*chains):
    results = [None] * len(chains)
    going = list(range(len(chains)))
    while going:
        for n in list(going):
            try:
                next(chains[n])
            except StopIteration as stop:
                results[n] = stop.value
                going.remove(n)
    return results


def alone(chain):
    return take_turns(chain)[0]


class Window:
    def __init__(self, ref, begin, width):
        self.ref, self.begin = ref, begin
        self.shape = tuple(ref.shape[:-1]) + (width,)

    def _at(self, index):
        rank = len(self.shape)
        if index is Ellipsis:
            index = ()
        index = index if isinstance(index, tuple) else (index,)
        index = index + (slice(None),) * (rank - len(index))
        low, high, _ = index[-1].indices(self.shape[-1])
        return index[:-1] + (slice(self.begin + low, self.begin + high),)

    def __getitem__(self, index):
        return self.ref[self._at(index)]

    def __setitem__(self, index, value):
        self.ref[self._at(index)] = value


def lanes(tile):
    return slice(tile * LANES, (tile + 1) * LANES)


def jacobian_apply(jac, tile, parts):
    result = [None] * NV
    for group in range(3):
        for d in range(3):
            for inner in range(3):
                q = 3 * group + inner
                value = parts(d, q)
                for p in range(NV):
                    term = jac[p, q, d : d + 1, lanes(tile)] * value
                    result[p] = term if result[p] is None else result[p] + term
    return result


def packed_split(fields, group):
    packed = [pack_three(tile[3 * group : 3 * group + 3]) for tile in fields]
    return split(jnp.concatenate(packed, axis=1))


def split_fields(fields):
    pairs = [packed_split(fields, group) for group in range(3)]
    return jnp.concatenate([a for a, _ in pairs] + [b for _, b in pairs], axis=0)


def predict(chains, w_pred):
    for state, _, sums in chains:
        for ref, scale in sums:
            for p in range(NV):
                ref[p] = scale[0] * state[p]

    def degree_step(degree, carry):
        turned = []
        for state, _, _ in chains:
            now = load_field(state)
            turned.append([dot(w_pred[...], stacked(*packed_split(now, group))) for group in range(3)])
        for (state, jac, sums), of in zip(chains, turned):
            scales = [jnp.where(degree == 1, s[1], jnp.where(degree == 2, s[2], s[3])) for _, s in sums]
            for t in range(state.shape[2] // LANES):
                at = lanes(t)
                result = jacobian_apply(
                    jac, t, lambda d, q: of[q // 3][d * 72 + (q % 3) * NBP : d * 72 + (q % 3) * NBP + NBP, at]
                )
                for p in range(NV):
                    state[p, :, at] = result[p]
                    for (ref, _), scale in zip(sums, scales):
                        ref[p, :, at] = ref[p, :, at] + scale * result[p]
        return carry

    lax.fori_loop(1, NORDER, degree_step, 0)


def face_products(gathered, table, tiles):
    outers = []
    for t in tiles:
        outer = [None] * NV
        for b in range(NB):
            values = table[b * NQ : (b + 1) * NQ, lanes(t)]
            for p in range(NV):
                at = packed_row(p, b)
                term = gathered[at : at + 1, lanes(t)] * values
                outer[p] = term if outer[p] is None else outer[p] + term
        outers.append(outer)
    return [
        stacked(*split(jnp.concatenate([jnp.concatenate(o[3 * g : 3 * g + 3], axis=0) for o in outers], axis=1)))
        for g in range(3)
    ]


def table_of(code, w_table):
    hot = one_hot(iota((16, code.shape[1]), 0).astype(f32) == code)
    return dot(w_table, jnp.concatenate([hot, hot], axis=0))


class NearChain:
    def __init__(self, near, weights, small, aux, gathered, table, by_face, parts):
        self.near, self.small, self.aux, self.gathered, self.table = near, small, aux, gathered, table
        self.by_face, self.parts = by_face, parts
        self.weights = weights
        self.count = aux.shape[-1]
        self.tiles = range(self.count // LANES)

    def begin(self, own):
        for group in range(3):
            rows = slice(64 * group, 64 * group + 64)
            lower = slice(PACK + 64 * group, PACK + 64 * group + 64)
            mine = dot(self.weights[:LIFT_AT, :], stacked(own[rows], own[lower]))
            for inner in range(3):
                q = 3 * group + inner
                of = [mine[72 * block + NBP * inner : 72 * block + NBP * inner + NBP] for block in range(8)]
                for d in range(3):
                    self.parts[d * NV + q] = of[d]
                for face in range(4):
                    self.by_face[face, q] = of[3 + face]
                self.parts[3 * NV + q] = of[7]

    def gather(self, face):
        count = self.count
        slots = iota((KEEP, count), 0).astype(jnp.int16)
        index = jnp.broadcast_to(self.aux[pl.ds(face, 1), :], (16, count)).astype(jnp.int16)
        index = jnp.concatenate([index] * (KEEP // 16), axis=0)
        both = dot(self.near[...], jnp.where(slots == index, jnp.ones((), bf16), jnp.zeros((), bf16)))
        self.gathered[...] = both[:PACK] + both[PACK:]
        self.table[...] = table_of(self.small[pl.ds(ORIENT + face, 1), :], self.weights[TABLE_AT:, :32])

    def products(self, face):
        normals = [self.small[pl.ds(3 * face + d, 1), :] for d in range(3)]
        for group, points in enumerate(face_products(self.gathered, self.table, self.tiles)):
            lifted = dot(self.weights[pl.ds(pl.multiple_of(LIFT_AT + 144 * face, 16), 144), :144], points)
            for inner in range(3):
                q = 3 * group + inner
                at = inner * NBP
                mixed = lifted[at : at + NBP] + self.by_face[face, q]
                self.parts[3 * NV + q] = self.parts[3 * NV + q] + lifted[72 + at : 72 + at + NBP]
                for d in range(3):
                    self.parts[d * NV + q] = self.parts[d * NV + q] + normals[d] * mixed


def near_part(chains, owns, together):
    chains[0].gather(0)
    for chain, own in zip(chains, owns):
        chain.begin(own)

    def some_faces(step, carry):
        for n in range(together):
            face = step * together + n
            for other in chains[1:]:
                other.gather(face)
            chains[0].products(face)
            if together < 4 or n < 3:
                chains[0].gather((face + 1) & 3)
            for other in chains[1:]:
                other.products(face)
        return carry

    if together == 4:
        some_faces(0, 0)
    else:
        lax.fori_loop(0, 4 // together, some_faces, 0)


def update_chain(parts, far, small, aux, jac, w_far, w_table, gathered):
    volume, upwind = parts
    tiles = range(len(volume))
    count = len(volume) * LANES
    place = aux[4:5, :]
    both = dot(far, one_hot(iota((FAR, count), 0) == place))
    gathered[...] = both[:PACK] + both[PACK:]
    masks = [jnp.where((aux[face : face + 1, :] < 0) & (place >= 0), 1.0, 0.0) for face in range(4)]
    code = masks[0] * small[ORIENT : ORIENT + 1, :]
    normals = [masks[0] * small[d : d + 1, :] for d in range(3)]
    for face in range(1, 4):
        code = code + masks[face] * small[ORIENT + face : ORIENT + face + 1, :]
        normals = [n + masks[face] * small[3 * face + d : 3 * face + d + 1, :] for d, n in enumerate(normals)]
    changes = [[None] * NV for t in tiles]
    table = table_of(code, w_table)
    yield
    volume = [[list(v) for v in tile] for tile in volume]
    upwind = [list(tile) for tile in upwind]
    for group, points in enumerate(face_products(gathered, table, tiles)):
        lifted = dot(w_far, points)
        for t in tiles:
            for inner in range(3):
                q = 3 * group + inner
                mixed = None
                for face in range(4):
                    at = 72 * face + inner * NBP
                    term = masks[face][:, lanes(t)] * lifted[at : at + NBP, lanes(t)]
                    mixed = term if mixed is None else mixed + term
                upwind[t][q] = upwind[t][q] - mixed
                for d in range(3):
                    volume[t][d][q] = volume[t][d][q] + normals[d][:, lanes(t)] * mixed
    for t in tiles:
        change = jacobian_apply(jac, t, lambda d, q: volume[t][d][q])
        speed = small[SPEED : SPEED + 1, lanes(t)]
        changes[t] = [c + speed * u for c, u in zip(change, upwind[t])]
    return changes


def update(*args):
    return alone(update_chain(*args))


def load_parts(ref):
    tiles = range(ref.shape[2] // LANES)
    volume = [[[ref[d * NV + q, :, lanes(t)] for q in range(NV)] for d in range(3)] for t in tiles]
    return volume, [[ref[3 * NV + q, :, lanes(t)] for q in range(NV)] for t in tiles]


def load_state(q, padded):
    padded[:, NB:NBP, :] = jnp.zeros((NV, NBP - NB, padded.shape[2]), f32)
    for p in range(NV):
        padded[p, :NB, :] = q[p]
    return load_field(padded)


def load_field(ref):
    return [[ref[p, :, lanes(t)] for p in range(NV)] for t in range(ref.shape[2] // LANES)]


def store_field(ref, field):
    for t, tile in enumerate(field):
        for p in range(NV):
            ref[p, :, lanes(t)] = tile[p]


def store_result(out, base, change, small):
    for t in range(len(base)):
        occupied = small[OCCUPIED : OCCUPIED + 1, lanes(t)] > 0.5
        for p in range(NV):
            out[p, :, lanes(t)] = jnp.where(occupied, base[t][p] + change[t][p], 0.0)[:NB]


def first_kernel(
    q, jac, deriv, stiff, evals, lift, packed, slow, w_pred, w_near, w_far, padded, sums, square
):
    @pl.when(pl.program_id(0) == 0)
    def _():
        make_weights(deriv, stiff, evals, lift, w_pred, w_near, w_far, square)

    load_state(q, padded)
    chains = []
    for begin in range(0, BOTH, WIDE):
        state, jacobians, early, late = [Window(r, begin, WIDE) for r in (padded, jac, sums, slow)]
        chains.append((state, jacobians, [(early, FIRST), (late, SECOND)]))
    predict(chains, w_pred)
    packed[...] = split_fields(load_field(sums))


def near_kernel(own, near, small, aux, w_near, *refs):
    parts, gathered, table, by_face = refs[-4:]
    chains, owns = [], []
    for begin in range(0, BOTH, WIDE):
        windows = [Window(r, begin, WIDE) for r in (small, aux, gathered, table, by_face, parts)]
        chains.append(NearChain(near, w_near, *windows))
        owns.append(Window(own, begin, WIDE))
    near_part(chains, owns, 4)


def middle_steps(chains, far, w_pred, w_far, w_table):
    updates = []
    for _, parts, jac, small, _, aux, gathered, _, _, _ in chains:
        updates.append(update_chain(load_parts(parts), far, small, aux, jac, w_far, w_table, gathered))
    for chain, change in zip(chains, take_turns(*updates)):
        q, _, _, small, _, _, _, base, state, _ = chain
        start = load_state(q, state)
        for t in range(len(start)):
            fast = small[CLUSTER : CLUSTER + 1, lanes(t)] < 0.5
            for p in range(NV):
                now = start[t][p] + change[t][p]
                base[p, :, lanes(t)] = now
                state[p, :, lanes(t)] = jnp.where(fast, now, start[t][p])
    predict([(chain[8], chain[2], [(chain[9], FIRST)]) for chain in chains], w_pred)
    results = []
    for _, _, _, small, slow, _, _, _, _, sums in chains:
        second = []
        for t, (late, later) in enumerate(zip(load_field(slow), load_field(sums))):
            fast = small[CLUSTER : CLUSTER + 1, lanes(t)] < 0.5
            second.append([jnp.where(fast, a, b) for a, b in zip(later, late)])
        results.append(split_fields(second))
    return results


def middle_kernel(devices, steps, q, jac, small, slow, parts, near, aux, asks, *refs):
    messages = refs[:5]
    w_pred, w_far, w_near, base, packed, *outs, padded, sums, gathered, far = refs[5:]
    step = pl.program_id(0)

    @pl.when(step == 0)
    def _():
        far[...] = far_table(devices, 0, messages)

    refs = (q, parts, jac, small, slow, aux, gathered, base, padded, sums)
    chains = [[Window(r, begin, WIDE) for r in refs] for begin in range(0, BOTH, WIDE)]
    second = jnp.concatenate(middle_steps(chains, far[...], w_pred, w_far[...], w_near[TABLE_AT:, :32]), axis=1)
    packed[:, pl.ds(pl.multiple_of(step * BOTH, BOTH), BOTH)] = second

    @pl.when(step == steps - 1)
    def _():
        answer_again(devices, asks, messages, near[...], packed[:, :KEEP], outs)


def last_kernel(
    devices, steps, base, jac, small, parts, aux, q_moved, jac_moved, small_moved, aux_moved, near, later, *refs
):
    messages = refs[:5]
    w_pred, w_near, w_far, out, gathered, far = refs[5:11]
    padded, gathered_moved, table, by_face, parts_moved, early, late, now = refs[11:]
    w_table = w_near[TABLE_AT:, :32]
    step = pl.program_id(0)

    @pl.when(step == 0)
    def _():
        far[...] = far_table(devices, 0, messages)

    @pl.when(step < steps)
    def _():
        table_far = far[...]
        chains, stores = [], []
        for begin in range(0, BOTH, WIDE):
            w = [Window(r, begin, WIDE) for r in (parts, small, aux, jac, gathered, out, base)]
            chains.append(
                update_chain(load_parts(w[0]), table_far, w[1], w[2], w[3], w_far[...], w_table, w[4])
            )
            stores.append((w[5], w[6], w[1]))
        for (to, start, fields), change in zip(stores, take_turns(*chains)):
            store_result(to, load_field(start), change, fields)

    @pl.when(step == steps)
    def _():
        load_state(q_moved, padded)
        predict([(padded, jac_moved, [(early, FIRST), (late, SECOND)])], w_pred)
        chain = NearChain(
            near, w_near, small_moved, aux_moved, gathered_moved, table, by_face, parts_moved
        )
        near_part([chain], [split_fields(load_field(early))], 1)
        fields = (q_moved, parts_moved, jac_moved, small_moved, late, aux_moved, gathered_moved, now, padded, early)
        far_first = far_table(devices, 1, messages)
        (second,) = middle_steps([fields], far_first, w_pred, w_far[...], w_table)
        chain.near = later
        near_part([chain], [second], 1)
        change = update(
            load_parts(parts_moved), far[...], small_moved, aux_moved, jac_moved, w_far[...], w_table,
            gathered_moved,
        )
        store_result(out, load_field(now), change, small_moved)


def whole_spec(array):
    rank = array.ndim
    return pl.BlockSpec(array.shape, lambda i: (0,) * rank)


def lane_spec(*lead, last=None):
    rank = len(lead)
    if last is None:
        return pl.BlockSpec(lead + (WIDE,), lambda i: (0,) * rank + (i,))
    return pl.BlockSpec(lead + (BOTH,), lambda i: (0,) * rank + (jnp.minimum(i, last),))


Q_SPEC = lane_spec(NV, NB)
J_SPEC = lane_spec(NV, NV, 3)
S_SPEC = lane_spec(SMALL)
A_SPEC = lane_spec(8)
F_SPEC = lane_spec(NV, NBP)
X_SPEC = lane_spec(2 * PACK)
N_SPEC = pl.BlockSpec((2 * PACK, KEEP), lambda i: (0, 0))


def padded_scratch(width):
    return pltpu.VMEM((NV, NBP, width), f32)


def gathered_scratch(width):
    return pltpu.VMEM((PACK, width), f32)


def near_scratch(width):
    return [gathered_scratch(width), pltpu.VMEM((320, width), f32), pltpu.VMEM((4, NV, NBP, width), f32)]


def per_device(
    element_freedom_values,
    scaled_jacobian_matrices,
    outward_face_normals,
    largest_wave_speed,
    element_cluster_index,
    element_new_slot,
    neighbours,
    face_rotation_codes,
    deriv_mats,
    stiff_mats,
    face_eval,
    face_lift,
):
    count = element_freedom_values.shape[2]
    steps = count // WIDE
    devices = lax.axis_size("dom")
    q = element_freedom_values
    jac = jnp.transpose(scaled_jacobian_matrices, (1, 2, 0, 3))

    def shift(array, by):
        return lax.ppermute(array, "dom", [(i, (i + by) % devices) for i in range(devices)])

    def swap(array, groups):
        return lax.all_to_all(array, "dom", split_axis=0, concat_axis=0, axis_index_groups=groups, tiled=True)

    def on_ring(body):
        def kernel(*refs):
            body(devices, *refs)

        return kernel

    small, aux, asks, group, one = prepare(
        jnp.transpose(outward_face_normals, (1, 0, 2)),
        largest_wave_speed[None],
        element_cluster_index[None],
        element_new_slot[None],
        neighbours,
        face_rotation_codes,
        q,
        jac,
        devices,
    )
    asks = swap(asks, None)
    asks, group, one = lax.optimization_barrier((asks, group, one))
    stride = devices // GROUPS
    group = swap(group, [[r + stride * j for j in range(GROUPS)] for r in range(stride)])
    one = shift(one, 1)
    packed_shape = jax.ShapeDtypeStruct((2 * PACK, count), bf16)
    field_shape = jax.ShapeDtypeStruct((NV, NBP, count), f32)
    far = pltpu.VMEM((2 * PACK, FAR), bf16)
    weight_shapes = [
        jax.ShapeDtypeStruct((ROWS, PACK), bf16),
        jax.ShapeDtypeStruct((NEAR_ROWS, PACK), bf16),
        jax.ShapeDtypeStruct((288, 144), bf16),
    ]
    evals = jnp.transpose(face_eval, (0, 2, 1)).reshape(12 * NQ, NB)
    matrices = [deriv_mats, stiff_mats, evals, face_lift]
    halves = count // BOTH

    def part_spec(begin, *lead):
        rank = len(lead)
        return pl.BlockSpec(lead + (BOTH,), lambda i: (0,) * rank + (i + begin,))

    first, slow, w_pred, w_near, w_far = pl.pallas_call(
        first_kernel,
        grid=(halves,),
        in_specs=[part_spec(0, NV, NB), part_spec(0, NV, NV, 3)] + [whole_spec(m) for m in matrices],
        out_specs=[part_spec(0, 2 * PACK), part_spec(0, NV, NBP)] + [whole_spec(w) for w in weight_shapes],
        out_shape=[packed_shape, field_shape] + weight_shapes,
        scratch_shapes=[padded_scratch(BOTH), padded_scratch(BOTH), pltpu.VMEM((LANES, LANES), f32)],
        compiler_params=MOST,
        name="first",
    )(q, jac, *matrices)

    moved_shapes = [
        jax.ShapeDtypeStruct((NV, NB, LANES), f32),
        jax.ShapeDtypeStruct((NV, NV, 3, LANES), f32),
        jax.ShapeDtypeStruct((SMALL, LANES), f32),
        jax.ShapeDtypeStruct((8, LANES), i32),
    ]
    out_shape = moved_shapes + message_shapes(MESSAGE1)
    *moved, m0, m1, m2, m3, m4 = pl.pallas_call(
        on_ring(unpack_kernel),
        grid=(1,),
        in_specs=[whole_spec(a) for a in (group, one, asks)] + [N_SPEC],
        out_specs=[whole_spec(o) for o in out_shape],
        out_shape=out_shape,
        compiler_params=MOST,
        name="unpack",
    )(group, one, asks, first)
    of_near = [w_near]
    parts_shape = jax.ShapeDtypeStruct((4 * NV, NBP, count), f32)

    def near_steps(field, begin, number, parts):
        def spec(*lead):
            return part_spec(begin, *lead)

        return pl.pallas_call(
            near_kernel,
            grid=(number,),
            in_specs=[spec(2 * PACK), N_SPEC, spec(SMALL), spec(8)]
            + [whole_spec(w) for w in of_near]
            + [pl.BlockSpec(memory_space=pl.ANY)] * len(parts),
            out_specs=spec(4 * NV, NBP),
            out_shape=parts_shape,
            scratch_shapes=near_scratch(BOTH),
            input_output_aliases={5: 0} if parts else {},
            cost_estimate=pl.CostEstimate(flops=int(4e9) * number, bytes_accessed=4 << 20, transcendentals=0),
            compiler_params=PARAMS,
            name="near",
        )(field, field, small, aux, *of_near, *parts)

    def exchange_beside(answers, field):
        half = halves // 2
        plus, minus, own_plus, own_minus, opposite = answers
        got_plus, got_minus, opposite = shift(plus, 1), shift(minus, -1), shift(opposite, devices // 2)
        parts = near_steps(field, 0, half, [])
        got_plus, got_minus, opposite, parts = lax.optimization_barrier((got_plus, got_minus, opposite, parts))
        on_plus, on_minus = pl.pallas_call(
            relay_kernel,
            out_shape=[jax.ShapeDtypeStruct(plus.shape, f32)] * 2,
            compiler_params=pltpu.CompilerParams(vmem_limit_bytes=4 << 20),
            name="relay",
        )(got_plus, got_minus, own_plus, own_minus)
        on_plus, on_minus = shift(on_plus, 3), shift(on_minus, -3)
        parts = near_steps(field, half, halves - half, [parts])
        return (got_plus, got_minus, on_plus, on_minus, opposite), parts

    messages, parts = exchange_beside((m0, m1, m2, m3, m4), first)

    def middle(*refs):
        middle_kernel(devices, halves, *refs)

    weights = [w_pred, w_far, w_near]
    out_shape = [field_shape, packed_shape] + message_shapes(2 * REQ)
    base, second, *answers = pl.pallas_call(
        middle,
        grid=(halves,),
        in_specs=[
            part_spec(0, NV, NB),
            part_spec(0, NV, NV, 3),
            part_spec(0, SMALL),
            part_spec(0, NV, NBP),
            part_spec(0, 4 * NV, NBP),
            N_SPEC,
            part_spec(0, 8),
            whole_spec(asks),
        ]
        + [whole_spec(a) for a in (*messages, *weights)],
        out_specs=[part_spec(0, NV, NBP)] + [whole_spec(o) for o in out_shape[1:]],
        out_shape=out_shape,
        scratch_shapes=[padded_scratch(BOTH), padded_scratch(BOTH), gathered_scratch(BOTH), far],
        compiler_params=PARAMS,
        name="middle",
    )(q, jac, small, slow, parts, first, aux, asks, *messages, *weights)
    messages, parts = exchange_beside(answers, second)

    def last(*refs):
        last_kernel(devices, halves, *refs)

    end = halves - 1
    weights = [w_pred, w_near, w_far]
    return pl.pallas_call(
        last,
        grid=(halves + 1,),
        in_specs=[
            lane_spec(NV, NBP, last=end),
            lane_spec(NV, NV, 3, last=end),
            lane_spec(SMALL, last=end),
            lane_spec(4 * NV, NBP, last=end),
            lane_spec(8, last=end),
        ]
        + [whole_spec(a) for a in moved]
        + [N_SPEC, N_SPEC]
        + [whole_spec(a) for a in (*messages, *weights)],
        out_specs=part_spec(0, NV, NB),
        out_shape=jax.ShapeDtypeStruct((NV, NB, PARTITION_SLOTS), f32),
        scratch_shapes=[
            gathered_scratch(BOTH),
            far,
            padded_scratch(LANES),
            *near_scratch(LANES),
            pltpu.VMEM((4 * NV, NBP, LANES), f32),
            *[padded_scratch(LANES)] * 3,
        ],
        compiler_params=PARAMS,
        name="last",
    )(base, jac, small, parts, aux, *moved, first, second, *messages, *weights)


def solution(mesh):
    placed = (
        P(None, None, "dom"),
        P(None, None, None, "dom"),
        P(None, None, "dom"),
        P("dom"),
        P("dom"),
        P("dom"),
        P(None, "dom"),
        P(None, "dom"),
        P(),
        P(),
        P(),
        P(),
    )
    return jax.shard_map(
        per_device, mesh=mesh, in_specs=placed, out_specs=P(None, None, "dom"), check_vma=False
    )
```
